32 devices in a mesh: dp: 16 (over z, y, core), mp: 2 (over x).
Axes of the slice: x: 2, y: 2, z: 4, core: 2. Of those that a mesh axis runs over, the one named last changes fastest.
Arguments:
- tokens: bfloat16 [32768, 1152], P(('dp', 'mp')), may hold values from -6 to 6
- conditioning: bfloat16 [128, 1152], P('dp'), may hold values from -6 to 6
- kept_ids: int32 [128, 179], P('dp'), may hold values from 0 to 255, as said below
- ada_weight: bfloat16 [1152, 6912], P(None, 'mp'), may hold values from -0.1875 to 0.1875
- ada_bias: float32 [6912], P('mp'), may hold values from -3 to 3
- attn_qkv: bfloat16 [1152, 3, 1152], P(None, None, 'mp'), may hold values from -0.1875 to 0.1875
- attn_out: bfloat16 [1152, 1152], P('mp'), may hold values from -0.75 to 0.75
- mlp_up: bfloat16 [1152, 4608], P(None, 'mp'), may hold values from -0.1875 to 0.1875
- mlp_down: bfloat16 [4608, 1152], P('mp'), may hold values from -0.09375 to 0.09375
- rel_table: float32 [16, 961], P('mp'), may hold values from -4 to 4
- grad_out_kept: bfloat16 [22912, 1152], P(('dp', 'mp')), may hold values from -6 to 6
- grad_out_full: bfloat16 [32768, 1152], P(('dp', 'mp')), may hold values from -6 to 6
Outputs:
- out_kept: bfloat16 [22912, 1152], P(('dp', 'mp'))
- out_full: bfloat16 [32768, 1152], P(('dp', 'mp'))
- grad_tokens: bfloat16 [32768, 1152], P(('dp', 'mp'))
- grad_cond: bfloat16 [128, 1152], P(('dp', 'mp'))
- grad_ada_weight: float32 [1152, 6912], P('dp', 'mp')
- grad_ada_bias: float32 [6912], P('mp')
- grad_attn_qkv: float32 [1152, 3, 1152], P('dp', None, 'mp')
- grad_attn_out: float32 [1152, 1152], P('mp', 'dp')
- grad_mlp_up: float32 [1152, 4608], P('dp', 'mp')
- grad_mlp_down: float32 [4608, 1152], P('mp', 'dp')
- grad_rel_table: float32 [16, 961], P('mp')
The draws below stay inside these ranges and needn't reach their ends.
Inputs may be any that keep to these rules, and one draw needn't show every extreme that they name: `kept_ids`: each row holds 179 distinct patch indices of its image in ascending order.
All inputs are finite; a program needn't handle non-finite values.
Results may differ from the reference program's by a relative error of at most 0.02.
The reference program's roundings to bfloat16 on the way count: a program that leaves them out, or rounds other values in their place, can miss the bound.
Values may be sent and summed in bfloat16 or wider, within the bound.
A program may use at most 448 MiB of HBM per device.

```python
import jax
import jax.numpy as jnp
from jax import lax

D = 1152
HEADS = 16
HEAD_DIM = 72
FF = 4608
GRID = 16
IMG_DEV = 8
PATCHES = 256
KEEP = 179
BUCKETS = 961
IMG = 128
TOKENS = 32768


def draw_kept_ids(key, part):
    image_keys = jax.random.split(key, IMG)
    shuffled = jax.vmap(lambda one_key: jax.random.permutation(one_key, PATCHES))(image_keys)
    return jnp.sort(shuffled[:, :KEEP], axis=1).astype(jnp.int32)


def levels(rng, extent, pieces, low, top_value):
    def one(axis_at, blocks):
        heights = jax.random.uniform(jax.random.fold_in(jax.random.fold_in(rng, 6), axis_at), (blocks,), jnp.float32, low / len(pieces), top_value / len(pieces))
        return jnp.repeat(jnp.exp(heights), extent[axis_at] // blocks).reshape((-1,) + (1,) * (len(extent) - axis_at - 1))

    factor_of = one(*pieces[0])
    for cut in pieces[1:]:
        factor_of = factor_of * one(*cut)
    return factor_of


def centred(rng, extent, width, limit, cuts=(), kind=jnp.bfloat16):
    loudness = levels(rng, extent, cuts, -0.22, 0.18) if cuts else 1.0
    entries = jax.random.normal(rng, extent, jnp.float32) * width * loudness
    return jnp.minimum(jnp.maximum(entries, -limit), limit).astype(kind)


def setup_inputs(seed: int = 0) -> dict:
    keys = jax.random.split(jax.random.key(seed), 13)
    tokens = centred(keys[0], (TOKENS, D), 1.0, 6.0, ((0, 32),))
    conditioning = centred(keys[1], (IMG, D), 1.0, 6.0, ((0, 16),))
    kept_ids = draw_kept_ids(jax.random.fold_in(keys[12], 71), 0)
    ada_weight = centred(keys[3], (D, 6 * D), D ** -0.5, 0.1875, ((1, 2),))
    ada_bias = centred(keys[4], (6 * D,), 0.5, 3.0, ((0, 2),), jnp.float32)
    attn_qkv = centred(keys[5], (D, 3, D), D ** -0.5, 0.1875, ((2, 2),))
    attn_out = centred(keys[6], (D, D), (D // 16) ** -0.5, 0.75, ((0, 2),))
    mlp_up = centred(keys[7], (D, FF), D ** -0.5, 0.1875, ((1, 2),))
    mlp_down = centred(keys[8], (FF, D), FF ** -0.5, 0.09375, ((0, 2),))
    rel_table = centred(keys[9], (HEADS, BUCKETS), 1.0, 4.0, ((0, 2),), jnp.float32)
    grad_out_kept = centred(keys[10], (IMG * KEEP, D), 1.0, 6.0, ((0, 32),))
    grad_out_full = centred(keys[11], (TOKENS, D), 1.0, 6.0, ((0, 32),))
    return {"tokens": tokens, "conditioning": conditioning, "kept_ids": kept_ids, "ada_weight": ada_weight, "ada_bias": ada_bias, "attn_qkv": attn_qkv, "attn_out": attn_out, "mlp_up": mlp_up, "mlp_down": mlp_down, "rel_table": rel_table, "grad_out_kept": grad_out_kept, "grad_out_full": grad_out_full}


EPSILON = 1e-06
PRECISE = lax.Precision.HIGHEST

@jax.custom_vjp
def low(v):
    return lax.optimization_barrier(v.astype(jnp.bfloat16)).astype(jnp.float32)

@jax.custom_vjp
def low_back(v):
    return v

def low_keep(v):
    return (low(v), None)

def low_pass(kept, grad):
    return (grad,)

def back_keep(v):
    return (v, None)

def back_low(kept, grad):
    return (low(grad),)
low.defvjp(low_keep, low_pass)
low_back.defvjp(back_keep, back_low)

def normalize(rows):
    row_mean = lax.optimization_barrier(jnp.mean(rows, axis=-1, keepdims=True))
    centered = rows - row_mean
    return centered * lax.rsqrt(lax.optimization_barrier(jnp.mean(centered * centered, axis=-1, keepdims=True)) + EPSILON)

def relative_index(query_pos, key_pos):
    bucket_span = 2 * GRID - 1
    row_gap = query_pos[..., :, None] // GRID - key_pos[..., None, :] // GRID + GRID - 1
    column_gap = query_pos[..., :, None] % GRID - key_pos[..., None, :] % GRID + GRID - 1
    return (row_gap * bucket_span + column_gap).astype(jnp.int32)

def layer_pass(resid, modulation, bias, weights):
    attn_qkv, attn_out, mlp_up, mlp_down = weights
    shift_one, scale_one, gate_one, shift_two, scale_two, gate_two = [modulation[:, column][:, None, :] for column in range(6)]
    image_count, row_count, model_width = resid.shape
    first_in = low(normalize(resid) * (1.0 + scale_one) + shift_one)
    projected = jnp.einsum('nld,dce->nlce', first_in, attn_qkv, precision=PRECISE)
    projected = projected.reshape(image_count, row_count, 3, HEADS, HEAD_DIM)
    queries = low_back(low(projected[:, :, 0]))
    key_rows = low_back(low(projected[:, :, 1]))
    values = low_back(low(projected[:, :, 2]))
    scores = low_back(jnp.einsum('nqhd,nkhd->nhqk', queries, key_rows, precision=PRECISE) * HEAD_DIM ** (-0.5) + bias)
    attn_probs = low(jax.nn.softmax(scores, axis=-1))
    attended = low_back(low(jnp.einsum('nhqk,nkhd->nqhd', attn_probs, values, precision=PRECISE)))
    attended = attended.reshape(image_count, row_count, model_width)
    branch_attn = low_back(jnp.einsum('nld,de->nle', attended, attn_out, precision=PRECISE))
    middle = resid + gate_one * branch_attn
    second = low(normalize(middle) * (1.0 + scale_two) + shift_two)
    hidden_pre = low_back(jnp.einsum('nld,df->nlf', second, mlp_up, precision=PRECISE))
    hidden = low(jax.nn.gelu(hidden_pre, approximate=True))
    branch_mlp = low_back(jnp.einsum('nlf,fd->nld', hidden, mlp_down, precision=PRECISE))
    return middle + gate_two * branch_mlp

def group_layer(token_group, cond_group, kept_group, params):
    ada_weight, ada_bias, attn_qkv, attn_out, mlp_up, mlp_down, rel_table = params
    image_count = cond_group.shape[0]
    modulation = low(jnp.dot(low(jax.nn.silu(cond_group)), ada_weight, precision=PRECISE) + ada_bias)
    modulation = modulation.reshape(image_count, 6, D)
    patch_ids = jnp.arange(PATCHES, dtype=jnp.int32)
    picker = (kept_group[:, :, None] == patch_ids[None, None, :]).astype(jnp.float32)
    kept_rows = jnp.einsum('nkp,npd->nkd', picker, token_group, precision=PRECISE)
    bias_full = jnp.take(rel_table, relative_index(patch_ids, patch_ids), axis=1)[None]
    bias_kept = jnp.transpose(jnp.take(rel_table, relative_index(kept_group, kept_group), axis=1), (1, 0, 2, 3))
    weights = (attn_qkv, attn_out, mlp_up, mlp_down)
    return (layer_pass(kept_rows, modulation, bias_kept, weights), layer_pass(token_group, modulation, bias_full, weights))

def layer_forward(token_values, cond_values, kept_ids, params):
    groups = cond_values.shape[0] // IMG_DEV
    group_items = (token_values.reshape(groups, IMG_DEV, PATCHES, D), cond_values.reshape(groups, IMG_DEV, D), kept_ids.reshape(groups, IMG_DEV, KEEP))
    step_layer = jax.checkpoint(lambda items: group_layer(items[0], items[1], items[2], params))
    outs_kept, outs_full = lax.map(step_layer, group_items)
    return (outs_kept.reshape(-1, D), outs_full.reshape(-1, D))

def reference(tokens, conditioning, kept_ids, ada_weight, ada_bias, attn_qkv, attn_out, mlp_up, mlp_down, rel_table, grad_out_kept, grad_out_full):
    primals = tuple((member.astype(jnp.float32) for member in (tokens, conditioning, ada_weight, ada_bias, attn_qkv, attn_out, mlp_up, mlp_down, rel_table)))

    def forward(token_values, cond_values, *params):
        return layer_forward(token_values, cond_values, kept_ids, params)
    (outs_kept, outs_full), pullback = jax.vjp(forward, *primals)
    gradients = pullback((grad_out_kept.astype(jnp.float32), grad_out_full.astype(jnp.float32)))
    return (outs_kept.astype(jnp.bfloat16), outs_full.astype(jnp.bfloat16), gradients[0].astype(jnp.bfloat16), gradients[1].astype(jnp.bfloat16), gradients[2], gradients[3], gradients[4], gradients[5], gradients[6], gradients[7], gradients[8])
```

```python
import functools
import math

import jax
import jax.numpy as jnp
from jax import lax
from jax.experimental import pallas as pl
from jax.experimental.pallas import tpu as pltpu
from jax.sharding import PartitionSpec as P

HEAD_DIM = 72
GRID = 16
PATCHES = 256
BUCKETS = 961
SPAN = 2 * GRID - 1
EPSILON = 1e-06
PRECISE = lax.Precision.HIGHEST
BF = jnp.bfloat16
F32 = jnp.float32
LOG2E = math.log2(math.e)
VMEM_LIMIT = 60 * 1024 * 1024


def dot(a, b, dims):
    return lax.dot_general(a, b, ((dims[0:1], dims[1:2]), ((), ())), preferred_element_type=F32)


def nn(a, b):
    return dot(a, b, (1, 0))


def nt(a, b):
    return dot(a, b, (1, 1))


def tn(a, b):
    return dot(a, b, (0, 0))


def normalize(rows):
    centered = rows - jnp.mean(rows, axis=-1, keepdims=True)
    inverse = lax.rsqrt(jnp.mean(centered * centered, axis=-1, keepdims=True) + EPSILON)
    return centered * inverse, inverse


def norm_back(normed, inverse, upstream):
    return inverse * (
        upstream
        - jnp.mean(upstream, axis=-1, keepdims=True)
        - normed * jnp.mean(upstream * normed, axis=-1, keepdims=True)
    )


def params(n_grid=1):
    return pltpu.CompilerParams(
        vmem_limit_bytes=VMEM_LIMIT, dimension_semantics=("arbitrary",) * n_grid
    )


def cost(flops, bytes_accessed, transcendentals=0):
    return pl.CostEstimate(
        flops=int(flops), bytes_accessed=int(bytes_accessed), transcendentals=int(transcendentals)
    )


def const_spec(shape):
    return pl.BlockSpec(shape, lambda *_: (0,) * len(shape), pipeline_mode=pl.Buffered(1))


def bias_kernel(strip_ref, bias_ref):
    strip = strip_ref[0]
    for key_row in range(GRID):
        start = (GRID - 1 - key_row) * GRID
        bias_ref[0, key_row * GRID : (key_row + 1) * GRID, :] = strip[:, start : start + PATCHES]


def bias_whole(table):
    heads = table.shape[0]
    grid_table = table.reshape(heads, SPAN, SPAN) * LOG2E
    strip = jnp.stack(
        [grid_table[:, :, GRID - 1 - c : 2 * GRID - 1 - c] for c in range(GRID)], axis=1
    ).reshape(heads, GRID, SPAN * GRID)
    strip = jnp.pad(strip, ((0, 0), (0, 0), (0, 512 - SPAN * GRID)))
    return pl.pallas_call(
        bias_kernel,
        grid=(heads,),
        in_specs=[pl.BlockSpec((1, GRID, 512), lambda h: (h, 0, 0))],
        out_specs=pl.BlockSpec((1, PATCHES, PATCHES), lambda h: (h, 0, 0)),
        out_shape=jax.ShapeDtypeStruct((heads, PATCHES, PATCHES), F32),
        compiler_params=params(),
        cost_estimate=cost(0, heads * PATCHES * PATCHES * 4),
    )(strip)


def table_of_strips(strips):
    heads = strips.shape[0]
    parts = strips[:, :, : SPAN * GRID].reshape(heads, GRID, SPAN, GRID)
    total = jnp.zeros((heads, SPAN, SPAN), F32)
    for c in range(GRID):
        total = total + jnp.pad(parts[:, c], ((0, 0), (0, 0), (GRID - 1 - c, c)))
    return total.reshape(heads, BUCKETS)


def head_rows(head, per_block):
    base = (head // per_block) * (3 * per_block * HEAD_DIM) + (head % per_block) * HEAD_DIM
    step = per_block * HEAD_DIM
    return [pl.ds(pl.multiple_of(base + c * step, 8), HEAD_DIM) for c in range(3)]


def key_mask(pick):
    ones = jnp.ones((pick.shape[0], PATCHES), BF)
    return (tn(pick, ones) - 1.0) * 1e30


def forward_kernel(
    per_block, tok_ref, mod_ref, pick_ref, weight_ref, out_w_ref, bias_ref,
    first_ref, qkv_ref, att_ref, lse_ref, middle_ref, second_ref, branch_ref,
    qkv_s, att_s, attk_s,
):
    heads = bias_ref.shape[0]
    tok = tok_ref[...].astype(F32)
    shift_one, scale_one, gate_one = mod_ref[0, 0:1], mod_ref[0, 1:2], mod_ref[0, 2:3]
    shift_two, scale_two = mod_ref[0, 3:4], mod_ref[0, 4:5]
    normed, _ = normalize(tok)
    first = (normed * (1.0 + scale_one) + shift_one).astype(BF)
    first_ref[...] = first
    step = weight_ref.shape[0] // 6
    for c in range(6):
        rows = slice(c * step, (c + 1) * step)
        part = nt(weight_ref[rows, :], first)
        qkv_s[rows, :] = part
        qkv_ref[rows, :] = part.astype(BF)
    pick = pick_ref[0]
    mask = key_mask(pick)
    scale = HEAD_DIM ** (-0.5) * LOG2E

    def one_head(head, carry):
        q_at, k_at, v_at = head_rows(head, per_block)
        queries = qkv_s[q_at, :].astype(BF)
        keys = qkv_s[k_at, :].astype(BF)
        values = qkv_s[v_at, :].astype(BF)
        scores = tn(keys, queries) * scale + bias_ref[head]
        here = pl.ds(pl.multiple_of(head * HEAD_DIM, 8), HEAD_DIM)

        def attend(scores):
            top = jnp.max(scores, axis=0, keepdims=True)
            weights = jnp.exp2(scores - top)
            total = jnp.sum(weights, axis=0, keepdims=True)
            probs = (weights * (1.0 / total)).astype(BF)
            return nn(values, probs), top + jnp.log2(total)

        att_s[here, :], lse_ref[0, pl.ds(head, 1), :] = attend(scores)
        attk_s[here, :], lse_ref[0, pl.ds(heads + head, 1), :] = attend(scores + mask)
        return carry

    lax.fori_loop(0, heads, one_head, 0, unroll=2)
    att = att_s[...].astype(BF)
    att_kept = attk_s[...].astype(BF)
    att_ref[:, :PATCHES] = att
    att_ref[:, PATCHES:] = att_kept
    out_w = out_w_ref[...]
    kept_att = nt(pick, att_kept).astype(BF)
    for rows, source, residual in (
        (slice(0, PATCHES), att.T, tok),
        (slice(PATCHES, PATCHES + pick.shape[0]), kept_att, nn(pick, tok_ref[...])),
    ):
        branch = nn(source, out_w)
        branch_ref[rows, :] = branch.astype(BF)
        middle = residual + gate_one * branch
        middle_ref[rows, :] = middle
        second_ref[rows, :] = (normalize(middle)[0] * (1.0 + scale_two) + shift_two).astype(BF)


def forward(tokens, mod, pick, weight_t, out_w, bias, per_block):
    images, padded = pick.shape[0], pick.shape[1]
    width = tokens.shape[1]
    rows = PATCHES + padded
    heads = bias.shape[0]
    proj = weight_t.shape[0]
    return pl.pallas_call(
        functools.partial(forward_kernel, per_block),
        grid=(images,),
        in_specs=[
            pl.BlockSpec((PATCHES, width), lambda i: (i, 0)),
            pl.BlockSpec((1, 8, width), lambda i: (i, 0, 0)),
            pl.BlockSpec((1, padded, PATCHES), lambda i: (i, 0, 0)),
            const_spec(weight_t.shape),
            const_spec(out_w.shape),
            const_spec(bias.shape),
        ],
        out_specs=[
            pl.BlockSpec((PATCHES, width), lambda i: (i, 0)),
            pl.BlockSpec((proj, PATCHES), lambda i: (0, i)),
            pl.BlockSpec((width, 2 * PATCHES), lambda i: (0, i)),
            pl.BlockSpec((1, 2 * heads, PATCHES), lambda i: (i, 0, 0)),
            pl.BlockSpec((rows, width), lambda i: (i, 0)),
            pl.BlockSpec((rows, width), lambda i: (i, 0)),
            pl.BlockSpec((rows, width), lambda i: (i, 0)),
        ],
        out_shape=[
            jax.ShapeDtypeStruct((images * PATCHES, width), BF),
            jax.ShapeDtypeStruct((proj, images * PATCHES), BF),
            jax.ShapeDtypeStruct((width, images * 2 * PATCHES), BF),
            jax.ShapeDtypeStruct((images, 2 * heads, PATCHES), F32),
            jax.ShapeDtypeStruct((images * rows, width), F32),
            jax.ShapeDtypeStruct((images * rows, width), BF),
            jax.ShapeDtypeStruct((images * rows, width), BF),
        ],
        scratch_shapes=[
            pltpu.VMEM((proj, PATCHES), F32),
            pltpu.VMEM((width, PATCHES), F32),
            pltpu.VMEM((width, PATCHES), F32),
        ],
        compiler_params=params(),
        cost_estimate=cost(images * 1.3e10, images * 8e6, images * heads * PATCHES * PATCHES * 2),
    )(tokens, mod, pick, weight_t, out_w, bias)


def gelu_pair(pre):
    root = math.sqrt(2.0 / math.pi)
    square = pre * pre
    bend = jnp.tanh(pre * (root + (root * 0.044715) * square))
    half = 0.5 + 0.5 * bend
    slope = half + (0.5 * pre) * (1.0 - bend * bend) * (root + (3.0 * root * 0.044715) * square)
    return pre * half, slope


def mlp_kernel(
    chunk, fresh, second_ref, dmlp_ref, up_ref, down_ref, *refs
):
    if fresh:
        branch_ref, dsecond_ref, grads_ref, second_t, dmlp_t, hidden_s, dpre_s, sem = refs
    else:
        branch_in, dsecond_in, branch_ref, dsecond_ref, grads_ref = refs[:5]
        second_t, dmlp_t, hidden_s, dpre_s, sem = refs[5:]
    rows = second_ref.shape[0]
    tile = up_ref.shape[1]
    width = second_ref.shape[1]

    @pl.when(pl.program_id(0) == 0)
    def _():
        if fresh:
            branch_ref[...] = jnp.zeros_like(branch_ref)
            dsecond_ref[...] = jnp.zeros_like(dsecond_ref)
        else:
            one = pltpu.make_async_copy(branch_in, branch_ref, sem.at[0])
            two = pltpu.make_async_copy(dsecond_in, dsecond_ref, sem.at[1])
            one.start()
            two.start()
        for at in range(0, rows, chunk):
            second_t[:, at : at + chunk] = second_ref[at : at + chunk, :].T
            dmlp_t[:, at : at + chunk] = dmlp_ref[at : at + chunk, :].T
        if not fresh:
            one.wait()
            two.wait()

    def one_chunk(index, carry):
        at = pl.ds(pl.multiple_of(index * chunk, chunk), chunk)
        pre = nn(second_ref[at, :], up_ref[...])
        dhidden = nt(dmlp_ref[at, :], down_ref[...])
        value, slope = gelu_pair(pre)
        hidden = value.astype(BF)
        dpre = (dhidden * slope).astype(BF)
        hidden_s[at, :] = hidden
        dpre_s[at, :] = dpre
        branch_ref[at, :] += nn(hidden, down_ref[...])
        dsecond_ref[at, :] += nt(dpre, up_ref[...])
        return carry

    lax.fori_loop(0, rows // chunk, one_chunk, 0)
    part = width // 3
    for c in range(3):
        at = slice(c * part, (c + 1) * part)
        grads_ref[at, :tile] = nn(second_t[at, :], dpre_s[...]).astype(BF)
        grads_ref[at, tile:] = nn(dmlp_t[at, :], hidden_s[...]).astype(BF)


def mlp_chunk(rows):
    for chunk in (896, 448, 64):
        if rows % chunk == 0:
            return chunk
    return rows


def mlp(second, dmlp, up, down, sums=None):
    rows, width = second.shape
    hidden = up.shape[1]
    tile = 768 if hidden % 768 == 0 else hidden
    fresh = sums is None
    chunk = mlp_chunk(rows)
    in_specs = [
        const_spec(second.shape),
        const_spec(second.shape),
        pl.BlockSpec((width, tile), lambda f: (0, f)),
        pl.BlockSpec((tile, width), lambda f: (f, 0)),
    ]
    operands = [second, dmlp, up, down]
    if not fresh:
        in_specs += [pl.BlockSpec(memory_space=pl.ANY)] * 2
        operands += list(sums)
    return pl.pallas_call(
        functools.partial(mlp_kernel, chunk, fresh),
        grid=(hidden // tile,),
        in_specs=in_specs,
        out_specs=[
            const_spec(second.shape),
            const_spec(second.shape),
            pl.BlockSpec((width, 2 * tile), lambda f: (0, f)),
        ],
        out_shape=[
            jax.ShapeDtypeStruct(second.shape, F32),
            jax.ShapeDtypeStruct(second.shape, F32),
            jax.ShapeDtypeStruct((width, 2 * hidden), BF),
        ],
        scratch_shapes=[
            pltpu.VMEM((width, rows), BF),
            pltpu.VMEM((width, rows), BF),
            pltpu.VMEM((rows, tile), BF),
            pltpu.VMEM((rows, tile), BF),
            pltpu.SemaphoreType.DMA((2,)),
        ],
        compiler_params=params(),
        cost_estimate=cost(12 * rows * width * hidden * 1.7, 30e6, rows * hidden),
    )(*operands), tile


def split_mlp_grads(grads, tile):
    parts = grads.reshape(grads.shape[0], -1, 2, tile)
    return (
        parts[:, :, 0].reshape(grads.shape[0], -1),
        parts[:, :, 1].reshape(grads.shape[0], -1),
    )


def backward_kernel(
    per_block, tok_ref, mod_ref, pick_ref, weight_ref, out_w_ref, bias_ref,
    qkv_ref, lse_ref, middle_ref, branch_ref, mlp_ref, dsecond_ref, grad_ref,
    out_ref, dtok_ref, dmod_ref, dattn_ref, dqkv_ref, strips_ref,
    qkv_s, datt_s, dattk_s, dscores_s,
):
    heads = bias_ref.shape[0]
    step = pl.program_id(0)
    shift_one, scale_one, gate_one = mod_ref[0, 0:1], mod_ref[0, 1:2], mod_ref[0, 2:3]
    scale_two, gate_two = mod_ref[0, 4:5], mod_ref[0, 5:6]
    pick = pick_ref[0]
    dmiddles = []
    sums = [0.0, 0.0, 0.0, 0.0]
    for rows in (slice(0, PATCHES), slice(PATCHES, PATCHES + pick.shape[0])):
        middle = middle_ref[rows, :]
        branch_mlp = mlp_ref[rows, :]
        dsecond = dsecond_ref[rows, :]
        grad = grad_ref[rows, :].astype(F32)
        out_ref[rows, :] = (middle + gate_two * branch_mlp).astype(BF)
        normed, inverse = normalize(middle)
        dmiddle = grad + norm_back(normed, inverse, dsecond * (1.0 + scale_two))
        branch = branch_ref[rows, :].astype(F32)
        for c, term in enumerate(
            (dmiddle * branch, dsecond, dsecond * normed, grad * branch_mlp)
        ):
            sums[c] = sums[c] + jnp.sum(term, axis=0, keepdims=True)
        dmiddles.append(dmiddle)
    for c in range(4):
        dmod_ref[0, 2 + c : 3 + c, :] = sums[c]
    dattn = (gate_one * dmiddles[0]).astype(BF)
    dattn_kept = tn(pick, (gate_one * dmiddles[1]).astype(BF)).astype(BF)
    dattn_ref[:PATCHES, :] = dattn
    dattn_ref[PATCHES:, :] = dattn_kept
    high = dmiddles[1].astype(BF)
    low = (dmiddles[1] - high.astype(F32)).astype(BF)
    dresid = dmiddles[0] + tn(pick, high) + tn(pick, low)
    datt_s[...] = nt(out_w_ref[...], dattn)
    dattk_s[...] = nt(out_w_ref[...], dattn_kept)
    qkv_s[...] = qkv_ref[...].astype(F32)
    mask = key_mask(pick)
    scale = HEAD_DIM ** (-0.5)

    @pl.when(step == 0)
    def _():
        dscores_s[...] = jnp.zeros_like(dscores_s)

    def one_head(head, carry):
        q_at, k_at, v_at = head_rows(head, per_block)
        queries = qkv_s[q_at, :].astype(BF)
        keys = qkv_s[k_at, :].astype(BF)
        values = qkv_s[v_at, :].astype(BF)
        here = pl.ds(pl.multiple_of(head * HEAD_DIM, 8), HEAD_DIM)
        scores = tn(keys, queries) * (scale * LOG2E) + bias_ref[head]

        def pull(scores, top, upstream):
            probs = jnp.exp2(scores - top)
            dprobs = tn(values, upstream)
            dvalues = nt(upstream, probs.astype(BF))
            weighted = jnp.sum(probs * dprobs, axis=0, keepdims=True)
            return probs * (dprobs - weighted), dvalues

        dscores, dvalues = pull(
            scores, lse_ref[0, pl.ds(head, 1), :], datt_s[here, :].astype(BF)
        )
        dscores_kept, dvalues_kept = pull(
            scores + mask, lse_ref[0, pl.ds(heads + head, 1), :], dattk_s[here, :].astype(BF)
        )
        dscores = dscores + dscores_kept
        dscores_s[head] += dscores
        rounded = dscores.astype(BF)
        qkv_s[q_at, :] = nn(keys, rounded) * scale
        qkv_s[k_at, :] = nt(queries, rounded) * scale
        qkv_s[v_at, :] = dvalues + dvalues_kept
        return carry

    lax.fori_loop(0, heads, one_head, 0, unroll=2)
    dqkv = qkv_s[...].astype(BF)
    dqkv_ref[...] = dqkv
    dfirst = tn(dqkv, weight_ref[...])
    normed, inverse = normalize(tok_ref[...].astype(F32))
    dmod_ref[0, 0:1, :] = jnp.sum(dfirst, axis=0, keepdims=True)
    dmod_ref[0, 1:2, :] = jnp.sum(dfirst * normed, axis=0, keepdims=True)
    dmod_ref[0, 6:8, :] = jnp.zeros((2, dfirst.shape[1]), F32)
    dtok_ref[...] = (dresid + norm_back(normed, inverse, dfirst * (1.0 + scale_one))).astype(BF)

    @pl.when(step == pl.num_programs(0) - 1)
    def _():
        def fold(head, carry):
            strip = jnp.zeros((GRID, 512), F32)
            for key_row in range(GRID):
                start = (GRID - 1 - key_row) * GRID
                block = dscores_s[head, key_row * GRID : (key_row + 1) * GRID, :]
                block = jnp.concatenate([block, jnp.zeros((GRID, 512 - PATCHES), F32)], axis=1)
                strip = strip + pltpu.roll(block, start, 1)
            strips_ref[head] = strip
            return carry

        lax.fori_loop(0, heads, fold, 0)


def backward(
    tokens, mod, pick, weight_t, out_w, bias, qkv, lse, middle, branch, branch_mlp, dsecond,
    grads, per_block,
):
    images, padded = pick.shape[0], pick.shape[1]
    width = tokens.shape[1]
    rows = PATCHES + padded
    heads = bias.shape[0]
    proj = weight_t.shape[0]
    by_row = pl.BlockSpec((rows, width), lambda i: (i, 0))
    one_row = pl.BlockSpec((rows, width), lambda i: (i, 0), pipeline_mode=pl.Buffered(1))
    return pl.pallas_call(
        functools.partial(backward_kernel, per_block),
        grid=(images,),
        in_specs=[
            pl.BlockSpec((PATCHES, width), lambda i: (i, 0)),
            pl.BlockSpec((1, 8, width), lambda i: (i, 0, 0)),
            pl.BlockSpec((1, padded, PATCHES), lambda i: (i, 0, 0)),
            const_spec(weight_t.shape),
            const_spec(out_w.shape),
            const_spec(bias.shape),
            pl.BlockSpec((proj, PATCHES), lambda i: (0, i)),
            pl.BlockSpec((1, 2 * heads, PATCHES), lambda i: (i, 0, 0)),
            by_row,
            by_row,
            by_row,
            by_row,
            by_row,
        ],
        out_specs=[
            by_row,
            pl.BlockSpec((PATCHES, width), lambda i: (i, 0)),
            pl.BlockSpec((1, 8, width), lambda i: (i, 0, 0)),
            pl.BlockSpec((2 * PATCHES, width), lambda i: (i, 0)),
            pl.BlockSpec((proj, PATCHES), lambda i: (0, i)),
            const_spec((heads, GRID, 512)),
        ],
        out_shape=[
            jax.ShapeDtypeStruct((images * rows, width), BF),
            jax.ShapeDtypeStruct((images * PATCHES, width), BF),
            jax.ShapeDtypeStruct((images, 8, width), F32),
            jax.ShapeDtypeStruct((images * 2 * PATCHES, width), BF),
            jax.ShapeDtypeStruct((proj, images * PATCHES), BF),
            jax.ShapeDtypeStruct((heads, GRID, 512), F32),
        ],
        scratch_shapes=[
            pltpu.VMEM((proj, PATCHES), F32),
            pltpu.VMEM((width, PATCHES), F32),
            pltpu.VMEM((width, PATCHES), F32),
            pltpu.VMEM((heads, PATCHES, PATCHES), F32),
        ],
        compiler_params=params(),
        cost_estimate=cost(images * 2.2e10, images * 1e7, images * heads * PATCHES * PATCHES * 2),
    )(
        tokens, mod, pick, weight_t, out_w, bias, qkv, lse, middle, branch, branch_mlp,
        dsecond, grads,
    )


def shift_mp(value, steps):
    ways = lax.axis_size("mp")
    return lax.ppermute(value, "mp", [(i, (i - steps) % ways) for i in range(ways)])


def from_others(block):
    ways, places = lax.axis_size("mp"), lax.axis_size("dp")
    half = block.shape[0] // 2
    core = lax.axis_index("dp") % 2
    mine = lax.dynamic_slice_in_dim(block, core * half, half, 0)
    got = []
    for steps in range(1, ways):
        near = shift_mp(mine, steps)
        far = lax.ppermute(near, "dp", [(i, i ^ 1) for i in range(places)])
        whole = jnp.zeros_like(block)
        whole = lax.dynamic_update_slice_in_dim(whole, near, core * half, 0)
        whole = lax.dynamic_update_slice_in_dim(whole, far, (1 - core) * half, 0)
        got.append(whole)
    return got


def home(parts):
    total = parts[0].astype(F32)
    for steps in range(1, len(parts)):
        total = total + shift_mp(parts[steps], -steps).astype(F32)
    return total


def scatter_dp(part):
    return lax.psum_scatter(part, "dp", scatter_dimension=0, tiled=True)


def local(
    tokens, conditioning, kept_ids, ada_weight, ada_bias, attn_qkv, attn_out, mlp_up, mlp_down,
    rel_table, grad_out_kept, grad_out_full,
):
    ways = lax.axis_size("mp")
    place = lax.axis_index("mp")
    images_group = conditioning.shape[0]
    images = images_group // ways
    width = tokens.shape[1]
    keep = kept_ids.shape[1]
    padded = -(-keep // 64) * 64
    per_block = rel_table.shape[0]
    cols = ada_bias.shape[0]

    silu_cond = jax.nn.silu(conditioning.astype(F32)).astype(BF)
    columns = (jnp.dot(silu_cond, ada_weight, preferred_element_type=F32) + ada_bias).astype(BF)
    mod = lax.all_to_all(columns, "mp", split_axis=0, concat_axis=1, tiled=True)
    mod = jnp.pad(mod.astype(F32).reshape(images, 6, width), ((0, 0), (0, 2), (0, 0)))

    weight_own = jnp.transpose(attn_qkv.reshape(width, -1))
    weight_t = jnp.concatenate([weight_own] + from_others(weight_own), axis=0)
    out_w = jnp.concatenate([attn_out] + from_others(attn_out), axis=0)
    table = jnp.concatenate(
        [rel_table] + [shift_mp(rel_table, s) for s in range(1, ways)], axis=0
    )
    bias = bias_whole(table)
    weight_t, out_w, late_up, late_down = lax.optimization_barrier(
        (weight_t, out_w, mlp_up, mlp_down)
    )
    up_others = from_others(late_up)
    down_others = from_others(late_down)

    own_kept = lax.dynamic_slice_in_dim(kept_ids, place * images, images, 0)
    own_kept = jnp.pad(own_kept, ((0, 0), (0, padded - keep)), constant_values=-1)
    pick = (own_kept[:, :, None] == jnp.arange(PATCHES, dtype=jnp.int32)).astype(BF)
    grads = jnp.concatenate(
        [
            grad_out_full.reshape(images, PATCHES, width),
            jnp.pad(
                grad_out_kept.reshape(images, keep, width), ((0, 0), (0, padded - keep), (0, 0))
            ),
        ],
        axis=1,
    )
    dmlp = (mod[:, 5:6] * grads.astype(F32)).astype(BF).reshape(-1, width)
    grads = grads.reshape(-1, width)

    first, qkv, att, lse, middle, second, branch = forward(
        tokens, mod, pick, weight_t, out_w, bias, per_block
    )
    (branch_mlp, dsecond, grads_own), tile_own = mlp(second, dmlp, mlp_up, mlp_down)
    reduced = [scatter_dp(grads_own)]
    for up, down in zip(up_others, down_others):
        (branch_mlp, dsecond, grads_next), _ = mlp(
            second, dmlp, up, down, (branch_mlp, dsecond)
        )
        reduced.append(scatter_dp(grads_next))
    out, dtok, dmod, dattn, dqkv, strips = backward(
        tokens, mod, pick, weight_t, out_w, bias, qkv, lse, middle, branch, branch_mlp, dsecond,
        grads, per_block,
    )
    dweight = dot(first, dqkv, (0, 1)).astype(BF)
    dout_t = dot(dattn, att, (0, 1)).astype(BF)
    proj_block, out_block = weight_own.shape[0], attn_out.shape[0]
    dweight, dout_t, *reduced = lax.optimization_barrier((dweight, dout_t, *reduced))
    attn_sums = scatter_dp(jnp.concatenate([dweight, dout_t], axis=1))
    split = ways * proj_block
    attn_parts = [
        jnp.concatenate(
            [
                attn_sums[:, j * proj_block : (j + 1) * proj_block],
                attn_sums[:, split + j * out_block : split + (j + 1) * out_block],
            ],
            axis=1,
        )
        for j in range(ways)
    ]
    mlp_grads = home(reduced)
    attn_grads = home(attn_parts)
    grad_up, grad_down_t = split_mlp_grads(mlp_grads, tile_own)
    grad_qkv = attn_grads[:, :proj_block].reshape(-1, 3, proj_block // 3)
    grad_out = jnp.transpose(attn_grads[:, proj_block:])

    dmod_rows = dmod[:, :6].reshape(images, 6 * width)
    dcolumns = lax.all_to_all(dmod_rows, "mp", split_axis=1, concat_axis=0, tiled=True)
    dtable = home(list(jnp.split(table_of_strips(strips), ways, axis=0)))
    flat = jnp.concatenate([dcolumns.reshape(-1), dtable.reshape(-1)])
    count = flat.shape[0]
    packed = jnp.pad(flat, (0, -count % 1024)).reshape(-1, 128)
    every = lax.all_gather(packed, "dp", axis=0, tiled=True)
    every = every.reshape(lax.axis_size("dp"), -1)[:, :count]
    all_columns = every[:, : images_group * cols].reshape(-1, cols)
    dtable = jnp.sum(every[:, images_group * cols :], axis=0).reshape(rel_table.shape)
    all_cond = lax.all_gather(silu_cond, "dp", axis=0, tiled=True)
    slice_width = width // lax.axis_size("dp")
    cond_slice = lax.dynamic_slice_in_dim(
        all_cond, lax.axis_index("dp") * slice_width, slice_width, 1
    )
    grad_ada_weight = lax.dot_general(
        cond_slice.astype(F32), all_columns, (((0,), (0,)), ((), ())), precision=PRECISE
    )
    grad_ada_bias = jnp.sum(all_columns, axis=0)
    silu_part = lax.dot_general(
        dcolumns, ada_weight.astype(F32), (((1,), (1,)), ((), ())), precision=PRECISE
    )
    shares = lax.all_to_all(
        silu_part.astype(BF).reshape(ways, images, width), "mp", split_axis=0, concat_axis=0,
        tiled=True,
    )
    grad_silu = jnp.sum(shares.astype(F32), axis=0)
    own_cond = lax.dynamic_slice_in_dim(conditioning, place * images, images, 0).astype(F32)
    grad_cond = jax.vjp(jax.nn.silu, own_cond)[1](grad_silu)[0].astype(BF)

    out = out.reshape(images, PATCHES + padded, width)
    out_full = out[:, :PATCHES].reshape(-1, width)
    out_kept = out[:, PATCHES : PATCHES + keep].reshape(-1, width)
    return (
        out_kept, out_full, dtok, grad_cond, grad_ada_weight, grad_ada_bias, grad_qkv, grad_out,
        grad_up, jnp.transpose(grad_down_t), dtable,
    )


def solution(mesh):
    both = P(("dp", "mp"), None)
    return jax.shard_map(
        local,
        mesh=mesh,
        in_specs=(
            both, P("dp", None), P("dp", None), P(None, "mp"), P("mp"), P(None, None, "mp"),
            P("mp", None), P(None, "mp"), P("mp", None), P("mp", None), both, both,
        ),
        out_specs=(
            both, both, both, both, P("dp", "mp"), P("mp"), P("dp", None, "mp"), P("mp", "dp"),
            P("dp", "mp"), P("mp", "dp"), P("mp", None),
        ),
        check_vma=False,
    )
```

```python
import functools
import math

import jax
import jax.numpy as jnp
from jax import lax
from jax.experimental import pallas as pl
from jax.experimental.pallas import tpu as pltpu
from jax.sharding import PartitionSpec as P

HEAD_DIM = 72
GRID = 16
PATCHES = 256
BUCKETS = 961
SPAN = 2 * GRID - 1
EPSILON = 1e-06
PRECISE = lax.Precision.HIGHEST
BF = jnp.bfloat16
F32 = jnp.float32
LOG2E = math.log2(math.e)
VMEM_LIMIT = 60 * 1024 * 1024


def dot(a, b, dims):
    return lax.dot_general(a, b, ((dims[0:1], dims[1:2]), ((), ())), preferred_element_type=F32)


def nn(a, b):
    return dot(a, b, (1, 0))


def nt(a, b):
    return dot(a, b, (1, 1))


def tn(a, b):
    return dot(a, b, (0, 0))


def normalize(rows):
    centered = rows - jnp.mean(rows, axis=-1, keepdims=True)
    inverse = lax.rsqrt(jnp.mean(centered * centered, axis=-1, keepdims=True) + EPSILON)
    return centered * inverse, inverse


def norm_back(normed, inverse, upstream):
    return inverse * (
        upstream
        - jnp.mean(upstream, axis=-1, keepdims=True)
        - normed * jnp.mean(upstream * normed, axis=-1, keepdims=True)
    )


def params(n_grid=1):
    return pltpu.CompilerParams(
        vmem_limit_bytes=VMEM_LIMIT, dimension_semantics=("arbitrary",) * n_grid
    )


def cost(flops, bytes_accessed, transcendentals=0):
    return pl.CostEstimate(
        flops=int(flops), bytes_accessed=int(bytes_accessed), transcendentals=int(transcendentals)
    )


def const_spec(shape):
    return pl.BlockSpec(shape, lambda *_: (0,) * len(shape), pipeline_mode=pl.Buffered(1))


def bias_kernel(strip_ref, bias_ref):
    strip = strip_ref[0]
    for key_row in range(GRID):
        start = (GRID - 1 - key_row) * GRID
        bias_ref[0, key_row * GRID : (key_row + 1) * GRID, :] = strip[:, start : start + PATCHES]


def bias_whole(table):
    heads = table.shape[0]
    grid_table = table.reshape(heads, SPAN, SPAN) * LOG2E
    strip = jnp.stack(
        [grid_table[:, :, GRID - 1 - c : 2 * GRID - 1 - c] for c in range(GRID)], axis=1
    ).reshape(heads, GRID, SPAN * GRID)
    strip = jnp.pad(strip, ((0, 0), (0, 0), (0, 512 - SPAN * GRID)))
    return pl.pallas_call(
        bias_kernel,
        grid=(heads,),
        in_specs=[pl.BlockSpec((1, GRID, 512), lambda h: (h, 0, 0))],
        out_specs=pl.BlockSpec((1, PATCHES, PATCHES), lambda h: (h, 0, 0)),
        out_shape=jax.ShapeDtypeStruct((heads, PATCHES, PATCHES), F32),
        compiler_params=params(),
        cost_estimate=cost(0, heads * PATCHES * PATCHES * 4),
    )(strip)


def table_of_strips(strips):
    heads = strips.shape[0]
    parts = strips[:, :, : SPAN * GRID].reshape(heads, GRID, SPAN, GRID)
    total = jnp.zeros((heads, SPAN, SPAN), F32)
    for c in range(GRID):
        total = total + jnp.pad(parts[:, c], ((0, 0), (0, 0), (GRID - 1 - c, c)))
    return total.reshape(heads, BUCKETS)


def head_rows(head, per_block):
    base = (head // per_block) * (3 * per_block * HEAD_DIM) + (head % per_block) * HEAD_DIM
    step = per_block * HEAD_DIM
    return [pl.ds(pl.multiple_of(base + c * step, 8), HEAD_DIM) for c in range(3)]


def key_mask(pick):
    ones = jnp.ones((pick.shape[0], PATCHES), BF)
    return (tn(pick, ones) - 1.0) * 1e30


def forward_kernel(
    per_block, tok_ref, mod_ref, pick_ref, weight_ref, out_w_ref, bias_ref,
    first_ref, qkv_ref, att_ref, lse_ref, middle_ref, second_ref, branch_ref,
    qkv_s, att_s, attk_s,
):
    heads = bias_ref.shape[0]
    tok = tok_ref[...].astype(F32)
    shift_one, scale_one, gate_one = mod_ref[0, 0:1], mod_ref[0, 1:2], mod_ref[0, 2:3]
    shift_two, scale_two = mod_ref[0, 3:4], mod_ref[0, 4:5]
    normed, _ = normalize(tok)
    first = (normed * (1.0 + scale_one) + shift_one).astype(BF)
    first_ref[...] = first
    step = weight_ref.shape[0] // 6
    for c in range(6):
        rows = slice(c * step, (c + 1) * step)
        part = nt(weight_ref[rows, :], first)
        qkv_s[rows, :] = part
        qkv_ref[rows, :] = part.astype(BF)
    pick = pick_ref[0]
    mask = key_mask(pick)
    scale = HEAD_DIM ** (-0.5) * LOG2E

    def one_head(head, carry):
        q_at, k_at, v_at = head_rows(head, per_block)
        queries = qkv_s[q_at, :].astype(BF)
        keys = qkv_s[k_at, :].astype(BF)
        values = qkv_s[v_at, :].astype(BF)
        scores = tn(keys, queries) * scale + bias_ref[head]
        here = pl.ds(pl.multiple_of(head * HEAD_DIM, 8), HEAD_DIM)

        def attend(scores):
            top = jnp.max(scores, axis=0, keepdims=True)
            weights = jnp.exp2(scores - top)
            total = jnp.sum(weights, axis=0, keepdims=True)
            probs = (weights * (1.0 / total)).astype(BF)
            return nn(values, probs), top + jnp.log2(total)

        att_s[here, :], lse_ref[0, pl.ds(head, 1), :] = attend(scores)
        attk_s[here, :], lse_ref[0, pl.ds(heads + head, 1), :] = attend(scores + mask)
        return carry

    lax.fori_loop(0, heads, one_head, 0, unroll=2)
    att = att_s[...].astype(BF)
    att_kept = attk_s[...].astype(BF)
    att_ref[:, :PATCHES] = att
    att_ref[:, PATCHES:] = att_kept
    out_w = out_w_ref[...]
    kept_att = nt(pick, att_kept).astype(BF)
    for rows, source, residual in (
        (slice(0, PATCHES), att.T, tok),
        (slice(PATCHES, PATCHES + pick.shape[0]), kept_att, nn(pick, tok_ref[...])),
    ):
        branch = nn(source, out_w)
        branch_ref[rows, :] = branch.astype(BF)
        middle = residual + gate_one * branch
        middle_ref[rows, :] = middle
        second_ref[rows, :] = (normalize(middle)[0] * (1.0 + scale_two) + shift_two).astype(BF)


def forward(tokens, mod, pick, weight_t, out_w, bias, per_block):
    images, padded = pick.shape[0], pick.shape[1]
    width = tokens.shape[1]
    rows = PATCHES + padded
    heads = bias.shape[0]
    proj = weight_t.shape[0]
    return pl.pallas_call(
        functools.partial(forward_kernel, per_block),
        grid=(images,),
        in_specs=[
            pl.BlockSpec((PATCHES, width), lambda i: (i, 0)),
            pl.BlockSpec((1, 8, width), lambda i: (i, 0, 0)),
            pl.BlockSpec((1, padded, PATCHES), lambda i: (i, 0, 0)),
            const_spec(weight_t.shape),
            const_spec(out_w.shape),
            const_spec(bias.shape),
        ],
        out_specs=[
            pl.BlockSpec((PATCHES, width), lambda i: (i, 0)),
            pl.BlockSpec((proj, PATCHES), lambda i: (0, i)),
            pl.BlockSpec((width, 2 * PATCHES), lambda i: (0, i)),
            pl.BlockSpec((1, 2 * heads, PATCHES), lambda i: (i, 0, 0)),
            pl.BlockSpec((rows, width), lambda i: (i, 0)),
            pl.BlockSpec((rows, width), lambda i: (i, 0)),
            pl.BlockSpec((rows, width), lambda i: (i, 0)),
        ],
        out_shape=[
            jax.ShapeDtypeStruct((images * PATCHES, width), BF),
            jax.ShapeDtypeStruct((proj, images * PATCHES), BF),
            jax.ShapeDtypeStruct((width, images * 2 * PATCHES), BF),
            jax.ShapeDtypeStruct((images, 2 * heads, PATCHES), F32),
            jax.ShapeDtypeStruct((images * rows, width), F32),
            jax.ShapeDtypeStruct((images * rows, width), BF),
            jax.ShapeDtypeStruct((images * rows, width), BF),
        ],
        scratch_shapes=[
            pltpu.VMEM((proj, PATCHES), F32),
            pltpu.VMEM((width, PATCHES), F32),
            pltpu.VMEM((width, PATCHES), F32),
        ],
        compiler_params=params(),
        cost_estimate=cost(images * 2e9, images * 8e6),
    )(tokens, mod, pick, weight_t, out_w, bias)


def gelu_pair(pre):
    root = math.sqrt(2.0 / math.pi)
    square = pre * pre
    bend = jnp.tanh(pre * (root + (root * 0.044715) * square))
    half = 0.5 + 0.5 * bend
    slope = half + (0.5 * pre) * (1.0 - bend * bend) * (root + (3.0 * root * 0.044715) * square)
    return pre * half, slope


def mlp_kernel(
    chunk, fresh, second_ref, dmlp_ref, up_ref, down_ref, *refs
):
    if fresh:
        branch_ref, dsecond_ref, grads_ref, second_t, dmlp_t, hidden_s, dpre_s, sem = refs
    else:
        branch_in, dsecond_in, branch_ref, dsecond_ref, grads_ref = refs[:5]
        second_t, dmlp_t, hidden_s, dpre_s, sem = refs[5:]
    rows = second_ref.shape[0]
    tile = up_ref.shape[1]
    width = second_ref.shape[1]

    @pl.when(pl.program_id(0) == 0)
    def _():
        if fresh:
            branch_ref[...] = jnp.zeros_like(branch_ref)
            dsecond_ref[...] = jnp.zeros_like(dsecond_ref)
        else:
            one = pltpu.make_async_copy(branch_in, branch_ref, sem.at[0])
            two = pltpu.make_async_copy(dsecond_in, dsecond_ref, sem.at[1])
            one.start()
            two.start()
        for at in range(0, rows, chunk):
            second_t[:, at : at + chunk] = second_ref[at : at + chunk, :].T
            dmlp_t[:, at : at + chunk] = dmlp_ref[at : at + chunk, :].T
        if not fresh:
            one.wait()
            two.wait()

    def one_chunk(index, carry):
        at = pl.ds(pl.multiple_of(index * chunk, chunk), chunk)
        pre = nn(second_ref[at, :], up_ref[...])
        dhidden = nt(dmlp_ref[at, :], down_ref[...])
        value, slope = gelu_pair(pre)
        hidden = value.astype(BF)
        dpre = (dhidden * slope).astype(BF)
        hidden_s[at, :] = hidden
        dpre_s[at, :] = dpre
        branch_ref[at, :] += nn(hidden, down_ref[...])
        dsecond_ref[at, :] += nt(dpre, up_ref[...])
        return carry

    lax.fori_loop(0, rows // chunk, one_chunk, 0)
    part = width // 3
    for c in range(3):
        at = slice(c * part, (c + 1) * part)
        grads_ref[at, :tile] = nn(second_t[at, :], dpre_s[...]).astype(BF)
        grads_ref[at, tile:] = nn(dmlp_t[at, :], hidden_s[...]).astype(BF)


def mlp_chunk(rows):
    for chunk in (896, 448, 64):
        if rows % chunk == 0:
            return chunk
    return rows


def mlp(second, dmlp, up, down, sums=None):
    rows, width = second.shape
    hidden = up.shape[1]
    tile = 768 if hidden % 768 == 0 else hidden
    fresh = sums is None
    chunk = mlp_chunk(rows)
    in_specs = [
        const_spec(second.shape),
        const_spec(second.shape),
        pl.BlockSpec((width, tile), lambda f: (0, f)),
        pl.BlockSpec((tile, width), lambda f: (f, 0)),
    ]
    operands = [second, dmlp, up, down]
    if not fresh:
        in_specs += [pl.BlockSpec(memory_space=pl.ANY)] * 2
        operands += list(sums)
    return pl.pallas_call(
        functools.partial(mlp_kernel, chunk, fresh),
        grid=(hidden // tile,),
        in_specs=in_specs,
        out_specs=[
            const_spec(second.shape),
            const_spec(second.shape),
            pl.BlockSpec((width, 2 * tile), lambda f: (0, f)),
        ],
        out_shape=[
            jax.ShapeDtypeStruct(second.shape, F32),
            jax.ShapeDtypeStruct(second.shape, F32),
            jax.ShapeDtypeStruct((width, 2 * hidden), BF),
        ],
        scratch_shapes=[
            pltpu.VMEM((width, rows), BF),
            pltpu.VMEM((width, rows), BF),
            pltpu.VMEM((rows, tile), BF),
            pltpu.VMEM((rows, tile), BF),
            pltpu.SemaphoreType.DMA((2,)),
        ],
        compiler_params=params(),
        cost_estimate=cost(6e10, 6e7) if fresh else cost(1e7, 1e5),
    )(*operands), tile


def split_mlp_grads(grads, tile):
    parts = grads.reshape(grads.shape[0], -1, 2, tile)
    return (
        parts[:, :, 0].reshape(grads.shape[0], -1),
        parts[:, :, 1].reshape(grads.shape[0], -1),
    )


def backward_kernel(
    per_block, tok_ref, mod_ref, pick_ref, weight_ref, out_w_ref, bias_ref,
    qkv_ref, lse_ref, middle_ref, branch_ref, mlp_ref, dsecond_ref, grad_ref,
    out_ref, dtok_ref, dmod_ref, dattn_ref, dqkv_ref, strips_ref,
    qkv_s, datt_s, dattk_s, dscores_s,
):
    heads = bias_ref.shape[0]
    step = pl.program_id(0)
    shift_one, scale_one, gate_one = mod_ref[0, 0:1], mod_ref[0, 1:2], mod_ref[0, 2:3]
    scale_two, gate_two = mod_ref[0, 4:5], mod_ref[0, 5:6]
    pick = pick_ref[0]
    dmiddles = []
    sums = [0.0, 0.0, 0.0, 0.0]
    for rows in (slice(0, PATCHES), slice(PATCHES, PATCHES + pick.shape[0])):
        middle = middle_ref[rows, :]
        branch_mlp = mlp_ref[rows, :]
        dsecond = dsecond_ref[rows, :]
        grad = grad_ref[rows, :].astype(F32)
        out_ref[rows, :] = (middle + gate_two * branch_mlp).astype(BF)
        normed, inverse = normalize(middle)
        dmiddle = grad + norm_back(normed, inverse, dsecond * (1.0 + scale_two))
        branch = branch_ref[rows, :].astype(F32)
        for c, term in enumerate(
            (dmiddle * branch, dsecond, dsecond * normed, grad * branch_mlp)
        ):
            sums[c] = sums[c] + jnp.sum(term, axis=0, keepdims=True)
        dmiddles.append(dmiddle)
    for c in range(4):
        dmod_ref[0, 2 + c : 3 + c, :] = sums[c]
    dattn = (gate_one * dmiddles[0]).astype(BF)
    dattn_kept = tn(pick, (gate_one * dmiddles[1]).astype(BF)).astype(BF)
    dattn_ref[:PATCHES, :] = dattn
    dattn_ref[PATCHES:, :] = dattn_kept
    high = dmiddles[1].astype(BF)
    low = (dmiddles[1] - high.astype(F32)).astype(BF)
    dresid = dmiddles[0] + tn(pick, high) + tn(pick, low)
    datt_s[...] = nt(out_w_ref[...], dattn)
    dattk_s[...] = nt(out_w_ref[...], dattn_kept)
    qkv_s[...] = qkv_ref[...].astype(F32)
    mask = key_mask(pick)
    scale = HEAD_DIM ** (-0.5)

    @pl.when(step == 0)
    def _():
        dscores_s[...] = jnp.zeros_like(dscores_s)

    def one_head(head, carry):
        q_at, k_at, v_at = head_rows(head, per_block)
        queries = qkv_s[q_at, :].astype(BF)
        keys = qkv_s[k_at, :].astype(BF)
        values = qkv_s[v_at, :].astype(BF)
        here = pl.ds(pl.multiple_of(head * HEAD_DIM, 8), HEAD_DIM)
        scores = tn(keys, queries) * (scale * LOG2E) + bias_ref[head]

        def pull(scores, top, upstream):
            probs = jnp.exp2(scores - top)
            dprobs = tn(values, upstream)
            dvalues = nt(upstream, probs.astype(BF))
            weighted = jnp.sum(probs * dprobs, axis=0, keepdims=True)
            return probs * (dprobs - weighted), dvalues

        dscores, dvalues = pull(
            scores, lse_ref[0, pl.ds(head, 1), :], datt_s[here, :].astype(BF)
        )
        dscores_kept, dvalues_kept = pull(
            scores + mask, lse_ref[0, pl.ds(heads + head, 1), :], dattk_s[here, :].astype(BF)
        )
        dscores = dscores + dscores_kept
        dscores_s[head] += dscores
        rounded = dscores.astype(BF)
        qkv_s[q_at, :] = nn(keys, rounded) * scale
        qkv_s[k_at, :] = nt(queries, rounded) * scale
        qkv_s[v_at, :] = dvalues + dvalues_kept
        return carry

    lax.fori_loop(0, heads, one_head, 0, unroll=2)
    dqkv = qkv_s[...].astype(BF)
    dqkv_ref[...] = dqkv
    dfirst = tn(dqkv, weight_ref[...])
    normed, inverse = normalize(tok_ref[...].astype(F32))
    dmod_ref[0, 0:1, :] = jnp.sum(dfirst, axis=0, keepdims=True)
    dmod_ref[0, 1:2, :] = jnp.sum(dfirst * normed, axis=0, keepdims=True)
    dmod_ref[0, 6:8, :] = jnp.zeros((2, dfirst.shape[1]), F32)
    dtok_ref[...] = (dresid + norm_back(normed, inverse, dfirst * (1.0 + scale_one))).astype(BF)

    @pl.when(step == pl.num_programs(0) - 1)
    def _():
        def fold(head, carry):
            strip = jnp.zeros((GRID, 512), F32)
            for key_row in range(GRID):
                start = (GRID - 1 - key_row) * GRID
                block = dscores_s[head, key_row * GRID : (key_row + 1) * GRID, :]
                block = jnp.concatenate([block, jnp.zeros((GRID, 512 - PATCHES), F32)], axis=1)
                strip = strip + pltpu.roll(block, start, 1)
            strips_ref[head] = strip
            return carry

        lax.fori_loop(0, heads, fold, 0)


def backward(
    tokens, mod, pick, weight_t, out_w, bias, qkv, lse, middle, branch, branch_mlp, dsecond,
    grads, per_block,
):
    images, padded = pick.shape[0], pick.shape[1]
    width = tokens.shape[1]
    rows = PATCHES + padded
    heads = bias.shape[0]
    proj = weight_t.shape[0]
    by_row = pl.BlockSpec((rows, width), lambda i: (i, 0))
    one_row = pl.BlockSpec((rows, width), lambda i: (i, 0), pipeline_mode=pl.Buffered(1))
    return pl.pallas_call(
        functools.partial(backward_kernel, per_block),
        grid=(images,),
        in_specs=[
            pl.BlockSpec((PATCHES, width), lambda i: (i, 0)),
            pl.BlockSpec((1, 8, width), lambda i: (i, 0, 0)),
            pl.BlockSpec((1, padded, PATCHES), lambda i: (i, 0, 0)),
            const_spec(weight_t.shape),
            const_spec(out_w.shape),
            const_spec(bias.shape),
            pl.BlockSpec((proj, PATCHES), lambda i: (0, i)),
            pl.BlockSpec((1, 2 * heads, PATCHES), lambda i: (i, 0, 0)),
            by_row,
            by_row,
            by_row,
            by_row,
            by_row,
        ],
        out_specs=[
            by_row,
            pl.BlockSpec((PATCHES, width), lambda i: (i, 0)),
            pl.BlockSpec((1, 8, width), lambda i: (i, 0, 0)),
            pl.BlockSpec((2 * PATCHES, width), lambda i: (i, 0)),
            pl.BlockSpec((proj, PATCHES), lambda i: (0, i)),
            const_spec((heads, GRID, 512)),
        ],
        out_shape=[
            jax.ShapeDtypeStruct((images * rows, width), BF),
            jax.ShapeDtypeStruct((images * PATCHES, width), BF),
            jax.ShapeDtypeStruct((images, 8, width), F32),
            jax.ShapeDtypeStruct((images * 2 * PATCHES, width), BF),
            jax.ShapeDtypeStruct((proj, images * PATCHES), BF),
            jax.ShapeDtypeStruct((heads, GRID, 512), F32),
        ],
        scratch_shapes=[
            pltpu.VMEM((proj, PATCHES), F32),
            pltpu.VMEM((width, PATCHES), F32),
            pltpu.VMEM((width, PATCHES), F32),
            pltpu.VMEM((heads, PATCHES, PATCHES), F32),
        ],
        compiler_params=params(),
        cost_estimate=cost(1e7, 1e5),
    )(
        tokens, mod, pick, weight_t, out_w, bias, qkv, lse, middle, branch, branch_mlp,
        dsecond, grads,
    )


SUM_PLACES = 16
HALVING = (1, 2, 8)
FINAL = 4


def place_bit(place, bit):
    return (place // bit) % 2


def unit_start(owner, share):
    index = 0
    for bit in HALVING + (FINAL,):
        index = index * 2 + place_bit(owner, bit)
    return index * share


def store_by_owner(buffer, tile, at, block, share):
    first_owner = at // share
    owners = block.shape[0] // share
    for k in range(owners):
        owner = first_owner + k
        if place_bit(owner, FINAL):
            continue
        pair = k + FINAL
        both = jnp.concatenate(
            [block[k * share : (k + 1) * share], block[pair * share : (pair + 1) * share]], axis=0
        )
        start = unit_start(owner, share)
        buffer[tile, start : start + 2 * share, :] = both.astype(BF)


class DpSum:
    def __init__(self, buffer, lands, sends, recvs):
        self.buffer, self.lands, self.sends, self.recvs = buffer, lands, sends, recvs
        self.place = lax.axis_index("dp")
        self.rows = buffer.shape[1]

    def partner(self, bit):
        return self.place + bit - 2 * bit * place_bit(self.place, bit)

    def greet(self, barrier):
        for bit in HALVING + (FINAL,):
            pl.semaphore_signal(
                barrier, inc=1, device_id={"dp": self.partner(bit)},
                device_id_type=pl.DeviceIdType.MESH,
            )

    def spans(self, stage):
        start, size = 0, self.rows
        for k, bit in enumerate(HALVING):
            size = size // 2
            mine = place_bit(self.place, bit)
            if k == stage:
                return start + mine * size, start + (1 - mine) * size, size
            start = start + mine * size
        return start, start, size

    def copy(self, stage, tile):
        bit = (HALVING + (FINAL,))[stage]
        _, away, size = self.spans(stage)
        return pltpu.make_async_remote_copy(
            src_ref=self.buffer.at[tile, pl.ds(pl.multiple_of(away, 16), size), :],
            dst_ref=self.lands[stage].at[tile],
            send_sem=self.sends.at[stage, tile],
            recv_sem=self.recvs.at[stage, tile],
            device_id={"dp": self.partner(bit)},
            device_id_type=pl.DeviceIdType.MESH,
        )

    def gather_stage(self, stage, tile):
        self.copy(stage, tile).wait_recv()
        keep, _, size = self.spans(stage)
        at = pl.ds(pl.multiple_of(keep, 16), size)
        return at, self.buffer[tile, at, :].astype(F32) + self.lands[stage][tile].astype(F32)

    def advance(self, stage, tile):
        at, total = self.gather_stage(stage, tile)
        self.buffer[tile, at, :] = total.astype(BF)
        self.copy(stage + 1, tile).start()


class PackGather:
    def __init__(self, own, other, packs, sends, recvs):
        self.own, self.other, self.packs, self.sends, self.recvs = own, other, packs, sends, recvs
        self.place, self.side = lax.axis_index("dp"), lax.axis_index("mp")
        self.stages = SUM_PLACES.bit_length() - 1

    def greet(self, barrier):
        pl.semaphore_signal(
            barrier, inc=1, device_id={"mp": 1 - self.side}, device_id_type=pl.DeviceIdType.MESH
        )

    def cross(self):
        return pltpu.make_async_remote_copy(
            src_ref=self.other,
            dst_ref=self.packs.at[self.place, self.side],
            send_sem=self.sends.at[self.stages],
            recv_sem=self.recvs.at[self.stages],
            device_id={"mp": 1 - self.side},
            device_id_type=pl.DeviceIdType.MESH,
        )

    def copy(self, stage):
        bit = 1 << stage
        rows = self.packs.at[pl.ds((self.place // bit) * bit, bit)]
        return pltpu.make_async_remote_copy(
            src_ref=rows,
            dst_ref=rows,
            send_sem=self.sends.at[stage],
            recv_sem=self.recvs.at[stage],
            device_id={"dp": self.place + bit - 2 * bit * place_bit(self.place, bit)},
            device_id_type=pl.DeviceIdType.MESH,
        )

    def start(self):
        self.packs[self.place, self.side] = self.own[...]
        self.cross().start()

    def advance(self, stage):
        (self.cross() if stage == 0 else self.copy(stage - 1)).wait_recv()
        self.copy(stage).start()

    def finish(self):
        self.copy(self.stages - 1).wait_recv()
        self.cross().wait_send()
        for stage in range(self.stages):
            self.copy(stage).wait_send()


def attn_grads_kernel(
    first_ref, dattn_ref, dqkv_ref, att_ref, pack_own_ref, pack_other_ref, sums_ref, every_ref,
    first_t, dattn_t, buffer, land0, land1, land2, land3, sends, recvs,
    packs, pack_sends, pack_recvs,
):
    width = first_t.shape[0]
    tiles, _, columns = buffer.shape
    proj_tiles = dqkv_ref.shape[0] // columns
    share = width // SUM_PLACES
    total = DpSum(buffer, (land0, land1, land2, land3), sends, recvs)
    ring = PackGather(pack_own_ref, pack_other_ref, packs, pack_sends, pack_recvs)
    barrier = pltpu.get_barrier_semaphore()
    total.greet(barrier)
    ring.greet(barrier)
    pl.semaphore_wait(barrier, len(HALVING) + 2)
    ring.start()
    for source, target in ((first_ref, first_t), (dattn_ref, dattn_t)):
        for at in range(0, source.shape[0], 512):
            target[:, at : at + 512] = source[at : at + 512, :].T
    half = width // 2

    def step(s, carry):
        @pl.when(s < proj_tiles)
        def _():
            right = dqkv_ref[pl.ds(pl.multiple_of(s * columns, 128), columns), :]
            for at in (0, half):
                store_by_owner(buffer, s, at, nt(first_t[at : at + half, :], right), share)
            total.copy(0, s).start()

        @pl.when(jnp.logical_and(s >= proj_tiles, s < tiles))
        def _():
            right = att_ref[pl.ds(pl.multiple_of((s - proj_tiles) * columns, 128), columns), :]
            for at in (0, half):
                store_by_owner(buffer, s, at, nt(dattn_t[at : at + half, :], right), share)
            total.copy(0, s).start()

        for stage in range(3):
            tile = s - 1 - stage

            @pl.when(jnp.logical_and(tile >= 0, tile < tiles))
            def _():
                total.advance(stage, tile)

        for stage in range(ring.stages):

            @pl.when(s == 2 + 2 * stage)
            def _():
                ring.advance(stage)

        tile = s - 4

        @pl.when(tile >= 0)
        def _():
            sums_ref[tile] = total.gather_stage(3, tile)[1].astype(BF)

        return carry

    lax.fori_loop(0, tiles + 4, step, 0)
    ring.finish()
    every_ref[...] = packs[...]

    def finish(tile, carry):
        for stage in range(4):
            total.copy(stage, tile).wait_send()
        return carry

    lax.fori_loop(0, tiles, finish, 0)


def can_sum_here(width, columns):
    places = lax.axis_size("dp")
    return places == SUM_PLACES and width % (8 * places) == 0 and columns % 384 == 0


def attn_grads(first, dattn, dqkv, att, pack_own, pack_other):
    width = first.shape[1]
    tile = 384
    tiles = (dqkv.shape[0] + att.shape[0]) // tile
    share = width // SUM_PLACES
    vmem = pl.BlockSpec(memory_space=pltpu.VMEM)
    sums, every = pl.pallas_call(
        attn_grads_kernel,
        in_specs=[vmem] * 6,
        out_specs=[vmem] * 2,
        out_shape=[
            jax.ShapeDtypeStruct((tiles, 2 * share, tile), BF),
            jax.ShapeDtypeStruct((SUM_PLACES, 2) + pack_own.shape, F32),
        ],
        scratch_shapes=[
            pltpu.VMEM((width, first.shape[0]), BF),
            pltpu.VMEM((width, dattn.shape[0]), BF),
            pltpu.VMEM((tiles, width, tile), BF),
            pltpu.VMEM((tiles, width // 2, tile), BF),
            pltpu.VMEM((tiles, width // 4, tile), BF),
            pltpu.VMEM((tiles, width // 8, tile), BF),
            pltpu.VMEM((tiles, width // 8, tile), BF),
            pltpu.SemaphoreType.DMA((4, tiles)),
            pltpu.SemaphoreType.DMA((4, tiles)),
            pltpu.VMEM((SUM_PLACES, 2) + pack_own.shape, F32),
            pltpu.SemaphoreType.DMA((SUM_PLACES.bit_length(),)),
            pltpu.SemaphoreType.DMA((SUM_PLACES.bit_length(),)),
        ],
        compiler_params=pltpu.CompilerParams(
            vmem_limit_bytes=VMEM_LIMIT, collective_id=1, has_side_effects=True
        ),
        cost_estimate=cost(1e7, 1e5),
    )(first, dattn, dqkv, att, pack_own, pack_other)
    here = place_bit(lax.axis_index("dp"), FINAL) * share
    mine = lax.dynamic_slice_in_dim(sums, here, share, 1)
    return jnp.transpose(mine, (1, 0, 2)).reshape(share, -1), every


def shift_mp(value, steps):
    ways = lax.axis_size("mp")
    return lax.ppermute(value, "mp", [(i, (i - steps) % ways) for i in range(ways)])


def near_halves(block):
    half = block.shape[0] // 2
    core = lax.axis_index("dp") % 2
    mine = lax.dynamic_slice_in_dim(block, core * half, half, 0)
    return [shift_mp(mine, steps) for steps in range(1, lax.axis_size("mp"))]


def with_far_halves(nears):
    places = lax.axis_size("dp")
    core = lax.axis_index("dp") % 2
    got = []
    for near in nears:
        half = near.shape[0]
        far = lax.ppermute(near, "dp", [(i, i ^ 1) for i in range(places)])
        whole = jnp.zeros((2 * half,) + near.shape[1:], near.dtype)
        whole = lax.dynamic_update_slice_in_dim(whole, near, core * half, 0)
        got.append(lax.dynamic_update_slice_in_dim(whole, far, (1 - core) * half, 0))
    return got


def from_others(block):
    return with_far_halves(near_halves(block))


def home(parts):
    total = parts[0].astype(F32)
    for steps in range(1, len(parts)):
        total = total + shift_mp(parts[steps], -steps).astype(F32)
    return total


def to_lanes_rows(size):
    return -(-size // 1024) * 8


def to_lanes(part):
    flat = part.reshape(-1)
    rows = to_lanes_rows(flat.shape[0])
    return jnp.pad(flat, (0, rows * 128 - flat.shape[0])).reshape(rows, 128)


def scatter_dp(part):
    return lax.psum_scatter(part, "dp", scatter_dimension=0, tiled=True)


def local(
    tokens, conditioning, kept_ids, ada_weight, ada_bias, attn_qkv, attn_out, mlp_up, mlp_down,
    rel_table, grad_out_kept, grad_out_full,
):
    ways = lax.axis_size("mp")
    place = lax.axis_index("mp")
    images_group = conditioning.shape[0]
    images = images_group // ways
    width = tokens.shape[1]
    keep = kept_ids.shape[1]
    padded = -(-keep // 64) * 64
    per_block = rel_table.shape[0]
    cols = ada_bias.shape[0]

    silu_cond = jax.nn.silu(conditioning.astype(F32)).astype(BF)
    columns = (jnp.dot(silu_cond, ada_weight, preferred_element_type=F32) + ada_bias).astype(BF)
    mod = lax.all_to_all(columns, "mp", split_axis=0, concat_axis=1, tiled=True)
    mod = jnp.pad(mod.astype(F32).reshape(images, 6, width), ((0, 0), (0, 2), (0, 0)))

    weight_own = jnp.transpose(attn_qkv.reshape(width, -1))
    weight_t = jnp.concatenate([weight_own] + from_others(weight_own), axis=0)
    out_w = jnp.concatenate([attn_out] + from_others(attn_out), axis=0)
    table = jnp.concatenate(
        [rel_table] + [shift_mp(rel_table, s) for s in range(1, ways)], axis=0
    )
    bias = bias_whole(table)
    weight_t, out_w, late_up, late_down = lax.optimization_barrier(
        (weight_t, out_w, mlp_up, mlp_down)
    )
    near_up = near_halves(late_up)

    own_kept = lax.dynamic_slice_in_dim(kept_ids, place * images, images, 0)
    own_kept = jnp.pad(own_kept, ((0, 0), (0, padded - keep)), constant_values=-1)
    pick = (own_kept[:, :, None] == jnp.arange(PATCHES, dtype=jnp.int32)).astype(BF)
    grads = jnp.concatenate(
        [
            grad_out_full.reshape(images, PATCHES, width),
            jnp.pad(
                grad_out_kept.reshape(images, keep, width), ((0, 0), (0, padded - keep), (0, 0))
            ),
        ],
        axis=1,
    )
    dmlp = (mod[:, 5:6] * grads.astype(F32)).astype(BF).reshape(-1, width)
    grads = grads.reshape(-1, width)

    near_up, bias, mod, late_down = lax.optimization_barrier((near_up, bias, mod, late_down))
    near_down = near_halves(late_down)
    up_others = with_far_halves(near_up)
    first, qkv, att, lse, middle, second, branch = forward(
        tokens, mod, pick, weight_t, out_w, bias, per_block
    )
    near_down, second = lax.optimization_barrier((near_down, second))
    down_others = with_far_halves(near_down)
    (branch_mlp, dsecond, grads_own), tile_own = mlp(second, dmlp, mlp_up, mlp_down)
    reduced = [scatter_dp(grads_own)]
    for up, down in zip(up_others, down_others):
        (branch_mlp, dsecond, grads_next), _ = mlp(
            second, dmlp, up, down, (branch_mlp, dsecond)
        )
        reduced.append(scatter_dp(grads_next))
    out, dtok, dmod, dattn, dqkv, strips = backward(
        tokens, mod, pick, weight_t, out_w, bias, qkv, lse, middle, branch, branch_mlp, dsecond,
        grads, per_block,
    )
    proj_block, out_block = weight_own.shape[0], attn_out.shape[0]
    dqkv, reduced[0] = lax.optimization_barrier((dqkv, reduced[0]))
    dmod_rows = dmod[:, :6].reshape(images, 6 * width)
    dtables = table_of_strips(strips)
    here = can_sum_here(width, dqkv.shape[0]) and att.shape[0] % 384 == 0 and ways == 2
    if here:
        own_cond_rows = lax.dynamic_slice_in_dim(silu_cond, place * images, images, 0)
        packs = []
        for steps in range(ways):
            at = (place + steps) % ways
            parts = (
                lax.dynamic_slice_in_dim(dmod_rows, at * cols, cols, 1),
                dtables[steps * per_block : (steps + 1) * per_block],
                own_cond_rows.astype(F32),
            )
            packs.append(jnp.concatenate([to_lanes(part) for part in parts], axis=0))
        attn_sums, every = attn_grads(first, dattn, dqkv, att, *packs)
        places = every.shape[0]
        every = every.reshape(places * ways, -1, 128)
        got, end = [], 0
        for part in parts:
            start, end = end, end + to_lanes_rows(part.size)
            got.append(every[:, start:end].reshape(places * ways, -1)[:, : part.size])
        all_columns = got[0].reshape(-1, cols)
        dtable = jnp.sum(got[1], axis=0).reshape(rel_table.shape)
        all_cond = got[2].reshape(-1, width)
        dcolumns = lax.dynamic_slice_in_dim(
            all_columns, lax.axis_index("dp") * images_group, images_group, 0
        )
    else:
        dweight = dot(first, dqkv, (0, 1)).astype(BF)
        dout_t = dot(dattn, att, (0, 1)).astype(BF)
        attn_sums = scatter_dp(jnp.concatenate([dweight, dout_t], axis=1))
        dcolumns = lax.all_to_all(dmod_rows, "mp", split_axis=1, concat_axis=0, tiled=True)
        dtable = home(list(jnp.split(dtables, ways, axis=0)))
        all_columns = lax.all_gather(dcolumns, "dp", axis=0, tiled=True)
        dtable = lax.psum(dtable, "dp")
        all_cond = lax.all_gather(silu_cond, "dp", axis=0, tiled=True).astype(F32)
    split = ways * proj_block
    attn_parts = [
        jnp.concatenate(
            [
                attn_sums[:, j * proj_block : (j + 1) * proj_block],
                attn_sums[:, split + j * out_block : split + (j + 1) * out_block],
            ],
            axis=1,
        )
        for j in range(ways)
    ]
    mlp_grads = home(reduced)
    attn_total = home(attn_parts)
    grad_up, grad_down_t = split_mlp_grads(mlp_grads, tile_own)
    grad_qkv = attn_total[:, :proj_block].reshape(-1, 3, proj_block // 3)
    grad_out = jnp.transpose(attn_total[:, proj_block:])

    slice_width = width // lax.axis_size("dp")
    cond_slice = lax.dynamic_slice_in_dim(
        all_cond, lax.axis_index("dp") * slice_width, slice_width, 1
    )
    grad_ada_weight = lax.dot_general(
        cond_slice, all_columns, (((0,), (0,)), ((), ())), precision=PRECISE
    )
    grad_ada_bias = jnp.sum(all_columns, axis=0)
    dcolumns_high = dcolumns.astype(BF)
    dcolumns_low = (dcolumns - dcolumns_high.astype(F32)).astype(BF)
    silu_part = nt(jnp.concatenate([dcolumns_high, dcolumns_low], axis=0), ada_weight)
    silu_part = silu_part[:images_group] + silu_part[images_group:]
    shares = lax.all_to_all(
        silu_part.astype(BF).reshape(ways, images, width), "mp", split_axis=0, concat_axis=0,
        tiled=True,
    )
    grad_silu = jnp.sum(shares.astype(F32), axis=0)
    own_cond = lax.dynamic_slice_in_dim(conditioning, place * images, images, 0).astype(F32)
    grad_cond = jax.vjp(jax.nn.silu, own_cond)[1](grad_silu)[0].astype(BF)

    out = out.reshape(images, PATCHES + padded, width)
    out_full = out[:, :PATCHES].reshape(-1, width)
    out_kept = out[:, PATCHES : PATCHES + keep].reshape(-1, width)
    return (
        out_kept, out_full, dtok, grad_cond, grad_ada_weight, grad_ada_bias, grad_qkv, grad_out,
        grad_up, jnp.transpose(grad_down_t), dtable,
    )


def solution(mesh):
    both = P(("dp", "mp"), None)
    return jax.shard_map(
        local,
        mesh=mesh,
        in_specs=(
            both, P("dp", None), P("dp", None), P(None, "mp"), P("mp"), P(None, None, "mp"),
            P("mp", None), P(None, "mp"), P("mp", None), P("mp", None), both, both,
        ),
        out_specs=(
            both, both, both, both, P("dp", "mp"), P("mp"), P("dp", None, "mp"), P("mp", "dp"),
            P("dp", "mp"), P("mp", "dp"), P("mp", None),
        ),
        check_vma=False,
    )
```

```python
import functools
import math

import jax
import jax.numpy as jnp
from jax import lax
from jax.experimental import pallas as pl
from jax.experimental.pallas import tpu as pltpu
from jax.sharding import PartitionSpec as P

HEAD_DIM = 72
GRID = 16
PATCHES = 256
BUCKETS = 961
SPAN = 2 * GRID - 1
EPSILON = 1e-06
PRECISE = lax.Precision.HIGHEST
BF = jnp.bfloat16
F32 = jnp.float32
LOG2E = math.log2(math.e)
VMEM_LIMIT = 60 * 1024 * 1024


def dot(a, b, dims):
    return lax.dot_general(a, b, ((dims[0:1], dims[1:2]), ((), ())), preferred_element_type=F32)


def nn(a, b):
    return dot(a, b, (1, 0))


def nt(a, b):
    return dot(a, b, (1, 1))


def tn(a, b):
    return dot(a, b, (0, 0))


def normalize(rows):
    centered = rows - jnp.mean(rows, axis=-1, keepdims=True)
    inverse = lax.rsqrt(jnp.mean(centered * centered, axis=-1, keepdims=True) + EPSILON)
    return centered * inverse, inverse


def norm_back(normed, inverse, upstream):
    return inverse * (
        upstream
        - jnp.mean(upstream, axis=-1, keepdims=True)
        - normed * jnp.mean(upstream * normed, axis=-1, keepdims=True)
    )


def params(n_grid=1):
    return pltpu.CompilerParams(
        vmem_limit_bytes=VMEM_LIMIT, dimension_semantics=("arbitrary",) * n_grid
    )


def cost(flops, bytes_accessed, transcendentals=0):
    return pl.CostEstimate(
        flops=int(flops), bytes_accessed=int(bytes_accessed), transcendentals=int(transcendentals)
    )


def const_spec(shape):
    return pl.BlockSpec(shape, lambda *_: (0,) * len(shape), pipeline_mode=pl.Buffered(1))


def bias_kernel(strip_ref, bias_ref):
    strip = strip_ref[0]
    for key_row in range(GRID):
        start = (GRID - 1 - key_row) * GRID
        bias_ref[0, key_row * GRID : (key_row + 1) * GRID, :] = strip[:, start : start + PATCHES]


def bias_whole(table):
    heads = table.shape[0]
    grid_table = table.reshape(heads, SPAN, SPAN) * LOG2E
    strip = jnp.stack(
        [grid_table[:, :, GRID - 1 - c : 2 * GRID - 1 - c] for c in range(GRID)], axis=1
    ).reshape(heads, GRID, SPAN * GRID)
    strip = jnp.pad(strip, ((0, 0), (0, 0), (0, 512 - SPAN * GRID)))
    return pl.pallas_call(
        bias_kernel,
        grid=(heads,),
        in_specs=[pl.BlockSpec((1, GRID, 512), lambda h: (h, 0, 0))],
        out_specs=pl.BlockSpec((1, PATCHES, PATCHES), lambda h: (h, 0, 0)),
        out_shape=jax.ShapeDtypeStruct((heads, PATCHES, PATCHES), F32),
        compiler_params=params(),
        cost_estimate=cost(0, heads * PATCHES * PATCHES * 4),
    )(strip)


def table_of_strips(strips):
    heads = strips.shape[0]
    parts = strips[:, :, : SPAN * GRID].reshape(heads, GRID, SPAN, GRID)
    total = jnp.zeros((heads, SPAN, SPAN), F32)
    for c in range(GRID):
        total = total + jnp.pad(parts[:, c], ((0, 0), (0, 0), (GRID - 1 - c, c)))
    return total.reshape(heads, BUCKETS)


def head_rows(head, per_block):
    base = (head // per_block) * (3 * per_block * HEAD_DIM) + (head % per_block) * HEAD_DIM
    step = per_block * HEAD_DIM
    return [pl.ds(pl.multiple_of(base + c * step, 8), HEAD_DIM) for c in range(3)]


def key_mask(pick):
    ones = jnp.ones((pick.shape[0], PATCHES), BF)
    return (tn(pick, ones) - 1.0) * 1e30


def part_copies(layout, parts, whole, sems):
    core = lax.axis_index("dp") % 2
    copies = []
    for index, ((base, half, near), part) in enumerate(zip(layout, parts)):
        start = base + (core if near else 1 - core) * half
        rows = pl.ds(pl.multiple_of(start, 16), part.shape[0])
        copies.append(pltpu.make_async_copy(part, whole.at[rows, :], sems.at[index]))
    return copies


def run_copies(copies):
    for copy in copies:
        copy.start()
    for copy in copies:
        copy.wait()


def start_fetch(own, target, sems):
    half = target.shape[0]
    start = (lax.axis_index("dp") % 2) * half
    return pltpu.make_async_remote_copy(
        src_ref=own.at[pl.ds(pl.multiple_of(start, 16), half), :],
        dst_ref=target,
        send_sem=sems.at[0],
        recv_sem=sems.at[1],
        device_id={"mp": 1 - lax.axis_index("mp")},
        device_id_type=pl.DeviceIdType.MESH,
    )


def greet_peers(with_core):
    barrier = pltpu.get_barrier_semaphore()
    peers = [{"mp": 1 - lax.axis_index("mp")}]
    if with_core:
        place = lax.axis_index("dp")
        peers.append({"dp": place + 1 - 2 * (place % 2)})
    for peer in peers:
        pl.semaphore_signal(
            barrier, inc=1, device_id=peer, device_id_type=pl.DeviceIdType.MESH
        )
    pl.semaphore_wait(barrier, len(peers))


def forward_kernel(per_block, weight_layout, out_layout, fetch, *refs):
    tok_ref, mod_ref, pick_ref, bias_ref = refs[:4]
    refs = refs[4:]
    weight_parts, refs = refs[: len(weight_layout)], refs[len(weight_layout) :]
    out_parts, refs = refs[: len(out_layout)], refs[len(out_layout) :]
    if fetch:
        send_ref, refs = refs[0], refs[1:]
    first_ref, qkv_ref, att_ref, lse_ref, middle_ref, second_ref, branch_ref = refs[:7]
    refs = refs[7:]
    if fetch:
        got_ref, refs = refs[0], refs[1:]
    qkv_s, att_s, attk_s, weight_ref, out_w_ref, part_sems, fetch_sems = refs

    @pl.when(pl.program_id(0) == 0)
    def _():
        copies = part_copies(weight_layout, weight_parts, weight_ref, part_sems.at[0])
        copies += part_copies(out_layout, out_parts, out_w_ref, part_sems.at[1])
        if fetch:
            greet_peers(False)
            start_fetch(send_ref, got_ref, fetch_sems).start()
        run_copies(copies)

    forward_body(
        per_block, tok_ref, mod_ref, pick_ref, weight_ref, out_w_ref, bias_ref,
        first_ref, qkv_ref, att_ref, lse_ref, middle_ref, second_ref, branch_ref,
        qkv_s, att_s, attk_s,
    )
    if fetch:

        @pl.when(pl.program_id(0) == pl.num_programs(0) - 1)
        def _():
            start_fetch(send_ref, got_ref, fetch_sems).wait()


def forward_body(
    per_block, tok_ref, mod_ref, pick_ref, weight_ref, out_w_ref, bias_ref,
    first_ref, qkv_ref, att_ref, lse_ref, middle_ref, second_ref, branch_ref,
    qkv_s, att_s, attk_s,
):
    heads = bias_ref.shape[0]
    tok = tok_ref[...].astype(F32)
    shift_one, scale_one, gate_one = mod_ref[0, 0:1], mod_ref[0, 1:2], mod_ref[0, 2:3]
    shift_two, scale_two = mod_ref[0, 3:4], mod_ref[0, 4:5]
    normed, _ = normalize(tok)
    first = (normed * (1.0 + scale_one) + shift_one).astype(BF)
    first_ref[...] = first
    step = weight_ref.shape[0] // 6
    for c in range(6):
        rows = slice(c * step, (c + 1) * step)
        part = nt(weight_ref[rows, :], first)
        qkv_s[rows, :] = part
        qkv_ref[rows, :] = part.astype(BF)
    pick = pick_ref[0]
    mask = key_mask(pick)
    scale = HEAD_DIM ** (-0.5) * LOG2E

    def one_head(head, carry):
        q_at, k_at, v_at = head_rows(head, per_block)
        queries = qkv_s[q_at, :].astype(BF)
        keys = qkv_s[k_at, :].astype(BF)
        values = qkv_s[v_at, :].astype(BF)
        scores = tn(keys, queries) * scale + bias_ref[head]
        here = pl.ds(pl.multiple_of(head * HEAD_DIM, 8), HEAD_DIM)

        def attend(scores):
            top = jnp.max(scores, axis=0, keepdims=True)
            weights = jnp.exp2(scores - top)
            total = jnp.sum(weights, axis=0, keepdims=True)
            probs = (weights * (1.0 / total)).astype(BF)
            return nn(values, probs), top + jnp.log2(total)

        att_s[here, :], lse_ref[0, pl.ds(head, 1), :] = attend(scores)
        attk_s[here, :], lse_ref[0, pl.ds(heads + head, 1), :] = attend(scores + mask)
        return carry

    lax.fori_loop(0, heads, one_head, 0, unroll=2)
    att = att_s[...].astype(BF)
    att_kept = attk_s[...].astype(BF)
    att_ref[:, :PATCHES] = att
    att_ref[:, PATCHES:] = att_kept
    out_w = out_w_ref[...]
    kept_att = nt(pick, att_kept).astype(BF)
    for rows, source, residual in (
        (slice(0, PATCHES), att.T, tok),
        (slice(PATCHES, PATCHES + pick.shape[0]), kept_att, nn(pick, tok_ref[...])),
    ):
        branch = nn(source, out_w)
        branch_ref[rows, :] = branch.astype(BF)
        middle = residual + gate_one * branch
        middle_ref[rows, :] = middle
        second_ref[rows, :] = (normalize(middle)[0] * (1.0 + scale_two) + shift_two).astype(BF)


def whole_rows(layout, parts):
    return sum(part.shape[0] for part in parts)


ANYWHERE = pl.BlockSpec(memory_space=pl.ANY)


def forward(tokens, mod, pick, bias, weight, out_weight, per_block, send=None):
    images, padded = pick.shape[0], pick.shape[1]
    width = tokens.shape[1]
    rows = PATCHES + padded
    heads = bias.shape[0]
    (weight_layout, weight_parts), (out_layout, out_parts) = weight, out_weight
    proj = whole_rows(*weight)
    fetch = send is not None
    most = max(len(weight_parts), len(out_parts))
    extra_shapes, extra = [], []
    compiler_params = params()
    if fetch:
        extra_shapes = [jax.ShapeDtypeStruct((send.shape[0] // 2, send.shape[1]), BF)]
        extra = [send]
        compiler_params = pltpu.CompilerParams(
            vmem_limit_bytes=VMEM_LIMIT, dimension_semantics=("arbitrary",),
            collective_id=2, has_side_effects=True,
        )
    return pl.pallas_call(
        functools.partial(forward_kernel, per_block, weight_layout, out_layout, fetch),
        grid=(images,),
        in_specs=[
            pl.BlockSpec((PATCHES, width), lambda i: (i, 0)),
            pl.BlockSpec((1, 8, width), lambda i: (i, 0, 0)),
            pl.BlockSpec((1, padded, PATCHES), lambda i: (i, 0, 0)),
            const_spec(bias.shape),
        ]
        + [ANYWHERE] * (len(weight_parts) + len(out_parts) + len(extra)),
        out_specs=[
            pl.BlockSpec((PATCHES, width), lambda i: (i, 0)),
            pl.BlockSpec((proj, PATCHES), lambda i: (0, i)),
            pl.BlockSpec((width, 2 * PATCHES), lambda i: (0, i)),
            pl.BlockSpec((1, 2 * heads, PATCHES), lambda i: (i, 0, 0)),
            pl.BlockSpec((rows, width), lambda i: (i, 0)),
            pl.BlockSpec((rows, width), lambda i: (i, 0)),
            pl.BlockSpec((rows, width), lambda i: (i, 0)),
        ]
        + [ANYWHERE] * len(extra),
        out_shape=[
            jax.ShapeDtypeStruct((images * PATCHES, width), BF),
            jax.ShapeDtypeStruct((proj, images * PATCHES), BF),
            jax.ShapeDtypeStruct((width, images * 2 * PATCHES), BF),
            jax.ShapeDtypeStruct((images, 2 * heads, PATCHES), F32),
            jax.ShapeDtypeStruct((images * rows, width), F32),
            jax.ShapeDtypeStruct((images * rows, width), BF),
            jax.ShapeDtypeStruct((images * rows, width), BF),
        ]
        + extra_shapes,
        scratch_shapes=[
            pltpu.VMEM((proj, PATCHES), F32),
            pltpu.VMEM((width, PATCHES), F32),
            pltpu.VMEM((width, PATCHES), F32),
            pltpu.VMEM((proj, width), BF),
            pltpu.VMEM((width, width), BF),
            pltpu.SemaphoreType.DMA((2, most)),
            pltpu.SemaphoreType.DMA((2,)),
        ],
        compiler_params=compiler_params,
        cost_estimate=cost(images * 2e9, images * 8e6),
    )(tokens, mod, pick, bias, *weight_parts, *out_parts, *extra)


def gelu_pair(pre):
    root = math.sqrt(2.0 / math.pi)
    square = pre * pre
    bend = jnp.tanh(pre * (root + (root * 0.044715) * square))
    half = 0.5 + 0.5 * bend
    slope = half + (0.5 * pre) * (1.0 - bend * bend) * (root + (3.0 * root * 0.044715) * square)
    return pre * half, slope


def mlp_kernel(
    chunk, fresh, fetch, second_ref, dmlp_ref, up_ref, down_ref, *refs
):
    if fetch:
        near_ref, send_ref = refs[:2]
        *refs, moves, fetch_sems = refs[2:]
        up_all, down_all = refs[3:5]
        refs = refs[:3] + refs[5:]
    if fresh:
        branch_ref, dsecond_ref, grads_ref, second_t, dmlp_t, hidden_s, dpre_s, sem = refs
    else:
        branch_in, dsecond_in, branch_ref, dsecond_ref, grads_ref = refs[:5]
        second_t, dmlp_t, hidden_s, dpre_s, sem = refs[5:]
    rows = second_ref.shape[0]
    tile = up_ref.shape[1]
    width = second_ref.shape[1]

    def half_moves(source, target, at):
        place = lax.axis_index("dp")
        half = source.shape[0]
        rows = target.at[pl.ds(pl.multiple_of((place % 2) * half, 16), half), :]
        return pltpu.make_async_remote_copy(
            src_ref=source,
            dst_ref=rows,
            send_sem=moves.at[at],
            recv_sem=moves.at[at + 1],
            device_id={"dp": place + 1 - 2 * (place % 2)},
            device_id_type=pl.DeviceIdType.MESH,
        ), pltpu.make_async_copy(source, rows, moves.at[at + 2])

    def down_half():
        half = down_all.shape[0] // 2
        start = (lax.axis_index("dp") % 2) * half
        return down_all.at[pl.ds(pl.multiple_of(start, 16), half), :]

    @pl.when(pl.program_id(0) == 0)
    def _():
        if fetch:
            greet_peers(True)
            start_fetch(send_ref, down_half(), fetch_sems).start()
            for copy in half_moves(near_ref, up_all, 0):
                copy.start()
        if fresh:
            branch_ref[...] = jnp.zeros_like(branch_ref)
            dsecond_ref[...] = jnp.zeros_like(dsecond_ref)
        else:
            one = pltpu.make_async_copy(branch_in, branch_ref, sem.at[0])
            two = pltpu.make_async_copy(dsecond_in, dsecond_ref, sem.at[1])
            one.start()
            two.start()
        for at in range(0, rows, chunk):
            second_t[:, at : at + chunk] = second_ref[at : at + chunk, :].T
            dmlp_t[:, at : at + chunk] = dmlp_ref[at : at + chunk, :].T
        if not fresh:
            one.wait()
            two.wait()

    def one_chunk(index, carry):
        at = pl.ds(pl.multiple_of(index * chunk, chunk), chunk)
        pre = nn(second_ref[at, :], up_ref[...])
        dhidden = nt(dmlp_ref[at, :], down_ref[...])
        value, slope = gelu_pair(pre)
        hidden = value.astype(BF)
        dpre = (dhidden * slope).astype(BF)
        hidden_s[at, :] = hidden
        dpre_s[at, :] = dpre
        branch_ref[at, :] += nn(hidden, down_ref[...])
        dsecond_ref[at, :] += nt(dpre, up_ref[...])
        return carry

    lax.fori_loop(0, rows // chunk, one_chunk, 0)
    part = width // 3
    for c in range(3):
        at = slice(c * part, (c + 1) * part)
        grads_ref[at, :tile] = nn(second_t[at, :], dpre_s[...]).astype(BF)
        grads_ref[at, tile:] = nn(dmlp_t[at, :], hidden_s[...]).astype(BF)

    if fetch:

        @pl.when(pl.program_id(0) == pl.num_programs(0) - 1)
        def _():
            start_fetch(send_ref, down_half(), fetch_sems).wait()
            last = half_moves(down_half(), down_all, 3)[0]
            last.start()
            for copy in half_moves(near_ref, up_all, 0):
                copy.wait()
            last.wait()


def mlp_chunk(rows):
    for chunk in (896, 448, 64):
        if rows % chunk == 0:
            return chunk
    return rows


def mlp(second, dmlp, up, down, sums=None, fetch=None):
    rows, width = second.shape
    hidden = up.shape[1]
    tile = 768 if hidden % 768 == 0 else hidden
    fresh = sums is None
    chunk = mlp_chunk(rows)
    in_specs = [
        const_spec(second.shape),
        const_spec(second.shape),
        pl.BlockSpec((width, tile), lambda f: (0, f)),
        pl.BlockSpec((tile, width), lambda f: (f, 0)),
    ]
    operands = [second, dmlp, up, down]
    out_specs = [
        const_spec(second.shape),
        const_spec(second.shape),
        pl.BlockSpec((width, 2 * tile), lambda f: (0, f)),
    ]
    out_shape = [
        jax.ShapeDtypeStruct(second.shape, F32),
        jax.ShapeDtypeStruct(second.shape, F32),
        jax.ShapeDtypeStruct((width, 2 * hidden), BF),
    ]
    scratch = [
        pltpu.VMEM((width, rows), BF),
        pltpu.VMEM((width, rows), BF),
        pltpu.VMEM((rows, tile), BF),
        pltpu.VMEM((rows, tile), BF),
        pltpu.SemaphoreType.DMA((2,)),
    ]
    compiler_params = params()
    if not fresh:
        in_specs += [ANYWHERE] * 2
        operands += list(sums)
    if fetch is not None:
        in_specs += [ANYWHERE] * 2
        operands += list(fetch)
        out_specs += [ANYWHERE] * 2
        out_shape += [jax.ShapeDtypeStruct(up.shape, BF), jax.ShapeDtypeStruct(down.shape, BF)]
        scratch += [pltpu.SemaphoreType.DMA((6,)), pltpu.SemaphoreType.DMA((2,))]
        compiler_params = pltpu.CompilerParams(
            vmem_limit_bytes=VMEM_LIMIT, dimension_semantics=("arbitrary",),
            collective_id=3, has_side_effects=True,
        )
    return pl.pallas_call(
        functools.partial(mlp_kernel, chunk, fresh, fetch is not None),
        grid=(hidden // tile,),
        in_specs=in_specs,
        out_specs=out_specs,
        out_shape=out_shape,
        scratch_shapes=scratch,
        compiler_params=compiler_params,
        cost_estimate=cost(6e10, 6e7) if fresh else cost(1e7, 1e5),
    )(*operands), tile


def split_mlp_grads(grads, tile):
    parts = grads.reshape(grads.shape[0], -1, 2, tile)
    return (
        parts[:, :, 0].reshape(grads.shape[0], -1),
        parts[:, :, 1].reshape(grads.shape[0], -1),
    )


def backward_kernel(per_block, weight_layout, out_layout, *refs):
    count = len(weight_layout) + len(out_layout)
    weight_parts = refs[: len(weight_layout)]
    out_parts = refs[len(weight_layout) : count]
    weight_ref, out_w_ref, sems = refs[-3:]

    @pl.when(pl.program_id(0) == 0)
    def _():
        run_copies(
            part_copies(weight_layout, weight_parts, weight_ref, sems.at[0])
            + part_copies(out_layout, out_parts, out_w_ref, sems.at[1])
        )

    backward_body(per_block, weight_ref, out_w_ref, *refs[count:-3])


def backward_body(
    per_block, weight_ref, out_w_ref, tok_ref, mod_ref, pick_ref, bias_ref,
    qkv_ref, lse_ref, middle_ref, branch_ref, mlp_ref, dsecond_ref, grad_ref,
    out_ref, dtok_ref, dmod_ref, dattn_ref, dqkv_ref, strips_ref,
    qkv_s, datt_s, dattk_s, dscores_s,
):
    heads = bias_ref.shape[0]
    step = pl.program_id(0)
    shift_one, scale_one, gate_one = mod_ref[0, 0:1], mod_ref[0, 1:2], mod_ref[0, 2:3]
    scale_two, gate_two = mod_ref[0, 4:5], mod_ref[0, 5:6]
    pick = pick_ref[0]
    dmiddles = []
    sums = [0.0, 0.0, 0.0, 0.0]
    for rows in (slice(0, PATCHES), slice(PATCHES, PATCHES + pick.shape[0])):
        middle = middle_ref[rows, :]
        branch_mlp = mlp_ref[rows, :]
        dsecond = dsecond_ref[rows, :]
        grad = grad_ref[rows, :].astype(F32)
        out_ref[rows, :] = (middle + gate_two * branch_mlp).astype(BF)
        normed, inverse = normalize(middle)
        dmiddle = grad + norm_back(normed, inverse, dsecond * (1.0 + scale_two))
        branch = branch_ref[rows, :].astype(F32)
        for c, term in enumerate(
            (dmiddle * branch, dsecond, dsecond * normed, grad * branch_mlp)
        ):
            sums[c] = sums[c] + jnp.sum(term, axis=0, keepdims=True)
        dmiddles.append(dmiddle)
    for c in range(4):
        dmod_ref[0, 2 + c : 3 + c, :] = sums[c]
    dattn = (gate_one * dmiddles[0]).astype(BF)
    dattn_kept = tn(pick, (gate_one * dmiddles[1]).astype(BF)).astype(BF)
    dattn_ref[:PATCHES, :] = dattn
    dattn_ref[PATCHES:, :] = dattn_kept
    high = dmiddles[1].astype(BF)
    low = (dmiddles[1] - high.astype(F32)).astype(BF)
    dresid = dmiddles[0] + tn(pick, high) + tn(pick, low)
    datt_s[...] = nt(out_w_ref[...], dattn)
    dattk_s[...] = nt(out_w_ref[...], dattn_kept)
    qkv_s[...] = qkv_ref[...].astype(F32)
    mask = key_mask(pick)
    scale = HEAD_DIM ** (-0.5)

    @pl.when(step == 0)
    def _():
        dscores_s[...] = jnp.zeros_like(dscores_s)

    def one_head(head, carry):
        q_at, k_at, v_at = head_rows(head, per_block)
        queries = qkv_s[q_at, :].astype(BF)
        keys = qkv_s[k_at, :].astype(BF)
        values = qkv_s[v_at, :].astype(BF)
        here = pl.ds(pl.multiple_of(head * HEAD_DIM, 8), HEAD_DIM)
        scores = tn(keys, queries) * (scale * LOG2E) + bias_ref[head]

        def pull(scores, top, upstream):
            probs = jnp.exp2(scores - top)
            dprobs = tn(values, upstream)
            dvalues = nt(upstream, probs.astype(BF))
            weighted = jnp.sum(probs * dprobs, axis=0, keepdims=True)
            return probs * (dprobs - weighted), dvalues

        dscores, dvalues = pull(
            scores, lse_ref[0, pl.ds(head, 1), :], datt_s[here, :].astype(BF)
        )
        dscores_kept, dvalues_kept = pull(
            scores + mask, lse_ref[0, pl.ds(heads + head, 1), :], dattk_s[here, :].astype(BF)
        )
        dscores = dscores + dscores_kept
        dscores_s[head] += dscores
        rounded = dscores.astype(BF)
        qkv_s[q_at, :] = nn(keys, rounded) * scale
        qkv_s[k_at, :] = nt(queries, rounded) * scale
        qkv_s[v_at, :] = dvalues + dvalues_kept
        return carry

    lax.fori_loop(0, heads, one_head, 0, unroll=2)
    dqkv = qkv_s[...].astype(BF)
    dqkv_ref[...] = dqkv
    dfirst = tn(dqkv, weight_ref[...])
    normed, inverse = normalize(tok_ref[...].astype(F32))
    dmod_ref[0, 0:1, :] = jnp.sum(dfirst, axis=0, keepdims=True)
    dmod_ref[0, 1:2, :] = jnp.sum(dfirst * normed, axis=0, keepdims=True)
    dmod_ref[0, 6:8, :] = jnp.zeros((2, dfirst.shape[1]), F32)
    dtok_ref[...] = (dresid + norm_back(normed, inverse, dfirst * (1.0 + scale_one))).astype(BF)

    @pl.when(step == pl.num_programs(0) - 1)
    def _():
        def fold(head, carry):
            strip = jnp.zeros((GRID, 512), F32)
            for key_row in range(GRID):
                start = (GRID - 1 - key_row) * GRID
                block = dscores_s[head, key_row * GRID : (key_row + 1) * GRID, :]
                block = jnp.concatenate([block, jnp.zeros((GRID, 512 - PATCHES), F32)], axis=1)
                strip = strip + pltpu.roll(block, start, 1)
            strips_ref[head] = strip
            return carry

        lax.fori_loop(0, heads, fold, 0)


def backward(
    tokens, mod, pick, bias, qkv, lse, middle, branch, branch_mlp, dsecond, grads,
    weight, out_weight, per_block,
):
    (weight_layout, weight_parts), (out_layout, out_parts) = weight, out_weight
    most = max(len(weight_parts), len(out_parts))
    proj = whole_rows(*weight)
    images, padded = pick.shape[0], pick.shape[1]
    width = tokens.shape[1]
    rows = PATCHES + padded
    heads = bias.shape[0]
    by_row = pl.BlockSpec((rows, width), lambda i: (i, 0))
    return pl.pallas_call(
        functools.partial(backward_kernel, per_block, weight_layout, out_layout),
        grid=(images,),
        in_specs=[ANYWHERE] * (len(weight_parts) + len(out_parts))
        + [
            pl.BlockSpec((PATCHES, width), lambda i: (i, 0)),
            pl.BlockSpec((1, 8, width), lambda i: (i, 0, 0)),
            pl.BlockSpec((1, padded, PATCHES), lambda i: (i, 0, 0)),
            const_spec(bias.shape),
            pl.BlockSpec((proj, PATCHES), lambda i: (0, i)),
            pl.BlockSpec((1, 2 * heads, PATCHES), lambda i: (i, 0, 0)),
            by_row,
            by_row,
            by_row,
            by_row,
            by_row,
        ],
        out_specs=[
            by_row,
            pl.BlockSpec((PATCHES, width), lambda i: (i, 0)),
            pl.BlockSpec((1, 8, width), lambda i: (i, 0, 0)),
            pl.BlockSpec((2 * PATCHES, width), lambda i: (i, 0)),
            pl.BlockSpec((proj, PATCHES), lambda i: (0, i)),
            const_spec((heads, GRID, 512)),
        ],
        out_shape=[
            jax.ShapeDtypeStruct((images * rows, width), BF),
            jax.ShapeDtypeStruct((images * PATCHES, width), BF),
            jax.ShapeDtypeStruct((images, 8, width), F32),
            jax.ShapeDtypeStruct((images * 2 * PATCHES, width), BF),
            jax.ShapeDtypeStruct((proj, images * PATCHES), BF),
            jax.ShapeDtypeStruct((heads, GRID, 512), F32),
        ],
        scratch_shapes=[
            pltpu.VMEM((proj, PATCHES), F32),
            pltpu.VMEM((width, PATCHES), F32),
            pltpu.VMEM((width, PATCHES), F32),
            pltpu.VMEM((heads, PATCHES, PATCHES), F32),
            pltpu.VMEM((proj, width), BF),
            pltpu.VMEM((width, width), BF),
            pltpu.SemaphoreType.DMA((2, most)),
        ],
        compiler_params=params(),
        cost_estimate=cost(1e7, 1e5),
    )(
        *weight_parts, *out_parts, tokens, mod, pick, bias, qkv, lse, middle, branch, branch_mlp,
        dsecond, grads,
    )


SUM_PLACES = 16
HALVING = (1, 2, 8)
FINAL = 4


def place_bit(place, bit):
    return (place // bit) % 2


def unit_start(owner, share):
    index = 0
    for bit in HALVING + (FINAL,):
        index = index * 2 + place_bit(owner, bit)
    return index * share


def store_by_owner(buffer, tile, at, block, share):
    first_owner = at // share
    owners = block.shape[0] // share
    for k in range(owners):
        owner = first_owner + k
        if place_bit(owner, FINAL):
            continue
        pair = k + FINAL
        both = jnp.concatenate(
            [block[k * share : (k + 1) * share], block[pair * share : (pair + 1) * share]], axis=0
        )
        start = unit_start(owner, share)
        buffer[tile, start : start + 2 * share, :] = both.astype(BF)


class DpSum:
    def __init__(self, buffer, lands, sends, recvs):
        self.buffer, self.lands, self.sends, self.recvs = buffer, lands, sends, recvs
        self.place = lax.axis_index("dp")
        self.rows = buffer.shape[1]

    def partner(self, bit):
        return self.place + bit - 2 * bit * place_bit(self.place, bit)

    def greet(self, barrier):
        for bit in HALVING + (FINAL,):
            pl.semaphore_signal(
                barrier, inc=1, device_id={"dp": self.partner(bit)},
                device_id_type=pl.DeviceIdType.MESH,
            )

    def spans(self, stage):
        start, size = 0, self.rows
        for k, bit in enumerate(HALVING):
            size = size // 2
            mine = place_bit(self.place, bit)
            if k == stage:
                return start + mine * size, start + (1 - mine) * size, size
            start = start + mine * size
        return start, start, size

    def copy(self, stage, tile):
        bit = (HALVING + (FINAL,))[stage]
        _, away, size = self.spans(stage)
        return pltpu.make_async_remote_copy(
            src_ref=self.buffer.at[tile, pl.ds(pl.multiple_of(away, 16), size), :],
            dst_ref=self.lands[stage].at[tile],
            send_sem=self.sends.at[stage, tile],
            recv_sem=self.recvs.at[stage, tile],
            device_id={"dp": self.partner(bit)},
            device_id_type=pl.DeviceIdType.MESH,
        )

    def gather_stage(self, stage, tile):
        self.copy(stage, tile).wait_recv()
        keep, _, size = self.spans(stage)
        at = pl.ds(pl.multiple_of(keep, 16), size)
        return at, self.buffer[tile, at, :].astype(F32) + self.lands[stage][tile].astype(F32)

    def advance(self, stage, tile):
        at, total = self.gather_stage(stage, tile)
        self.buffer[tile, at, :] = total.astype(BF)
        self.copy(stage + 1, tile).start()


def pack_slot(place):
    return sum(
        place_bit(place, SUM_PLACES >> (k + 1)) << k for k in range(SUM_PLACES.bit_length() - 1)
    )


class PackGather:
    def __init__(self, own, other, packs, sends, recvs):
        self.own, self.other, self.packs, self.sends, self.recvs = own, other, packs, sends, recvs
        self.place, self.side = lax.axis_index("dp"), lax.axis_index("mp")
        self.stages = SUM_PLACES.bit_length() - 1
        self.slot = pack_slot(self.place)

    def greet(self, barrier):
        pl.semaphore_signal(
            barrier, inc=1, device_id={"mp": 1 - self.side}, device_id_type=pl.DeviceIdType.MESH
        )

    def cross(self):
        return pltpu.make_async_remote_copy(
            src_ref=self.other,
            dst_ref=self.packs.at[self.slot, self.side],
            send_sem=self.sends.at[self.stages],
            recv_sem=self.recvs.at[self.stages],
            device_id={"mp": 1 - self.side},
            device_id_type=pl.DeviceIdType.MESH,
        )

    def copy(self, stage):
        size = 1 << stage
        bit = SUM_PLACES >> (stage + 1)
        rows = self.packs.at[pl.ds((self.slot // size) * size, size)]
        return pltpu.make_async_remote_copy(
            src_ref=rows,
            dst_ref=rows,
            send_sem=self.sends.at[stage],
            recv_sem=self.recvs.at[stage],
            device_id={"dp": self.place + bit - 2 * bit * place_bit(self.place, bit)},
            device_id_type=pl.DeviceIdType.MESH,
        )

    def start(self):
        self.packs[self.slot, self.side] = self.own[...]
        self.cross().start()

    def advance(self, stage):
        (self.cross() if stage == 0 else self.copy(stage - 1)).wait_recv()
        self.copy(stage).start()

    def finish(self):
        self.copy(self.stages - 1).wait_recv()
        self.cross().wait_send()
        for stage in range(self.stages):
            self.copy(stage).wait_send()


def attn_grads_kernel(
    first_ref, dattn_ref, dqkv_ref, att_ref, pack_own_ref, pack_other_ref, sums_ref, every_ref,
    first_t, dattn_t, buffer, land0, land1, land2, land3, sends, recvs,
    packs, pack_sends, pack_recvs,
):
    width = first_t.shape[0]
    tiles, _, columns = buffer.shape
    proj_tiles = dqkv_ref.shape[0] // columns
    share = width // SUM_PLACES
    total = DpSum(buffer, (land0, land1, land2, land3), sends, recvs)
    ring = PackGather(pack_own_ref, pack_other_ref, packs, pack_sends, pack_recvs)
    barrier = pltpu.get_barrier_semaphore()
    total.greet(barrier)
    ring.greet(barrier)
    pl.semaphore_wait(barrier, len(HALVING) + 2)
    ring.start()
    for source, target in ((first_ref, first_t), (dattn_ref, dattn_t)):
        for at in range(0, source.shape[0], 512):
            target[:, at : at + 512] = source[at : at + 512, :].T
    half = width // 2

    def step(s, carry):
        @pl.when(s < proj_tiles)
        def _():
            right = dqkv_ref[pl.ds(pl.multiple_of(s * columns, 128), columns), :]
            for at in (0, half):
                store_by_owner(buffer, s, at, nt(first_t[at : at + half, :], right), share)
            total.copy(0, s).start()

        @pl.when(jnp.logical_and(s >= proj_tiles, s < tiles))
        def _():
            right = att_ref[pl.ds(pl.multiple_of((s - proj_tiles) * columns, 128), columns), :]
            for at in (0, half):
                store_by_owner(buffer, s, at, nt(dattn_t[at : at + half, :], right), share)
            total.copy(0, s).start()

        for stage in range(3):
            tile = s - 1 - stage

            @pl.when(jnp.logical_and(tile >= 0, tile < tiles))
            def _():
                total.advance(stage, tile)

        for stage in range(ring.stages):

            @pl.when(s == 2 + 2 * stage)
            def _():
                ring.advance(stage)

        tile = s - 4

        @pl.when(tile >= 0)
        def _():
            sums_ref[tile] = total.gather_stage(3, tile)[1].astype(BF)

        return carry

    lax.fori_loop(0, tiles + 4, step, 0)
    ring.finish()
    every_ref[...] = packs[...]

    def finish(tile, carry):
        for stage in range(4):
            total.copy(stage, tile).wait_send()
        return carry

    lax.fori_loop(0, tiles, finish, 0)


def can_sum_here(width, columns):
    places = lax.axis_size("dp")
    return places == SUM_PLACES and width % (8 * places) == 0 and columns % 384 == 0


def attn_grads(first, dattn, dqkv, att, pack_own, pack_other):
    width = first.shape[1]
    tile = 384
    tiles = (dqkv.shape[0] + att.shape[0]) // tile
    share = width // SUM_PLACES
    vmem = pl.BlockSpec(memory_space=pltpu.VMEM)
    sums, every = pl.pallas_call(
        attn_grads_kernel,
        in_specs=[vmem] * 6,
        out_specs=[vmem] * 2,
        out_shape=[
            jax.ShapeDtypeStruct((tiles, 2 * share, tile), BF),
            jax.ShapeDtypeStruct((SUM_PLACES, 2) + pack_own.shape, BF),
        ],
        scratch_shapes=[
            pltpu.VMEM((width, first.shape[0]), BF),
            pltpu.VMEM((width, dattn.shape[0]), BF),
            pltpu.VMEM((tiles, width, tile), BF),
            pltpu.VMEM((tiles, width // 2, tile), BF),
            pltpu.VMEM((tiles, width // 4, tile), BF),
            pltpu.VMEM((tiles, width // 8, tile), BF),
            pltpu.VMEM((tiles, width // 8, tile), BF),
            pltpu.SemaphoreType.DMA((4, tiles)),
            pltpu.SemaphoreType.DMA((4, tiles)),
            pltpu.VMEM((SUM_PLACES, 2) + pack_own.shape, BF),
            pltpu.SemaphoreType.DMA((SUM_PLACES.bit_length(),)),
            pltpu.SemaphoreType.DMA((SUM_PLACES.bit_length(),)),
        ],
        compiler_params=pltpu.CompilerParams(
            vmem_limit_bytes=VMEM_LIMIT, collective_id=1, has_side_effects=True
        ),
        cost_estimate=cost(1e7, 1e5),
    )(first, dattn, dqkv, att, pack_own, pack_other)
    here = place_bit(lax.axis_index("dp"), FINAL) * share
    mine = lax.dynamic_slice_in_dim(sums, here, share, 1)
    return jnp.transpose(mine, (1, 0, 2)).reshape(share, -1), every


def shift_mp(value, steps):
    ways = lax.axis_size("mp")
    return lax.ppermute(value, "mp", [(i, (i - steps) % ways) for i in range(ways)])


def near_halves(block):
    half = block.shape[0] // 2
    core = lax.axis_index("dp") % 2
    mine = lax.dynamic_slice_in_dim(block, core * half, half, 0)
    return [shift_mp(mine, steps) for steps in range(1, lax.axis_size("mp"))]


def with_far_halves(nears):
    places = lax.axis_size("dp")
    core = lax.axis_index("dp") % 2
    got = []
    for near in nears:
        half = near.shape[0]
        far = lax.ppermute(near, "dp", [(i, i ^ 1) for i in range(places)])
        whole = jnp.zeros((2 * half,) + near.shape[1:], near.dtype)
        whole = lax.dynamic_update_slice_in_dim(whole, near, core * half, 0)
        got.append(lax.dynamic_update_slice_in_dim(whole, far, (1 - core) * half, 0))
    return got


def gathered_parts(own, nears):
    half = own.shape[0] // 2
    if half % 16:
        return [(0, 0, True)], [jnp.concatenate([own] + with_far_halves(nears), axis=0)]
    places = lax.axis_size("dp")
    layout, parts = [(0, 0, True)], [own]
    for j, near in enumerate(nears):
        base = (j + 1) * own.shape[0]
        far = lax.ppermute(near, "dp", [(i, i ^ 1) for i in range(places)])
        layout += [(base, half, True), (base, half, False)]
        parts += [near, far]
    return layout, parts


def home(parts):
    total = parts[0].astype(F32)
    for steps in range(1, len(parts)):
        total = total + shift_mp(parts[steps], -steps).astype(F32)
    return total


def to_lanes_rows(size):
    return -(-size // 2048) * 16


def to_lanes(part):
    flat = part.reshape(-1)
    rows = to_lanes_rows(flat.shape[0])
    return jnp.pad(flat, (0, rows * 128 - flat.shape[0])).reshape(rows, 128)


def scatter_dp(part):
    return lax.psum_scatter(part, "dp", scatter_dimension=0, tiled=True)


def local(
    tokens, conditioning, kept_ids, ada_weight, ada_bias, attn_qkv, attn_out, mlp_up, mlp_down,
    rel_table, grad_out_kept, grad_out_full,
):
    ways = lax.axis_size("mp")
    place = lax.axis_index("mp")
    images_group = conditioning.shape[0]
    images = images_group // ways
    width = tokens.shape[1]
    keep = kept_ids.shape[1]
    padded = -(-keep // 64) * 64
    per_block = rel_table.shape[0]
    cols = ada_bias.shape[0]

    silu_cond = jax.nn.silu(conditioning.astype(F32)).astype(BF)
    columns = (jnp.dot(silu_cond, ada_weight, preferred_element_type=F32) + ada_bias).astype(BF)
    mod = lax.all_to_all(columns, "mp", split_axis=0, concat_axis=1, tiled=True)
    mod = jnp.pad(mod.astype(F32).reshape(images, 6, width), ((0, 0), (0, 2), (0, 0)))

    weight_own = jnp.transpose(attn_qkv.reshape(width, -1))
    tables = [rel_table] + [shift_mp(rel_table, s) for s in range(1, ways)]
    mod, tables, weight_sent, out_sent = lax.optimization_barrier(
        (mod, tables, weight_own, attn_out)
    )
    near_w, near_o = near_halves(weight_sent), near_halves(out_sent)
    weight = gathered_parts(weight_own, near_w)
    out_weight = gathered_parts(attn_out, near_o)
    fetch = ways == 2 and lax.axis_size("dp") % 2 == 0 and mlp_up.shape[0] % 32 == 0
    fetch = fetch and mlp_down.shape[0] % 32 == 0
    bias = bias_whole(jnp.concatenate(tables, axis=0))

    own_kept = lax.dynamic_slice_in_dim(kept_ids, place * images, images, 0)
    own_kept = jnp.pad(own_kept, ((0, 0), (0, padded - keep)), constant_values=-1)
    pick = (own_kept[:, :, None] == jnp.arange(PATCHES, dtype=jnp.int32)).astype(BF)
    grads = jnp.concatenate(
        [
            grad_out_full.reshape(images, PATCHES, width),
            jnp.pad(
                grad_out_kept.reshape(images, keep, width), ((0, 0), (0, padded - keep), (0, 0))
            ),
        ],
        axis=1,
    )
    dmlp = (mod[:, 5:6] * grads.astype(F32)).astype(BF).reshape(-1, width)
    grads = grads.reshape(-1, width)

    first, qkv, att, lse, middle, second, branch, *near_up = forward(
        tokens, mod, pick, bias, weight, out_weight, per_block, mlp_up if fetch else None
    )
    (branch_mlp, dsecond, grads_own, *whole), tile_own = mlp(
        second, dmlp, mlp_up, mlp_down, None, (near_up[0], mlp_down) if fetch else None
    )
    if fetch:
        up_others, down_others = [whole[0]], [whole[1]]
    else:
        up_others = with_far_halves(near_halves(mlp_up))
        down_others = with_far_halves(near_halves(mlp_down))
    reduced = [scatter_dp(grads_own)]
    for up, down in zip(up_others, down_others):
        (branch_mlp, dsecond, grads_next), _ = mlp(
            second, dmlp, up, down, (branch_mlp, dsecond)
        )
        reduced.append(scatter_dp(grads_next))
    out, dtok, dmod, dattn, dqkv, strips = backward(
        tokens, mod, pick, bias, qkv, lse, middle, branch, branch_mlp, dsecond, grads,
        weight, out_weight, per_block,
    )
    proj_block, out_block = weight_own.shape[0], attn_out.shape[0]
    dqkv, reduced[0] = lax.optimization_barrier((dqkv, reduced[0]))
    dmod_rows = dmod[:, :6].reshape(images, 6 * width)
    dtables = table_of_strips(strips)
    here = can_sum_here(width, dqkv.shape[0]) and att.shape[0] % 384 == 0 and ways == 2
    if here:
        own_cond_rows = lax.dynamic_slice_in_dim(silu_cond, place * images, images, 0)
        packs = []
        for steps in range(ways):
            at = (place + steps) % ways
            parts = (
                lax.dynamic_slice_in_dim(dmod_rows, at * cols, cols, 1),
                dtables[steps * per_block : (steps + 1) * per_block],
                own_cond_rows,
            )
            packs.append(jnp.concatenate([to_lanes(part.astype(BF)) for part in parts], axis=0))
        attn_sums, every = attn_grads(first, dattn, dqkv, att, *packs)
        places = every.shape[0]
        every = every.astype(F32).reshape(places * ways, -1, 128)
        got, end = [], 0
        for part in parts:
            start, end = end, end + to_lanes_rows(part.size)
            got.append(every[:, start:end].reshape(places * ways, -1)[:, : part.size])
        all_columns = got[0].reshape(-1, cols)
        dtable = jnp.sum(got[1], axis=0).reshape(rel_table.shape)
        all_cond = got[2].reshape(-1, width)
        dcolumns = lax.dynamic_slice_in_dim(
            all_columns, pack_slot(lax.axis_index("dp")) * images_group, images_group, 0
        )
    else:
        dweight = dot(first, dqkv, (0, 1)).astype(BF)
        dout_t = dot(dattn, att, (0, 1)).astype(BF)
        attn_sums = scatter_dp(jnp.concatenate([dweight, dout_t], axis=1))
        dcolumns = lax.all_to_all(dmod_rows, "mp", split_axis=1, concat_axis=0, tiled=True)
        dtable = home(list(jnp.split(dtables, ways, axis=0)))
        all_columns = lax.all_gather(dcolumns, "dp", axis=0, tiled=True)
        dtable = lax.psum(dtable, "dp")
        all_cond = lax.all_gather(silu_cond, "dp", axis=0, tiled=True).astype(F32)
    split = ways * proj_block
    attn_parts = [
        jnp.concatenate(
            [
                attn_sums[:, j * proj_block : (j + 1) * proj_block],
                attn_sums[:, split + j * out_block : split + (j + 1) * out_block],
            ],
            axis=1,
        )
        for j in range(ways)
    ]
    mlp_grads = home(reduced)
    attn_total = home(attn_parts)
    grad_up, grad_down_t = split_mlp_grads(mlp_grads, tile_own)
    grad_qkv = attn_total[:, :proj_block].reshape(-1, 3, proj_block // 3)
    grad_out = jnp.transpose(attn_total[:, proj_block:])

    slice_width = width // lax.axis_size("dp")
    cond_slice = lax.dynamic_slice_in_dim(
        all_cond, lax.axis_index("dp") * slice_width, slice_width, 1
    )
    grad_ada_weight = lax.dot_general(
        cond_slice, all_columns, (((0,), (0,)), ((), ())), precision=PRECISE
    )
    grad_ada_bias = jnp.sum(all_columns, axis=0)
    dcolumns_high = dcolumns.astype(BF)
    dcolumns_low = (dcolumns - dcolumns_high.astype(F32)).astype(BF)
    silu_part = nt(jnp.concatenate([dcolumns_high, dcolumns_low], axis=0), ada_weight)
    silu_part = silu_part[:images_group] + silu_part[images_group:]
    shares = lax.all_to_all(
        silu_part.astype(BF).reshape(ways, images, width), "mp", split_axis=0, concat_axis=0,
        tiled=True,
    )
    grad_silu = jnp.sum(shares.astype(F32), axis=0)
    own_cond = lax.dynamic_slice_in_dim(conditioning, place * images, images, 0).astype(F32)
    grad_cond = jax.vjp(jax.nn.silu, own_cond)[1](grad_silu)[0].astype(BF)

    out = out.reshape(images, PATCHES + padded, width)
    out_full = out[:, :PATCHES].reshape(-1, width)
    out_kept = out[:, PATCHES : PATCHES + keep].reshape(-1, width)
    return (
        out_kept, out_full, dtok, grad_cond, grad_ada_weight, grad_ada_bias, grad_qkv, grad_out,
        grad_up, jnp.transpose(grad_down_t), dtable,
    )


def solution(mesh):
    both = P(("dp", "mp"), None)
    return jax.shard_map(
        local,
        mesh=mesh,
        in_specs=(
            both, P("dp", None), P("dp", None), P(None, "mp"), P("mp"), P(None, None, "mp"),
            P("mp", None), P(None, "mp"), P("mp", None), P("mp", None), both, both,
        ),
        out_specs=(
            both, both, both, both, P("dp", "mp"), P("mp"), P("dp", None, "mp"), P("mp", "dp"),
            P("dp", "mp"), P("mp", "dp"), P("mp", None),
        ),
        check_vma=False,
    )
```

```python
import functools
import math

import jax
import jax.numpy as jnp
from jax import lax
from jax.experimental import pallas as pl
from jax.experimental.pallas import tpu as pltpu
from jax.sharding import PartitionSpec as P

HEAD_DIM = 72
GRID = 16
PATCHES = 256
BUCKETS = 961
SPAN = 2 * GRID - 1
EPSILON = 1e-06
PRECISE = lax.Precision.HIGHEST
BF = jnp.bfloat16
F32 = jnp.float32
LOG2E = math.log2(math.e)
VMEM_LIMIT = 60 * 1024 * 1024


def dot(a, b, dims):
    return lax.dot_general(a, b, ((dims[0:1], dims[1:2]), ((), ())), preferred_element_type=F32)


def nn(a, b):
    return dot(a, b, (1, 0))


def nt(a, b):
    return dot(a, b, (1, 1))


def tn(a, b):
    return dot(a, b, (0, 0))


def normalize(rows):
    centered = rows - jnp.mean(rows, axis=-1, keepdims=True)
    inverse = lax.rsqrt(jnp.mean(centered * centered, axis=-1, keepdims=True) + EPSILON)
    return centered * inverse, inverse


def norm_back(normed, inverse, upstream):
    return inverse * (
        upstream
        - jnp.mean(upstream, axis=-1, keepdims=True)
        - normed * jnp.mean(upstream * normed, axis=-1, keepdims=True)
    )


def params(n_grid=1):
    return pltpu.CompilerParams(
        vmem_limit_bytes=VMEM_LIMIT, dimension_semantics=("arbitrary",) * n_grid
    )


def cost(flops, bytes_accessed, transcendentals=0):
    return pl.CostEstimate(
        flops=int(flops), bytes_accessed=int(bytes_accessed), transcendentals=int(transcendentals)
    )


def const_spec(shape):
    return pl.BlockSpec(shape, lambda *_: (0,) * len(shape), pipeline_mode=pl.Buffered(1))


def bias_kernel(strip_ref, bias_ref):
    strip = strip_ref[0]
    for key_row in range(GRID):
        start = (GRID - 1 - key_row) * GRID
        bias_ref[0, key_row * GRID : (key_row + 1) * GRID, :] = strip[:, start : start + PATCHES]


def bias_whole(table):
    heads = table.shape[0]
    grid_table = table.reshape(heads, SPAN, SPAN) * LOG2E
    strip = jnp.stack(
        [grid_table[:, :, GRID - 1 - c : 2 * GRID - 1 - c] for c in range(GRID)], axis=1
    ).reshape(heads, GRID, SPAN * GRID)
    strip = jnp.pad(strip, ((0, 0), (0, 0), (0, 512 - SPAN * GRID)))
    return pl.pallas_call(
        bias_kernel,
        grid=(heads,),
        in_specs=[pl.BlockSpec((1, GRID, 512), lambda h: (h, 0, 0))],
        out_specs=pl.BlockSpec((1, PATCHES, PATCHES), lambda h: (h, 0, 0)),
        out_shape=jax.ShapeDtypeStruct((heads, PATCHES, PATCHES), F32),
        compiler_params=params(),
        cost_estimate=cost(1e6, 1e5),
    )(strip)


def table_of_strips(strips):
    heads = strips.shape[0]
    parts = strips[:, :, : SPAN * GRID].reshape(heads, GRID, SPAN, GRID)
    total = jnp.zeros((heads, SPAN, SPAN), F32)
    for c in range(GRID):
        total = total + jnp.pad(parts[:, c], ((0, 0), (0, 0), (GRID - 1 - c, c)))
    return total.reshape(heads, BUCKETS)


def head_rows(head, per_block):
    base = (head // per_block) * (3 * per_block * HEAD_DIM) + (head % per_block) * HEAD_DIM
    step = per_block * HEAD_DIM
    return [pl.ds(pl.multiple_of(base + c * step, 8), HEAD_DIM) for c in range(3)]


def key_mask(pick):
    ones = jnp.ones((pick.shape[0], PATCHES), BF)
    return (tn(pick, ones) - 1.0) * 1e30


def part_copies(layout, parts, whole, sems):
    core = lax.axis_index("dp") % 2
    copies = []
    for index, ((base, half, near), part) in enumerate(zip(layout, parts)):
        start = base + (core if near else 1 - core) * half
        rows = pl.ds(pl.multiple_of(start, 16), part.shape[0])
        copies.append(pltpu.make_async_copy(part, whole.at[rows, :], sems.at[index]))
    return copies


def run_copies(copies):
    for copy in copies:
        copy.start()
    for copy in copies:
        copy.wait()


def core_rows(half, skip, count):
    start = (lax.axis_index("dp") % 2) * half + skip
    return pl.ds(pl.multiple_of(start, 16), count)


def fetch_copy(own, rows, target, sems, at):
    return pltpu.make_async_remote_copy(
        src_ref=own.at[rows, :],
        dst_ref=target,
        send_sem=sems.at[at],
        recv_sem=sems.at[at + 1],
        device_id={"mp": 1 - lax.axis_index("mp")},
        device_id_type=pl.DeviceIdType.MESH,
    )


def core_copy(source, target, sems, at):
    place = lax.axis_index("dp")
    return pltpu.make_async_remote_copy(
        src_ref=source,
        dst_ref=target,
        send_sem=sems.at[at],
        recv_sem=sems.at[at + 1],
        device_id={"dp": place + 1 - 2 * (place % 2)},
        device_id_type=pl.DeviceIdType.MESH,
    )


def greet_peers(with_core):
    barrier = pltpu.get_barrier_semaphore()
    peers = [{"mp": 1 - lax.axis_index("mp")}]
    if with_core:
        place = lax.axis_index("dp")
        peers.append({"dp": place + 1 - 2 * (place % 2)})
    for peer in peers:
        pl.semaphore_signal(
            barrier, inc=1, device_id=peer, device_id_type=pl.DeviceIdType.MESH
        )
    pl.semaphore_wait(barrier, len(peers))


def project(weight_ref, first, qkv_s, qkv_ref, base):
    step = weight_ref.shape[0] // 3
    for c in range(3):
        part = nt(weight_ref[c * step : (c + 1) * step, :], first)
        qkv_s[c * step : (c + 1) * step, :] = part
        qkv_ref[base + c * step : base + (c + 1) * step, :] = part.astype(BF)


def attend_heads(per_block, first_head, qkv_s, bias_ref, mask, att_s, attk_s, lse_s):
    scale = HEAD_DIM ** (-0.5) * LOG2E
    heads = qkv_s.shape[0] // (3 * HEAD_DIM)

    def one_head(head, carry):
        q_at, k_at, v_at = head_rows(head, per_block)
        queries = qkv_s[q_at, :].astype(BF)
        keys = qkv_s[k_at, :].astype(BF)
        values = qkv_s[v_at, :].astype(BF)
        scores = tn(keys, queries) * scale + bias_ref[first_head + head]
        here = pl.ds(pl.multiple_of(head * HEAD_DIM, 8), HEAD_DIM)

        def attend(scores):
            top = jnp.max(scores, axis=0, keepdims=True)
            weights = jnp.exp2(scores - top)
            total = jnp.sum(weights, axis=0, keepdims=True)
            probs = (weights * (1.0 / total)).astype(BF)
            return nn(values, probs), top + jnp.log2(total)

        att_s[here, :], lse_s[pl.ds(head, 1), :] = attend(scores)
        attk_s[here, :], lse_s[pl.ds(heads + head, 1), :] = attend(scores + mask)
        return carry

    lax.fori_loop(0, heads, one_head, 0, unroll=4 if heads % 4 == 0 else 2)


def own_heads_kernel(
    per_block, tok_ref, mod_ref, pick_ref, bias_ref, weight_ref,
    first_ref, qkv_ref, att_ref, lse_ref, qkv_s, att_s, attk_s, lse_s,
):
    shift_one, scale_one = mod_ref[0, 0:1], mod_ref[0, 1:2]
    normed, _ = normalize(tok_ref[...].astype(F32))
    first = (normed * (1.0 + scale_one) + shift_one).astype(BF)
    first_ref[...] = first
    project(weight_ref, first, qkv_s, qkv_ref, 0)
    mask = key_mask(pick_ref[0])
    attend_heads(per_block, 0, qkv_s, bias_ref, mask, att_s, attk_s, lse_s)
    att_ref[:, :PATCHES] = att_s[...].astype(BF)
    att_ref[:, PATCHES:] = attk_s[...].astype(BF)
    lse_ref[0] = lse_s[...]


def own_heads(tokens, mod, pick, bias, weight, per_block):
    images, padded = pick.shape[0], pick.shape[1]
    width = tokens.shape[1]
    proj = weight.shape[0]
    heads = proj // (3 * HEAD_DIM)
    inner = heads * HEAD_DIM
    return pl.pallas_call(
        functools.partial(own_heads_kernel, per_block),
        grid=(images,),
        in_specs=[
            pl.BlockSpec((PATCHES, width), lambda i: (i, 0)),
            pl.BlockSpec((1, 8, width), lambda i: (i, 0, 0)),
            pl.BlockSpec((1, padded, PATCHES), lambda i: (i, 0, 0)),
            const_spec(bias.shape),
            const_spec(weight.shape),
        ],
        out_specs=[
            pl.BlockSpec((PATCHES, width), lambda i: (i, 0)),
            pl.BlockSpec((proj, PATCHES), lambda i: (0, i)),
            pl.BlockSpec((inner, 2 * PATCHES), lambda i: (0, i)),
            pl.BlockSpec((1, 2 * heads, PATCHES), lambda i: (i, 0, 0)),
        ],
        out_shape=[
            jax.ShapeDtypeStruct((images * PATCHES, width), BF),
            jax.ShapeDtypeStruct((proj, images * PATCHES), BF),
            jax.ShapeDtypeStruct((inner, images * 2 * PATCHES), BF),
            jax.ShapeDtypeStruct((images, 2 * heads, PATCHES), F32),
        ],
        scratch_shapes=[
            pltpu.VMEM((proj, PATCHES), F32),
            pltpu.VMEM((inner, PATCHES), F32),
            pltpu.VMEM((inner, PATCHES), F32),
            pltpu.VMEM((2 * heads, PATCHES), F32),
        ],
        compiler_params=params(),
        cost_estimate=cost(1e7, 1e5),
    )(tokens, mod, pick, bias, weight)


def forward_kernel(per_block, weight_layout, out_layout, fetch, *refs):
    first_ref, own_qkv, own_att, own_lse, tok_ref, mod_ref, pick_ref, bias_ref = refs[:8]
    refs = refs[8:]
    weight_parts, refs = refs[: len(weight_layout)], refs[len(weight_layout) :]
    out_parts, refs = refs[: len(out_layout)], refs[len(out_layout) :]
    if fetch:
        send_ref, refs = refs[0], refs[1:]
    qkv_ref, att_ref, lse_ref, middle_ref, second_ref, branch_ref = refs[:6]
    refs = refs[6:]
    if fetch:
        got_ref, refs = refs[0], refs[1:]
    qkv_s, att_s, attk_s, lse_s, weight_ref, out_w_ref, part_sems, fetch_sems = refs

    def fetching():
        half = send_ref.shape[0] // 2
        return fetch_copy(send_ref, core_rows(half, 0, got_ref.shape[0]), got_ref, fetch_sems, 0)

    @pl.when(pl.program_id(0) == 0)
    def _():
        copies = part_copies(weight_layout, weight_parts, weight_ref, part_sems.at[0])
        copies += part_copies(out_layout, out_parts, out_w_ref, part_sems.at[1])
        if fetch:
            greet_peers(False)
            fetching().start()
        run_copies(copies)

    own = own_qkv.shape[0]
    own_inner = own // 3
    own_count = own_inner // HEAD_DIM
    heads = bias_ref.shape[0]
    others = heads - own_count
    pick = pick_ref[0]
    qkv_ref[:own, :] = own_qkv[...]
    project(weight_ref, first_ref[...], qkv_s, qkv_ref, own)
    mask = key_mask(pick)
    attend_heads(per_block, own_count, qkv_s, bias_ref, mask, att_s, attk_s, lse_s)
    att_ref[:own_inner, :] = own_att[...]
    att_ref[own_inner:, :PATCHES] = att_s[...].astype(BF)
    att_ref[own_inner:, PATCHES:] = attk_s[...].astype(BF)
    lse_ref[0, :own_count, :] = own_lse[0, :own_count]
    lse_ref[0, own_count:heads, :] = lse_s[:others]
    lse_ref[0, heads : heads + own_count, :] = own_lse[0, own_count:]
    lse_ref[0, heads + own_count :, :] = lse_s[others:]
    gate_one = mod_ref[0, 2:3]
    shift_two, scale_two = mod_ref[0, 3:4], mod_ref[0, 4:5]
    out_w = out_w_ref[...]
    kept_att = nt(pick, att_ref[:, PATCHES:]).astype(BF)
    for rows, source, residual in (
        (slice(0, PATCHES), att_ref[:, :PATCHES].T, tok_ref[...].astype(F32)),
        (slice(PATCHES, PATCHES + pick.shape[0]), kept_att, nn(pick, tok_ref[...])),
    ):
        branch = nn(source, out_w)
        branch_ref[rows, :] = branch.astype(BF)
        middle = residual + gate_one * branch
        middle_ref[rows, :] = middle
        second_ref[rows, :] = (normalize(middle)[0] * (1.0 + scale_two) + shift_two).astype(BF)
    if fetch:

        @pl.when(pl.program_id(0) == pl.num_programs(0) - 1)
        def _():
            fetching().wait()


def whole_rows(layout, parts):
    return sum(part.shape[0] for part in parts)


ANYWHERE = pl.BlockSpec(memory_space=pl.ANY)


def forward(own, tokens, mod, pick, bias, weight, out_weight, per_block, send=None, count=0):
    images, padded = pick.shape[0], pick.shape[1]
    width = tokens.shape[1]
    rows = PATCHES + padded
    heads = bias.shape[0]
    (weight_layout, weight_parts), (out_layout, out_parts) = weight, out_weight
    proj_others = whole_rows(*weight)
    proj = own[1].shape[0] + proj_others
    own_inner, own_heads_count = own[2].shape[0], own[3].shape[1] // 2
    others = heads - own_heads_count
    fetch = send is not None
    most = max(len(weight_parts), len(out_parts))
    extra_shapes, extra = [], []
    compiler_params = params()
    if fetch:
        extra_shapes = [jax.ShapeDtypeStruct((count, send.shape[1]), BF)]
        extra = [send]
        compiler_params = pltpu.CompilerParams(
            vmem_limit_bytes=VMEM_LIMIT, dimension_semantics=("arbitrary",),
            collective_id=2, has_side_effects=True,
        )
    by_row = pl.BlockSpec((rows, width), lambda i: (i, 0))
    return pl.pallas_call(
        functools.partial(forward_kernel, per_block, weight_layout, out_layout, fetch),
        grid=(images,),
        in_specs=[
            pl.BlockSpec((PATCHES, width), lambda i: (i, 0)),
            pl.BlockSpec((own[1].shape[0], PATCHES), lambda i: (0, i)),
            pl.BlockSpec((own_inner, 2 * PATCHES), lambda i: (0, i)),
            pl.BlockSpec((1, 2 * own_heads_count, PATCHES), lambda i: (i, 0, 0)),
            pl.BlockSpec((PATCHES, width), lambda i: (i, 0)),
            pl.BlockSpec((1, 8, width), lambda i: (i, 0, 0)),
            pl.BlockSpec((1, padded, PATCHES), lambda i: (i, 0, 0)),
            const_spec(bias.shape),
        ]
        + [ANYWHERE] * (len(weight_parts) + len(out_parts) + len(extra)),
        out_specs=[
            pl.BlockSpec((proj, PATCHES), lambda i: (0, i)),
            pl.BlockSpec((width, 2 * PATCHES), lambda i: (0, i)),
            pl.BlockSpec((1, 2 * heads, PATCHES), lambda i: (i, 0, 0)),
            by_row,
            by_row,
            by_row,
        ]
        + [ANYWHERE] * len(extra),
        out_shape=[
            jax.ShapeDtypeStruct((proj, images * PATCHES), BF),
            jax.ShapeDtypeStruct((width, images * 2 * PATCHES), BF),
            jax.ShapeDtypeStruct((images, 2 * heads, PATCHES), F32),
            jax.ShapeDtypeStruct((images * rows, width), F32),
            jax.ShapeDtypeStruct((images * rows, width), BF),
            jax.ShapeDtypeStruct((images * rows, width), BF),
        ]
        + extra_shapes,
        scratch_shapes=[
            pltpu.VMEM((proj_others, PATCHES), F32),
            pltpu.VMEM((others * HEAD_DIM, PATCHES), F32),
            pltpu.VMEM((others * HEAD_DIM, PATCHES), F32),
            pltpu.VMEM((2 * others, PATCHES), F32),
            pltpu.VMEM((proj_others, width), BF),
            pltpu.VMEM((width, width), BF),
            pltpu.SemaphoreType.DMA((2, most)),
            pltpu.SemaphoreType.DMA((2,)),
        ],
        compiler_params=compiler_params,
        cost_estimate=cost(images * 2e9, images * 8e6),
    )(*own, tokens, mod, pick, bias, *weight_parts, *out_parts, *extra)


def gelu_pair(pre):
    root = math.sqrt(2.0 / math.pi)
    square = pre * pre
    bend = jnp.tanh(pre * (root + (root * 0.044715) * square))
    half = 0.5 + 0.5 * bend
    slope = half + (0.5 * pre) * (1.0 - bend * bend) * (root + (3.0 * root * 0.044715) * square)
    return pre * half, slope


def mlp_kernel(
    chunk, fresh, fetch, second_ref, dmlp_ref, up_ref, down_ref, *refs
):
    if fetch:
        near_ref, send_up, send_down = refs[:3]
        *refs, moves, fetch_sems = refs[3:]
        up_all, down_all = refs[3:5]
        refs = refs[:3] + refs[5:]
    if fresh:
        branch_ref, dsecond_ref, grads_ref, second_t, dmlp_t, hidden_s, dpre_s, sem = refs
    else:
        branch_in, dsecond_in, branch_ref, dsecond_ref, grads_ref = refs[:5]
        second_t, dmlp_t, hidden_s, dpre_s, sem = refs[5:]
    rows = second_ref.shape[0]
    tile = up_ref.shape[1]
    width = second_ref.shape[1]

    if fetch:
        up_half, down_half = up_all.shape[0] // 2, down_all.shape[0] // 2
        cut = near_ref.shape[0]
        up_a = up_all.at[core_rows(up_half, 0, cut), :]
        up_b = up_all.at[core_rows(up_half, cut, up_half - cut), :]
        down_a = down_all.at[core_rows(down_half, 0, down_half), :]
        lay_a = pltpu.make_async_copy(near_ref, up_a, moves.at[0])
        pass_a = core_copy(near_ref, up_a, moves, 1)
        pass_b = core_copy(up_b, up_b, moves, 3)
        pass_down = core_copy(down_a, down_a, moves, 5)
        fetch_b = fetch_copy(
            send_up, core_rows(up_half, cut, up_half - cut), up_b, fetch_sems, 0
        )
        fetch_down = fetch_copy(
            send_down, core_rows(down_half, 0, down_half), down_a, fetch_sems, 2
        )
    step, last = pl.program_id(0), pl.num_programs(0) - 1

    @pl.when(step == 0)
    def _():
        if fetch:
            greet_peers(True)
            fetch_b.start()
            fetch_down.start()
            lay_a.start()
            pass_a.start()
        if fresh:
            branch_ref[...] = jnp.zeros_like(branch_ref)
            dsecond_ref[...] = jnp.zeros_like(dsecond_ref)
        else:
            one = pltpu.make_async_copy(branch_in, branch_ref, sem.at[0])
            two = pltpu.make_async_copy(dsecond_in, dsecond_ref, sem.at[1])
            one.start()
            two.start()
        for at in range(0, rows, chunk):
            second_t[:, at : at + chunk] = second_ref[at : at + chunk, :].T
            dmlp_t[:, at : at + chunk] = dmlp_ref[at : at + chunk, :].T
        if not fresh:
            one.wait()
            two.wait()

    def one_chunk(index, carry):
        at = pl.ds(pl.multiple_of(index * chunk, chunk), chunk)
        pre = nn(second_ref[at, :], up_ref[...])
        dhidden = nt(dmlp_ref[at, :], down_ref[...])
        value, slope = gelu_pair(pre)
        hidden = value.astype(BF)
        dpre = (dhidden * slope).astype(BF)
        hidden_s[at, :] = hidden
        dpre_s[at, :] = dpre
        branch_ref[at, :] += nn(hidden, down_ref[...])
        dsecond_ref[at, :] += nt(dpre, up_ref[...])
        return carry

    lax.fori_loop(0, rows // chunk, one_chunk, 0)
    if fetch:

        @pl.when(step == last // 2)
        def _():
            fetch_b.wait_recv()
            pass_b.start()

        @pl.when(step == last)
        def _():
            fetch_down.wait_recv()
            pass_down.start()

    part = width // 3
    for c in range(3):
        at = slice(c * part, (c + 1) * part)
        grads_ref[at, :tile] = nn(second_t[at, :], dpre_s[...]).astype(BF)
        grads_ref[at, tile:] = nn(dmlp_t[at, :], hidden_s[...]).astype(BF)

    if fetch:

        @pl.when(step == last)
        def _():
            for copy in (lay_a, pass_a, pass_b, pass_down):
                copy.wait()
            fetch_b.wait_send()
            fetch_down.wait_send()


def mlp_chunk(rows):
    for chunk in (896, 448, 64):
        if rows % chunk == 0:
            return chunk
    return rows


def mlp(second, dmlp, up, down, sums=None, fetch=None):
    rows, width = second.shape
    hidden = up.shape[1]
    tile = 768 if hidden % 768 == 0 else hidden
    fresh = sums is None
    chunk = mlp_chunk(rows)
    in_specs = [
        const_spec(second.shape),
        const_spec(second.shape),
        pl.BlockSpec((width, tile), lambda f: (0, f)),
        pl.BlockSpec((tile, width), lambda f: (f, 0)),
    ]
    operands = [second, dmlp, up, down]
    out_specs = [
        const_spec(second.shape),
        const_spec(second.shape),
        pl.BlockSpec((width, 2 * tile), lambda f: (0, f)),
    ]
    out_shape = [
        jax.ShapeDtypeStruct(second.shape, F32),
        jax.ShapeDtypeStruct(second.shape, F32),
        jax.ShapeDtypeStruct((width, 2 * hidden), BF),
    ]
    scratch = [
        pltpu.VMEM((width, rows), BF),
        pltpu.VMEM((width, rows), BF),
        pltpu.VMEM((rows, tile), BF),
        pltpu.VMEM((rows, tile), BF),
        pltpu.SemaphoreType.DMA((2,)),
    ]
    compiler_params = params()
    if not fresh:
        in_specs += [ANYWHERE] * 2
        operands += list(sums)
    if fetch is not None:
        in_specs += [ANYWHERE] * 3
        operands += list(fetch)
        out_specs += [ANYWHERE] * 2
        out_shape += [jax.ShapeDtypeStruct(up.shape, BF), jax.ShapeDtypeStruct(down.shape, BF)]
        scratch += [pltpu.SemaphoreType.DMA((7,)), pltpu.SemaphoreType.DMA((4,))]
        compiler_params = pltpu.CompilerParams(
            vmem_limit_bytes=VMEM_LIMIT, dimension_semantics=("arbitrary",),
            collective_id=3, has_side_effects=True,
        )
    return pl.pallas_call(
        functools.partial(mlp_kernel, chunk, fresh, fetch is not None),
        grid=(hidden // tile,),
        in_specs=in_specs,
        out_specs=out_specs,
        out_shape=out_shape,
        scratch_shapes=scratch,
        compiler_params=compiler_params,
        cost_estimate=cost(6e10, 6e7) if fresh else cost(1e7, 1e5),
    )(*operands), tile


def split_mlp_grads(grads, tile):
    parts = grads.reshape(grads.shape[0], -1, 2, tile)
    return (
        parts[:, :, 0].reshape(grads.shape[0], -1),
        parts[:, :, 1].reshape(grads.shape[0], -1),
    )


def backward_kernel(per_block, weight_layout, out_layout, *refs):
    count = len(weight_layout) + len(out_layout)
    weight_parts = refs[: len(weight_layout)]
    out_parts = refs[len(weight_layout) : count]
    weight_ref, out_w_ref, sems = refs[-3:]

    @pl.when(pl.program_id(0) == 0)
    def _():
        run_copies(
            part_copies(weight_layout, weight_parts, weight_ref, sems.at[0])
            + part_copies(out_layout, out_parts, out_w_ref, sems.at[1])
        )

    backward_body(per_block, weight_ref, out_w_ref, *refs[count:-3])


def backward_body(
    per_block, weight_ref, out_w_ref, tok_ref, mod_ref, pick_ref, bias_ref,
    qkv_ref, lse_ref, middle_ref, branch_ref, mlp_ref, dsecond_ref, grad_ref,
    out_ref, dtok_ref, dmod_ref, dattn_ref, dqkv_ref, strips_ref,
    qkv_s, datt_s, dattk_s, dscores_s,
):
    heads = bias_ref.shape[0]
    step = pl.program_id(0)
    shift_one, scale_one, gate_one = mod_ref[0, 0:1], mod_ref[0, 1:2], mod_ref[0, 2:3]
    scale_two, gate_two = mod_ref[0, 4:5], mod_ref[0, 5:6]
    pick = pick_ref[0]
    dmiddles = []
    sums = [0.0, 0.0, 0.0, 0.0]
    for rows in (slice(0, PATCHES), slice(PATCHES, PATCHES + pick.shape[0])):
        middle = middle_ref[rows, :]
        branch_mlp = mlp_ref[rows, :]
        dsecond = dsecond_ref[rows, :]
        grad = grad_ref[rows, :].astype(F32)
        out_ref[rows, :] = (middle + gate_two * branch_mlp).astype(BF)
        normed, inverse = normalize(middle)
        dmiddle = grad + norm_back(normed, inverse, dsecond * (1.0 + scale_two))
        branch = branch_ref[rows, :].astype(F32)
        for c, term in enumerate(
            (dmiddle * branch, dsecond, dsecond * normed, grad * branch_mlp)
        ):
            sums[c] = sums[c] + jnp.sum(term, axis=0, keepdims=True)
        dmiddles.append(dmiddle)
    for c in range(4):
        dmod_ref[0, 2 + c : 3 + c, :] = sums[c]
    dattn = (gate_one * dmiddles[0]).astype(BF)
    dattn_kept = tn(pick, (gate_one * dmiddles[1]).astype(BF)).astype(BF)
    dattn_ref[:PATCHES, :] = dattn
    dattn_ref[PATCHES:, :] = dattn_kept
    high = dmiddles[1].astype(BF)
    low = (dmiddles[1] - high.astype(F32)).astype(BF)
    dresid = dmiddles[0] + tn(pick, high) + tn(pick, low)
    datt_s[...] = nt(out_w_ref[...], dattn)
    dattk_s[...] = nt(out_w_ref[...], dattn_kept)
    qkv_s[...] = qkv_ref[...].astype(F32)
    mask = key_mask(pick)
    scale = HEAD_DIM ** (-0.5)

    @pl.when(step == 0)
    def _():
        dscores_s[...] = jnp.zeros_like(dscores_s)

    def one_head(head, carry):
        q_at, k_at, v_at = head_rows(head, per_block)
        queries = qkv_s[q_at, :].astype(BF)
        keys = qkv_s[k_at, :].astype(BF)
        values = qkv_s[v_at, :].astype(BF)
        here = pl.ds(pl.multiple_of(head * HEAD_DIM, 8), HEAD_DIM)
        scores = tn(keys, queries) * (scale * LOG2E) + bias_ref[head]

        def pull(scores, top, upstream):
            probs = jnp.exp2(scores - top)
            dprobs = tn(values, upstream)
            dvalues = nt(upstream, probs.astype(BF))
            weighted = jnp.sum(probs * dprobs, axis=0, keepdims=True)
            return probs * (dprobs - weighted), dvalues

        dscores, dvalues = pull(
            scores, lse_ref[0, pl.ds(head, 1), :], datt_s[here, :].astype(BF)
        )
        dscores_kept, dvalues_kept = pull(
            scores + mask, lse_ref[0, pl.ds(heads + head, 1), :], dattk_s[here, :].astype(BF)
        )
        dscores = dscores + dscores_kept
        dscores_s[head] += dscores
        rounded = dscores.astype(BF)
        qkv_s[q_at, :] = nn(keys, rounded) * scale
        qkv_s[k_at, :] = nt(queries, rounded) * scale
        qkv_s[v_at, :] = dvalues + dvalues_kept
        return carry

    lax.fori_loop(0, heads, one_head, 0, unroll=4)
    dqkv = qkv_s[...].astype(BF)
    dqkv_ref[...] = dqkv
    dfirst = tn(dqkv, weight_ref[...])
    normed, inverse = normalize(tok_ref[...].astype(F32))
    dmod_ref[0, 0:1, :] = jnp.sum(dfirst, axis=0, keepdims=True)
    dmod_ref[0, 1:2, :] = jnp.sum(dfirst * normed, axis=0, keepdims=True)
    dmod_ref[0, 6:8, :] = jnp.zeros((2, dfirst.shape[1]), F32)
    dtok_ref[...] = (dresid + norm_back(normed, inverse, dfirst * (1.0 + scale_one))).astype(BF)

    @pl.when(step == pl.num_programs(0) - 1)
    def _():
        def fold(head, carry):
            strip = jnp.zeros((GRID, 512), F32)
            for key_row in range(GRID):
                start = (GRID - 1 - key_row) * GRID
                block = dscores_s[head, key_row * GRID : (key_row + 1) * GRID, :]
                block = jnp.concatenate([block, jnp.zeros((GRID, 512 - PATCHES), F32)], axis=1)
                strip = strip + pltpu.roll(block, start, 1)
            strips_ref[head] = strip
            return carry

        lax.fori_loop(0, heads, fold, 0)


def backward(
    tokens, mod, pick, bias, qkv, lse, middle, branch, branch_mlp, dsecond, grads,
    weight, out_weight, per_block,
):
    (weight_layout, weight_parts), (out_layout, out_parts) = weight, out_weight
    most = max(len(weight_parts), len(out_parts))
    proj = whole_rows(*weight)
    images, padded = pick.shape[0], pick.shape[1]
    width = tokens.shape[1]
    rows = PATCHES + padded
    heads = bias.shape[0]
    by_row = pl.BlockSpec((rows, width), lambda i: (i, 0))
    return pl.pallas_call(
        functools.partial(backward_kernel, per_block, weight_layout, out_layout),
        grid=(images,),
        in_specs=[ANYWHERE] * (len(weight_parts) + len(out_parts))
        + [
            pl.BlockSpec((PATCHES, width), lambda i: (i, 0)),
            pl.BlockSpec((1, 8, width), lambda i: (i, 0, 0)),
            pl.BlockSpec((1, padded, PATCHES), lambda i: (i, 0, 0)),
            const_spec(bias.shape),
            pl.BlockSpec((proj, PATCHES), lambda i: (0, i)),
            pl.BlockSpec((1, 2 * heads, PATCHES), lambda i: (i, 0, 0)),
            by_row,
            by_row,
            by_row,
            by_row,
            by_row,
        ],
        out_specs=[
            by_row,
            pl.BlockSpec((PATCHES, width), lambda i: (i, 0)),
            pl.BlockSpec((1, 8, width), lambda i: (i, 0, 0)),
            pl.BlockSpec((2 * PATCHES, width), lambda i: (i, 0)),
            pl.BlockSpec((proj, PATCHES), lambda i: (0, i)),
            const_spec((heads, GRID, 512)),
        ],
        out_shape=[
            jax.ShapeDtypeStruct((images * rows, width), BF),
            jax.ShapeDtypeStruct((images * PATCHES, width), BF),
            jax.ShapeDtypeStruct((images, 8, width), F32),
            jax.ShapeDtypeStruct((images * 2 * PATCHES, width), BF),
            jax.ShapeDtypeStruct((proj, images * PATCHES), BF),
            jax.ShapeDtypeStruct((heads, GRID, 512), F32),
        ],
        scratch_shapes=[
            pltpu.VMEM((proj, PATCHES), F32),
            pltpu.VMEM((width, PATCHES), F32),
            pltpu.VMEM((width, PATCHES), F32),
            pltpu.VMEM((heads, PATCHES, PATCHES), F32),
            pltpu.VMEM((proj, width), BF),
            pltpu.VMEM((width, width), BF),
            pltpu.SemaphoreType.DMA((2, most)),
        ],
        compiler_params=params(),
        cost_estimate=cost(1e7, 1e5),
    )(
        *weight_parts, *out_parts, tokens, mod, pick, bias, qkv, lse, middle, branch, branch_mlp,
        dsecond, grads,
    )


SUM_PLACES = 16
HALVING = (1, 2, 8)
FINAL = 4


def place_bit(place, bit):
    return (place // bit) % 2


def unit_start(owner, share):
    index = 0
    for bit in HALVING + (FINAL,):
        index = index * 2 + place_bit(owner, bit)
    return index * share


def store_by_owner(buffer, tile, at, block, share):
    first_owner = at // share
    owners = block.shape[0] // share
    for k in range(owners):
        owner = first_owner + k
        if place_bit(owner, FINAL):
            continue
        pair = k + FINAL
        both = jnp.concatenate(
            [block[k * share : (k + 1) * share], block[pair * share : (pair + 1) * share]], axis=0
        )
        start = unit_start(owner, share)
        buffer[tile, start : start + 2 * share, :] = both.astype(BF)


class DpSum:
    def __init__(self, buffer, lands, sends, recvs):
        self.buffer, self.lands, self.sends, self.recvs = buffer, lands, sends, recvs
        self.place = lax.axis_index("dp")
        self.rows = buffer.shape[1]

    def partner(self, bit):
        return self.place + bit - 2 * bit * place_bit(self.place, bit)

    def greet(self, barrier):
        for bit in HALVING + (FINAL,):
            pl.semaphore_signal(
                barrier, inc=1, device_id={"dp": self.partner(bit)},
                device_id_type=pl.DeviceIdType.MESH,
            )

    def spans(self, stage):
        start, size = 0, self.rows
        for k, bit in enumerate(HALVING):
            size = size // 2
            mine = place_bit(self.place, bit)
            if k == stage:
                return start + mine * size, start + (1 - mine) * size, size
            start = start + mine * size
        return start, start, size

    def copy(self, stage, tile):
        bit = (HALVING + (FINAL,))[stage]
        _, away, size = self.spans(stage)
        return pltpu.make_async_remote_copy(
            src_ref=self.buffer.at[tile, pl.ds(pl.multiple_of(away, 16), size), :],
            dst_ref=self.lands[stage].at[tile],
            send_sem=self.sends.at[stage, tile],
            recv_sem=self.recvs.at[stage, tile],
            device_id={"dp": self.partner(bit)},
            device_id_type=pl.DeviceIdType.MESH,
        )

    def gather_stage(self, stage, tile):
        self.copy(stage, tile).wait_recv()
        keep, _, size = self.spans(stage)
        at = pl.ds(pl.multiple_of(keep, 16), size)
        return at, self.buffer[tile, at, :].astype(F32) + self.lands[stage][tile].astype(F32)

    def advance(self, stage, tile):
        at, total = self.gather_stage(stage, tile)
        self.buffer[tile, at, :] = total.astype(BF)
        self.copy(stage + 1, tile).start()


def pack_slot(place):
    return sum(
        place_bit(place, SUM_PLACES >> (k + 1)) << k for k in range(SUM_PLACES.bit_length() - 1)
    )


class PackGather:
    def __init__(self, own, other, packs, sends, recvs):
        self.own, self.other, self.packs, self.sends, self.recvs = own, other, packs, sends, recvs
        self.place, self.side = lax.axis_index("dp"), lax.axis_index("mp")
        self.stages = SUM_PLACES.bit_length() - 1
        self.slot = pack_slot(self.place)

    def greet(self, barrier):
        pl.semaphore_signal(
            barrier, inc=1, device_id={"mp": 1 - self.side}, device_id_type=pl.DeviceIdType.MESH
        )

    def cross(self):
        return pltpu.make_async_remote_copy(
            src_ref=self.other,
            dst_ref=self.packs.at[self.slot, self.side],
            send_sem=self.sends.at[self.stages],
            recv_sem=self.recvs.at[self.stages],
            device_id={"mp": 1 - self.side},
            device_id_type=pl.DeviceIdType.MESH,
        )

    def copy(self, stage):
        size = 1 << stage
        bit = SUM_PLACES >> (stage + 1)
        rows = self.packs.at[pl.ds((self.slot // size) * size, size)]
        return pltpu.make_async_remote_copy(
            src_ref=rows,
            dst_ref=rows,
            send_sem=self.sends.at[stage],
            recv_sem=self.recvs.at[stage],
            device_id={"dp": self.place + bit - 2 * bit * place_bit(self.place, bit)},
            device_id_type=pl.DeviceIdType.MESH,
        )

    def start(self):
        self.packs[self.slot, self.side] = self.own[...]
        self.cross().start()

    def advance(self, stage):
        (self.cross() if stage == 0 else self.copy(stage - 1)).wait_recv()
        self.copy(stage).start()

    def finish(self):
        self.copy(self.stages - 1).wait_recv()
        self.cross().wait_send()
        for stage in range(self.stages):
            self.copy(stage).wait_send()


def attn_grads_kernel(
    first_ref, dattn_ref, dqkv_ref, att_ref, pack_own_ref, pack_other_ref, sums_ref, every_ref,
    first_t, dattn_t, buffer, land0, land1, land2, land3, sends, recvs,
    packs, pack_sends, pack_recvs,
):
    width = first_t.shape[0]
    tiles, _, columns = buffer.shape
    proj_tiles = dqkv_ref.shape[0] // columns
    share = width // SUM_PLACES
    total = DpSum(buffer, (land0, land1, land2, land3), sends, recvs)
    ring = PackGather(pack_own_ref, pack_other_ref, packs, pack_sends, pack_recvs)
    barrier = pltpu.get_barrier_semaphore()
    total.greet(barrier)
    ring.greet(barrier)
    pl.semaphore_wait(barrier, len(HALVING) + 2)
    ring.start()
    for source, target in ((first_ref, first_t), (dattn_ref, dattn_t)):
        for at in range(0, source.shape[0], 512):
            target[:, at : at + 512] = source[at : at + 512, :].T
    half = width // 2

    def step(s, carry):
        @pl.when(s < proj_tiles)
        def _():
            right = dqkv_ref[pl.ds(pl.multiple_of(s * columns, 128), columns), :]
            for at in (0, half):
                store_by_owner(buffer, s, at, nt(first_t[at : at + half, :], right), share)
            total.copy(0, s).start()

        @pl.when(jnp.logical_and(s >= proj_tiles, s < tiles))
        def _():
            right = att_ref[pl.ds(pl.multiple_of((s - proj_tiles) * columns, 128), columns), :]
            for at in (0, half):
                store_by_owner(buffer, s, at, nt(dattn_t[at : at + half, :], right), share)
            total.copy(0, s).start()

        for stage in range(3):
            tile = s - 1 - stage

            @pl.when(jnp.logical_and(tile >= 0, tile < tiles))
            def _():
                total.advance(stage, tile)

        for stage in range(ring.stages):

            @pl.when(s == 2 + 2 * stage)
            def _():
                ring.advance(stage)

        tile = s - 4

        @pl.when(tile >= 0)
        def _():
            sums_ref[tile] = total.gather_stage(3, tile)[1].astype(BF)

        return carry

    lax.fori_loop(0, tiles + 4, step, 0)
    ring.finish()
    every_ref[...] = packs[...]

    def finish(tile, carry):
        for stage in range(4):
            total.copy(stage, tile).wait_send()
        return carry

    lax.fori_loop(0, tiles, finish, 0)


def can_sum_here(width, columns):
    places = lax.axis_size("dp")
    return places == SUM_PLACES and width % (8 * places) == 0 and columns % 384 == 0


def attn_grads(first, dattn, dqkv, att, pack_own, pack_other):
    width = first.shape[1]
    tile = 384
    tiles = (dqkv.shape[0] + att.shape[0]) // tile
    share = width // SUM_PLACES
    vmem = pl.BlockSpec(memory_space=pltpu.VMEM)
    sums, every = pl.pallas_call(
        attn_grads_kernel,
        in_specs=[vmem] * 6,
        out_specs=[vmem] * 2,
        out_shape=[
            jax.ShapeDtypeStruct((tiles, 2 * share, tile), BF),
            jax.ShapeDtypeStruct((SUM_PLACES, 2) + pack_own.shape, BF),
        ],
        scratch_shapes=[
            pltpu.VMEM((width, first.shape[0]), BF),
            pltpu.VMEM((width, dattn.shape[0]), BF),
            pltpu.VMEM((tiles, width, tile), BF),
            pltpu.VMEM((tiles, width // 2, tile), BF),
            pltpu.VMEM((tiles, width // 4, tile), BF),
            pltpu.VMEM((tiles, width // 8, tile), BF),
            pltpu.VMEM((tiles, width // 8, tile), BF),
            pltpu.SemaphoreType.DMA((4, tiles)),
            pltpu.SemaphoreType.DMA((4, tiles)),
            pltpu.VMEM((SUM_PLACES, 2) + pack_own.shape, BF),
            pltpu.SemaphoreType.DMA((SUM_PLACES.bit_length(),)),
            pltpu.SemaphoreType.DMA((SUM_PLACES.bit_length(),)),
        ],
        compiler_params=pltpu.CompilerParams(
            vmem_limit_bytes=VMEM_LIMIT, collective_id=1, has_side_effects=True
        ),
        cost_estimate=cost(1e7, 1e5),
    )(first, dattn, dqkv, att, pack_own, pack_other)
    here = place_bit(lax.axis_index("dp"), FINAL) * share
    mine = lax.dynamic_slice_in_dim(sums, here, share, 1)
    return jnp.transpose(mine, (1, 0, 2)).reshape(share, -1), every


def shift_mp(value, steps):
    ways = lax.axis_size("mp")
    return lax.ppermute(value, "mp", [(i, (i - steps) % ways) for i in range(ways)])


def near_halves(block):
    half = block.shape[0] // 2
    core = lax.axis_index("dp") % 2
    mine = lax.dynamic_slice_in_dim(block, core * half, half, 0)
    return [shift_mp(mine, steps) for steps in range(1, lax.axis_size("mp"))]


def with_far_halves(nears):
    places = lax.axis_size("dp")
    core = lax.axis_index("dp") % 2
    got = []
    for near in nears:
        half = near.shape[0]
        far = lax.ppermute(near, "dp", [(i, i ^ 1) for i in range(places)])
        whole = jnp.zeros((2 * half,) + near.shape[1:], near.dtype)
        whole = lax.dynamic_update_slice_in_dim(whole, near, core * half, 0)
        got.append(lax.dynamic_update_slice_in_dim(whole, far, (1 - core) * half, 0))
    return got


def gathered_parts(nears, own=None):
    half = nears[0].shape[0]
    layout, parts, base = [], [], 0
    if own is not None:
        layout, parts, base = [(0, 0, True)], [own], own.shape[0]
    if half % 16:
        return [(0, 0, True)], [jnp.concatenate(parts + with_far_halves(nears), axis=0)]
    places = lax.axis_size("dp")
    for near in nears:
        far = lax.ppermute(near, "dp", [(i, i ^ 1) for i in range(places)])
        layout += [(base, half, True), (base, half, False)]
        parts += [near, far]
        base += 2 * half
    return layout, parts


def after_own(gathered, own):
    layout, parts = gathered
    return [(0, 0, True)] + [(base + own.shape[0], half, near) for base, half, near in layout], [
        own
    ] + parts


def home(parts):
    total = parts[0].astype(F32)
    for steps in range(1, len(parts)):
        total = total + shift_mp(parts[steps], -steps).astype(F32)
    return total


def to_lanes_rows(size):
    return -(-size // 2048) * 16


def to_lanes(part):
    flat = part.reshape(-1)
    rows = to_lanes_rows(flat.shape[0])
    return jnp.pad(flat, (0, rows * 128 - flat.shape[0])).reshape(rows, 128)


def scatter_dp(part):
    return lax.psum_scatter(part, "dp", scatter_dimension=0, tiled=True)


def local(
    tokens, conditioning, kept_ids, ada_weight, ada_bias, attn_qkv, attn_out, mlp_up, mlp_down,
    rel_table, grad_out_kept, grad_out_full,
):
    ways = lax.axis_size("mp")
    place = lax.axis_index("mp")
    images_group = conditioning.shape[0]
    images = images_group // ways
    width = tokens.shape[1]
    keep = kept_ids.shape[1]
    padded = -(-keep // 64) * 64
    per_block = rel_table.shape[0]
    cols = ada_bias.shape[0]

    silu_cond = jax.nn.silu(conditioning.astype(F32)).astype(BF)
    columns = (jnp.dot(silu_cond, ada_weight, preferred_element_type=F32) + ada_bias).astype(BF)
    mod = lax.all_to_all(columns, "mp", split_axis=0, concat_axis=1, tiled=True)
    mod = jnp.pad(mod.astype(F32).reshape(images, 6, width), ((0, 0), (0, 2), (0, 0)))

    weight_own = jnp.transpose(attn_qkv.reshape(width, -1))
    tables = [rel_table] + [shift_mp(rel_table, s) for s in range(1, ways)]
    mod, tables, weight_sent, out_sent = lax.optimization_barrier(
        (mod, tables, weight_own, attn_out)
    )
    near_w, near_o = near_halves(weight_sent), near_halves(out_sent)
    fetch = ways == 2 and lax.axis_size("dp") % 2 == 0 and mlp_up.shape[0] % 32 == 0
    fetch = fetch and mlp_down.shape[0] % 32 == 0
    bias = bias_whole(jnp.concatenate(tables, axis=0))

    own_kept = lax.dynamic_slice_in_dim(kept_ids, place * images, images, 0)
    own_kept = jnp.pad(own_kept, ((0, 0), (0, padded - keep)), constant_values=-1)
    pick = (own_kept[:, :, None] == jnp.arange(PATCHES, dtype=jnp.int32)).astype(BF)
    grads = jnp.concatenate(
        [
            grad_out_full.reshape(images, PATCHES, width),
            jnp.pad(
                grad_out_kept.reshape(images, keep, width), ((0, 0), (0, padded - keep), (0, 0))
            ),
        ],
        axis=1,
    )
    dmlp = (mod[:, 5:6] * grads.astype(F32)).astype(BF).reshape(-1, width)
    grads = grads.reshape(-1, width)

    own = own_heads(tokens, mod, pick, bias, weight_own, per_block)
    near_w, near_o, own = lax.optimization_barrier((near_w, near_o, own))
    first = own[0]
    weight_others = gathered_parts(near_w)
    weight = after_own(weight_others, weight_own)
    out_weight = gathered_parts(near_o, attn_out)
    cut = (mlp_up.shape[0] * 5 // 18) // 16 * 16
    qkv, att, lse, middle, second, branch, *near_up = forward(
        own, tokens, mod, pick, bias, weight_others, out_weight, per_block,
        mlp_up if fetch else None, cut,
    )
    (branch_mlp, dsecond, grads_own, *whole), tile_own = mlp(
        second, dmlp, mlp_up, mlp_down, None, (near_up[0], mlp_up, mlp_down) if fetch else None
    )
    if fetch:
        up_others, down_others = [whole[0]], [whole[1]]
    else:
        up_others = with_far_halves(near_halves(mlp_up))
        down_others = with_far_halves(near_halves(mlp_down))
    reduced = [scatter_dp(grads_own)]
    for up, down in zip(up_others, down_others):
        (branch_mlp, dsecond, grads_next), _ = mlp(
            second, dmlp, up, down, (branch_mlp, dsecond)
        )
        reduced.append(scatter_dp(grads_next))
    out, dtok, dmod, dattn, dqkv, strips = backward(
        tokens, mod, pick, bias, qkv, lse, middle, branch, branch_mlp, dsecond, grads,
        weight, out_weight, per_block,
    )
    proj_block, out_block = weight_own.shape[0], attn_out.shape[0]
    dqkv, reduced[0] = lax.optimization_barrier((dqkv, reduced[0]))
    dmod_rows = dmod[:, :6].reshape(images, 6 * width)
    dtables = table_of_strips(strips)
    here = can_sum_here(width, dqkv.shape[0]) and att.shape[0] % 384 == 0 and ways == 2
    if here:
        own_cond_rows = lax.dynamic_slice_in_dim(silu_cond, place * images, images, 0)
        packs = []
        for steps in range(ways):
            at = (place + steps) % ways
            parts = (
                lax.dynamic_slice_in_dim(dmod_rows, at * cols, cols, 1),
                dtables[steps * per_block : (steps + 1) * per_block],
                own_cond_rows,
            )
            packs.append(jnp.concatenate([to_lanes(part.astype(BF)) for part in parts], axis=0))
        attn_sums, every = attn_grads(first, dattn, dqkv, att, *packs)
        places = every.shape[0]
        every = every.astype(F32).reshape(places * ways, -1, 128)
        got, end = [], 0
        for part in parts:
            start, end = end, end + to_lanes_rows(part.size)
            got.append(every[:, start:end].reshape(places * ways, -1)[:, : part.size])
        all_columns = got[0].reshape(-1, cols)
        dtable = jnp.sum(got[1], axis=0).reshape(rel_table.shape)
        all_cond = got[2].reshape(-1, width)
        dcolumns = lax.dynamic_slice_in_dim(
            all_columns, pack_slot(lax.axis_index("dp")) * images_group, images_group, 0
        )
    else:
        dweight = dot(first, dqkv, (0, 1)).astype(BF)
        dout_t = dot(dattn, att, (0, 1)).astype(BF)
        attn_sums = scatter_dp(jnp.concatenate([dweight, dout_t], axis=1))
        dcolumns = lax.all_to_all(dmod_rows, "mp", split_axis=1, concat_axis=0, tiled=True)
        dtable = home(list(jnp.split(dtables, ways, axis=0)))
        all_columns = lax.all_gather(dcolumns, "dp", axis=0, tiled=True)
        dtable = lax.psum(dtable, "dp")
        all_cond = lax.all_gather(silu_cond, "dp", axis=0, tiled=True).astype(F32)
    split = ways * proj_block
    attn_parts = [
        jnp.concatenate(
            [
                attn_sums[:, j * proj_block : (j + 1) * proj_block],
                attn_sums[:, split + j * out_block : split + (j + 1) * out_block],
            ],
            axis=1,
        )
        for j in range(ways)
    ]
    mlp_grads = home(reduced)
    attn_total = home(attn_parts)
    grad_up, grad_down_t = split_mlp_grads(mlp_grads, tile_own)
    grad_qkv = attn_total[:, :proj_block].reshape(-1, 3, proj_block // 3)
    grad_out = jnp.transpose(attn_total[:, proj_block:])

    slice_width = width // lax.axis_size("dp")
    cond_slice = lax.dynamic_slice_in_dim(
        all_cond, lax.axis_index("dp") * slice_width, slice_width, 1
    )
    grad_ada_weight = lax.dot_general(
        cond_slice, all_columns, (((0,), (0,)), ((), ())), precision=PRECISE
    )
    grad_ada_bias = jnp.sum(all_columns, axis=0)
    dcolumns_high = dcolumns.astype(BF)
    dcolumns_low = (dcolumns - dcolumns_high.astype(F32)).astype(BF)
    silu_part = nt(jnp.concatenate([dcolumns_high, dcolumns_low], axis=0), ada_weight)
    silu_part = silu_part[:images_group] + silu_part[images_group:]
    shares = lax.all_to_all(
        silu_part.astype(BF).reshape(ways, images, width), "mp", split_axis=0, concat_axis=0,
        tiled=True,
    )
    grad_silu = jnp.sum(shares.astype(F32), axis=0)
    own_cond = lax.dynamic_slice_in_dim(conditioning, place * images, images, 0).astype(F32)
    grad_cond = jax.vjp(jax.nn.silu, own_cond)[1](grad_silu)[0].astype(BF)

    out = out.reshape(images, PATCHES + padded, width)
    out_full = out[:, :PATCHES].reshape(-1, width)
    out_kept = out[:, PATCHES : PATCHES + keep].reshape(-1, width)
    return (
        out_kept, out_full, dtok, grad_cond, grad_ada_weight, grad_ada_bias, grad_qkv, grad_out,
        grad_up, jnp.transpose(grad_down_t), dtable,
    )


def solution(mesh):
    both = P(("dp", "mp"), None)
    return jax.shard_map(
        local,
        mesh=mesh,
        in_specs=(
            both, P("dp", None), P("dp", None), P(None, "mp"), P("mp"), P(None, None, "mp"),
            P("mp", None), P(None, "mp"), P("mp", None), P("mp", None), both, both,
        ),
        out_specs=(
            both, both, both, both, P("dp", "mp"), P("mp"), P("dp", None, "mp"), P("mp", "dp"),
            P("dp", "mp"), P("mp", "dp"), P("mp", None),
        ),
        check_vma=False,
    )
```

```python
import functools
import math

import jax
import jax.numpy as jnp
from jax import lax
from jax.experimental import pallas as pl
from jax.experimental.pallas import tpu as pltpu
from jax.sharding import PartitionSpec as P

HEAD_DIM = 72
GRID = 16
PATCHES = 256
BUCKETS = 961
SPAN = 2 * GRID - 1
EPSILON = 1e-06
PRECISE = lax.Precision.HIGHEST
BF = jnp.bfloat16
F32 = jnp.float32
LOG2E = math.log2(math.e)
VMEM_LIMIT = 60 * 1024 * 1024


def dot(a, b, dims):
    return lax.dot_general(a, b, ((dims[0:1], dims[1:2]), ((), ())), preferred_element_type=F32)


def nn(a, b):
    return dot(a, b, (1, 0))


def nt(a, b):
    return dot(a, b, (1, 1))


def tn(a, b):
    return dot(a, b, (0, 0))


def normalize(rows):
    centered = rows - jnp.mean(rows, axis=-1, keepdims=True)
    inverse = lax.rsqrt(jnp.mean(centered * centered, axis=-1, keepdims=True) + EPSILON)
    return centered * inverse, inverse


def norm_back(normed, inverse, upstream):
    return inverse * (
        upstream
        - jnp.mean(upstream, axis=-1, keepdims=True)
        - normed * jnp.mean(upstream * normed, axis=-1, keepdims=True)
    )


def params(n_grid=1):
    return pltpu.CompilerParams(
        vmem_limit_bytes=VMEM_LIMIT, dimension_semantics=("arbitrary",) * n_grid
    )


def cost(flops, bytes_accessed, transcendentals=0):
    return pl.CostEstimate(
        flops=int(flops), bytes_accessed=int(bytes_accessed), transcendentals=int(transcendentals)
    )


def const_spec(shape):
    return pl.BlockSpec(shape, lambda *_: (0,) * len(shape), pipeline_mode=pl.Buffered(1))


def bias_kernel(strip_ref, bias_ref):
    strip = strip_ref[0]
    for key_row in range(GRID):
        start = (GRID - 1 - key_row) * GRID
        bias_ref[0, key_row * GRID : (key_row + 1) * GRID, :] = strip[:, start : start + PATCHES]


def bias_whole(table):
    heads = table.shape[0]
    grid_table = table.reshape(heads, SPAN, SPAN) * LOG2E
    strip = jnp.stack(
        [grid_table[:, :, GRID - 1 - c : 2 * GRID - 1 - c] for c in range(GRID)], axis=1
    ).reshape(heads, GRID, SPAN * GRID)
    strip = jnp.pad(strip, ((0, 0), (0, 0), (0, 512 - SPAN * GRID)))
    return pl.pallas_call(
        bias_kernel,
        grid=(heads,),
        in_specs=[pl.BlockSpec((1, GRID, 512), lambda h: (h, 0, 0))],
        out_specs=pl.BlockSpec((1, PATCHES, PATCHES), lambda h: (h, 0, 0)),
        out_shape=jax.ShapeDtypeStruct((heads, PATCHES, PATCHES), F32),
        compiler_params=params(),
        cost_estimate=cost(1e6, 1e5),
    )(strip)


def table_of_strips(strips):
    heads = strips.shape[0]
    parts = strips[:, :, : SPAN * GRID].reshape(heads, GRID, SPAN, GRID)
    total = jnp.zeros((heads, SPAN, SPAN), F32)
    for c in range(GRID):
        total = total + jnp.pad(parts[:, c], ((0, 0), (0, 0), (GRID - 1 - c, c)))
    return total.reshape(heads, BUCKETS)


def head_rows(head, per_block):
    base = (head // per_block) * (3 * per_block * HEAD_DIM) + (head % per_block) * HEAD_DIM
    step = per_block * HEAD_DIM
    return [pl.ds(pl.multiple_of(base + c * step, 8), HEAD_DIM) for c in range(3)]


def key_mask(pick):
    ones = jnp.ones((pick.shape[0], PATCHES), BF)
    return (tn(pick, ones) - 1.0) * 1e30


def part_copies(layout, parts, whole, sems):
    core = lax.axis_index("dp") % 2
    copies = []
    for index, ((base, half, near), part) in enumerate(zip(layout, parts)):
        start = base + (core if near else 1 - core) * half
        rows = pl.ds(pl.multiple_of(start, 16), part.shape[0])
        copies.append(pltpu.make_async_copy(part, whole.at[rows, :], sems.at[index]))
    return copies


def run_copies(copies):
    for copy in copies:
        copy.start()
    for copy in copies:
        copy.wait()


def core_rows(half, skip, count):
    start = (lax.axis_index("dp") % 2) * half + skip
    return pl.ds(pl.multiple_of(start, 16), count)


def fetch_copy(own, rows, target, sems, at):
    return pltpu.make_async_remote_copy(
        src_ref=own.at[rows, :],
        dst_ref=target,
        send_sem=sems.at[at],
        recv_sem=sems.at[at + 1],
        device_id={"mp": 1 - lax.axis_index("mp")},
        device_id_type=pl.DeviceIdType.MESH,
    )


def core_copy(source, target, sems, at):
    place = lax.axis_index("dp")
    return pltpu.make_async_remote_copy(
        src_ref=source,
        dst_ref=target,
        send_sem=sems.at[at],
        recv_sem=sems.at[at + 1],
        device_id={"dp": place + 1 - 2 * (place % 2)},
        device_id_type=pl.DeviceIdType.MESH,
    )


def greet_peers(bits):
    barrier = pltpu.get_barrier_semaphore()
    peers = [{"mp": 1 - lax.axis_index("mp")}]
    place = lax.axis_index("dp")
    for bit in bits:
        peers.append({"dp": place + bit - 2 * bit * place_bit(place, bit)})
    for peer in peers:
        pl.semaphore_signal(
            barrier, inc=1, device_id=peer, device_id_type=pl.DeviceIdType.MESH
        )
    pl.semaphore_wait(barrier, len(peers))


def project(weight_ref, first, qkv_s, qkv_ref, base):
    step = weight_ref.shape[0] // 3
    for c in range(3):
        part = nt(weight_ref[c * step : (c + 1) * step, :], first)
        qkv_s[c * step : (c + 1) * step, :] = part
        qkv_ref[base + c * step : base + (c + 1) * step, :] = part.astype(BF)


def attend_heads(per_block, first_head, qkv_s, bias_ref, mask, att_s, attk_s, lse_s):
    scale = HEAD_DIM ** (-0.5) * LOG2E
    heads = qkv_s.shape[0] // (3 * HEAD_DIM)

    def one_head(head, carry):
        q_at, k_at, v_at = head_rows(head, per_block)
        queries = qkv_s[q_at, :].astype(BF)
        keys = qkv_s[k_at, :].astype(BF)
        values = qkv_s[v_at, :].astype(BF)
        scores = tn(keys, queries) * scale + bias_ref[first_head + head]
        here = pl.ds(pl.multiple_of(head * HEAD_DIM, 8), HEAD_DIM)

        def attend(scores):
            top = jnp.max(scores, axis=0, keepdims=True)
            weights = jnp.exp2(scores - top)
            total = jnp.sum(weights, axis=0, keepdims=True)
            probs = (weights * (1.0 / total)).astype(BF)
            return nn(values, probs), top + jnp.log2(total)

        att_s[here, :], lse_s[pl.ds(head, 1), :] = attend(scores)
        attk_s[here, :], lse_s[pl.ds(heads + head, 1), :] = attend(scores + mask)
        return carry

    lax.fori_loop(0, heads, one_head, 0, unroll=4 if heads % 4 == 0 else 2)


def own_heads_kernel(
    per_block, tok_ref, mod_ref, pick_ref, bias_ref, weight_ref,
    first_ref, qkv_ref, att_ref, lse_ref, qkv_s, att_s, attk_s, lse_s,
):
    shift_one, scale_one = mod_ref[0, 0:1], mod_ref[0, 1:2]
    normed, _ = normalize(tok_ref[...].astype(F32))
    first = (normed * (1.0 + scale_one) + shift_one).astype(BF)
    first_ref[...] = first
    project(weight_ref, first, qkv_s, qkv_ref, 0)
    mask = key_mask(pick_ref[0])
    attend_heads(per_block, 0, qkv_s, bias_ref, mask, att_s, attk_s, lse_s)
    att_ref[:, :PATCHES] = att_s[...].astype(BF)
    att_ref[:, PATCHES:] = attk_s[...].astype(BF)
    lse_ref[0] = lse_s[...]


def own_heads(tokens, mod, pick, bias, weight, per_block):
    images, padded = pick.shape[0], pick.shape[1]
    width = tokens.shape[1]
    proj = weight.shape[0]
    heads = proj // (3 * HEAD_DIM)
    inner = heads * HEAD_DIM
    return pl.pallas_call(
        functools.partial(own_heads_kernel, per_block),
        grid=(images,),
        in_specs=[
            pl.BlockSpec((PATCHES, width), lambda i: (i, 0)),
            pl.BlockSpec((1, 8, width), lambda i: (i, 0, 0)),
            pl.BlockSpec((1, padded, PATCHES), lambda i: (i, 0, 0)),
            const_spec(bias.shape),
            const_spec(weight.shape),
        ],
        out_specs=[
            pl.BlockSpec((PATCHES, width), lambda i: (i, 0)),
            pl.BlockSpec((proj, PATCHES), lambda i: (0, i)),
            pl.BlockSpec((inner, 2 * PATCHES), lambda i: (0, i)),
            pl.BlockSpec((1, 2 * heads, PATCHES), lambda i: (i, 0, 0)),
        ],
        out_shape=[
            jax.ShapeDtypeStruct((images * PATCHES, width), BF),
            jax.ShapeDtypeStruct((proj, images * PATCHES), BF),
            jax.ShapeDtypeStruct((inner, images * 2 * PATCHES), BF),
            jax.ShapeDtypeStruct((images, 2 * heads, PATCHES), F32),
        ],
        scratch_shapes=[
            pltpu.VMEM((proj, PATCHES), F32),
            pltpu.VMEM((inner, PATCHES), F32),
            pltpu.VMEM((inner, PATCHES), F32),
            pltpu.VMEM((2 * heads, PATCHES), F32),
        ],
        compiler_params=params(),
        cost_estimate=cost(1e7, 1e5),
    )(tokens, mod, pick, bias, weight)


def forward_kernel(per_block, weight_layout, out_layout, fetch, *refs):
    first_ref, own_qkv, own_att, own_lse, tok_ref, mod_ref, pick_ref, bias_ref = refs[:8]
    refs = refs[8:]
    weight_parts, refs = refs[: len(weight_layout)], refs[len(weight_layout) :]
    out_parts, refs = refs[: len(out_layout)], refs[len(out_layout) :]
    if fetch:
        send_ref, refs = refs[0], refs[1:]
    qkv_ref, att_ref, lse_ref, middle_ref, second_ref, branch_ref = refs[:6]
    refs = refs[6:]
    if fetch:
        got_ref, refs = refs[0], refs[1:]
    qkv_s, att_s, attk_s, lse_s, weight_ref, out_w_ref, part_sems, fetch_sems = refs

    def fetching():
        half = send_ref.shape[0] // 2
        return fetch_copy(send_ref, core_rows(half, 0, got_ref.shape[0]), got_ref, fetch_sems, 0)

    @pl.when(pl.program_id(0) == 0)
    def _():
        copies = part_copies(weight_layout, weight_parts, weight_ref, part_sems.at[0])
        copies += part_copies(out_layout, out_parts, out_w_ref, part_sems.at[1])
        if fetch:
            greet_peers(())
            fetching().start()
        run_copies(copies)

    own = own_qkv.shape[0]
    own_inner = own // 3
    own_count = own_inner // HEAD_DIM
    heads = bias_ref.shape[0]
    others = heads - own_count
    pick = pick_ref[0]
    qkv_ref[:own, :] = own_qkv[...]
    project(weight_ref, first_ref[...], qkv_s, qkv_ref, own)
    mask = key_mask(pick)
    attend_heads(per_block, own_count, qkv_s, bias_ref, mask, att_s, attk_s, lse_s)
    att_ref[:own_inner, :] = own_att[...]
    att_ref[own_inner:, :PATCHES] = att_s[...].astype(BF)
    att_ref[own_inner:, PATCHES:] = attk_s[...].astype(BF)
    lse_ref[0, :own_count, :] = own_lse[0, :own_count]
    lse_ref[0, own_count:heads, :] = lse_s[:others]
    lse_ref[0, heads : heads + own_count, :] = own_lse[0, own_count:]
    lse_ref[0, heads + own_count :, :] = lse_s[others:]
    gate_one = mod_ref[0, 2:3]
    shift_two, scale_two = mod_ref[0, 3:4], mod_ref[0, 4:5]
    out_w = out_w_ref[...]
    kept_att = nt(pick, att_ref[:, PATCHES:]).astype(BF)
    for rows, source, residual in (
        (slice(0, PATCHES), att_ref[:, :PATCHES].T, tok_ref[...].astype(F32)),
        (slice(PATCHES, PATCHES + pick.shape[0]), kept_att, nn(pick, tok_ref[...])),
    ):
        branch = nn(source, out_w)
        branch_ref[rows, :] = branch.astype(BF)
        middle = residual + gate_one * branch
        middle_ref[rows, :] = middle
        second_ref[rows, :] = (normalize(middle)[0] * (1.0 + scale_two) + shift_two).astype(BF)
    if fetch:

        @pl.when(pl.program_id(0) == pl.num_programs(0) - 1)
        def _():
            fetching().wait()


def whole_rows(layout, parts):
    return sum(part.shape[0] for part in parts)


ANYWHERE = pl.BlockSpec(memory_space=pl.ANY)


def forward(own, tokens, mod, pick, bias, weight, out_weight, per_block, send=None, count=0):
    images, padded = pick.shape[0], pick.shape[1]
    width = tokens.shape[1]
    rows = PATCHES + padded
    heads = bias.shape[0]
    (weight_layout, weight_parts), (out_layout, out_parts) = weight, out_weight
    proj_others = whole_rows(*weight)
    proj = own[1].shape[0] + proj_others
    own_inner, own_heads_count = own[2].shape[0], own[3].shape[1] // 2
    others = heads - own_heads_count
    fetch = send is not None
    most = max(len(weight_parts), len(out_parts))
    extra_shapes, extra = [], []
    compiler_params = params()
    if fetch:
        extra_shapes = [jax.ShapeDtypeStruct((count, send.shape[1]), BF)]
        extra = [send]
        compiler_params = pltpu.CompilerParams(
            vmem_limit_bytes=VMEM_LIMIT, dimension_semantics=("arbitrary",),
            collective_id=2, has_side_effects=True,
        )
    by_row = pl.BlockSpec((rows, width), lambda i: (i, 0))
    return pl.pallas_call(
        functools.partial(forward_kernel, per_block, weight_layout, out_layout, fetch),
        grid=(images,),
        in_specs=[
            pl.BlockSpec((PATCHES, width), lambda i: (i, 0)),
            pl.BlockSpec((own[1].shape[0], PATCHES), lambda i: (0, i)),
            pl.BlockSpec((own_inner, 2 * PATCHES), lambda i: (0, i)),
            pl.BlockSpec((1, 2 * own_heads_count, PATCHES), lambda i: (i, 0, 0)),
            pl.BlockSpec((PATCHES, width), lambda i: (i, 0)),
            pl.BlockSpec((1, 8, width), lambda i: (i, 0, 0)),
            pl.BlockSpec((1, padded, PATCHES), lambda i: (i, 0, 0)),
            const_spec(bias.shape),
        ]
        + [ANYWHERE] * (len(weight_parts) + len(out_parts) + len(extra)),
        out_specs=[
            pl.BlockSpec((proj, PATCHES), lambda i: (0, i)),
            pl.BlockSpec((width, 2 * PATCHES), lambda i: (0, i)),
            pl.BlockSpec((1, 2 * heads, PATCHES), lambda i: (i, 0, 0)),
            by_row,
            by_row,
            by_row,
        ]
        + [ANYWHERE] * len(extra),
        out_shape=[
            jax.ShapeDtypeStruct((proj, images * PATCHES), BF),
            jax.ShapeDtypeStruct((width, images * 2 * PATCHES), BF),
            jax.ShapeDtypeStruct((images, 2 * heads, PATCHES), F32),
            jax.ShapeDtypeStruct((images * rows, width), F32),
            jax.ShapeDtypeStruct((images * rows, width), BF),
            jax.ShapeDtypeStruct((images * rows, width), BF),
        ]
        + extra_shapes,
        scratch_shapes=[
            pltpu.VMEM((proj_others, PATCHES), F32),
            pltpu.VMEM((others * HEAD_DIM, PATCHES), F32),
            pltpu.VMEM((others * HEAD_DIM, PATCHES), F32),
            pltpu.VMEM((2 * others, PATCHES), F32),
            pltpu.VMEM((proj_others, width), BF),
            pltpu.VMEM((width, width), BF),
            pltpu.SemaphoreType.DMA((2, most)),
            pltpu.SemaphoreType.DMA((2,)),
        ],
        compiler_params=compiler_params,
        cost_estimate=cost(images * 2e9, images * 8e6),
    )(*own, tokens, mod, pick, bias, *weight_parts, *out_parts, *extra)


def gelu_pair(pre):
    root = math.sqrt(2.0 / math.pi)
    square = pre * pre
    bend = jnp.tanh(pre * (root + (root * 0.044715) * square))
    half = 0.5 + 0.5 * bend
    slope = half + (0.5 * pre) * (1.0 - bend * bend) * (root + (3.0 * root * 0.044715) * square)
    return pre * half, slope


def mlp_kernel(
    chunk, fresh, fetch, second_ref, dmlp_ref, up_ref, down_ref, *refs
):
    if fetch:
        near_ref, send_up, send_down = refs[:3]
        *refs, moves, fetch_sems = refs[3:]
        up_all, down_all = refs[3:5]
        refs = refs[:3] + refs[5:]
    if fresh:
        branch_ref, dsecond_ref, grads_ref, second_t, dmlp_t, hidden_s, dpre_s, sem = refs
    else:
        branch_in, dsecond_in, branch_ref, dsecond_ref, grads_ref = refs[:5]
        second_t, dmlp_t, hidden_s, dpre_s, sem = refs[5:]
    rows = second_ref.shape[0]
    tile = up_ref.shape[1]
    width = second_ref.shape[1]

    if fetch:
        up_half, down_half = up_all.shape[0] // 2, down_all.shape[0] // 2
        cut, quarter = near_ref.shape[0], down_half // 2
        place = lax.axis_index("dp")
        side = place_bit(place, 2)
        up_a = up_all.at[core_rows(up_half, 0, cut), :]
        up_b = up_all.at[core_rows(up_half, cut, up_half - cut), :]
        down_a = down_all.at[core_rows(down_half, 0, down_half), :]
        down_q_rows = core_rows(down_half, side * quarter, quarter)
        down_q = down_all.at[down_q_rows, :]
        lay_a = pltpu.make_async_copy(near_ref, up_a, moves.at[0])
        pass_a = core_copy(near_ref, up_a, moves, 1)
        pass_b = core_copy(up_b, up_b, moves, 3)
        pass_down = core_copy(down_a, down_a, moves, 5)
        pass_y = pltpu.make_async_remote_copy(
            src_ref=down_q,
            dst_ref=down_q,
            send_sem=moves.at[7],
            recv_sem=moves.at[8],
            device_id={"dp": place + 2 - 4 * side},
            device_id_type=pl.DeviceIdType.MESH,
        )
        fetch_b = fetch_copy(
            send_up, core_rows(up_half, cut, up_half - cut), up_b, fetch_sems, 0
        )
        fetch_down = fetch_copy(send_down, down_q_rows, down_q, fetch_sems, 2)
    step, last = pl.program_id(0), pl.num_programs(0) - 1

    @pl.when(step == 0)
    def _():
        if fetch:
            greet_peers((1, 2))
            fetch_down.start()
            lay_a.start()
            pass_a.start()
        if fresh:
            branch_ref[...] = jnp.zeros_like(branch_ref)
            dsecond_ref[...] = jnp.zeros_like(dsecond_ref)
        else:
            one = pltpu.make_async_copy(branch_in, branch_ref, sem.at[0])
            two = pltpu.make_async_copy(dsecond_in, dsecond_ref, sem.at[1])
            one.start()
            two.start()
        for at in range(0, rows, chunk):
            second_t[:, at : at + chunk] = second_ref[at : at + chunk, :].T
            dmlp_t[:, at : at + chunk] = dmlp_ref[at : at + chunk, :].T
        if not fresh:
            one.wait()
            two.wait()

    def one_chunk(index, carry):
        at = pl.ds(pl.multiple_of(index * chunk, chunk), chunk)
        pre = nn(second_ref[at, :], up_ref[...])
        dhidden = nt(dmlp_ref[at, :], down_ref[...])
        value, slope = gelu_pair(pre)
        hidden = value.astype(BF)
        dpre = (dhidden * slope).astype(BF)
        hidden_s[at, :] = hidden
        dpre_s[at, :] = dpre
        branch_ref[at, :] += nn(hidden, down_ref[...])
        dsecond_ref[at, :] += nt(dpre, up_ref[...])
        if fetch:

            @pl.when(jnp.logical_and(step == jnp.minimum(1, last), index == 0))
            def _():
                fetch_down.wait_recv()
                pass_y.start()
                fetch_b.start()

        return carry

    lax.fori_loop(0, rows // chunk, one_chunk, 0)
    if fetch:

        @pl.when(step == last)
        def _():
            fetch_b.wait_recv()
            pass_b.start()
            pass_y.wait_recv()
            pass_down.start()

    part = width // 3
    for c in range(3):
        at = slice(c * part, (c + 1) * part)
        grads_ref[at, :tile] = nn(second_t[at, :], dpre_s[...]).astype(BF)
        grads_ref[at, tile:] = nn(dmlp_t[at, :], hidden_s[...]).astype(BF)

    if fetch:

        @pl.when(step == last)
        def _():
            for copy in (lay_a, pass_a, pass_b, pass_down):
                copy.wait()
            pass_y.wait_send()
            fetch_b.wait_send()
            fetch_down.wait_send()


def mlp_chunk(rows):
    for chunk in (896, 448, 64):
        if rows % chunk == 0:
            return chunk
    return rows


def mlp(second, dmlp, up, down, sums=None, fetch=None):
    rows, width = second.shape
    hidden = up.shape[1]
    tile = 768 if hidden % 768 == 0 else hidden
    fresh = sums is None
    chunk = mlp_chunk(rows)
    in_specs = [
        const_spec(second.shape),
        const_spec(second.shape),
        pl.BlockSpec((width, tile), lambda f: (0, f)),
        pl.BlockSpec((tile, width), lambda f: (f, 0)),
    ]
    operands = [second, dmlp, up, down]
    out_specs = [
        const_spec(second.shape),
        const_spec(second.shape),
        pl.BlockSpec((width, 2 * tile), lambda f: (0, f)),
    ]
    out_shape = [
        jax.ShapeDtypeStruct(second.shape, F32),
        jax.ShapeDtypeStruct(second.shape, F32),
        jax.ShapeDtypeStruct((width, 2 * hidden), BF),
    ]
    scratch = [
        pltpu.VMEM((width, rows), BF),
        pltpu.VMEM((width, rows), BF),
        pltpu.VMEM((rows, tile), BF),
        pltpu.VMEM((rows, tile), BF),
        pltpu.SemaphoreType.DMA((2,)),
    ]
    compiler_params = params()
    if not fresh:
        in_specs += [ANYWHERE] * 2
        operands += list(sums)
    if fetch is not None:
        in_specs += [ANYWHERE] * 3
        operands += list(fetch)
        out_specs += [ANYWHERE] * 2
        out_shape += [jax.ShapeDtypeStruct(up.shape, BF), jax.ShapeDtypeStruct(down.shape, BF)]
        scratch += [pltpu.SemaphoreType.DMA((9,)), pltpu.SemaphoreType.DMA((4,))]
        compiler_params = pltpu.CompilerParams(
            vmem_limit_bytes=VMEM_LIMIT, dimension_semantics=("arbitrary",),
            collective_id=3, has_side_effects=True,
        )
    return pl.pallas_call(
        functools.partial(mlp_kernel, chunk, fresh, fetch is not None),
        grid=(hidden // tile,),
        in_specs=in_specs,
        out_specs=out_specs,
        out_shape=out_shape,
        scratch_shapes=scratch,
        compiler_params=compiler_params,
        cost_estimate=cost(6e10, 6e7) if fresh else cost(1e7, 1e5),
    )(*operands), tile


def split_mlp_grads(grads, tile):
    parts = grads.reshape(grads.shape[0], -1, 2, tile)
    return (
        parts[:, :, 0].reshape(grads.shape[0], -1),
        parts[:, :, 1].reshape(grads.shape[0], -1),
    )


def backward_kernel(per_block, weight_layout, out_layout, *refs):
    count = len(weight_layout) + len(out_layout)
    weight_parts = refs[: len(weight_layout)]
    out_parts = refs[len(weight_layout) : count]
    weight_ref, out_w_ref, sems = refs[-3:]

    @pl.when(pl.program_id(0) == 0)
    def _():
        run_copies(
            part_copies(weight_layout, weight_parts, weight_ref, sems.at[0])
            + part_copies(out_layout, out_parts, out_w_ref, sems.at[1])
        )

    backward_body(per_block, weight_ref, out_w_ref, *refs[count:-3])


def backward_body(
    per_block, weight_ref, out_w_ref, tok_ref, mod_ref, pick_ref, bias_ref,
    qkv_ref, lse_ref, middle_ref, branch_ref, mlp_ref, dsecond_ref, grad_ref,
    out_ref, dtok_ref, dmod_ref, dattn_ref, dqkv_ref, strips_ref,
    qkv_s, datt_s, dattk_s, dscores_s,
):
    heads = bias_ref.shape[0]
    step = pl.program_id(0)
    shift_one, scale_one, gate_one = mod_ref[0, 0:1], mod_ref[0, 1:2], mod_ref[0, 2:3]
    scale_two, gate_two = mod_ref[0, 4:5], mod_ref[0, 5:6]
    pick = pick_ref[0]
    dmiddles = []
    sums = [0.0, 0.0, 0.0, 0.0]
    for rows in (slice(0, PATCHES), slice(PATCHES, PATCHES + pick.shape[0])):
        middle = middle_ref[rows, :]
        branch_mlp = mlp_ref[rows, :]
        dsecond = dsecond_ref[rows, :]
        grad = grad_ref[rows, :].astype(F32)
        out_ref[rows, :] = (middle + gate_two * branch_mlp).astype(BF)
        normed, inverse = normalize(middle)
        dmiddle = grad + norm_back(normed, inverse, dsecond * (1.0 + scale_two))
        branch = branch_ref[rows, :].astype(F32)
        for c, term in enumerate(
            (dmiddle * branch, dsecond, dsecond * normed, grad * branch_mlp)
        ):
            sums[c] = sums[c] + jnp.sum(term, axis=0, keepdims=True)
        dmiddles.append(dmiddle)
    for c in range(4):
        dmod_ref[0, 2 + c : 3 + c, :] = sums[c]
    dattn = (gate_one * dmiddles[0]).astype(BF)
    dattn_kept = tn(pick, (gate_one * dmiddles[1]).astype(BF)).astype(BF)
    dattn_ref[:PATCHES, :] = dattn
    dattn_ref[PATCHES:, :] = dattn_kept
    high = dmiddles[1].astype(BF)
    low = (dmiddles[1] - high.astype(F32)).astype(BF)
    dresid = dmiddles[0] + tn(pick, high) + tn(pick, low)
    datt_s[...] = nt(out_w_ref[...], dattn)
    dattk_s[...] = nt(out_w_ref[...], dattn_kept)
    qkv_s[...] = qkv_ref[...].astype(F32)
    mask = key_mask(pick)
    scale = HEAD_DIM ** (-0.5)

    @pl.when(step == 0)
    def _():
        dscores_s[...] = jnp.zeros_like(dscores_s)

    def one_head(head, carry):
        q_at, k_at, v_at = head_rows(head, per_block)
        queries = qkv_s[q_at, :].astype(BF)
        keys = qkv_s[k_at, :].astype(BF)
        values = qkv_s[v_at, :].astype(BF)
        here = pl.ds(pl.multiple_of(head * HEAD_DIM, 8), HEAD_DIM)
        scores = tn(keys, queries) * (scale * LOG2E) + bias_ref[head]

        def pull(scores, top, upstream):
            probs = jnp.exp2(scores - top)
            dprobs = tn(values, upstream)
            dvalues = nt(upstream, probs.astype(BF))
            weighted = jnp.sum(probs * dprobs, axis=0, keepdims=True)
            return probs * (dprobs - weighted), dvalues

        dscores, dvalues = pull(
            scores, lse_ref[0, pl.ds(head, 1), :], datt_s[here, :].astype(BF)
        )
        dscores_kept, dvalues_kept = pull(
            scores + mask, lse_ref[0, pl.ds(heads + head, 1), :], dattk_s[here, :].astype(BF)
        )
        dscores = dscores + dscores_kept
        dscores_s[head] += dscores
        rounded = dscores.astype(BF)
        qkv_s[q_at, :] = nn(keys, rounded) * scale
        qkv_s[k_at, :] = nt(queries, rounded) * scale
        qkv_s[v_at, :] = dvalues + dvalues_kept
        return carry

    lax.fori_loop(0, heads, one_head, 0, unroll=4)
    dqkv = qkv_s[...].astype(BF)
    dqkv_ref[...] = dqkv
    dfirst = tn(dqkv, weight_ref[...])
    normed, inverse = normalize(tok_ref[...].astype(F32))
    dmod_ref[0, 0:1, :] = jnp.sum(dfirst, axis=0, keepdims=True)
    dmod_ref[0, 1:2, :] = jnp.sum(dfirst * normed, axis=0, keepdims=True)
    dmod_ref[0, 6:8, :] = jnp.zeros((2, dfirst.shape[1]), F32)
    dtok_ref[...] = (dresid + norm_back(normed, inverse, dfirst * (1.0 + scale_one))).astype(BF)

    @pl.when(step == pl.num_programs(0) - 1)
    def _():
        def fold(head, carry):
            strip = jnp.zeros((GRID, 512), F32)
            for key_row in range(GRID):
                start = (GRID - 1 - key_row) * GRID
                block = dscores_s[head, key_row * GRID : (key_row + 1) * GRID, :]
                block = jnp.concatenate([block, jnp.zeros((GRID, 512 - PATCHES), F32)], axis=1)
                strip = strip + pltpu.roll(block, start, 1)
            strips_ref[head] = strip
            return carry

        lax.fori_loop(0, heads, fold, 0)


def backward(
    tokens, mod, pick, bias, qkv, lse, middle, branch, branch_mlp, dsecond, grads,
    weight, out_weight, per_block,
):
    (weight_layout, weight_parts), (out_layout, out_parts) = weight, out_weight
    most = max(len(weight_parts), len(out_parts))
    proj = whole_rows(*weight)
    images, padded = pick.shape[0], pick.shape[1]
    width = tokens.shape[1]
    rows = PATCHES + padded
    heads = bias.shape[0]
    by_row = pl.BlockSpec((rows, width), lambda i: (i, 0))
    return pl.pallas_call(
        functools.partial(backward_kernel, per_block, weight_layout, out_layout),
        grid=(images,),
        in_specs=[ANYWHERE] * (len(weight_parts) + len(out_parts))
        + [
            pl.BlockSpec((PATCHES, width), lambda i: (i, 0)),
            pl.BlockSpec((1, 8, width), lambda i: (i, 0, 0)),
            pl.BlockSpec((1, padded, PATCHES), lambda i: (i, 0, 0)),
            const_spec(bias.shape),
            pl.BlockSpec((proj, PATCHES), lambda i: (0, i)),
            pl.BlockSpec((1, 2 * heads, PATCHES), lambda i: (i, 0, 0)),
            by_row,
            by_row,
            by_row,
            by_row,
            by_row,
        ],
        out_specs=[
            by_row,
            pl.BlockSpec((PATCHES, width), lambda i: (i, 0)),
            pl.BlockSpec((1, 8, width), lambda i: (i, 0, 0)),
            pl.BlockSpec((2 * PATCHES, width), lambda i: (i, 0)),
            pl.BlockSpec((proj, PATCHES), lambda i: (0, i)),
            const_spec((heads, GRID, 512)),
        ],
        out_shape=[
            jax.ShapeDtypeStruct((images * rows, width), BF),
            jax.ShapeDtypeStruct((images * PATCHES, width), BF),
            jax.ShapeDtypeStruct((images, 8, width), F32),
            jax.ShapeDtypeStruct((images * 2 * PATCHES, width), BF),
            jax.ShapeDtypeStruct((proj, images * PATCHES), BF),
            jax.ShapeDtypeStruct((heads, GRID, 512), F32),
        ],
        scratch_shapes=[
            pltpu.VMEM((proj, PATCHES), F32),
            pltpu.VMEM((width, PATCHES), F32),
            pltpu.VMEM((width, PATCHES), F32),
            pltpu.VMEM((heads, PATCHES, PATCHES), F32),
            pltpu.VMEM((proj, width), BF),
            pltpu.VMEM((width, width), BF),
            pltpu.SemaphoreType.DMA((2, most)),
        ],
        compiler_params=params(),
        cost_estimate=cost(1e7, 1e5),
    )(
        *weight_parts, *out_parts, tokens, mod, pick, bias, qkv, lse, middle, branch, branch_mlp,
        dsecond, grads,
    )


SUM_PLACES = 16
HALVING = (1, 2, 8)
FINAL = 4


def place_bit(place, bit):
    return (place // bit) % 2


def unit_start(owner, share):
    index = 0
    for bit in HALVING + (FINAL,):
        index = index * 2 + place_bit(owner, bit)
    return index * share


def store_by_owner(buffer, tile, at, block, share):
    first_owner = at // share
    owners = block.shape[0] // share
    for k in range(owners):
        owner = first_owner + k
        if place_bit(owner, FINAL):
            continue
        pair = k + FINAL
        both = jnp.concatenate(
            [block[k * share : (k + 1) * share], block[pair * share : (pair + 1) * share]], axis=0
        )
        start = unit_start(owner, share)
        buffer[tile, start : start + 2 * share, :] = both.astype(BF)


class DpSum:
    def __init__(self, buffer, lands, sends, recvs):
        self.buffer, self.lands, self.sends, self.recvs = buffer, lands, sends, recvs
        self.place = lax.axis_index("dp")
        self.rows = buffer.shape[1]

    def partner(self, bit):
        return self.place + bit - 2 * bit * place_bit(self.place, bit)

    def greet(self, barrier):
        for bit in HALVING + (FINAL,):
            pl.semaphore_signal(
                barrier, inc=1, device_id={"dp": self.partner(bit)},
                device_id_type=pl.DeviceIdType.MESH,
            )

    def spans(self, stage):
        start, size = 0, self.rows
        for k, bit in enumerate(HALVING):
            size = size // 2
            mine = place_bit(self.place, bit)
            if k == stage:
                return start + mine * size, start + (1 - mine) * size, size
            start = start + mine * size
        return start, start, size

    def copy(self, stage, tile):
        bit = (HALVING + (FINAL,))[stage]
        _, away, size = self.spans(stage)
        return pltpu.make_async_remote_copy(
            src_ref=self.buffer.at[tile, pl.ds(pl.multiple_of(away, 16), size), :],
            dst_ref=self.lands[stage].at[tile],
            send_sem=self.sends.at[stage, tile],
            recv_sem=self.recvs.at[stage, tile],
            device_id={"dp": self.partner(bit)},
            device_id_type=pl.DeviceIdType.MESH,
        )

    def gather_stage(self, stage, tile):
        self.copy(stage, tile).wait_recv()
        keep, _, size = self.spans(stage)
        at = pl.ds(pl.multiple_of(keep, 16), size)
        return at, self.buffer[tile, at, :].astype(F32) + self.lands[stage][tile].astype(F32)

    def advance(self, stage, tile):
        at, total = self.gather_stage(stage, tile)
        self.buffer[tile, at, :] = total.astype(BF)
        self.copy(stage + 1, tile).start()


def pack_slot(place):
    return sum(
        place_bit(place, SUM_PLACES >> (k + 1)) << k for k in range(SUM_PLACES.bit_length() - 1)
    )


class PackGather:
    def __init__(self, own, other, packs, sends, recvs):
        self.own, self.other, self.packs, self.sends, self.recvs = own, other, packs, sends, recvs
        self.place, self.side = lax.axis_index("dp"), lax.axis_index("mp")
        self.stages = SUM_PLACES.bit_length() - 1
        self.slot = pack_slot(self.place)

    def greet(self, barrier):
        pl.semaphore_signal(
            barrier, inc=1, device_id={"mp": 1 - self.side}, device_id_type=pl.DeviceIdType.MESH
        )

    def cross(self):
        return pltpu.make_async_remote_copy(
            src_ref=self.other,
            dst_ref=self.packs.at[self.slot, self.side],
            send_sem=self.sends.at[self.stages],
            recv_sem=self.recvs.at[self.stages],
            device_id={"mp": 1 - self.side},
            device_id_type=pl.DeviceIdType.MESH,
        )

    def copy(self, stage):
        size = 1 << stage
        bit = SUM_PLACES >> (stage + 1)
        rows = self.packs.at[pl.ds((self.slot // size) * size, size)]
        return pltpu.make_async_remote_copy(
            src_ref=rows,
            dst_ref=rows,
            send_sem=self.sends.at[stage],
            recv_sem=self.recvs.at[stage],
            device_id={"dp": self.place + bit - 2 * bit * place_bit(self.place, bit)},
            device_id_type=pl.DeviceIdType.MESH,
        )

    def start(self):
        self.packs[self.slot, self.side] = self.own[...]
        self.cross().start()

    def advance(self, stage):
        (self.cross() if stage == 0 else self.copy(stage - 1)).wait_recv()
        self.copy(stage).start()

    def finish(self):
        self.copy(self.stages - 1).wait_recv()
        self.cross().wait_send()
        for stage in range(self.stages):
            self.copy(stage).wait_send()


def attn_grads_kernel(
    first_ref, dattn_ref, dqkv_ref, att_ref, pack_own_ref, pack_other_ref, sums_ref, every_ref,
    first_t, dattn_t, buffer, land0, land1, land2, land3, sends, recvs,
    packs, pack_sends, pack_recvs,
):
    width = first_t.shape[0]
    tiles, _, columns = buffer.shape
    proj_tiles = dqkv_ref.shape[0] // columns
    share = width // SUM_PLACES
    total = DpSum(buffer, (land0, land1, land2, land3), sends, recvs)
    ring = PackGather(pack_own_ref, pack_other_ref, packs, pack_sends, pack_recvs)
    barrier = pltpu.get_barrier_semaphore()
    total.greet(barrier)
    ring.greet(barrier)
    pl.semaphore_wait(barrier, len(HALVING) + 2)
    ring.start()
    for source, target in ((first_ref, first_t), (dattn_ref, dattn_t)):
        for at in range(0, source.shape[0], 512):
            target[:, at : at + 512] = source[at : at + 512, :].T
    half = width // 2

    def step(s, carry):
        @pl.when(s < proj_tiles)
        def _():
            right = dqkv_ref[pl.ds(pl.multiple_of(s * columns, 128), columns), :]
            for at in (0, half):
                store_by_owner(buffer, s, at, nt(first_t[at : at + half, :], right), share)
            total.copy(0, s).start()

        @pl.when(jnp.logical_and(s >= proj_tiles, s < tiles))
        def _():
            right = att_ref[pl.ds(pl.multiple_of((s - proj_tiles) * columns, 128), columns), :]
            for at in (0, half):
                store_by_owner(buffer, s, at, nt(dattn_t[at : at + half, :], right), share)
            total.copy(0, s).start()

        for stage in range(3):
            tile = s - 1 - stage

            @pl.when(jnp.logical_and(tile >= 0, tile < tiles))
            def _():
                total.advance(stage, tile)

        for stage in range(ring.stages):

            @pl.when(s == 2 + 2 * stage)
            def _():
                ring.advance(stage)

        tile = s - 4

        @pl.when(tile >= 0)
        def _():
            sums_ref[tile] = total.gather_stage(3, tile)[1].astype(BF)

        return carry

    lax.fori_loop(0, tiles + 4, step, 0)
    ring.finish()
    every_ref[...] = packs[...]

    def finish(tile, carry):
        for stage in range(4):
            total.copy(stage, tile).wait_send()
        return carry

    lax.fori_loop(0, tiles, finish, 0)


def can_sum_here(width, columns):
    places = lax.axis_size("dp")
    return places == SUM_PLACES and width % (8 * places) == 0 and columns % 384 == 0


def attn_grads(first, dattn, dqkv, att, pack_own, pack_other):
    width = first.shape[1]
    tile = 384
    tiles = (dqkv.shape[0] + att.shape[0]) // tile
    share = width // SUM_PLACES
    vmem = pl.BlockSpec(memory_space=pltpu.VMEM)
    sums, every = pl.pallas_call(
        attn_grads_kernel,
        in_specs=[vmem] * 6,
        out_specs=[vmem] * 2,
        out_shape=[
            jax.ShapeDtypeStruct((tiles, 2 * share, tile), BF),
            jax.ShapeDtypeStruct((SUM_PLACES, 2) + pack_own.shape, BF),
        ],
        scratch_shapes=[
            pltpu.VMEM((width, first.shape[0]), BF),
            pltpu.VMEM((width, dattn.shape[0]), BF),
            pltpu.VMEM((tiles, width, tile), BF),
            pltpu.VMEM((tiles, width // 2, tile), BF),
            pltpu.VMEM((tiles, width // 4, tile), BF),
            pltpu.VMEM((tiles, width // 8, tile), BF),
            pltpu.VMEM((tiles, width // 8, tile), BF),
            pltpu.SemaphoreType.DMA((4, tiles)),
            pltpu.SemaphoreType.DMA((4, tiles)),
            pltpu.VMEM((SUM_PLACES, 2) + pack_own.shape, BF),
            pltpu.SemaphoreType.DMA((SUM_PLACES.bit_length(),)),
            pltpu.SemaphoreType.DMA((SUM_PLACES.bit_length(),)),
        ],
        compiler_params=pltpu.CompilerParams(
            vmem_limit_bytes=VMEM_LIMIT, collective_id=1, has_side_effects=True
        ),
        cost_estimate=cost(1e7, 1e5),
    )(first, dattn, dqkv, att, pack_own, pack_other)
    here = place_bit(lax.axis_index("dp"), FINAL) * share
    mine = lax.dynamic_slice_in_dim(sums, here, share, 1)
    return jnp.transpose(mine, (1, 0, 2)).reshape(share, -1), every


def shift_mp(value, steps):
    ways = lax.axis_size("mp")
    return lax.ppermute(value, "mp", [(i, (i - steps) % ways) for i in range(ways)])


def near_halves(block):
    half = block.shape[0] // 2
    core = lax.axis_index("dp") % 2
    mine = lax.dynamic_slice_in_dim(block, core * half, half, 0)
    return [shift_mp(mine, steps) for steps in range(1, lax.axis_size("mp"))]


def with_far_halves(nears):
    places = lax.axis_size("dp")
    core = lax.axis_index("dp") % 2
    got = []
    for near in nears:
        half = near.shape[0]
        far = lax.ppermute(near, "dp", [(i, i ^ 1) for i in range(places)])
        whole = jnp.zeros((2 * half,) + near.shape[1:], near.dtype)
        whole = lax.dynamic_update_slice_in_dim(whole, near, core * half, 0)
        got.append(lax.dynamic_update_slice_in_dim(whole, far, (1 - core) * half, 0))
    return got


def gathered_parts(nears, own=None):
    half = nears[0].shape[0]
    layout, parts, base = [], [], 0
    if own is not None:
        layout, parts, base = [(0, 0, True)], [own], own.shape[0]
    if half % 16:
        return [(0, 0, True)], [jnp.concatenate(parts + with_far_halves(nears), axis=0)]
    places = lax.axis_size("dp")
    for near in nears:
        far = lax.ppermute(near, "dp", [(i, i ^ 1) for i in range(places)])
        layout += [(base, half, True), (base, half, False)]
        parts += [near, far]
        base += 2 * half
    return layout, parts


def after_own(gathered, own):
    layout, parts = gathered
    return [(0, 0, True)] + [(base + own.shape[0], half, near) for base, half, near in layout], [
        own
    ] + parts


def home(parts):
    total = parts[0].astype(F32)
    for steps in range(1, len(parts)):
        total = total + shift_mp(parts[steps], -steps).astype(F32)
    return total


def scatter_dp(part):
    return lax.psum_scatter(part, "dp", scatter_dimension=0, tiled=True)


def local(
    tokens, conditioning, kept_ids, ada_weight, ada_bias, attn_qkv, attn_out, mlp_up, mlp_down,
    rel_table, grad_out_kept, grad_out_full,
):
    ways = lax.axis_size("mp")
    place = lax.axis_index("mp")
    images_group = conditioning.shape[0]
    images = images_group // ways
    width = tokens.shape[1]
    keep = kept_ids.shape[1]
    padded = -(-keep // 64) * 64
    per_block = rel_table.shape[0]
    cols = ada_bias.shape[0]

    silu_cond = jax.nn.silu(conditioning.astype(F32)).astype(BF)
    columns = (jnp.dot(silu_cond, ada_weight, preferred_element_type=F32) + ada_bias).astype(BF)
    mod = lax.all_to_all(columns, "mp", split_axis=0, concat_axis=1, tiled=True)
    mod = jnp.pad(mod.astype(F32).reshape(images, 6, width), ((0, 0), (0, 2), (0, 0)))

    weight_own = jnp.transpose(attn_qkv.reshape(width, -1))
    tables = [rel_table] + [shift_mp(rel_table, s) for s in range(1, ways)]
    mod, tables, weight_sent, out_sent = lax.optimization_barrier(
        (mod, tables, weight_own, attn_out)
    )
    near_w, near_o = near_halves(weight_sent), near_halves(out_sent)
    fetch = ways == 2 and lax.axis_size("dp") % 4 == 0 and mlp_up.shape[0] % 32 == 0
    fetch = fetch and mlp_down.shape[0] % 64 == 0
    bias = bias_whole(jnp.concatenate(tables, axis=0))

    own_kept = lax.dynamic_slice_in_dim(kept_ids, place * images, images, 0)
    own_kept = jnp.pad(own_kept, ((0, 0), (0, padded - keep)), constant_values=-1)
    pick = (own_kept[:, :, None] == jnp.arange(PATCHES, dtype=jnp.int32)).astype(BF)
    grads = jnp.concatenate(
        [
            grad_out_full.reshape(images, PATCHES, width),
            jnp.pad(
                grad_out_kept.reshape(images, keep, width), ((0, 0), (0, padded - keep), (0, 0))
            ),
        ],
        axis=1,
    )
    dmlp = (mod[:, 5:6] * grads.astype(F32)).astype(BF).reshape(-1, width)
    grads = grads.reshape(-1, width)

    own = own_heads(tokens, mod, pick, bias, weight_own, per_block)
    near_w, near_o, own = lax.optimization_barrier((near_w, near_o, own))
    first = own[0]
    weight_others = gathered_parts(near_w)
    weight = after_own(weight_others, weight_own)
    out_weight = gathered_parts(near_o, attn_out)
    cut = (mlp_up.shape[0] * 5 // 18) // 16 * 16
    qkv, att, lse, middle, second, branch, *near_up = forward(
        own, tokens, mod, pick, bias, weight_others, out_weight, per_block,
        mlp_up if fetch else None, cut,
    )
    (branch_mlp, dsecond, grads_own, *whole), tile_own = mlp(
        second, dmlp, mlp_up, mlp_down, None, (near_up[0], mlp_up, mlp_down) if fetch else None
    )
    if fetch:
        up_others, down_others = [whole[0]], [whole[1]]
    else:
        up_others = with_far_halves(near_halves(mlp_up))
        down_others = with_far_halves(near_halves(mlp_down))
    reduced = [scatter_dp(grads_own)]
    for up, down in zip(up_others, down_others):
        (branch_mlp, dsecond, grads_next), _ = mlp(
            second, dmlp, up, down, (branch_mlp, dsecond)
        )
        reduced.append(scatter_dp(grads_next))
    out, dtok, dmod, dattn, dqkv, strips = backward(
        tokens, mod, pick, bias, qkv, lse, middle, branch, branch_mlp, dsecond, grads,
        weight, out_weight, per_block,
    )
    proj_block, out_block = weight_own.shape[0], attn_out.shape[0]
    dqkv, reduced[0] = lax.optimization_barrier((dqkv, reduced[0]))
    dtables = table_of_strips(strips)
    here = can_sum_here(width, dqkv.shape[0]) and att.shape[0] % 384 == 0 and ways == 2
    here = here and cols % width == 0
    if here:
        own_cond_rows = lax.dynamic_slice_in_dim(silu_cond, place * images, images, 0)
        pieces = cols // width
        packs = []
        for steps in range(ways):
            at = (place + steps) % ways
            table = dtables[steps * per_block : (steps + 1) * per_block]
            pack = jnp.concatenate(
                [
                    lax.dynamic_slice_in_dim(dmod, at * pieces, pieces, 1)
                    .astype(BF)
                    .reshape(-1, width),
                    own_cond_rows,
                    jnp.pad(table, ((0, 0), (0, width - BUCKETS))).astype(BF),
                ],
                axis=0,
            )
            packs.append(jnp.pad(pack, ((0, -pack.shape[0] % 16), (0, 0))))
        attn_sums, every = attn_grads(first, dattn, dqkv, att, *packs)
        places, first_cond = every.shape[0], images * pieces
        every = every.reshape((places * ways,) + every.shape[2:]).astype(F32)
        all_columns = every[:, :first_cond].reshape(-1, cols)
        all_cond = every[:, first_cond : first_cond + images].reshape(-1, width)
        dtable = jnp.sum(every[:, first_cond + images :], axis=0)[:per_block, :BUCKETS]
        dcolumns = lax.dynamic_slice_in_dim(
            all_columns, pack_slot(lax.axis_index("dp")) * images_group, images_group, 0
        )
    else:
        dweight = dot(first, dqkv, (0, 1)).astype(BF)
        dout_t = dot(dattn, att, (0, 1)).astype(BF)
        attn_sums = scatter_dp(jnp.concatenate([dweight, dout_t], axis=1))
        dmod_rows = dmod[:, :6].reshape(images, 6 * width)
        dcolumns = lax.all_to_all(dmod_rows, "mp", split_axis=1, concat_axis=0, tiled=True)
        dtable = home(list(jnp.split(dtables, ways, axis=0)))
        all_columns = lax.all_gather(dcolumns, "dp", axis=0, tiled=True)
        dtable = lax.psum(dtable, "dp")
        all_cond = lax.all_gather(silu_cond, "dp", axis=0, tiled=True).astype(F32)
    split = ways * proj_block
    attn_parts = [
        jnp.concatenate(
            [
                attn_sums[:, j * proj_block : (j + 1) * proj_block],
                attn_sums[:, split + j * out_block : split + (j + 1) * out_block],
            ],
            axis=1,
        )
        for j in range(ways)
    ]
    totals = home([jnp.concatenate(pair, axis=1) for pair in zip(reduced, attn_parts)])
    mlp_grads, attn_total = totals[:, : reduced[0].shape[1]], totals[:, reduced[0].shape[1] :]
    grad_up, grad_down_t = split_mlp_grads(mlp_grads, tile_own)
    grad_qkv = attn_total[:, :proj_block].reshape(-1, 3, proj_block // 3)
    grad_out = jnp.transpose(attn_total[:, proj_block:])

    slice_width = width // lax.axis_size("dp")
    cond_slice = lax.dynamic_slice_in_dim(
        all_cond, lax.axis_index("dp") * slice_width, slice_width, 1
    )
    grad_ada_weight = lax.dot_general(
        cond_slice, all_columns, (((0,), (0,)), ((), ())), precision=PRECISE
    )
    grad_ada_bias = jnp.sum(all_columns, axis=0)
    dcolumns_high = dcolumns.astype(BF)
    dcolumns_low = (dcolumns - dcolumns_high.astype(F32)).astype(BF)
    silu_part = nt(jnp.concatenate([dcolumns_high, dcolumns_low], axis=0), ada_weight)
    silu_part = silu_part[:images_group] + silu_part[images_group:]
    shares = lax.all_to_all(
        silu_part.astype(BF).reshape(ways, images, width), "mp", split_axis=0, concat_axis=0,
        tiled=True,
    )
    grad_silu = jnp.sum(shares.astype(F32), axis=0)
    own_cond = lax.dynamic_slice_in_dim(conditioning, place * images, images, 0).astype(F32)
    grad_cond = jax.vjp(jax.nn.silu, own_cond)[1](grad_silu)[0].astype(BF)

    out = out.reshape(images, PATCHES + padded, width)
    out_full = out[:, :PATCHES].reshape(-1, width)
    out_kept = out[:, PATCHES : PATCHES + keep].reshape(-1, width)
    return (
        out_kept, out_full, dtok, grad_cond, grad_ada_weight, grad_ada_bias, grad_qkv, grad_out,
        grad_up, jnp.transpose(grad_down_t), dtable,
    )


def solution(mesh):
    both = P(("dp", "mp"), None)
    return jax.shard_map(
        local,
        mesh=mesh,
        in_specs=(
            both, P("dp", None), P("dp", None), P(None, "mp"), P("mp"), P(None, None, "mp"),
            P("mp", None), P(None, "mp"), P("mp", None), P("mp", None), both, both,
        ),
        out_specs=(
            both, both, both, both, P("dp", "mp"), P("mp"), P("dp", None, "mp"), P("mp", "dp"),
            P("dp", "mp"), P("mp", "dp"), P("mp", None),
        ),
        check_vma=False,
    )
```

```python
import functools
import math

import jax
import jax.numpy as jnp
from jax import lax
from jax.experimental import pallas as pl
from jax.experimental.pallas import tpu as pltpu
from jax.sharding import PartitionSpec as P

HEAD_DIM = 72
GRID = 16
PATCHES = 256
BUCKETS = 961
SPAN = 2 * GRID - 1
EPSILON = 1e-06
PRECISE = lax.Precision.HIGHEST
BF = jnp.bfloat16
F32 = jnp.float32
LOG2E = math.log2(math.e)
VMEM_LIMIT = 60 * 1024 * 1024


def dot(a, b, dims):
    return lax.dot_general(a, b, ((dims[0:1], dims[1:2]), ((), ())), preferred_element_type=F32)


def nn(a, b):
    return dot(a, b, (1, 0))


def nt(a, b):
    return dot(a, b, (1, 1))


def tn(a, b):
    return dot(a, b, (0, 0))


def normalize(rows):
    centered = rows - jnp.mean(rows, axis=-1, keepdims=True)
    inverse = lax.rsqrt(jnp.mean(centered * centered, axis=-1, keepdims=True) + EPSILON)
    return centered * inverse, inverse


def norm_back(normed, inverse, upstream):
    return inverse * (
        upstream
        - jnp.mean(upstream, axis=-1, keepdims=True)
        - normed * jnp.mean(upstream * normed, axis=-1, keepdims=True)
    )


def params(n_grid=1):
    return pltpu.CompilerParams(
        vmem_limit_bytes=VMEM_LIMIT, dimension_semantics=("arbitrary",) * n_grid
    )


def cost(flops, bytes_accessed, transcendentals=0):
    return pl.CostEstimate(
        flops=int(flops), bytes_accessed=int(bytes_accessed), transcendentals=int(transcendentals)
    )


def const_spec(shape):
    return pl.BlockSpec(shape, lambda *_: (0,) * len(shape), pipeline_mode=pl.Buffered(1))


def bias_kernel(strip_ref, bias_ref):
    strip = strip_ref[0]
    for key_row in range(GRID):
        start = (GRID - 1 - key_row) * GRID
        bias_ref[0, key_row * GRID : (key_row + 1) * GRID, :] = strip[:, start : start + PATCHES]


def bias_whole(table):
    heads = table.shape[0]
    grid_table = table.reshape(heads, SPAN, SPAN) * LOG2E
    strip = jnp.stack(
        [grid_table[:, :, GRID - 1 - c : 2 * GRID - 1 - c] for c in range(GRID)], axis=1
    ).reshape(heads, GRID, SPAN * GRID)
    strip = jnp.pad(strip, ((0, 0), (0, 0), (0, 512 - SPAN * GRID)))
    return pl.pallas_call(
        bias_kernel,
        grid=(heads,),
        in_specs=[pl.BlockSpec((1, GRID, 512), lambda h: (h, 0, 0))],
        out_specs=pl.BlockSpec((1, PATCHES, PATCHES), lambda h: (h, 0, 0)),
        out_shape=jax.ShapeDtypeStruct((heads, PATCHES, PATCHES), F32),
        compiler_params=params(),
        cost_estimate=cost(1e6, 1e5),
    )(strip)


def table_of_strips(strips):
    heads = strips.shape[0]
    parts = strips[:, :, : SPAN * GRID].reshape(heads, GRID, SPAN, GRID)
    total = jnp.zeros((heads, SPAN, SPAN), F32)
    for c in range(GRID):
        total = total + jnp.pad(parts[:, c], ((0, 0), (0, 0), (GRID - 1 - c, c)))
    return total.reshape(heads, BUCKETS)


def head_rows(head, per_block):
    base = (head // per_block) * (3 * per_block * HEAD_DIM) + (head % per_block) * HEAD_DIM
    step = per_block * HEAD_DIM
    return [pl.ds(pl.multiple_of(base + c * step, 8), HEAD_DIM) for c in range(3)]


def key_mask(pick):
    ones = jnp.ones((pick.shape[0], PATCHES), BF)
    return (tn(pick, ones) - 1.0) * 1e30


def part_copies(layout, parts, whole, sems):
    core = lax.axis_index("dp") % 2
    copies = []
    for index, ((base, half, near), part) in enumerate(zip(layout, parts)):
        start = base + (core if near else 1 - core) * half
        rows = pl.ds(pl.multiple_of(start, 16), part.shape[0])
        copies.append(pltpu.make_async_copy(part, whole.at[rows, :], sems.at[index]))
    return copies


def run_copies(copies):
    for copy in copies:
        copy.start()
    for copy in copies:
        copy.wait()


def core_rows(half, skip, count):
    start = (lax.axis_index("dp") % 2) * half + skip
    return pl.ds(pl.multiple_of(start, 16), count)


def fetch_copy(own, rows, target, sems, at):
    return pltpu.make_async_remote_copy(
        src_ref=own.at[rows, :],
        dst_ref=target,
        send_sem=sems.at[at],
        recv_sem=sems.at[at + 1],
        device_id={"mp": 1 - lax.axis_index("mp")},
        device_id_type=pl.DeviceIdType.MESH,
    )


def core_copy(source, target, sems, at):
    place = lax.axis_index("dp")
    return pltpu.make_async_remote_copy(
        src_ref=source,
        dst_ref=target,
        send_sem=sems.at[at],
        recv_sem=sems.at[at + 1],
        device_id={"dp": place + 1 - 2 * (place % 2)},
        device_id_type=pl.DeviceIdType.MESH,
    )


def greet_peers(bits):
    barrier = pltpu.get_barrier_semaphore()
    peers = [{"mp": 1 - lax.axis_index("mp")}]
    place = lax.axis_index("dp")
    for bit in bits:
        peers.append({"dp": place + bit - 2 * bit * place_bit(place, bit)})
    for peer in peers:
        pl.semaphore_signal(
            barrier, inc=1, device_id=peer, device_id_type=pl.DeviceIdType.MESH
        )
    pl.semaphore_wait(barrier, len(peers))


def project(weight_ref, first, qkv_s, qkv_ref, base):
    step = weight_ref.shape[0] // 3
    for c in range(3):
        part = nt(weight_ref[c * step : (c + 1) * step, :], first)
        qkv_s[c * step : (c + 1) * step, :] = part
        qkv_ref[base + c * step : base + (c + 1) * step, :] = part.astype(BF)


def attend_heads(per_block, first_head, qkv_s, bias_ref, mask, att_s, attk_s, lse_s):
    scale = HEAD_DIM ** (-0.5) * LOG2E
    heads = qkv_s.shape[0] // (3 * HEAD_DIM)

    def one_head(head, carry):
        q_at, k_at, v_at = head_rows(head, per_block)
        queries = qkv_s[q_at, :].astype(BF)
        keys = qkv_s[k_at, :].astype(BF)
        values = qkv_s[v_at, :].astype(BF)
        scores = tn(keys, queries) * scale + bias_ref[first_head + head]
        here = pl.ds(pl.multiple_of(head * HEAD_DIM, 8), HEAD_DIM)

        def attend(scores):
            top = jnp.max(scores, axis=0, keepdims=True)
            weights = jnp.exp2(scores - top)
            total = jnp.sum(weights, axis=0, keepdims=True)
            probs = (weights * (1.0 / total)).astype(BF)
            return nn(values, probs), top + jnp.log2(total)

        att_s[here, :], lse_s[pl.ds(head, 1), :] = attend(scores)
        attk_s[here, :], lse_s[pl.ds(heads + head, 1), :] = attend(scores + mask)
        return carry

    lax.fori_loop(0, heads, one_head, 0, unroll=4 if heads % 4 == 0 else 2)


def own_heads_kernel(
    per_block, tok_ref, mod_ref, pick_ref, bias_ref, weight_ref,
    first_ref, qkv_ref, att_ref, lse_ref, qkv_s, att_s, attk_s, lse_s,
):
    shift_one, scale_one = mod_ref[0, 0:1], mod_ref[0, 1:2]
    normed, _ = normalize(tok_ref[...].astype(F32))
    first = (normed * (1.0 + scale_one) + shift_one).astype(BF)
    first_ref[...] = first
    project(weight_ref, first, qkv_s, qkv_ref, 0)
    mask = key_mask(pick_ref[0])
    attend_heads(per_block, 0, qkv_s, bias_ref, mask, att_s, attk_s, lse_s)
    att_ref[:, :PATCHES] = att_s[...].astype(BF)
    att_ref[:, PATCHES:] = attk_s[...].astype(BF)
    lse_ref[0] = lse_s[...]


def own_heads(tokens, mod, pick, bias, weight, per_block):
    images, padded = pick.shape[0], pick.shape[1]
    width = tokens.shape[1]
    proj = weight.shape[0]
    heads = proj // (3 * HEAD_DIM)
    inner = heads * HEAD_DIM
    return pl.pallas_call(
        functools.partial(own_heads_kernel, per_block),
        grid=(images,),
        in_specs=[
            pl.BlockSpec((PATCHES, width), lambda i: (i, 0)),
            pl.BlockSpec((1, 8, width), lambda i: (i, 0, 0)),
            pl.BlockSpec((1, padded, PATCHES), lambda i: (i, 0, 0)),
            const_spec(bias.shape),
            const_spec(weight.shape),
        ],
        out_specs=[
            pl.BlockSpec((PATCHES, width), lambda i: (i, 0)),
            pl.BlockSpec((proj, PATCHES), lambda i: (0, i)),
            pl.BlockSpec((inner, 2 * PATCHES), lambda i: (0, i)),
            pl.BlockSpec((1, 2 * heads, PATCHES), lambda i: (i, 0, 0)),
        ],
        out_shape=[
            jax.ShapeDtypeStruct((images * PATCHES, width), BF),
            jax.ShapeDtypeStruct((proj, images * PATCHES), BF),
            jax.ShapeDtypeStruct((inner, images * 2 * PATCHES), BF),
            jax.ShapeDtypeStruct((images, 2 * heads, PATCHES), F32),
        ],
        scratch_shapes=[
            pltpu.VMEM((proj, PATCHES), F32),
            pltpu.VMEM((inner, PATCHES), F32),
            pltpu.VMEM((inner, PATCHES), F32),
            pltpu.VMEM((2 * heads, PATCHES), F32),
        ],
        compiler_params=params(),
        cost_estimate=cost(1e7, 1e5),
    )(tokens, mod, pick, bias, weight)


def forward_kernel(per_block, weight_layout, out_layout, fetch, *refs):
    first_ref, own_qkv, own_att, own_lse, tok_ref, mod_ref, pick_ref, bias_ref = refs[:8]
    refs = refs[8:]
    weight_parts, refs = refs[: len(weight_layout)], refs[len(weight_layout) :]
    out_parts, refs = refs[: len(out_layout)], refs[len(out_layout) :]
    if fetch:
        send_ref, refs = refs[0], refs[1:]
    qkv_ref, att_ref, lse_ref, middle_ref, second_ref, branch_ref = refs[:6]
    refs = refs[6:]
    if fetch:
        got_ref, refs = refs[0], refs[1:]
    qkv_s, att_s, attk_s, lse_s, weight_ref, out_w_ref, part_sems, fetch_sems = refs

    def fetching():
        half = send_ref.shape[0] // 2
        return fetch_copy(send_ref, core_rows(half, 0, got_ref.shape[0]), got_ref, fetch_sems, 0)

    @pl.when(pl.program_id(0) == 0)
    def _():
        copies = part_copies(weight_layout, weight_parts, weight_ref, part_sems.at[0])
        copies += part_copies(out_layout, out_parts, out_w_ref, part_sems.at[1])
        if fetch:
            greet_peers(())
            fetching().start()
        run_copies(copies)

    own = own_qkv.shape[0]
    own_inner = own // 3
    own_count = own_inner // HEAD_DIM
    heads = bias_ref.shape[0]
    others = heads - own_count
    pick = pick_ref[0]
    qkv_ref[:own, :] = own_qkv[...]
    project(weight_ref, first_ref[...], qkv_s, qkv_ref, own)
    mask = key_mask(pick)
    attend_heads(per_block, own_count, qkv_s, bias_ref, mask, att_s, attk_s, lse_s)
    att_ref[:own_inner, :] = own_att[...]
    att_ref[own_inner:, :PATCHES] = att_s[...].astype(BF)
    att_ref[own_inner:, PATCHES:] = attk_s[...].astype(BF)
    lse_ref[0, :own_count, :] = own_lse[0, :own_count]
    lse_ref[0, own_count:heads, :] = lse_s[:others]
    lse_ref[0, heads : heads + own_count, :] = own_lse[0, own_count:]
    lse_ref[0, heads + own_count :, :] = lse_s[others:]
    gate_one = mod_ref[0, 2:3]
    shift_two, scale_two = mod_ref[0, 3:4], mod_ref[0, 4:5]
    out_w = out_w_ref[...]
    kept_att = nt(pick, att_ref[:, PATCHES:]).astype(BF)
    for rows, source, residual in (
        (slice(0, PATCHES), att_ref[:, :PATCHES].T, tok_ref[...].astype(F32)),
        (slice(PATCHES, PATCHES + pick.shape[0]), kept_att, nn(pick, tok_ref[...])),
    ):
        branch = nn(source, out_w)
        branch_ref[rows, :] = branch.astype(BF)
        middle = residual + gate_one * branch
        middle_ref[rows, :] = middle
        second_ref[rows, :] = (normalize(middle)[0] * (1.0 + scale_two) + shift_two).astype(BF)
    if fetch:

        @pl.when(pl.program_id(0) == pl.num_programs(0) - 1)
        def _():
            fetching().wait()


def whole_rows(layout, parts):
    return sum(part.shape[0] for part in parts)


ANYWHERE = pl.BlockSpec(memory_space=pl.ANY)


def forward(own, tokens, mod, pick, bias, weight, out_weight, per_block, send=None, count=0):
    images, padded = pick.shape[0], pick.shape[1]
    width = tokens.shape[1]
    rows = PATCHES + padded
    heads = bias.shape[0]
    (weight_layout, weight_parts), (out_layout, out_parts) = weight, out_weight
    proj_others = whole_rows(*weight)
    proj = own[1].shape[0] + proj_others
    own_inner, own_heads_count = own[2].shape[0], own[3].shape[1] // 2
    others = heads - own_heads_count
    fetch = send is not None
    most = max(len(weight_parts), len(out_parts))
    extra_shapes, extra = [], []
    compiler_params = params()
    if fetch:
        extra_shapes = [jax.ShapeDtypeStruct((count, send.shape[1]), BF)]
        extra = [send]
        compiler_params = pltpu.CompilerParams(
            vmem_limit_bytes=VMEM_LIMIT, dimension_semantics=("arbitrary",),
            collective_id=2, has_side_effects=True,
        )
    by_row = pl.BlockSpec((rows, width), lambda i: (i, 0))
    return pl.pallas_call(
        functools.partial(forward_kernel, per_block, weight_layout, out_layout, fetch),
        grid=(images,),
        in_specs=[
            pl.BlockSpec((PATCHES, width), lambda i: (i, 0)),
            pl.BlockSpec((own[1].shape[0], PATCHES), lambda i: (0, i)),
            pl.BlockSpec((own_inner, 2 * PATCHES), lambda i: (0, i)),
            pl.BlockSpec((1, 2 * own_heads_count, PATCHES), lambda i: (i, 0, 0)),
            pl.BlockSpec((PATCHES, width), lambda i: (i, 0)),
            pl.BlockSpec((1, 8, width), lambda i: (i, 0, 0)),
            pl.BlockSpec((1, padded, PATCHES), lambda i: (i, 0, 0)),
            const_spec(bias.shape),
        ]
        + [ANYWHERE] * (len(weight_parts) + len(out_parts) + len(extra)),
        out_specs=[
            pl.BlockSpec((proj, PATCHES), lambda i: (0, i)),
            pl.BlockSpec((width, 2 * PATCHES), lambda i: (0, i)),
            pl.BlockSpec((1, 2 * heads, PATCHES), lambda i: (i, 0, 0)),
            by_row,
            by_row,
            by_row,
        ]
        + [ANYWHERE] * len(extra),
        out_shape=[
            jax.ShapeDtypeStruct((proj, images * PATCHES), BF),
            jax.ShapeDtypeStruct((width, images * 2 * PATCHES), BF),
            jax.ShapeDtypeStruct((images, 2 * heads, PATCHES), F32),
            jax.ShapeDtypeStruct((images * rows, width), F32),
            jax.ShapeDtypeStruct((images * rows, width), BF),
            jax.ShapeDtypeStruct((images * rows, width), BF),
        ]
        + extra_shapes,
        scratch_shapes=[
            pltpu.VMEM((proj_others, PATCHES), F32),
            pltpu.VMEM((others * HEAD_DIM, PATCHES), F32),
            pltpu.VMEM((others * HEAD_DIM, PATCHES), F32),
            pltpu.VMEM((2 * others, PATCHES), F32),
            pltpu.VMEM((proj_others, width), BF),
            pltpu.VMEM((width, width), BF),
            pltpu.SemaphoreType.DMA((2, most)),
            pltpu.SemaphoreType.DMA((2,)),
        ],
        compiler_params=compiler_params,
        cost_estimate=cost(images * 2e9, images * 8e6),
    )(*own, tokens, mod, pick, bias, *weight_parts, *out_parts, *extra)


def gelu_pair(pre):
    root = math.sqrt(2.0 / math.pi)
    square = pre * pre
    bend = jnp.tanh(pre * (root + (root * 0.044715) * square))
    half = 0.5 + 0.5 * bend
    slope = half + (0.5 * pre) * (1.0 - bend * bend) * (root + (3.0 * root * 0.044715) * square)
    return pre * half, slope


def mlp_kernel(
    chunk, fresh, fetch, second_ref, dmlp_ref, up_ref, down_ref, *refs
):
    if fetch:
        near_ref, send_up, send_down = refs[:3]
        *refs, moves, fetch_sems = refs[3:]
        up_all, down_all = refs[3:5]
        refs = refs[:3] + refs[5:]
    if fresh:
        branch_ref, dsecond_ref, grads_ref, second_t, dmlp_t, hidden_s, dpre_s, sem = refs
    else:
        branch_in, dsecond_in, branch_ref, dsecond_ref, grads_ref = refs[:5]
        second_t, dmlp_t, hidden_s, dpre_s, sem = refs[5:]
    rows = second_ref.shape[0]
    tile = up_ref.shape[1]
    width = second_ref.shape[1]

    if fetch:
        up_half, down_half = up_all.shape[0] // 2, down_all.shape[0] // 2
        cut, quarter = near_ref.shape[0], down_half // 2
        place = lax.axis_index("dp")
        side = place_bit(place, 2)
        up_a = up_all.at[core_rows(up_half, 0, cut), :]
        up_b = up_all.at[core_rows(up_half, cut, up_half - cut), :]
        down_a = down_all.at[core_rows(down_half, 0, down_half), :]
        down_q_rows = core_rows(down_half, side * quarter, quarter)
        down_q = down_all.at[down_q_rows, :]
        lay_a = pltpu.make_async_copy(near_ref, up_a, moves.at[0])
        pass_a = core_copy(near_ref, up_a, moves, 1)
        pass_b = core_copy(up_b, up_b, moves, 3)
        pass_down = core_copy(down_a, down_a, moves, 5)
        pass_y = pltpu.make_async_remote_copy(
            src_ref=down_q,
            dst_ref=down_q,
            send_sem=moves.at[7],
            recv_sem=moves.at[8],
            device_id={"dp": place + 2 - 4 * side},
            device_id_type=pl.DeviceIdType.MESH,
        )
        fetch_b = fetch_copy(
            send_up, core_rows(up_half, cut, up_half - cut), up_b, fetch_sems, 0
        )
        fetch_down = fetch_copy(send_down, down_q_rows, down_q, fetch_sems, 2)
    step, last = pl.program_id(0), pl.num_programs(0) - 1

    @pl.when(step == 0)
    def _():
        if fetch:
            greet_peers((1, 2))
            fetch_down.start()
            lay_a.start()
            pass_a.start()
        if fresh:
            branch_ref[...] = jnp.zeros_like(branch_ref)
            dsecond_ref[...] = jnp.zeros_like(dsecond_ref)
        else:
            one = pltpu.make_async_copy(branch_in, branch_ref, sem.at[0])
            two = pltpu.make_async_copy(dsecond_in, dsecond_ref, sem.at[1])
            one.start()
            two.start()
        for at in range(0, rows, chunk):
            second_t[:, at : at + chunk] = second_ref[at : at + chunk, :].T
            dmlp_t[:, at : at + chunk] = dmlp_ref[at : at + chunk, :].T
        if not fresh:
            one.wait()
            two.wait()

    def one_chunk(index, carry):
        at = pl.ds(pl.multiple_of(index * chunk, chunk), chunk)
        pre = nn(second_ref[at, :], up_ref[...])
        dhidden = nt(dmlp_ref[at, :], down_ref[...])
        value, slope = gelu_pair(pre)
        hidden = value.astype(BF)
        dpre = (dhidden * slope).astype(BF)
        hidden_s[at, :] = hidden
        dpre_s[at, :] = dpre
        branch_ref[at, :] += nn(hidden, down_ref[...])
        dsecond_ref[at, :] += nt(dpre, up_ref[...])
        if fetch:

            @pl.when(jnp.logical_and(step == jnp.minimum(1, last), index == 0))
            def _():
                fetch_down.wait_recv()
                pass_y.start()
                fetch_b.start()

        return carry

    lax.fori_loop(0, rows // chunk, one_chunk, 0)
    if fetch:

        @pl.when(step == last)
        def _():
            fetch_b.wait_recv()
            pass_b.start()
            pass_y.wait_recv()
            pass_down.start()

    part = width // 3
    for c in range(3):
        at = slice(c * part, (c + 1) * part)
        grads_ref[at, :tile] = nn(second_t[at, :], dpre_s[...]).astype(BF)
        grads_ref[at, tile:] = nn(dmlp_t[at, :], hidden_s[...]).astype(BF)

    if fetch:

        @pl.when(step == last)
        def _():
            for copy in (lay_a, pass_a, pass_b, pass_down):
                copy.wait()
            pass_y.wait_send()
            fetch_b.wait_send()
            fetch_down.wait_send()


def mlp_chunk(rows):
    for chunk in (896, 448, 64):
        if rows % chunk == 0:
            return chunk
    return rows


def mlp(second, dmlp, up, down, sums=None, fetch=None):
    rows, width = second.shape
    hidden = up.shape[1]
    tile = 768 if hidden % 768 == 0 else hidden
    fresh = sums is None
    chunk = mlp_chunk(rows)
    in_specs = [
        const_spec(second.shape),
        const_spec(second.shape),
        pl.BlockSpec((width, tile), lambda f: (0, f)),
        pl.BlockSpec((tile, width), lambda f: (f, 0)),
    ]
    operands = [second, dmlp, up, down]
    out_specs = [
        const_spec(second.shape),
        const_spec(second.shape),
        pl.BlockSpec((width, 2 * tile), lambda f: (0, f)),
    ]
    out_shape = [
        jax.ShapeDtypeStruct(second.shape, F32),
        jax.ShapeDtypeStruct(second.shape, F32),
        jax.ShapeDtypeStruct((width, 2 * hidden), BF),
    ]
    scratch = [
        pltpu.VMEM((width, rows), BF),
        pltpu.VMEM((width, rows), BF),
        pltpu.VMEM((rows, tile), BF),
        pltpu.VMEM((rows, tile), BF),
        pltpu.SemaphoreType.DMA((2,)),
    ]
    compiler_params = params()
    if not fresh:
        in_specs += [ANYWHERE] * 2
        operands += list(sums)
    if fetch is not None:
        in_specs += [ANYWHERE] * 3
        operands += list(fetch)
        out_specs += [ANYWHERE] * 2
        out_shape += [jax.ShapeDtypeStruct(up.shape, BF), jax.ShapeDtypeStruct(down.shape, BF)]
        scratch += [pltpu.SemaphoreType.DMA((9,)), pltpu.SemaphoreType.DMA((4,))]
        compiler_params = pltpu.CompilerParams(
            vmem_limit_bytes=VMEM_LIMIT, dimension_semantics=("arbitrary",),
            collective_id=3, has_side_effects=True,
        )
    return pl.pallas_call(
        functools.partial(mlp_kernel, chunk, fresh, fetch is not None),
        grid=(hidden // tile,),
        in_specs=in_specs,
        out_specs=out_specs,
        out_shape=out_shape,
        scratch_shapes=scratch,
        compiler_params=compiler_params,
        cost_estimate=cost(6e10, 6e7) if fresh else cost(1e7, 1e5),
    )(*operands), tile


def split_mlp_grads(grads, tile):
    parts = grads.reshape(grads.shape[0], -1, 2, tile)
    return (
        parts[:, :, 0].reshape(grads.shape[0], -1),
        parts[:, :, 1].reshape(grads.shape[0], -1),
    )


def backward_kernel(per_block, weight_layout, out_layout, *refs):
    count = len(weight_layout) + len(out_layout)
    weight_parts = refs[: len(weight_layout)]
    out_parts = refs[len(weight_layout) : count]
    weight_ref, out_w_ref, sems = refs[-3:]

    @pl.when(pl.program_id(0) == 0)
    def _():
        run_copies(
            part_copies(weight_layout, weight_parts, weight_ref, sems.at[0])
            + part_copies(out_layout, out_parts, out_w_ref, sems.at[1])
        )

    backward_body(per_block, weight_ref, out_w_ref, *refs[count:-3])


def backward_body(
    per_block, weight_ref, out_w_ref, tok_ref, mod_ref, pick_ref, bias_ref,
    qkv_ref, lse_ref, middle_ref, branch_ref, mlp_ref, dsecond_ref, grad_ref,
    out_full_ref, out_kept_ref, dtok_ref, dmod_ref, dattn_ref, dqkv_ref, strips_ref,
    qkv_s, datt_s, dattk_s, dscores_s,
):
    heads = bias_ref.shape[0]
    step = pl.program_id(0)
    shift_one, scale_one, gate_one = mod_ref[0, 0:1], mod_ref[0, 1:2], mod_ref[0, 2:3]
    scale_two, gate_two = mod_ref[0, 4:5], mod_ref[0, 5:6]
    pick = pick_ref[0]
    dmiddles = []
    sums = [0.0, 0.0, 0.0, 0.0]
    for rows, out_ref in (
        (slice(0, PATCHES), out_full_ref),
        (slice(PATCHES, PATCHES + pick.shape[0]), out_kept_ref),
    ):
        middle = middle_ref[rows, :]
        branch_mlp = mlp_ref[rows, :]
        dsecond = dsecond_ref[rows, :]
        grad = grad_ref[rows, :].astype(F32)
        out_ref[...] = (middle + gate_two * branch_mlp).astype(BF)
        normed, inverse = normalize(middle)
        dmiddle = grad + norm_back(normed, inverse, dsecond * (1.0 + scale_two))
        branch = branch_ref[rows, :].astype(F32)
        for c, term in enumerate(
            (dmiddle * branch, dsecond, dsecond * normed, grad * branch_mlp)
        ):
            sums[c] = sums[c] + jnp.sum(term, axis=0, keepdims=True)
        dmiddles.append(dmiddle)
    for c in range(4):
        dmod_ref[0, 2 + c : 3 + c, :] = sums[c]
    dattn = (gate_one * dmiddles[0]).astype(BF)
    dattn_kept = tn(pick, (gate_one * dmiddles[1]).astype(BF)).astype(BF)
    dattn_ref[:PATCHES, :] = dattn
    dattn_ref[PATCHES:, :] = dattn_kept
    high = dmiddles[1].astype(BF)
    low = (dmiddles[1] - high.astype(F32)).astype(BF)
    dresid = dmiddles[0] + tn(pick, high) + tn(pick, low)
    datt_s[...] = nt(out_w_ref[...], dattn)
    dattk_s[...] = nt(out_w_ref[...], dattn_kept)
    qkv_s[...] = qkv_ref[...].astype(F32)
    mask = key_mask(pick)
    scale = HEAD_DIM ** (-0.5)

    @pl.when(step == 0)
    def _():
        dscores_s[...] = jnp.zeros_like(dscores_s)

    def one_head(head, carry):
        q_at, k_at, v_at = head_rows(head, per_block)
        queries = qkv_s[q_at, :].astype(BF)
        keys = qkv_s[k_at, :].astype(BF)
        values = qkv_s[v_at, :].astype(BF)
        here = pl.ds(pl.multiple_of(head * HEAD_DIM, 8), HEAD_DIM)
        scores = tn(keys, queries) * (scale * LOG2E) + bias_ref[head]

        def pull(scores, top, upstream):
            probs = jnp.exp2(scores - top)
            dprobs = tn(values, upstream)
            dvalues = nt(upstream, probs.astype(BF))
            weighted = jnp.sum(probs * dprobs, axis=0, keepdims=True)
            return probs * (dprobs - weighted), dvalues

        dscores, dvalues = pull(
            scores, lse_ref[0, pl.ds(head, 1), :], datt_s[here, :].astype(BF)
        )
        dscores_kept, dvalues_kept = pull(
            scores + mask, lse_ref[0, pl.ds(heads + head, 1), :], dattk_s[here, :].astype(BF)
        )
        dscores = dscores + dscores_kept
        dscores_s[head] += dscores
        rounded = dscores.astype(BF)
        qkv_s[q_at, :] = nn(keys, rounded) * scale
        qkv_s[k_at, :] = nt(queries, rounded) * scale
        qkv_s[v_at, :] = dvalues + dvalues_kept
        return carry

    lax.fori_loop(0, heads, one_head, 0, unroll=4)
    dqkv = qkv_s[...].astype(BF)
    dqkv_ref[...] = dqkv
    dfirst = tn(dqkv, weight_ref[...])
    normed, inverse = normalize(tok_ref[...].astype(F32))
    dmod_ref[0, 0:1, :] = jnp.sum(dfirst, axis=0, keepdims=True)
    dmod_ref[0, 1:2, :] = jnp.sum(dfirst * normed, axis=0, keepdims=True)
    dmod_ref[0, 6:8, :] = jnp.zeros((2, dfirst.shape[1]), F32)
    dtok_ref[...] = (dresid + norm_back(normed, inverse, dfirst * (1.0 + scale_one))).astype(BF)

    @pl.when(step == pl.num_programs(0) - 1)
    def _():
        def fold(head, carry):
            strip = jnp.zeros((GRID, 512), F32)
            for key_row in range(GRID):
                start = (GRID - 1 - key_row) * GRID
                block = dscores_s[head, key_row * GRID : (key_row + 1) * GRID, :]
                block = jnp.concatenate([block, jnp.zeros((GRID, 512 - PATCHES), F32)], axis=1)
                strip = strip + pltpu.roll(block, start, 1)
            strips_ref[head] = strip
            return carry

        lax.fori_loop(0, heads, fold, 0)


def backward(
    tokens, mod, pick, bias, qkv, lse, middle, branch, branch_mlp, dsecond, grads,
    weight, out_weight, per_block,
):
    (weight_layout, weight_parts), (out_layout, out_parts) = weight, out_weight
    most = max(len(weight_parts), len(out_parts))
    proj = whole_rows(*weight)
    images, padded = pick.shape[0], pick.shape[1]
    width = tokens.shape[1]
    rows = PATCHES + padded
    heads = bias.shape[0]
    by_row = pl.BlockSpec((rows, width), lambda i: (i, 0))
    return pl.pallas_call(
        functools.partial(backward_kernel, per_block, weight_layout, out_layout),
        grid=(images,),
        in_specs=[ANYWHERE] * (len(weight_parts) + len(out_parts))
        + [
            pl.BlockSpec((PATCHES, width), lambda i: (i, 0)),
            pl.BlockSpec((1, 8, width), lambda i: (i, 0, 0)),
            pl.BlockSpec((1, padded, PATCHES), lambda i: (i, 0, 0)),
            const_spec(bias.shape),
            pl.BlockSpec((proj, PATCHES), lambda i: (0, i)),
            pl.BlockSpec((1, 2 * heads, PATCHES), lambda i: (i, 0, 0)),
            by_row,
            by_row,
            by_row,
            by_row,
            by_row,
        ],
        out_specs=[
            pl.BlockSpec((PATCHES, width), lambda i: (i, 0)),
            pl.BlockSpec((padded, width), lambda i: (i, 0)),
            pl.BlockSpec((PATCHES, width), lambda i: (i, 0)),
            pl.BlockSpec((1, 8, width), lambda i: (i, 0, 0)),
            pl.BlockSpec((2 * PATCHES, width), lambda i: (i, 0)),
            pl.BlockSpec((proj, PATCHES), lambda i: (0, i)),
            const_spec((heads, GRID, 512)),
        ],
        out_shape=[
            jax.ShapeDtypeStruct((images * PATCHES, width), BF),
            jax.ShapeDtypeStruct((images * padded, width), BF),
            jax.ShapeDtypeStruct((images * PATCHES, width), BF),
            jax.ShapeDtypeStruct((images, 8, width), F32),
            jax.ShapeDtypeStruct((images * 2 * PATCHES, width), BF),
            jax.ShapeDtypeStruct((proj, images * PATCHES), BF),
            jax.ShapeDtypeStruct((heads, GRID, 512), F32),
        ],
        scratch_shapes=[
            pltpu.VMEM((proj, PATCHES), F32),
            pltpu.VMEM((width, PATCHES), F32),
            pltpu.VMEM((width, PATCHES), F32),
            pltpu.VMEM((heads, PATCHES, PATCHES), F32),
            pltpu.VMEM((proj, width), BF),
            pltpu.VMEM((width, width), BF),
            pltpu.SemaphoreType.DMA((2, most)),
        ],
        compiler_params=params(),
        cost_estimate=cost(1e7, 1e5),
    )(
        *weight_parts, *out_parts, tokens, mod, pick, bias, qkv, lse, middle, branch, branch_mlp,
        dsecond, grads,
    )


SUM_PLACES = 16
HALVING = (1, 2, 8)
FINAL = 4


def place_bit(place, bit):
    return (place // bit) % 2


def unit_start(owner, share):
    index = 0
    for bit in HALVING + (FINAL,):
        index = index * 2 + place_bit(owner, bit)
    return index * share


def store_by_owner(buffer, tile, at, block, share):
    first_owner = at // share
    owners = block.shape[0] // share
    for k in range(owners):
        owner = first_owner + k
        if place_bit(owner, FINAL):
            continue
        pair = k + FINAL
        both = jnp.concatenate(
            [block[k * share : (k + 1) * share], block[pair * share : (pair + 1) * share]], axis=0
        )
        start = unit_start(owner, share)
        buffer[tile, start : start + 2 * share, :] = both.astype(BF)


class GroupSum:
    def __init__(self, own, other, lands, land_other, land_cross, sends, recvs):
        self.own, self.other, self.lands = own, other, lands
        self.land_other, self.land_cross = land_other, land_cross
        self.sends, self.recvs = sends, recvs
        self.place = lax.axis_index("dp")
        self.rows = own.shape[1]

    def partner(self, bit):
        return {"dp": self.place + bit - 2 * bit * place_bit(self.place, bit)}

    def greet(self, barrier):
        for bit in HALVING + (FINAL,):
            pl.semaphore_signal(
                barrier, inc=1, device_id=self.partner(bit), device_id_type=pl.DeviceIdType.MESH
            )

    def spans(self, stage):
        start, size = 0, self.rows
        for k, bit in enumerate(HALVING):
            size = size // 2
            mine = place_bit(self.place, bit)
            if k == stage:
                return start + mine * size, start + (1 - mine) * size, size
            start = start + mine * size
        return start, start, size

    def remote(self, source, target, index, tile, peer):
        return pltpu.make_async_remote_copy(
            src_ref=source,
            dst_ref=target,
            send_sem=self.sends.at[index, tile],
            recv_sem=self.recvs.at[index, tile],
            device_id=peer,
            device_id_type=pl.DeviceIdType.MESH,
        )

    def copy(self, stage, tile):
        bit = (HALVING + (FINAL, HALVING[0]))[stage]
        buffer, land = (self.other, self.land_other) if stage == 4 else (self.own, self.lands[stage])
        _, away, size = self.spans(0 if stage == 4 else stage)
        rows = buffer.at[tile, pl.ds(pl.multiple_of(away, 16), size), :]
        return self.remote(rows, land.at[tile], stage, tile, self.partner(bit))

    def cross_rows(self, part):
        keep, away, size = self.spans(1)
        return (keep if part else away), size

    def cross(self, part, tile):
        start, size = self.cross_rows(part)
        base = self.spans(0)[0]
        return self.remote(
            self.other.at[tile, pl.ds(pl.multiple_of(start, 16), size), :],
            self.land_cross.at[tile, pl.ds(pl.multiple_of(start - base, 16), size), :],
            5 + part,
            tile,
            {"mp": 1 - lax.axis_index("mp")},
        )

    def total(self, stage, tile):
        self.copy(stage, tile).wait_recv()
        keep, _, size = self.spans(0 if stage == 4 else stage)
        at = pl.ds(pl.multiple_of(keep, 16), size)
        buffer, land = (self.other, self.land_other) if stage == 4 else (self.own, self.lands[stage])
        return buffer, at, buffer[tile, at, :].astype(F32) + land[tile].astype(F32)

    def add(self, stage, tile):
        buffer, at, total = self.total(stage, tile)
        buffer[tile, at, :] = total.astype(BF)

    def add_cross(self, part, tile):
        self.cross(part, tile).wait_recv()
        start, size = self.cross_rows(part)
        base = self.spans(0)[0]
        at = pl.ds(pl.multiple_of(start, 16), size)
        landed = pl.ds(pl.multiple_of(start - base, 16), size)
        total = self.own[tile, at, :].astype(F32) + self.land_cross[tile, landed, :].astype(F32)
        self.own[tile, at, :] = total.astype(BF)

    def wait_sends(self, tile):
        for stage in range(5):
            self.copy(stage, tile).wait_send()
        for part in range(2):
            self.cross(part, tile).wait_send()


def pack_slot(place):
    return sum(
        place_bit(place, SUM_PLACES >> (k + 1)) << k for k in range(SUM_PLACES.bit_length() - 1)
    )


class PackGather:
    def __init__(self, own, other, packs, sends, recvs):
        self.own, self.other, self.packs, self.sends, self.recvs = own, other, packs, sends, recvs
        self.place, self.side = lax.axis_index("dp"), lax.axis_index("mp")
        self.stages = SUM_PLACES.bit_length() - 1
        self.slot = pack_slot(self.place)

    def greet(self, barrier):
        pl.semaphore_signal(
            barrier, inc=1, device_id={"mp": 1 - self.side}, device_id_type=pl.DeviceIdType.MESH
        )

    def cross(self):
        return pltpu.make_async_remote_copy(
            src_ref=self.other,
            dst_ref=self.packs.at[self.slot, self.side],
            send_sem=self.sends.at[self.stages],
            recv_sem=self.recvs.at[self.stages],
            device_id={"mp": 1 - self.side},
            device_id_type=pl.DeviceIdType.MESH,
        )

    def copy(self, stage):
        size = 1 << stage
        bit = SUM_PLACES >> (stage + 1)
        rows = self.packs.at[pl.ds((self.slot // size) * size, size)]
        return pltpu.make_async_remote_copy(
            src_ref=rows,
            dst_ref=rows,
            send_sem=self.sends.at[stage],
            recv_sem=self.recvs.at[stage],
            device_id={"dp": self.place + bit - 2 * bit * place_bit(self.place, bit)},
            device_id_type=pl.DeviceIdType.MESH,
        )

    def start(self):
        self.packs[self.slot, self.side] = self.own[...]
        self.cross().start()

    def advance(self, stage):
        (self.cross() if stage == 0 else self.copy(stage - 1)).wait_recv()
        self.copy(stage).start()

    def finish(self):
        self.copy(self.stages - 1).wait_recv()
        self.cross().wait_send()
        for stage in range(self.stages):
            self.copy(stage).wait_send()


def attn_grads_kernel(
    first_ref, dattn_ref, dqkv_ref, att_ref, pack_own_ref, pack_other_ref, sums_ref, every_ref,
    first_t, dattn_t, own, other, land0, land1, land2, land3, land_other, land_cross,
    sends, recvs, packs, pack_sends, pack_recvs,
):
    width = first_t.shape[0]
    tiles, _, columns = own.shape
    share = width // SUM_PLACES
    group = GroupSum(own, other, (land0, land1, land2, land3), land_other, land_cross, sends, recvs)
    ring = PackGather(pack_own_ref, pack_other_ref, packs, pack_sends, pack_recvs)
    barrier = pltpu.get_barrier_semaphore()
    group.greet(barrier)
    ring.greet(barrier)
    pl.semaphore_wait(barrier, len(HALVING) + 2)
    ring.start()

    def turn(source, target):
        for at in range(0, source.shape[0], 512):
            target[:, at : at + 512] = source[at : at + 512, :].T

    turn(first_ref, first_t)
    half = width // 2

    def produce(s, left, right_ref, row):
        for buffer, offset, stage in ((other, right_ref.shape[0] // 2, 4), (own, 0, 0)):
            right = right_ref[pl.ds(pl.multiple_of(row + offset, 16), columns), :]
            for at in (0, half):
                store_by_owner(buffer, s, at, nt(left[at : at + half, :], right), share)
            group.copy(stage, s).start()

    def step(s, carry):
        @pl.when(s < tiles - 1)
        def _():
            produce(s, first_t, dqkv_ref, s * columns)

        @pl.when(s == tiles - 1)
        def _():
            produce(s, dattn_t, att_ref, 0)

        @pl.when(s < tiles)
        def _():
            group.add(4, s)
            group.cross(0, s).start()
            group.cross(1, s).start()

        @pl.when(s == 0)
        def _():
            turn(dattn_ref, dattn_t)

        for stage in range(ring.stages):

            @pl.when(s == 1 + stage)
            def _():
                ring.advance(stage)

        @pl.when(jnp.logical_and(s >= 1, s - 1 < tiles))
        def _():
            group.add(0, s - 1)
            group.add_cross(0, s - 1)
            group.copy(1, s - 1).start()
            group.add_cross(1, s - 1)

        for stage in (1, 2):
            tile = s - 1 - stage

            @pl.when(jnp.logical_and(tile >= 0, tile < tiles))
            def _():
                group.add(stage, tile)
                group.copy(stage + 1, tile).start()

        tile = s - 4

        @pl.when(tile >= 0)
        def _():
            sums_ref[tile] = group.total(3, tile)[2].astype(BF)

        return carry

    lax.fori_loop(0, tiles + 4, step, 0)
    ring.finish()
    every_ref[...] = packs[...]

    def finish(tile, carry):
        group.wait_sends(tile)
        return carry

    lax.fori_loop(0, tiles, finish, 0)


def can_sum_here(width, proj, inner):
    places = lax.axis_size("dp")
    return (
        places == SUM_PLACES
        and lax.axis_size("mp") == 2
        and width % (8 * places) == 0
        and proj == 3 * inner
        and inner % 32 == 0
    )


def attn_grads(first, dattn, dqkv, att, pack_own, pack_other):
    width = first.shape[1]
    tiles, tile = 4, att.shape[0] // 2
    share = width // SUM_PLACES
    vmem = pl.BlockSpec(memory_space=pltpu.VMEM)
    sums, every = pl.pallas_call(
        attn_grads_kernel,
        in_specs=[vmem] * 6,
        out_specs=[vmem] * 2,
        out_shape=[
            jax.ShapeDtypeStruct((tiles, 2 * share, tile), BF),
            jax.ShapeDtypeStruct((SUM_PLACES, 2) + pack_own.shape, BF),
        ],
        scratch_shapes=[
            pltpu.VMEM((width, first.shape[0]), BF),
            pltpu.VMEM((width, dattn.shape[0]), BF),
            pltpu.VMEM((tiles, width, tile), BF),
            pltpu.VMEM((tiles, width, tile), BF),
            pltpu.VMEM((tiles, width // 2, tile), BF),
            pltpu.VMEM((tiles, width // 4, tile), BF),
            pltpu.VMEM((tiles, width // 8, tile), BF),
            pltpu.VMEM((tiles, width // 8, tile), BF),
            pltpu.VMEM((tiles, width // 2, tile), BF),
            pltpu.VMEM((tiles, width // 2, tile), BF),
            pltpu.SemaphoreType.DMA((7, tiles)),
            pltpu.SemaphoreType.DMA((7, tiles)),
            pltpu.VMEM((SUM_PLACES, 2) + pack_own.shape, BF),
            pltpu.SemaphoreType.DMA((SUM_PLACES.bit_length(),)),
            pltpu.SemaphoreType.DMA((SUM_PLACES.bit_length(),)),
        ],
        compiler_params=pltpu.CompilerParams(
            vmem_limit_bytes=VMEM_LIMIT, collective_id=1, has_side_effects=True
        ),
        cost_estimate=cost(1e7, 1e5),
    )(first, dattn, dqkv, att, pack_own, pack_other)
    here = place_bit(lax.axis_index("dp"), FINAL) * share
    mine = lax.dynamic_slice_in_dim(sums, here, share, 1)
    return jnp.transpose(mine, (1, 0, 2)).reshape(share, -1), every


def shift_mp(value, steps):
    ways = lax.axis_size("mp")
    return lax.ppermute(value, "mp", [(i, (i - steps) % ways) for i in range(ways)])


def near_halves(block):
    half = block.shape[0] // 2
    core = lax.axis_index("dp") % 2
    mine = lax.dynamic_slice_in_dim(block, core * half, half, 0)
    return [shift_mp(mine, steps) for steps in range(1, lax.axis_size("mp"))]


def with_far_halves(nears):
    places = lax.axis_size("dp")
    core = lax.axis_index("dp") % 2
    got = []
    for near in nears:
        half = near.shape[0]
        far = lax.ppermute(near, "dp", [(i, i ^ 1) for i in range(places)])
        whole = jnp.zeros((2 * half,) + near.shape[1:], near.dtype)
        whole = lax.dynamic_update_slice_in_dim(whole, near, core * half, 0)
        got.append(lax.dynamic_update_slice_in_dim(whole, far, (1 - core) * half, 0))
    return got


def gathered_parts(nears, own=None):
    half = nears[0].shape[0]
    layout, parts, base = [], [], 0
    if own is not None:
        layout, parts, base = [(0, 0, True)], [own], own.shape[0]
    if half % 16:
        return [(0, 0, True)], [jnp.concatenate(parts + with_far_halves(nears), axis=0)]
    places = lax.axis_size("dp")
    for near in nears:
        far = lax.ppermute(near, "dp", [(i, i ^ 1) for i in range(places)])
        layout += [(base, half, True), (base, half, False)]
        parts += [near, far]
        base += 2 * half
    return layout, parts


def after_own(gathered, own):
    layout, parts = gathered
    return [(0, 0, True)] + [(base + own.shape[0], half, near) for base, half, near in layout], [
        own
    ] + parts


def home(parts):
    total = parts[0].astype(F32)
    for steps in range(1, len(parts)):
        total = total + shift_mp(parts[steps], -steps).astype(F32)
    return total


def scatter_dp(part):
    return lax.psum_scatter(part, "dp", scatter_dimension=0, tiled=True)


def local(
    tokens, conditioning, kept_ids, ada_weight, ada_bias, attn_qkv, attn_out, mlp_up, mlp_down,
    rel_table, grad_out_kept, grad_out_full,
):
    ways = lax.axis_size("mp")
    place = lax.axis_index("mp")
    images_group = conditioning.shape[0]
    images = images_group // ways
    width = tokens.shape[1]
    keep = kept_ids.shape[1]
    padded = -(-keep // 64) * 64
    per_block = rel_table.shape[0]
    cols = ada_bias.shape[0]

    silu_cond = jax.nn.silu(conditioning.astype(F32)).astype(BF)
    columns = (jnp.dot(silu_cond, ada_weight, preferred_element_type=F32) + ada_bias).astype(BF)
    mod = lax.all_to_all(columns, "mp", split_axis=0, concat_axis=1, tiled=True)
    mod = jnp.pad(mod.astype(F32).reshape(images, 6, width), ((0, 0), (0, 2), (0, 0)))

    weight_own = jnp.transpose(attn_qkv.reshape(width, -1))
    tables = [rel_table] + [shift_mp(rel_table, s) for s in range(1, ways)]
    near_o = near_halves(attn_out)
    mod, tables, weight_sent = lax.optimization_barrier((mod, tables, weight_own))
    near_w = near_halves(weight_sent)
    fetch = ways == 2 and lax.axis_size("dp") % 4 == 0 and mlp_up.shape[0] % 32 == 0
    fetch = fetch and mlp_down.shape[0] % 64 == 0
    bias = bias_whole(jnp.concatenate(tables, axis=0))

    own_kept = lax.dynamic_slice_in_dim(kept_ids, place * images, images, 0)
    own_kept = jnp.pad(own_kept, ((0, 0), (0, padded - keep)), constant_values=-1)
    pick = (own_kept[:, :, None] == jnp.arange(PATCHES, dtype=jnp.int32)).astype(BF)
    grads = jnp.concatenate(
        [
            grad_out_full.reshape(images, PATCHES, width),
            jnp.pad(
                grad_out_kept.reshape(images, keep, width), ((0, 0), (0, padded - keep), (0, 0))
            ),
        ],
        axis=1,
    )
    dmlp = (mod[:, 5:6] * grads.astype(F32)).astype(BF).reshape(-1, width)
    grads = grads.reshape(-1, width)

    own = own_heads(tokens, mod, pick, bias, weight_own, per_block)
    near_w, near_o, own = lax.optimization_barrier((near_w, near_o, own))
    first = own[0]
    weight_others = gathered_parts(near_w)
    weight = after_own(weight_others, weight_own)
    out_weight = gathered_parts(near_o, attn_out)
    cut = (mlp_up.shape[0] * 5 // 18) // 16 * 16
    qkv, att, lse, middle, second, branch, *near_up = forward(
        own, tokens, mod, pick, bias, weight_others, out_weight, per_block,
        mlp_up if fetch else None, cut,
    )
    (branch_mlp, dsecond, grads_own, *whole), tile_own = mlp(
        second, dmlp, mlp_up, mlp_down, None, (near_up[0], mlp_up, mlp_down) if fetch else None
    )
    if fetch:
        up_others, down_others = [whole[0]], [whole[1]]
    else:
        up_others = with_far_halves(near_halves(mlp_up))
        down_others = with_far_halves(near_halves(mlp_down))
    reduced = [scatter_dp(grads_own)]
    for up, down in zip(up_others, down_others):
        (branch_mlp, dsecond, grads_next), _ = mlp(
            second, dmlp, up, down, (branch_mlp, dsecond)
        )
        reduced.append(scatter_dp(grads_next))
    out_full, out_kept, dtok, dmod, dattn, dqkv, strips = backward(
        tokens, mod, pick, bias, qkv, lse, middle, branch, branch_mlp, dsecond, grads,
        weight, out_weight, per_block,
    )
    proj_block, out_block = weight_own.shape[0], attn_out.shape[0]
    dqkv, reduced[0] = lax.optimization_barrier((dqkv, reduced[0]))
    dtables = table_of_strips(strips)
    here = can_sum_here(width, dqkv.shape[0], att.shape[0]) and cols % width == 0
    if here:
        own_cond_rows = lax.dynamic_slice_in_dim(silu_cond, place * images, images, 0)
        pieces = cols // width
        packs = []
        for steps in range(ways):
            at = (place + steps) % ways
            table = dtables[steps * per_block : (steps + 1) * per_block]
            pack = jnp.concatenate(
                [
                    lax.dynamic_slice_in_dim(dmod, at * pieces, pieces, 1)
                    .astype(BF)
                    .reshape(-1, width),
                    own_cond_rows,
                    jnp.pad(table, ((0, 0), (0, width - BUCKETS))).astype(BF),
                ],
                axis=0,
            )
            packs.append(jnp.pad(pack, ((0, -pack.shape[0] % 16), (0, 0))))
        attn_total, every = attn_grads(first, dattn, dqkv, att, *packs)
        places, first_cond = every.shape[0], images * pieces
        every = every.reshape((places * ways,) + every.shape[2:]).astype(F32)
        all_columns = every[:, :first_cond].reshape(-1, cols)
        all_cond = every[:, first_cond : first_cond + images].reshape(-1, width)
        dtable = jnp.sum(every[:, first_cond + images :], axis=0)[:per_block, :BUCKETS]
        dcolumns = lax.dynamic_slice_in_dim(
            all_columns, pack_slot(lax.axis_index("dp")) * images_group, images_group, 0
        )
    else:
        dweight = dot(first, dqkv, (0, 1)).astype(BF)
        dout_t = dot(dattn, att, (0, 1)).astype(BF)
        attn_sums = scatter_dp(jnp.concatenate([dweight, dout_t], axis=1))
        dmod_rows = dmod[:, :6].reshape(images, 6 * width)
        dcolumns = lax.all_to_all(dmod_rows, "mp", split_axis=1, concat_axis=0, tiled=True)
        dtable = home(list(jnp.split(dtables, ways, axis=0)))
        all_columns = lax.all_gather(dcolumns, "dp", axis=0, tiled=True)
        dtable = lax.psum(dtable, "dp")
        all_cond = lax.all_gather(silu_cond, "dp", axis=0, tiled=True).astype(F32)
        split = ways * proj_block
        attn_total = home(
            [
                jnp.concatenate(
                    [
                        attn_sums[:, j * proj_block : (j + 1) * proj_block],
                        attn_sums[:, split + j * out_block : split + (j + 1) * out_block],
                    ],
                    axis=1,
                )
                for j in range(ways)
            ]
        )
    mlp_grads = home(reduced)
    attn_total = attn_total.astype(F32)
    grad_up, grad_down_t = split_mlp_grads(mlp_grads, tile_own)
    grad_qkv = attn_total[:, :proj_block].reshape(-1, 3, proj_block // 3)
    grad_out = jnp.transpose(attn_total[:, proj_block:])

    slice_width = width // lax.axis_size("dp")
    cond_slice = lax.dynamic_slice_in_dim(
        all_cond, lax.axis_index("dp") * slice_width, slice_width, 1
    )
    grad_ada_weight = lax.dot_general(
        cond_slice, all_columns, (((0,), (0,)), ((), ())), precision=PRECISE
    )
    grad_ada_bias = jnp.sum(all_columns, axis=0)
    dcolumns_high = dcolumns.astype(BF)
    dcolumns_low = (dcolumns - dcolumns_high.astype(F32)).astype(BF)
    silu_part = nt(jnp.concatenate([dcolumns_high, dcolumns_low], axis=0), ada_weight)
    silu_part = silu_part[:images_group] + silu_part[images_group:]
    shares = lax.all_to_all(
        silu_part.astype(BF).reshape(ways, images, width), "mp", split_axis=0, concat_axis=0,
        tiled=True,
    )
    grad_silu = jnp.sum(shares.astype(F32), axis=0)
    own_cond = lax.dynamic_slice_in_dim(conditioning, place * images, images, 0).astype(F32)
    grad_cond = jax.vjp(jax.nn.silu, own_cond)[1](grad_silu)[0].astype(BF)

    out_kept = out_kept.reshape(images, padded, width)[:, :keep].reshape(-1, width)
    return (
        out_kept, out_full, dtok, grad_cond, grad_ada_weight, grad_ada_bias, grad_qkv, grad_out,
        grad_up, jnp.transpose(grad_down_t), dtable,
    )


def solution(mesh):
    both = P(("dp", "mp"), None)
    return jax.shard_map(
        local,
        mesh=mesh,
        in_specs=(
            both, P("dp", None), P("dp", None), P(None, "mp"), P("mp"), P(None, None, "mp"),
            P("mp", None), P(None, "mp"), P("mp", None), P("mp", None), both, both,
        ),
        out_specs=(
            both, both, both, both, P("dp", "mp"), P("mp"), P("dp", None, "mp"), P("mp", "dp"),
            P("dp", "mp"), P("mp", "dp"), P("mp", None),
        ),
        check_vma=False,
    )
```

```python
import functools
import math

import jax
import jax.numpy as jnp
from jax import lax
from jax.experimental import pallas as pl
from jax.experimental.pallas import tpu as pltpu
from jax.sharding import PartitionSpec as P

HEAD_DIM = 72
GRID = 16
PATCHES = 256
BUCKETS = 961
SPAN = 2 * GRID - 1
EPSILON = 1e-06
PRECISE = lax.Precision.HIGHEST
BF = jnp.bfloat16
F32 = jnp.float32
LOG2E = math.log2(math.e)
VMEM_LIMIT = 60 * 1024 * 1024


def dot(a, b, dims):
    return lax.dot_general(a, b, ((dims[0:1], dims[1:2]), ((), ())), preferred_element_type=F32)


def nn(a, b):
    return dot(a, b, (1, 0))


def nt(a, b):
    return dot(a, b, (1, 1))


def tn(a, b):
    return dot(a, b, (0, 0))


def normalize(rows):
    centered = rows - jnp.mean(rows, axis=-1, keepdims=True)
    inverse = lax.rsqrt(jnp.mean(centered * centered, axis=-1, keepdims=True) + EPSILON)
    return centered * inverse, inverse


def norm_back(normed, inverse, upstream):
    return inverse * (
        upstream
        - jnp.mean(upstream, axis=-1, keepdims=True)
        - normed * jnp.mean(upstream * normed, axis=-1, keepdims=True)
    )


def params(n_grid=1):
    return pltpu.CompilerParams(
        vmem_limit_bytes=VMEM_LIMIT, dimension_semantics=("arbitrary",) * n_grid
    )


def cost(flops, bytes_accessed, transcendentals=0):
    return pl.CostEstimate(
        flops=int(flops), bytes_accessed=int(bytes_accessed), transcendentals=int(transcendentals)
    )


def const_spec(shape):
    return pl.BlockSpec(shape, lambda *_: (0,) * len(shape), pipeline_mode=pl.Buffered(1))


def bias_kernel(strip_ref, bias_ref):
    strip = strip_ref[0]
    for key_row in range(GRID):
        start = (GRID - 1 - key_row) * GRID
        bias_ref[0, key_row * GRID : (key_row + 1) * GRID, :] = strip[:, start : start + PATCHES]


def bias_whole(table):
    heads = table.shape[0]
    grid_table = table.reshape(heads, SPAN, SPAN) * LOG2E
    strip = jnp.stack(
        [grid_table[:, :, GRID - 1 - c : 2 * GRID - 1 - c] for c in range(GRID)], axis=1
    ).reshape(heads, GRID, SPAN * GRID)
    strip = jnp.pad(strip, ((0, 0), (0, 0), (0, 512 - SPAN * GRID)))
    return pl.pallas_call(
        bias_kernel,
        grid=(heads,),
        in_specs=[pl.BlockSpec((1, GRID, 512), lambda h: (h, 0, 0))],
        out_specs=pl.BlockSpec((1, PATCHES, PATCHES), lambda h: (h, 0, 0)),
        out_shape=jax.ShapeDtypeStruct((heads, PATCHES, PATCHES), F32),
        compiler_params=params(),
        cost_estimate=cost(1e6, 1e5),
    )(strip)


def table_of_strips(strips):
    heads = strips.shape[0]
    parts = strips[:, :, : SPAN * GRID].reshape(heads, GRID, SPAN, GRID)
    total = jnp.zeros((heads, SPAN, SPAN), F32)
    for c in range(GRID):
        total = total + jnp.pad(parts[:, c], ((0, 0), (0, 0), (GRID - 1 - c, c)))
    return total.reshape(heads, BUCKETS)


def head_rows(head, per_block):
    base = (head // per_block) * (3 * per_block * HEAD_DIM) + (head % per_block) * HEAD_DIM
    step = per_block * HEAD_DIM
    return [pl.ds(pl.multiple_of(base + c * step, 8), HEAD_DIM) for c in range(3)]


def key_mask(pick):
    ones = jnp.ones((pick.shape[0], PATCHES), BF)
    return (tn(pick, ones) - 1.0) * 1e30


def part_copies(layout, parts, whole, sems):
    core = lax.axis_index("dp") % 2
    copies = []
    for index, ((base, half, near), part) in enumerate(zip(layout, parts)):
        start = base + (core if near else 1 - core) * half
        rows = pl.ds(pl.multiple_of(start, 16), part.shape[0])
        copies.append(pltpu.make_async_copy(part, whole.at[rows, :], sems.at[index]))
    return copies


def run_copies(copies):
    for copy in copies:
        copy.start()
    for copy in copies:
        copy.wait()


def core_rows(half, skip, count):
    start = (lax.axis_index("dp") % 2) * half + skip
    return pl.ds(pl.multiple_of(start, 16), count)


def fetch_copy(own, rows, target, sems, at):
    return pltpu.make_async_remote_copy(
        src_ref=own.at[rows, :],
        dst_ref=target,
        send_sem=sems.at[at],
        recv_sem=sems.at[at + 1],
        device_id={"mp": 1 - lax.axis_index("mp")},
        device_id_type=pl.DeviceIdType.MESH,
    )


def core_copy(source, target, sems, at):
    place = lax.axis_index("dp")
    return pltpu.make_async_remote_copy(
        src_ref=source,
        dst_ref=target,
        send_sem=sems.at[at],
        recv_sem=sems.at[at + 1],
        device_id={"dp": place + 1 - 2 * (place % 2)},
        device_id_type=pl.DeviceIdType.MESH,
    )


def greet_peers(bits):
    barrier = pltpu.get_barrier_semaphore()
    peers = [{"mp": 1 - lax.axis_index("mp")}]
    place = lax.axis_index("dp")
    for bit in bits:
        peers.append({"dp": place + bit - 2 * bit * place_bit(place, bit)})
    for peer in peers:
        pl.semaphore_signal(
            barrier, inc=1, device_id=peer, device_id_type=pl.DeviceIdType.MESH
        )
    pl.semaphore_wait(barrier, len(peers))


def project(weight_ref, first, qkv_s, qkv_ref, base):
    step = weight_ref.shape[0] // 3
    for c in range(3):
        part = nt(weight_ref[c * step : (c + 1) * step, :], first)
        qkv_s[c * step : (c + 1) * step, :] = part
        qkv_ref[base + c * step : base + (c + 1) * step, :] = part.astype(BF)


def attend_heads(per_block, first_head, qkv_s, bias_ref, mask, att_s, attk_s, lse_s):
    scale = HEAD_DIM ** (-0.5) * LOG2E
    heads = qkv_s.shape[0] // (3 * HEAD_DIM)

    def one_head(head, carry):
        q_at, k_at, v_at = head_rows(head, per_block)
        queries = qkv_s[q_at, :].astype(BF)
        keys = qkv_s[k_at, :].astype(BF)
        values = qkv_s[v_at, :].astype(BF)
        scores = tn(keys, queries) * scale + bias_ref[first_head + head]
        here = pl.ds(pl.multiple_of(head * HEAD_DIM, 8), HEAD_DIM)

        def attend(scores):
            top = jnp.max(scores, axis=0, keepdims=True)
            weights = jnp.exp2(scores - top)
            total = jnp.sum(weights, axis=0, keepdims=True)
            probs = (weights * (1.0 / total)).astype(BF)
            return nn(values, probs), top + jnp.log2(total)

        att_s[here, :], lse_s[pl.ds(head, 1), :] = attend(scores)
        attk_s[here, :], lse_s[pl.ds(heads + head, 1), :] = attend(scores + mask)
        return carry

    lax.fori_loop(0, heads, one_head, 0, unroll=4 if heads % 4 == 0 else 2)


def own_heads_kernel(
    per_block, tok_ref, mod_ref, pick_ref, bias_ref, weight_ref,
    first_ref, qkv_ref, att_ref, lse_ref, qkv_s, att_s, attk_s, lse_s,
):
    shift_one, scale_one = mod_ref[0, 0:1], mod_ref[0, 1:2]
    normed, _ = normalize(tok_ref[...].astype(F32))
    first = (normed * (1.0 + scale_one) + shift_one).astype(BF)
    first_ref[...] = first
    project(weight_ref, first, qkv_s, qkv_ref, 0)
    mask = key_mask(pick_ref[0])
    attend_heads(per_block, 0, qkv_s, bias_ref, mask, att_s, attk_s, lse_s)
    att_ref[:, :PATCHES] = att_s[...].astype(BF)
    att_ref[:, PATCHES:] = attk_s[...].astype(BF)
    lse_ref[0] = lse_s[...]


def own_heads(tokens, mod, pick, bias, weight, per_block):
    images, padded = pick.shape[0], pick.shape[1]
    width = tokens.shape[1]
    proj = weight.shape[0]
    heads = proj // (3 * HEAD_DIM)
    inner = heads * HEAD_DIM
    return pl.pallas_call(
        functools.partial(own_heads_kernel, per_block),
        grid=(images,),
        in_specs=[
            pl.BlockSpec((PATCHES, width), lambda i: (i, 0)),
            pl.BlockSpec((1, 8, width), lambda i: (i, 0, 0)),
            pl.BlockSpec((1, padded, PATCHES), lambda i: (i, 0, 0)),
            const_spec(bias.shape),
            const_spec(weight.shape),
        ],
        out_specs=[
            pl.BlockSpec((PATCHES, width), lambda i: (i, 0)),
            pl.BlockSpec((proj, PATCHES), lambda i: (0, i)),
            pl.BlockSpec((inner, 2 * PATCHES), lambda i: (0, i)),
            pl.BlockSpec((1, 2 * heads, PATCHES), lambda i: (i, 0, 0)),
        ],
        out_shape=[
            jax.ShapeDtypeStruct((images * PATCHES, width), BF),
            jax.ShapeDtypeStruct((proj, images * PATCHES), BF),
            jax.ShapeDtypeStruct((inner, images * 2 * PATCHES), BF),
            jax.ShapeDtypeStruct((images, 2 * heads, PATCHES), F32),
        ],
        scratch_shapes=[
            pltpu.VMEM((proj, PATCHES), F32),
            pltpu.VMEM((inner, PATCHES), F32),
            pltpu.VMEM((inner, PATCHES), F32),
            pltpu.VMEM((2 * heads, PATCHES), F32),
        ],
        compiler_params=params(),
        cost_estimate=cost(1e7, 1e5),
    )(tokens, mod, pick, bias, weight)


def forward_kernel(per_block, weight_layout, out_layout, fetch, *refs):
    first_ref, own_qkv, own_att, own_lse, tok_ref, mod_ref, pick_ref, bias_ref = refs[:8]
    refs = refs[8:]
    weight_parts, refs = refs[: len(weight_layout)], refs[len(weight_layout) :]
    out_parts, refs = refs[: len(out_layout)], refs[len(out_layout) :]
    if fetch:
        send_ref, refs = refs[0], refs[1:]
    qkv_ref, att_ref, lse_ref, middle_ref, second_ref, branch_ref = refs[:6]
    refs = refs[6:]
    if fetch:
        got_ref, refs = refs[0], refs[1:]
    qkv_s, att_s, attk_s, lse_s, weight_ref, out_w_ref, part_sems, fetch_sems = refs

    def fetching():
        half = send_ref.shape[0] // 2
        return fetch_copy(send_ref, core_rows(half, 0, got_ref.shape[0]), got_ref, fetch_sems, 0)

    @pl.when(pl.program_id(0) == 0)
    def _():
        copies = part_copies(weight_layout, weight_parts, weight_ref, part_sems.at[0])
        copies += part_copies(out_layout, out_parts, out_w_ref, part_sems.at[1])
        if fetch:
            greet_peers(())
            fetching().start()
        run_copies(copies)

    own = own_qkv.shape[0]
    own_inner = own // 3
    own_count = own_inner // HEAD_DIM
    heads = bias_ref.shape[0]
    others = heads - own_count
    pick = pick_ref[0]
    qkv_ref[:own, :] = own_qkv[...]
    project(weight_ref, first_ref[...], qkv_s, qkv_ref, own)
    mask = key_mask(pick)
    attend_heads(per_block, own_count, qkv_s, bias_ref, mask, att_s, attk_s, lse_s)
    att_ref[:own_inner, :] = own_att[...]
    att_ref[own_inner:, :PATCHES] = att_s[...].astype(BF)
    att_ref[own_inner:, PATCHES:] = attk_s[...].astype(BF)
    lse_ref[0, :own_count, :] = own_lse[0, :own_count]
    lse_ref[0, own_count:heads, :] = lse_s[:others]
    lse_ref[0, heads : heads + own_count, :] = own_lse[0, own_count:]
    lse_ref[0, heads + own_count :, :] = lse_s[others:]
    gate_one = mod_ref[0, 2:3]
    shift_two, scale_two = mod_ref[0, 3:4], mod_ref[0, 4:5]
    out_w = out_w_ref[...]
    kept_att = nt(pick, att_ref[:, PATCHES:]).astype(BF)
    for rows, source, residual in (
        (slice(0, PATCHES), att_ref[:, :PATCHES].T, tok_ref[...].astype(F32)),
        (slice(PATCHES, PATCHES + pick.shape[0]), kept_att, nn(pick, tok_ref[...])),
    ):
        branch = nn(source, out_w)
        branch_ref[rows, :] = branch.astype(BF)
        middle = residual + gate_one * branch
        middle_ref[rows, :] = middle
        second_ref[rows, :] = (normalize(middle)[0] * (1.0 + scale_two) + shift_two).astype(BF)
    if fetch:

        @pl.when(pl.program_id(0) == pl.num_programs(0) - 1)
        def _():
            fetching().wait()


def whole_rows(layout, parts):
    return sum(part.shape[0] for part in parts)


ANYWHERE = pl.BlockSpec(memory_space=pl.ANY)


def forward(own, tokens, mod, pick, bias, weight, out_weight, per_block, send=None, count=0):
    images, padded = pick.shape[0], pick.shape[1]
    width = tokens.shape[1]
    rows = PATCHES + padded
    heads = bias.shape[0]
    (weight_layout, weight_parts), (out_layout, out_parts) = weight, out_weight
    proj_others = whole_rows(*weight)
    proj = own[1].shape[0] + proj_others
    own_inner, own_heads_count = own[2].shape[0], own[3].shape[1] // 2
    others = heads - own_heads_count
    fetch = send is not None
    most = max(len(weight_parts), len(out_parts))
    extra_shapes, extra = [], []
    compiler_params = params()
    if fetch:
        extra_shapes = [jax.ShapeDtypeStruct((count, send.shape[1]), BF)]
        extra = [send]
        compiler_params = pltpu.CompilerParams(
            vmem_limit_bytes=VMEM_LIMIT, dimension_semantics=("arbitrary",),
            collective_id=2, has_side_effects=True,
        )
    by_row = pl.BlockSpec((rows, width), lambda i: (i, 0))
    return pl.pallas_call(
        functools.partial(forward_kernel, per_block, weight_layout, out_layout, fetch),
        grid=(images,),
        in_specs=[
            pl.BlockSpec((PATCHES, width), lambda i: (i, 0)),
            pl.BlockSpec((own[1].shape[0], PATCHES), lambda i: (0, i)),
            pl.BlockSpec((own_inner, 2 * PATCHES), lambda i: (0, i)),
            pl.BlockSpec((1, 2 * own_heads_count, PATCHES), lambda i: (i, 0, 0)),
            pl.BlockSpec((PATCHES, width), lambda i: (i, 0)),
            pl.BlockSpec((1, 8, width), lambda i: (i, 0, 0)),
            pl.BlockSpec((1, padded, PATCHES), lambda i: (i, 0, 0)),
            const_spec(bias.shape),
        ]
        + [ANYWHERE] * (len(weight_parts) + len(out_parts) + len(extra)),
        out_specs=[
            pl.BlockSpec((proj, PATCHES), lambda i: (0, i)),
            pl.BlockSpec((width, 2 * PATCHES), lambda i: (0, i)),
            pl.BlockSpec((1, 2 * heads, PATCHES), lambda i: (i, 0, 0)),
            by_row,
            by_row,
            by_row,
        ]
        + [ANYWHERE] * len(extra),
        out_shape=[
            jax.ShapeDtypeStruct((proj, images * PATCHES), BF),
            jax.ShapeDtypeStruct((width, images * 2 * PATCHES), BF),
            jax.ShapeDtypeStruct((images, 2 * heads, PATCHES), F32),
            jax.ShapeDtypeStruct((images * rows, width), F32),
            jax.ShapeDtypeStruct((images * rows, width), BF),
            jax.ShapeDtypeStruct((images * rows, width), BF),
        ]
        + extra_shapes,
        scratch_shapes=[
            pltpu.VMEM((proj_others, PATCHES), F32),
            pltpu.VMEM((others * HEAD_DIM, PATCHES), F32),
            pltpu.VMEM((others * HEAD_DIM, PATCHES), F32),
            pltpu.VMEM((2 * others, PATCHES), F32),
            pltpu.VMEM((proj_others, width), BF),
            pltpu.VMEM((width, width), BF),
            pltpu.SemaphoreType.DMA((2, most)),
            pltpu.SemaphoreType.DMA((2,)),
        ],
        compiler_params=compiler_params,
        cost_estimate=cost(images * 2e9, images * 8e6),
    )(*own, tokens, mod, pick, bias, *weight_parts, *out_parts, *extra)


def gelu_pair(pre):
    root = math.sqrt(2.0 / math.pi)
    square = pre * pre
    bend = jnp.tanh(pre * (root + (root * 0.044715) * square))
    half = 0.5 + 0.5 * bend
    slope = half + (0.5 * pre) * (1.0 - bend * bend) * (root + (3.0 * root * 0.044715) * square)
    return pre * half, slope


def mlp_kernel(
    chunk, fresh, fetch, second_ref, dmlp_ref, up_ref, down_ref, *refs
):
    if fetch:
        near_ref, send_up, send_down = refs[:3]
        *refs, moves, fetch_sems = refs[3:]
        up_all, down_all = refs[3:5]
        refs = refs[:3] + refs[5:]
    if fresh:
        branch_ref, dsecond_ref, grads_ref, second_t, dmlp_t, hidden_s, dpre_s, sem = refs
    else:
        branch_in, dsecond_in, branch_ref, dsecond_ref, grads_ref = refs[:5]
        second_t, dmlp_t, hidden_s, dpre_s, sem = refs[5:]
    rows = second_ref.shape[0]
    tile = up_ref.shape[1]
    width = second_ref.shape[1]

    if fetch:
        up_half, down_half = up_all.shape[0] // 2, down_all.shape[0] // 2
        cut, quarter = near_ref.shape[0], down_half // 2
        place = lax.axis_index("dp")
        side = place_bit(place, 2)
        up_a = up_all.at[core_rows(up_half, 0, cut), :]
        up_b = up_all.at[core_rows(up_half, cut, up_half - cut), :]
        down_a = down_all.at[core_rows(down_half, 0, down_half), :]
        down_q_rows = core_rows(down_half, side * quarter, quarter)
        down_q = down_all.at[down_q_rows, :]
        lay_a = pltpu.make_async_copy(near_ref, up_a, moves.at[0])
        pass_a = core_copy(near_ref, up_a, moves, 1)
        pass_b = core_copy(up_b, up_b, moves, 3)
        pass_down = core_copy(down_a, down_a, moves, 5)
        pass_y = pltpu.make_async_remote_copy(
            src_ref=down_q,
            dst_ref=down_q,
            send_sem=moves.at[7],
            recv_sem=moves.at[8],
            device_id={"dp": place + 2 - 4 * side},
            device_id_type=pl.DeviceIdType.MESH,
        )
        fetch_b = fetch_copy(
            send_up, core_rows(up_half, cut, up_half - cut), up_b, fetch_sems, 0
        )
        fetch_down = fetch_copy(send_down, down_q_rows, down_q, fetch_sems, 2)
    step, last = pl.program_id(0), pl.num_programs(0) - 1

    @pl.when(step == 0)
    def _():
        if fetch:
            greet_peers((1, 2))
            fetch_down.start()
            lay_a.start()
            pass_a.start()
        if fresh:
            branch_ref[...] = jnp.zeros_like(branch_ref)
            dsecond_ref[...] = jnp.zeros_like(dsecond_ref)
        else:
            one = pltpu.make_async_copy(branch_in, branch_ref, sem.at[0])
            two = pltpu.make_async_copy(dsecond_in, dsecond_ref, sem.at[1])
            one.start()
            two.start()
        for at in range(0, rows, chunk):
            second_t[:, at : at + chunk] = second_ref[at : at + chunk, :].T
            dmlp_t[:, at : at + chunk] = dmlp_ref[at : at + chunk, :].T
        if not fresh:
            one.wait()
            two.wait()

    def one_chunk(index, carry):
        at = pl.ds(pl.multiple_of(index * chunk, chunk), chunk)
        pre = nn(second_ref[at, :], up_ref[...])
        dhidden = nt(dmlp_ref[at, :], down_ref[...])
        value, slope = gelu_pair(pre)
        hidden = value.astype(BF)
        dpre = (dhidden * slope).astype(BF)
        hidden_s[at, :] = hidden
        dpre_s[at, :] = dpre
        branch_ref[at, :] += nn(hidden, down_ref[...])
        dsecond_ref[at, :] += nt(dpre, up_ref[...])
        if fetch:

            @pl.when(jnp.logical_and(step == jnp.minimum(1, last), index == 0))
            def _():
                fetch_down.wait_recv()
                pass_y.start()
                fetch_b.start()

        return carry

    lax.fori_loop(0, rows // chunk, one_chunk, 0)
    if fetch:

        @pl.when(step == last)
        def _():
            fetch_b.wait_recv()
            pass_b.start()
            pass_y.wait_recv()
            pass_down.start()

    part = width // 3
    for c in range(3):
        at = slice(c * part, (c + 1) * part)
        grads_ref[at, :tile] = nn(second_t[at, :], dpre_s[...]).astype(BF)
        grads_ref[at, tile:] = nn(dmlp_t[at, :], hidden_s[...]).astype(BF)

    if fetch:

        @pl.when(step == last)
        def _():
            for copy in (lay_a, pass_a, pass_b, pass_down):
                copy.wait()
            pass_y.wait_send()
            fetch_b.wait_send()
            fetch_down.wait_send()


def mlp_chunk(rows):
    for chunk in (896, 448, 64):
        if rows % chunk == 0:
            return chunk
    return rows


def mlp(second, dmlp, up, down, sums=None, fetch=None):
    rows, width = second.shape
    hidden = up.shape[1]
    tile = 768 if hidden % 768 == 0 else hidden
    fresh = sums is None
    chunk = mlp_chunk(rows)
    in_specs = [
        const_spec(second.shape),
        const_spec(second.shape),
        pl.BlockSpec((width, tile), lambda f: (0, f)),
        pl.BlockSpec((tile, width), lambda f: (f, 0)),
    ]
    operands = [second, dmlp, up, down]
    out_specs = [
        const_spec(second.shape),
        const_spec(second.shape),
        pl.BlockSpec((width, 2 * tile), lambda f: (0, f)),
    ]
    out_shape = [
        jax.ShapeDtypeStruct(second.shape, F32),
        jax.ShapeDtypeStruct(second.shape, F32),
        jax.ShapeDtypeStruct((width, 2 * hidden), BF),
    ]
    scratch = [
        pltpu.VMEM((width, rows), BF),
        pltpu.VMEM((width, rows), BF),
        pltpu.VMEM((rows, tile), BF),
        pltpu.VMEM((rows, tile), BF),
        pltpu.SemaphoreType.DMA((2,)),
    ]
    compiler_params = params()
    if not fresh:
        in_specs += [ANYWHERE] * 2
        operands += list(sums)
    if fetch is not None:
        in_specs += [ANYWHERE] * 3
        operands += list(fetch)
        out_specs += [ANYWHERE] * 2
        out_shape += [jax.ShapeDtypeStruct(up.shape, BF), jax.ShapeDtypeStruct(down.shape, BF)]
        scratch += [pltpu.SemaphoreType.DMA((9,)), pltpu.SemaphoreType.DMA((4,))]
        compiler_params = pltpu.CompilerParams(
            vmem_limit_bytes=VMEM_LIMIT, dimension_semantics=("arbitrary",),
            collective_id=3, has_side_effects=True,
        )
    return pl.pallas_call(
        functools.partial(mlp_kernel, chunk, fresh, fetch is not None),
        grid=(hidden // tile,),
        in_specs=in_specs,
        out_specs=out_specs,
        out_shape=out_shape,
        scratch_shapes=scratch,
        compiler_params=compiler_params,
        cost_estimate=cost(6e10, 6e7) if fresh else cost(1e7, 1e5),
    )(*operands), tile


def split_mlp_grads(grads, tile):
    parts = grads.reshape(grads.shape[0], -1, 2, tile)
    return (
        parts[:, :, 0].reshape(grads.shape[0], -1),
        parts[:, :, 1].reshape(grads.shape[0], -1),
    )


def backward_kernel(per_block, weight_layout, out_layout, *refs):
    count = len(weight_layout) + len(out_layout)
    weight_parts = refs[: len(weight_layout)]
    out_parts = refs[len(weight_layout) : count]
    weight_ref, out_w_ref, sems = refs[-3:]

    @pl.when(pl.program_id(0) == 0)
    def _():
        run_copies(
            part_copies(weight_layout, weight_parts, weight_ref, sems.at[0])
            + part_copies(out_layout, out_parts, out_w_ref, sems.at[1])
        )

    backward_body(per_block, weight_ref, out_w_ref, *refs[count:-3])


def backward_body(
    per_block, weight_ref, out_w_ref, tok_ref, mod_ref, pick_ref, bias_ref,
    qkv_ref, lse_ref, middle_ref, branch_ref, mlp_ref, dsecond_ref, grad_ref,
    out_full_ref, out_kept_ref, dtok_ref, dmod_ref, dattn_ref, dqkv_ref, strips_ref,
    qkv_s, datt_s, dattk_s, dscores_s,
):
    heads = bias_ref.shape[0]
    step = pl.program_id(0)
    shift_one, scale_one, gate_one = mod_ref[0, 0:1], mod_ref[0, 1:2], mod_ref[0, 2:3]
    scale_two, gate_two = mod_ref[0, 4:5], mod_ref[0, 5:6]
    pick = pick_ref[0]
    dmiddles = []
    sums = [0.0, 0.0, 0.0, 0.0]
    for rows, out_ref in (
        (slice(0, PATCHES), out_full_ref),
        (slice(PATCHES, PATCHES + pick.shape[0]), out_kept_ref),
    ):
        middle = middle_ref[rows, :]
        branch_mlp = mlp_ref[rows, :]
        dsecond = dsecond_ref[rows, :]
        grad = grad_ref[rows, :].astype(F32)
        out_ref[...] = (middle + gate_two * branch_mlp).astype(BF)
        normed, inverse = normalize(middle)
        dmiddle = grad + norm_back(normed, inverse, dsecond * (1.0 + scale_two))
        branch = branch_ref[rows, :].astype(F32)
        for c, term in enumerate(
            (dmiddle * branch, dsecond, dsecond * normed, grad * branch_mlp)
        ):
            sums[c] = sums[c] + jnp.sum(term, axis=0, keepdims=True)
        dmiddles.append(dmiddle)
    for c in range(4):
        dmod_ref[0, 2 + c : 3 + c, :] = sums[c]
    dattn = (gate_one * dmiddles[0]).astype(BF)
    dattn_kept = tn(pick, (gate_one * dmiddles[1]).astype(BF)).astype(BF)
    dattn_ref[:PATCHES, :] = dattn
    dattn_ref[PATCHES:, :] = dattn_kept
    high = dmiddles[1].astype(BF)
    low = (dmiddles[1] - high.astype(F32)).astype(BF)
    dresid = dmiddles[0] + tn(pick, high) + tn(pick, low)
    datt_s[...] = nt(out_w_ref[...], dattn)
    dattk_s[...] = nt(out_w_ref[...], dattn_kept)
    qkv_s[...] = qkv_ref[...].astype(F32)
    mask = key_mask(pick)
    scale = HEAD_DIM ** (-0.5)

    @pl.when(step == 0)
    def _():
        dscores_s[...] = jnp.zeros_like(dscores_s)

    def one_head(head, carry):
        q_at, k_at, v_at = head_rows(head, per_block)
        queries = qkv_s[q_at, :].astype(BF)
        keys = qkv_s[k_at, :].astype(BF)
        values = qkv_s[v_at, :].astype(BF)
        here = pl.ds(pl.multiple_of(head * HEAD_DIM, 8), HEAD_DIM)
        scores = tn(keys, queries) * (scale * LOG2E) + bias_ref[head]

        def pull(scores, top, upstream):
            probs = jnp.exp2(scores - top)
            dprobs = tn(values, upstream)
            dvalues = nt(upstream, probs.astype(BF))
            weighted = jnp.sum(probs * dprobs, axis=0, keepdims=True)
            return probs * (dprobs - weighted), dvalues

        dscores, dvalues = pull(
            scores, lse_ref[0, pl.ds(head, 1), :], datt_s[here, :].astype(BF)
        )
        dscores_kept, dvalues_kept = pull(
            scores + mask, lse_ref[0, pl.ds(heads + head, 1), :], dattk_s[here, :].astype(BF)
        )
        dscores = dscores + dscores_kept
        dscores_s[head] += dscores
        rounded = dscores.astype(BF)
        qkv_s[q_at, :] = nn(keys, rounded) * scale
        qkv_s[k_at, :] = nt(queries, rounded) * scale
        qkv_s[v_at, :] = dvalues + dvalues_kept
        return carry

    lax.fori_loop(0, heads, one_head, 0, unroll=4)
    dqkv = qkv_s[...].astype(BF)
    dqkv_ref[...] = dqkv
    dfirst = tn(dqkv, weight_ref[...])
    normed, inverse = normalize(tok_ref[...].astype(F32))
    dmod_ref[0, 0:1, :] = jnp.sum(dfirst, axis=0, keepdims=True)
    dmod_ref[0, 1:2, :] = jnp.sum(dfirst * normed, axis=0, keepdims=True)
    dmod_ref[0, 6:8, :] = jnp.zeros((2, dfirst.shape[1]), F32)
    dtok_ref[...] = (dresid + norm_back(normed, inverse, dfirst * (1.0 + scale_one))).astype(BF)

    @pl.when(step == pl.num_programs(0) - 1)
    def _():
        def fold(head, carry):
            strip = jnp.zeros((GRID, 512), F32)
            for key_row in range(GRID):
                start = (GRID - 1 - key_row) * GRID
                block = dscores_s[head, key_row * GRID : (key_row + 1) * GRID, :]
                block = jnp.concatenate([block, jnp.zeros((GRID, 512 - PATCHES), F32)], axis=1)
                strip = strip + pltpu.roll(block, start, 1)
            strips_ref[head] = strip
            return carry

        lax.fori_loop(0, heads, fold, 0)


def backward(
    tokens, mod, pick, bias, qkv, lse, middle, branch, branch_mlp, dsecond, grads,
    weight, out_weight, per_block,
):
    (weight_layout, weight_parts), (out_layout, out_parts) = weight, out_weight
    most = max(len(weight_parts), len(out_parts))
    proj = whole_rows(*weight)
    images, padded = pick.shape[0], pick.shape[1]
    width = tokens.shape[1]
    rows = PATCHES + padded
    heads = bias.shape[0]
    by_row = pl.BlockSpec((rows, width), lambda i: (i, 0))
    return pl.pallas_call(
        functools.partial(backward_kernel, per_block, weight_layout, out_layout),
        grid=(images,),
        in_specs=[ANYWHERE] * (len(weight_parts) + len(out_parts))
        + [
            pl.BlockSpec((PATCHES, width), lambda i: (i, 0)),
            pl.BlockSpec((1, 8, width), lambda i: (i, 0, 0)),
            pl.BlockSpec((1, padded, PATCHES), lambda i: (i, 0, 0)),
            const_spec(bias.shape),
            pl.BlockSpec((proj, PATCHES), lambda i: (0, i)),
            pl.BlockSpec((1, 2 * heads, PATCHES), lambda i: (i, 0, 0)),
            by_row,
            by_row,
            by_row,
            by_row,
            by_row,
        ],
        out_specs=[
            pl.BlockSpec((PATCHES, width), lambda i: (i, 0)),
            pl.BlockSpec((padded, width), lambda i: (i, 0)),
            pl.BlockSpec((PATCHES, width), lambda i: (i, 0)),
            pl.BlockSpec((1, 8, width), lambda i: (i, 0, 0)),
            pl.BlockSpec((2 * PATCHES, width), lambda i: (i, 0)),
            pl.BlockSpec((proj, PATCHES), lambda i: (0, i)),
            const_spec((heads, GRID, 512)),
        ],
        out_shape=[
            jax.ShapeDtypeStruct((images * PATCHES, width), BF),
            jax.ShapeDtypeStruct((images * padded, width), BF),
            jax.ShapeDtypeStruct((images * PATCHES, width), BF),
            jax.ShapeDtypeStruct((images, 8, width), F32),
            jax.ShapeDtypeStruct((images * 2 * PATCHES, width), BF),
            jax.ShapeDtypeStruct((proj, images * PATCHES), BF),
            jax.ShapeDtypeStruct((heads, GRID, 512), F32),
        ],
        scratch_shapes=[
            pltpu.VMEM((proj, PATCHES), F32),
            pltpu.VMEM((width, PATCHES), F32),
            pltpu.VMEM((width, PATCHES), F32),
            pltpu.VMEM((heads, PATCHES, PATCHES), F32),
            pltpu.VMEM((proj, width), BF),
            pltpu.VMEM((width, width), BF),
            pltpu.SemaphoreType.DMA((2, most)),
        ],
        compiler_params=params(),
        cost_estimate=cost(1e7, 1e5),
    )(
        *weight_parts, *out_parts, tokens, mod, pick, bias, qkv, lse, middle, branch, branch_mlp,
        dsecond, grads,
    )


SUM_PLACES = 16
HALVING = (1, 2, 8)
FINAL = 4


def place_bit(place, bit):
    return (place // bit) % 2


def unit_start(owner, share):
    index = 0
    for bit in HALVING + (FINAL,):
        index = index * 2 + place_bit(owner, bit)
    return index * share


def store_by_owner(buffer, tile, at, block, share):
    first_owner = at // share
    owners = block.shape[0] // share
    for k in range(owners):
        owner = first_owner + k
        if place_bit(owner, FINAL):
            continue
        pair = k + FINAL
        both = jnp.concatenate(
            [block[k * share : (k + 1) * share], block[pair * share : (pair + 1) * share]], axis=0
        )
        start = unit_start(owner, share)
        buffer[tile, start : start + 2 * share, :] = both.astype(BF)


class GroupSum:
    def __init__(self, own, other, lands, land_other, land_cross, sends, recvs):
        self.own, self.other, self.lands = own, other, lands
        self.land_other, self.land_cross = land_other, land_cross
        self.sends, self.recvs = sends, recvs
        self.place = lax.axis_index("dp")
        self.rows = own.shape[1]

    def partner(self, bit):
        return {"dp": self.place + bit - 2 * bit * place_bit(self.place, bit)}

    def greet(self, barrier):
        for bit in HALVING + (FINAL,):
            pl.semaphore_signal(
                barrier, inc=1, device_id=self.partner(bit), device_id_type=pl.DeviceIdType.MESH
            )

    def spans(self, stage):
        start, size = 0, self.rows
        for k, bit in enumerate(HALVING):
            size = size // 2
            mine = place_bit(self.place, bit)
            if k == stage:
                return start + mine * size, start + (1 - mine) * size, size
            start = start + mine * size
        return start, start, size

    def remote(self, source, target, index, tile, peer):
        return pltpu.make_async_remote_copy(
            src_ref=source,
            dst_ref=target,
            send_sem=self.sends.at[index, tile],
            recv_sem=self.recvs.at[index, tile],
            device_id=peer,
            device_id_type=pl.DeviceIdType.MESH,
        )

    def copy(self, stage, tile):
        bit = (HALVING + (FINAL, HALVING[0]))[stage]
        buffer, land = (self.other, self.land_other) if stage == 4 else (self.own, self.lands[stage])
        _, away, size = self.spans(0 if stage == 4 else stage)
        rows = buffer.at[tile, pl.ds(pl.multiple_of(away, 16), size), :]
        return self.remote(rows, land.at[tile], stage, tile, self.partner(bit))

    def cross_rows(self, part):
        keep, away, size = self.spans(1)
        return (keep if part else away), size

    def cross(self, part, tile):
        start, size = self.cross_rows(part)
        base = self.spans(0)[0]
        return self.remote(
            self.other.at[tile, pl.ds(pl.multiple_of(start, 16), size), :],
            self.land_cross.at[tile, pl.ds(pl.multiple_of(start - base, 16), size), :],
            5 + part,
            tile,
            {"mp": 1 - lax.axis_index("mp")},
        )

    def total(self, stage, tile):
        self.copy(stage, tile).wait_recv()
        keep, _, size = self.spans(0 if stage == 4 else stage)
        at = pl.ds(pl.multiple_of(keep, 16), size)
        buffer, land = (self.other, self.land_other) if stage == 4 else (self.own, self.lands[stage])
        return buffer, at, buffer[tile, at, :].astype(F32) + land[tile].astype(F32)

    def add(self, stage, tile):
        buffer, at, total = self.total(stage, tile)
        buffer[tile, at, :] = total.astype(BF)

    def add_cross(self, part, tile):
        self.cross(part, tile).wait_recv()
        start, size = self.cross_rows(part)
        base = self.spans(0)[0]
        at = pl.ds(pl.multiple_of(start, 16), size)
        landed = pl.ds(pl.multiple_of(start - base, 16), size)
        total = self.own[tile, at, :].astype(F32) + self.land_cross[tile, landed, :].astype(F32)
        self.own[tile, at, :] = total.astype(BF)

    def wait_sends(self, tile):
        for stage in range(5):
            self.copy(stage, tile).wait_send()
        for part in range(2):
            self.cross(part, tile).wait_send()


def pack_slot(place):
    return sum(
        place_bit(place, SUM_PLACES >> (k + 1)) << k for k in range(SUM_PLACES.bit_length() - 1)
    )


class PackGather:
    def __init__(self, own, other, packs, sends, recvs):
        self.own, self.other, self.packs, self.sends, self.recvs = own, other, packs, sends, recvs
        self.place, self.side = lax.axis_index("dp"), lax.axis_index("mp")
        self.stages = SUM_PLACES.bit_length() - 1
        self.slot = pack_slot(self.place)

    def greet(self, barrier):
        pl.semaphore_signal(
            barrier, inc=1, device_id={"mp": 1 - self.side}, device_id_type=pl.DeviceIdType.MESH
        )

    def cross(self):
        return pltpu.make_async_remote_copy(
            src_ref=self.other,
            dst_ref=self.packs.at[self.slot, self.side],
            send_sem=self.sends.at[self.stages],
            recv_sem=self.recvs.at[self.stages],
            device_id={"mp": 1 - self.side},
            device_id_type=pl.DeviceIdType.MESH,
        )

    def copy(self, stage):
        size = 1 << stage
        bit = SUM_PLACES >> (stage + 1)
        rows = self.packs.at[pl.ds((self.slot // size) * size, size)]
        return pltpu.make_async_remote_copy(
            src_ref=rows,
            dst_ref=rows,
            send_sem=self.sends.at[stage],
            recv_sem=self.recvs.at[stage],
            device_id={"dp": self.place + bit - 2 * bit * place_bit(self.place, bit)},
            device_id_type=pl.DeviceIdType.MESH,
        )

    def start(self):
        self.packs[self.slot, self.side] = self.own[...]
        self.cross().start()

    def advance(self, stage):
        (self.cross() if stage == 0 else self.copy(stage - 1)).wait_recv()
        self.copy(stage).start()

    def finish(self):
        self.copy(self.stages - 1).wait_recv()
        self.cross().wait_send()
        for stage in range(self.stages):
            self.copy(stage).wait_send()


class SmallGrads:
    def __init__(
        self, images, pieces, table_rows, ring, ada, ada_s, part_s, silu_own, silu_got, sems
    ):
        self.images, self.pieces, self.table_rows = images, pieces, table_rows
        self.ring, self.ada, self.ada_s, self.part_s = ring, ada, ada_s, part_s
        self.silu_own, self.silu_got, self.sems = silu_own, silu_got, sems
        self.rows = ring.packs.shape[2]
        self.first_cond = images * pieces

    def row_of(self, shape, axis):
        return lax.broadcasted_iota(jnp.int32, shape, axis) & (self.rows - 1)

    def any_image(self, test):
        found = test(0)
        for image in range(1, self.images):
            found = jnp.logical_or(found, test(image))
        return found

    def of_piece(self, row, piece):
        return self.any_image(lambda image: row == image * self.pieces + piece)

    def piece(self, index):
        width = self.ada_s.shape[1]
        return pltpu.make_async_copy(
            self.ada.at[:, index * width : (index + 1) * width], self.ada_s, self.sems.at[0]
        )

    def exchange(self):
        return pltpu.make_async_remote_copy(
            src_ref=self.silu_own.at[1],
            dst_ref=self.silu_got,
            send_sem=self.sems.at[1],
            recv_sem=self.sems.at[2],
            device_id={"mp": 1 - self.ring.side},
            device_id_type=pl.DeviceIdType.MESH,
        )

    def add_piece(self, index):
        mine = self.ring.packs[self.ring.slot]
        mine = mine.reshape(2 * self.rows, mine.shape[-1]).astype(F32)
        masked = jnp.where(self.of_piece(self.row_of(mine.shape, 0), index), mine, 0.0)
        self.piece(index).wait()
        product = nt(masked.astype(BF), self.ada_s[...])
        if index:
            self.part_s[...] += product
        else:
            self.part_s[...] = product
        if index + 1 < self.pieces:
            self.piece(index + 1).start()
            return
        for k, side in enumerate((self.ring.side, 1 - self.ring.side)):
            block = self.part_s[pl.ds(pl.multiple_of(side * self.rows, 8), self.rows), :]
            found = [
                jnp.sum(block[n * self.pieces : (n + 1) * self.pieces], axis=0, keepdims=True)
                for n in range(self.images)
            ]
            found.append(jnp.zeros((self.silu_got.shape[0] - self.images, block.shape[1]), F32))
            self.silu_own[k] = jnp.concatenate(found, axis=0).astype(BF)
        self.exchange().start()

    def reduce(self, ada_grad_ref, small_ref):
        group = 128 // (2 * self.rows)
        width, share = self.ada_s.shape[1], ada_grad_ref.shape[1]
        left, right = self.row_of((128, 128), 0), self.row_of((128, 128), 1)
        left_all = lax.broadcasted_iota(jnp.int32, (128, 128), 0)
        right_all = lax.broadcasted_iota(jnp.int32, (128, 128), 1)
        same = (left_all - left) == (right_all - right)
        spread = jnp.logical_and(
            same,
            self.any_image(
                lambda n: jnp.logical_and(
                    jnp.logical_and(left >= n * self.pieces, left < (n + 1) * self.pieces),
                    right == self.first_cond + n,
                )
            ),
        )
        spread = jnp.where(spread, 1.0, 0.0).astype(BF)
        line = lax.broadcasted_iota(jnp.int32, (16, 128), 0)
        at = self.row_of((16, 128), 1)
        chosen = jnp.logical_and(
            jnp.logical_and(line >= self.pieces, line < self.pieces + self.table_rows),
            at == line - self.pieces + self.first_cond + self.images,
        )
        for p in range(self.pieces):
            chosen = jnp.logical_or(chosen, jnp.logical_and(line == p, self.of_piece(at, p)))
        chosen = jnp.where(chosen, 1.0, 0.0).astype(BF)
        wanted = lax.broadcasted_iota(jnp.int32, (width, 128), 0) - self.ring.place * share
        lane = lax.broadcasted_iota(jnp.int32, (width, 128), 1)
        wanted = jnp.where(wanted == lane, 1.0, 0.0).astype(BF)
        ada_grad_ref[...] = jnp.zeros_like(ada_grad_ref)
        small_ref[...] = jnp.zeros_like(small_ref)

        def one(k, carry):
            block = self.ring.packs[pl.ds(k * group, group)].reshape(128, width)
            cond = nn(spread, nn(block, wanted).astype(BF))
            for p in range(self.pieces):
                mine = jnp.where(self.of_piece(left, p), cond, 0.0).astype(BF)
                ada_grad_ref[p] += tn(mine, block)[:share]
            small_ref[...] += nn(chosen, block)
            return carry

        lax.fori_loop(0, SUM_PLACES // group, one, 0)

    def finish(self, silu_ref):
        self.exchange().wait()
        silu_ref[...] = self.silu_own[0].astype(F32) + self.silu_got[...].astype(F32)


def attn_grads_kernel(
    images, pieces, table_rows, first_ref, dattn_ref, dqkv_ref, att_ref, pack_own_ref,
    pack_other_ref, ada_ref, sums_ref, ada_grad_ref, small_ref, silu_ref, first_t,
    dattn_t, own, other, land0, land1, land2, land3, land_other, land_cross,
    sends, recvs, packs, pack_sends, pack_recvs, ada_s, part_s, silu_own, silu_got, small_sems,
):
    width = first_t.shape[0]
    tiles, _, columns = own.shape
    share = width // SUM_PLACES
    group = GroupSum(own, other, (land0, land1, land2, land3), land_other, land_cross, sends, recvs)
    ring = PackGather(pack_own_ref, pack_other_ref, packs, pack_sends, pack_recvs)
    barrier = pltpu.get_barrier_semaphore()
    small = SmallGrads(
        images, pieces, table_rows, ring, ada_ref, ada_s, part_s, silu_own, silu_got, small_sems
    )
    group.greet(barrier)
    ring.greet(barrier)
    pl.semaphore_wait(barrier, len(HALVING) + 2)
    ring.start()

    def turn(source, target):
        for at in range(0, source.shape[0], 512):
            target[:, at : at + 512] = source[at : at + 512, :].T

    turn(first_ref, first_t)
    half = width // 2

    def produce(s, left, right_ref, row):
        for buffer, offset, stage in ((other, right_ref.shape[0] // 2, 4), (own, 0, 0)):
            right = right_ref[pl.ds(pl.multiple_of(row + offset, 16), columns), :]
            for at in (0, half):
                store_by_owner(buffer, s, at, nt(left[at : at + half, :], right), share)
            group.copy(stage, s).start()

    def step(s, carry):
        @pl.when(s < tiles - 1)
        def _():
            produce(s, first_t, dqkv_ref, s * columns)

        @pl.when(s == tiles - 1)
        def _():
            produce(s, dattn_t, att_ref, 0)

        @pl.when(s < tiles)
        def _():
            group.add(4, s)
            group.cross(0, s).start()
            group.cross(1, s).start()

        @pl.when(s == 0)
        def _():
            small.piece(0).start()
            turn(dattn_ref, dattn_t)

        for stage in range(ring.stages):

            @pl.when(s == stage)
            def _():
                ring.advance(stage)

        for piece in range(pieces):

            @pl.when(s == 1 + piece)
            def _():
                small.add_piece(piece)

        @pl.when(s == ring.stages)
        def _():
            ring.finish()
            small.reduce(ada_grad_ref, small_ref)

        @pl.when(jnp.logical_and(s >= 1, s - 1 < tiles))
        def _():
            group.add(0, s - 1)
            group.add_cross(0, s - 1)
            group.copy(1, s - 1).start()
            group.add_cross(1, s - 1)

        for stage in (1, 2):
            tile = s - 1 - stage

            @pl.when(jnp.logical_and(tile >= 0, tile < tiles))
            def _():
                group.add(stage, tile)
                group.copy(stage + 1, tile).start()

        tile = s - 4

        @pl.when(tile >= 0)
        def _():
            sums_ref[tile] = group.total(3, tile)[2].astype(BF)

        return carry

    lax.fori_loop(0, tiles + 4, step, 0)
    small.finish(silu_ref)

    def finish(tile, carry):
        group.wait_sends(tile)
        return carry

    lax.fori_loop(0, tiles, finish, 0)


def can_sum_here(width, proj, inner):
    places = lax.axis_size("dp")
    return (
        places == SUM_PLACES
        and lax.axis_size("mp") == 2
        and width % (8 * places) == 0
        and proj == 3 * inner
        and inner % 32 == 0
    )


def attn_grads(first, dattn, dqkv, att, pack_own, pack_other, ada_weight, images, table_rows):
    width = first.shape[1]
    tiles, tile = 4, att.shape[0] // 2
    share = width // SUM_PLACES
    pieces = ada_weight.shape[1] // width
    vmem = pl.BlockSpec(memory_space=pltpu.VMEM)
    sums, ada_grad, small, silu = pl.pallas_call(
        functools.partial(attn_grads_kernel, images, pieces, table_rows),
        in_specs=[vmem] * 6 + [ANYWHERE],
        out_specs=[vmem] * 4,
        out_shape=[
            jax.ShapeDtypeStruct((tiles, 2 * share, tile), BF),
            jax.ShapeDtypeStruct((pieces, share, width), F32),
            jax.ShapeDtypeStruct((16, width), F32),
            jax.ShapeDtypeStruct((16, width), F32),
        ],
        scratch_shapes=[
            pltpu.VMEM((width, first.shape[0]), BF),
            pltpu.VMEM((width, dattn.shape[0]), BF),
            pltpu.VMEM((tiles, width, tile), BF),
            pltpu.VMEM((tiles, width, tile), BF),
            pltpu.VMEM((tiles, width // 2, tile), BF),
            pltpu.VMEM((tiles, width // 4, tile), BF),
            pltpu.VMEM((tiles, width // 8, tile), BF),
            pltpu.VMEM((tiles, width // 8, tile), BF),
            pltpu.VMEM((tiles, width // 2, tile), BF),
            pltpu.VMEM((tiles, width // 2, tile), BF),
            pltpu.SemaphoreType.DMA((7, tiles)),
            pltpu.SemaphoreType.DMA((7, tiles)),
            pltpu.VMEM((SUM_PLACES, 2) + pack_own.shape, BF),
            pltpu.SemaphoreType.DMA((SUM_PLACES.bit_length(),)),
            pltpu.SemaphoreType.DMA((SUM_PLACES.bit_length(),)),
            pltpu.VMEM((width, width), BF),
            pltpu.VMEM((2 * pack_own.shape[0], width), F32),
            pltpu.VMEM((2, 16, width), BF),
            pltpu.VMEM((16, width), BF),
            pltpu.SemaphoreType.DMA((3,)),
        ],
        compiler_params=pltpu.CompilerParams(
            vmem_limit_bytes=VMEM_LIMIT, collective_id=1, has_side_effects=True
        ),
        cost_estimate=cost(1e7, 1e5),
    )(first, dattn, dqkv, att, pack_own, pack_other, ada_weight)
    here = place_bit(lax.axis_index("dp"), FINAL) * share
    mine = lax.dynamic_slice_in_dim(sums, here, share, 1)
    return (
        jnp.transpose(mine, (1, 0, 2)).reshape(share, -1),
        jnp.transpose(ada_grad, (1, 0, 2)).reshape(share, -1),
        small[:pieces].reshape(-1),
        small[pieces : pieces + table_rows, :BUCKETS],
        silu[:images],
    )


def shift_mp(value, steps):
    ways = lax.axis_size("mp")
    return lax.ppermute(value, "mp", [(i, (i - steps) % ways) for i in range(ways)])


def near_halves(block):
    half = block.shape[0] // 2
    core = lax.axis_index("dp") % 2
    mine = lax.dynamic_slice_in_dim(block, core * half, half, 0)
    return [shift_mp(mine, steps) for steps in range(1, lax.axis_size("mp"))]


def with_far_halves(nears):
    places = lax.axis_size("dp")
    core = lax.axis_index("dp") % 2
    got = []
    for near in nears:
        half = near.shape[0]
        far = lax.ppermute(near, "dp", [(i, i ^ 1) for i in range(places)])
        whole = jnp.zeros((2 * half,) + near.shape[1:], near.dtype)
        whole = lax.dynamic_update_slice_in_dim(whole, near, core * half, 0)
        got.append(lax.dynamic_update_slice_in_dim(whole, far, (1 - core) * half, 0))
    return got


def gathered_parts(nears, own=None):
    half = nears[0].shape[0]
    layout, parts, base = [], [], 0
    if own is not None:
        layout, parts, base = [(0, 0, True)], [own], own.shape[0]
    if half % 16:
        return [(0, 0, True)], [jnp.concatenate(parts + with_far_halves(nears), axis=0)]
    places = lax.axis_size("dp")
    for near in nears:
        far = lax.ppermute(near, "dp", [(i, i ^ 1) for i in range(places)])
        layout += [(base, half, True), (base, half, False)]
        parts += [near, far]
        base += 2 * half
    return layout, parts


def after_own(gathered, own):
    layout, parts = gathered
    return [(0, 0, True)] + [(base + own.shape[0], half, near) for base, half, near in layout], [
        own
    ] + parts


def home(parts):
    total = parts[0].astype(F32)
    for steps in range(1, len(parts)):
        total = total + shift_mp(parts[steps], -steps).astype(F32)
    return total


def scatter_dp(part):
    return lax.psum_scatter(part, "dp", scatter_dimension=0, tiled=True)


def local(
    tokens, conditioning, kept_ids, ada_weight, ada_bias, attn_qkv, attn_out, mlp_up, mlp_down,
    rel_table, grad_out_kept, grad_out_full,
):
    ways = lax.axis_size("mp")
    place = lax.axis_index("mp")
    images_group = conditioning.shape[0]
    images = images_group // ways
    width = tokens.shape[1]
    keep = kept_ids.shape[1]
    padded = -(-keep // 64) * 64
    per_block = rel_table.shape[0]
    cols = ada_bias.shape[0]

    silu_cond = jax.nn.silu(conditioning.astype(F32)).astype(BF)
    columns = (jnp.dot(silu_cond, ada_weight, preferred_element_type=F32) + ada_bias).astype(BF)
    near_o = near_halves(attn_out)
    columns, near_o = lax.optimization_barrier((columns, near_o))
    mod = lax.all_to_all(columns, "mp", split_axis=0, concat_axis=1, tiled=True)
    mod = jnp.pad(mod.astype(F32).reshape(images, 6, width), ((0, 0), (0, 2), (0, 0)))

    weight_own = jnp.transpose(attn_qkv.reshape(width, -1))
    tables = [rel_table] + [shift_mp(rel_table, s) for s in range(1, ways)]
    mod, tables, weight_sent = lax.optimization_barrier((mod, tables, weight_own))
    near_w = near_halves(weight_sent)
    fetch = ways == 2 and lax.axis_size("dp") % 4 == 0 and mlp_up.shape[0] % 32 == 0
    fetch = fetch and mlp_down.shape[0] % 64 == 0
    bias = bias_whole(jnp.concatenate(tables, axis=0))

    own_kept = lax.dynamic_slice_in_dim(kept_ids, place * images, images, 0)
    own_kept = jnp.pad(own_kept, ((0, 0), (0, padded - keep)), constant_values=-1)
    pick = (own_kept[:, :, None] == jnp.arange(PATCHES, dtype=jnp.int32)).astype(BF)
    grads = jnp.concatenate(
        [
            grad_out_full.reshape(images, PATCHES, width),
            jnp.pad(
                grad_out_kept.reshape(images, keep, width), ((0, 0), (0, padded - keep), (0, 0))
            ),
        ],
        axis=1,
    )
    dmlp = (mod[:, 5:6] * grads.astype(F32)).astype(BF).reshape(-1, width)
    grads = grads.reshape(-1, width)

    own = own_heads(tokens, mod, pick, bias, weight_own, per_block)
    near_w, near_o, own = lax.optimization_barrier((near_w, near_o, own))
    first = own[0]
    weight_others = gathered_parts(near_w)
    weight = after_own(weight_others, weight_own)
    out_weight = gathered_parts(near_o, attn_out)
    cut = (mlp_up.shape[0] * 5 // 18) // 16 * 16
    qkv, att, lse, middle, second, branch, *near_up = forward(
        own, tokens, mod, pick, bias, weight_others, out_weight, per_block,
        mlp_up if fetch else None, cut,
    )
    (branch_mlp, dsecond, grads_own, *whole), tile_own = mlp(
        second, dmlp, mlp_up, mlp_down, None, (near_up[0], mlp_up, mlp_down) if fetch else None
    )
    if fetch:
        up_others, down_others = [whole[0]], [whole[1]]
    else:
        up_others = with_far_halves(near_halves(mlp_up))
        down_others = with_far_halves(near_halves(mlp_down))
    reduced = [scatter_dp(grads_own)]
    for up, down in zip(up_others, down_others):
        (branch_mlp, dsecond, grads_next), _ = mlp(
            second, dmlp, up, down, (branch_mlp, dsecond)
        )
        reduced.append(scatter_dp(grads_next))
    out_full, out_kept, dtok, dmod, dattn, dqkv, strips = backward(
        tokens, mod, pick, bias, qkv, lse, middle, branch, branch_mlp, dsecond, grads,
        weight, out_weight, per_block,
    )
    proj_block, out_block = weight_own.shape[0], attn_out.shape[0]
    dqkv, reduced[0] = lax.optimization_barrier((dqkv, reduced[0]))
    dtables = table_of_strips(strips)
    pieces = cols // width
    used = images * (pieces + 1) + per_block
    here = can_sum_here(width, dqkv.shape[0], att.shape[0]) and cols % width == 0
    here = here and used <= 32 and pieces + per_block <= 16 and pieces <= 3
    if here:
        own_cond_rows = lax.dynamic_slice_in_dim(silu_cond, place * images, images, 0)
        packs = []
        for steps in range(ways):
            at = (place + steps) % ways
            table = dtables[steps * per_block : (steps + 1) * per_block]
            pack = jnp.concatenate(
                [
                    lax.dynamic_slice_in_dim(dmod, at * pieces, pieces, 1)
                    .astype(BF)
                    .reshape(-1, width),
                    own_cond_rows,
                    jnp.pad(table, ((0, 0), (0, width - BUCKETS))).astype(BF),
                ],
                axis=0,
            )
            packs.append(jnp.pad(pack, ((0, 32 - used), (0, 0))))
        attn_total, grad_ada_weight, grad_ada_bias, dtable, grad_silu = attn_grads(
            first, dattn, dqkv, att, *packs, ada_weight, images, per_block
        )
    else:
        dweight = dot(first, dqkv, (0, 1)).astype(BF)
        dout_t = dot(dattn, att, (0, 1)).astype(BF)
        attn_sums = scatter_dp(jnp.concatenate([dweight, dout_t], axis=1))
        dmod_rows = dmod[:, :6].reshape(images, 6 * width)
        dcolumns = lax.all_to_all(dmod_rows, "mp", split_axis=1, concat_axis=0, tiled=True)
        dtable = home(list(jnp.split(dtables, ways, axis=0)))
        all_columns = lax.all_gather(dcolumns, "dp", axis=0, tiled=True)
        dtable = lax.psum(dtable, "dp")
        all_cond = lax.all_gather(silu_cond, "dp", axis=0, tiled=True).astype(F32)
        slice_width = width // lax.axis_size("dp")
        cond_slice = lax.dynamic_slice_in_dim(
            all_cond, lax.axis_index("dp") * slice_width, slice_width, 1
        )
        grad_ada_weight = lax.dot_general(
            cond_slice, all_columns, (((0,), (0,)), ((), ())), precision=PRECISE
        )
        grad_ada_bias = jnp.sum(all_columns, axis=0)
        dcolumns_high = dcolumns.astype(BF)
        dcolumns_low = (dcolumns - dcolumns_high.astype(F32)).astype(BF)
        silu_part = nt(jnp.concatenate([dcolumns_high, dcolumns_low], axis=0), ada_weight)
        silu_part = silu_part[:images_group] + silu_part[images_group:]
        shares = lax.all_to_all(
            silu_part.astype(BF).reshape(ways, images, width), "mp", split_axis=0, concat_axis=0,
            tiled=True,
        )
        grad_silu = jnp.sum(shares.astype(F32), axis=0)
        split = ways * proj_block
        attn_total = home(
            [
                jnp.concatenate(
                    [
                        attn_sums[:, j * proj_block : (j + 1) * proj_block],
                        attn_sums[:, split + j * out_block : split + (j + 1) * out_block],
                    ],
                    axis=1,
                )
                for j in range(ways)
            ]
        )
    mlp_grads = home(reduced)
    attn_total = attn_total.astype(F32)
    grad_up, grad_down_t = split_mlp_grads(mlp_grads, tile_own)
    grad_qkv = attn_total[:, :proj_block].reshape(-1, 3, proj_block // 3)
    grad_out = jnp.transpose(attn_total[:, proj_block:])

    own_cond = lax.dynamic_slice_in_dim(conditioning, place * images, images, 0).astype(F32)
    grad_cond = jax.vjp(jax.nn.silu, own_cond)[1](grad_silu)[0].astype(BF)

    out_kept = out_kept.reshape(images, padded, width)[:, :keep].reshape(-1, width)
    return (
        out_kept, out_full, dtok, grad_cond, grad_ada_weight, grad_ada_bias, grad_qkv, grad_out,
        grad_up, jnp.transpose(grad_down_t), dtable,
    )


def solution(mesh):
    both = P(("dp", "mp"), None)
    return jax.shard_map(
        local,
        mesh=mesh,
        in_specs=(
            both, P("dp", None), P("dp", None), P(None, "mp"), P("mp"), P(None, None, "mp"),
            P("mp", None), P(None, "mp"), P("mp", None), P("mp", None), both, both,
        ),
        out_specs=(
            both, both, both, both, P("dp", "mp"), P("mp"), P("dp", None, "mp"), P("mp", "dp"),
            P("dp", "mp"), P("mp", "dp"), P("mp", None),
        ),
        check_vma=False,
    )
```

```python
import functools
import math

import jax
import jax.numpy as jnp
import numpy as np
from jax import lax
from jax.experimental import pallas as pl
from jax.experimental.pallas import tpu as pltpu
from jax.sharding import PartitionSpec as P

HEAD_DIM = 72
GRID = 16
PATCHES = 256
BUCKETS = 961
SPAN = 2 * GRID - 1
EPSILON = 1e-06
PRECISE = lax.Precision.HIGHEST
BF = jnp.bfloat16
F32 = jnp.float32
LOG2E = math.log2(math.e)
VMEM_LIMIT = 60 * 1024 * 1024


def dot(a, b, dims):
    return lax.dot_general(a, b, ((dims[0:1], dims[1:2]), ((), ())), preferred_element_type=F32)


def nn(a, b):
    return dot(a, b, (1, 0))


def nt(a, b):
    return dot(a, b, (1, 1))


def tn(a, b):
    return dot(a, b, (0, 0))


def normalize(rows):
    centered = rows - jnp.mean(rows, axis=-1, keepdims=True)
    inverse = lax.rsqrt(jnp.mean(centered * centered, axis=-1, keepdims=True) + EPSILON)
    return centered * inverse, inverse


def norm_back(normed, inverse, upstream):
    return inverse * (
        upstream
        - jnp.mean(upstream, axis=-1, keepdims=True)
        - normed * jnp.mean(upstream * normed, axis=-1, keepdims=True)
    )


def params(n_grid=1):
    return pltpu.CompilerParams(
        vmem_limit_bytes=VMEM_LIMIT, dimension_semantics=("arbitrary",) * n_grid
    )


def cost(flops, bytes_accessed, transcendentals=0):
    return pl.CostEstimate(
        flops=int(flops), bytes_accessed=int(bytes_accessed), transcendentals=int(transcendentals)
    )


def const_spec(shape):
    return pl.BlockSpec(shape, lambda *_: (0,) * len(shape), pipeline_mode=pl.Buffered(1))


def bias_kernel(strip_ref, bias_ref):
    strip = strip_ref[0]
    for key_row in range(GRID):
        start = (GRID - 1 - key_row) * GRID
        bias_ref[0, key_row * GRID : (key_row + 1) * GRID, :] = strip[:, start : start + PATCHES]


def bias_whole(table):
    heads = table.shape[0]
    grid_table = table.reshape(heads * SPAN, SPAN) * LOG2E
    place = np.arange(GRID)
    gap = place[None, :] - place[:, None] + GRID - 1
    chooser = (np.arange(SPAN)[:, None, None] == gap[None]).astype(np.float32)
    strip = jnp.dot(grid_table, chooser.reshape(SPAN, GRID * GRID), precision=PRECISE)
    strip = strip.reshape(heads, SPAN, GRID, GRID).transpose(0, 2, 1, 3)
    strip = strip.reshape(heads, GRID, SPAN * GRID)
    strip = jnp.pad(strip, ((0, 0), (0, 0), (0, 512 - SPAN * GRID)))
    return pl.pallas_call(
        bias_kernel,
        grid=(heads,),
        in_specs=[pl.BlockSpec((1, GRID, 512), lambda h: (h, 0, 0))],
        out_specs=pl.BlockSpec((1, PATCHES, PATCHES), lambda h: (h, 0, 0)),
        out_shape=jax.ShapeDtypeStruct((heads, PATCHES, PATCHES), F32),
        compiler_params=params(),
        cost_estimate=cost(1e6, 1e5),
    )(strip)


def table_of_strips(strips):
    heads = strips.shape[0]
    parts = strips[:, :, : SPAN * GRID].reshape(heads, GRID, SPAN, GRID)
    total = jnp.zeros((heads, SPAN, SPAN), F32)
    for c in range(GRID):
        total = total + jnp.pad(parts[:, c], ((0, 0), (0, 0), (GRID - 1 - c, c)))
    return total.reshape(heads, BUCKETS)


def head_rows(head, per_block):
    base = (head // per_block) * (3 * per_block * HEAD_DIM) + (head % per_block) * HEAD_DIM
    step = per_block * HEAD_DIM
    return [pl.ds(pl.multiple_of(base + c * step, 8), HEAD_DIM) for c in range(3)]


def key_mask(pick):
    ones = jnp.ones((pick.shape[0], PATCHES), BF)
    return (tn(pick, ones) - 1.0) * 1e30


def part_copies(layout, parts, whole, sems):
    core = lax.axis_index("dp") % 2
    copies = []
    for index, ((base, half, near), part) in enumerate(zip(layout, parts)):
        start = base + (core if near else 1 - core) * half
        rows = pl.ds(pl.multiple_of(start, 16), part.shape[0])
        copies.append(pltpu.make_async_copy(part, whole.at[rows, :], sems.at[index]))
    return copies


def run_copies(copies):
    for copy in copies:
        copy.start()
    for copy in copies:
        copy.wait()


def core_rows(half, skip, count):
    start = (lax.axis_index("dp") % 2) * half + skip
    return pl.ds(pl.multiple_of(start, 16), count)


def fetch_copy(own, rows, target, sems, at):
    return pltpu.make_async_remote_copy(
        src_ref=own.at[rows, :],
        dst_ref=target,
        send_sem=sems.at[at],
        recv_sem=sems.at[at + 1],
        device_id={"mp": 1 - lax.axis_index("mp")},
        device_id_type=pl.DeviceIdType.MESH,
    )


def core_copy(source, target, sems, at):
    place = lax.axis_index("dp")
    return pltpu.make_async_remote_copy(
        src_ref=source,
        dst_ref=target,
        send_sem=sems.at[at],
        recv_sem=sems.at[at + 1],
        device_id={"dp": place + 1 - 2 * (place % 2)},
        device_id_type=pl.DeviceIdType.MESH,
    )


def greet_peers(bits):
    barrier = pltpu.get_barrier_semaphore()
    peers = [{"mp": 1 - lax.axis_index("mp")}]
    place = lax.axis_index("dp")
    for bit in bits:
        peers.append({"dp": place + bit - 2 * bit * place_bit(place, bit)})
    for peer in peers:
        pl.semaphore_signal(
            barrier, inc=1, device_id=peer, device_id_type=pl.DeviceIdType.MESH
        )
    pl.semaphore_wait(barrier, len(peers))


def project(weight_ref, first, qkv_s, qkv_ref, base):
    step = weight_ref.shape[0] // 3
    for c in range(3):
        part = nt(weight_ref[c * step : (c + 1) * step, :], first)
        qkv_s[c * step : (c + 1) * step, :] = part
        qkv_ref[base + c * step : base + (c + 1) * step, :] = part.astype(BF)


def attend_heads(per_block, first_head, qkv_s, bias_ref, mask, att_s, attk_s, lse_s):
    scale = HEAD_DIM ** (-0.5) * LOG2E
    heads = qkv_s.shape[0] // (3 * HEAD_DIM)

    def one_head(head, carry):
        q_at, k_at, v_at = head_rows(head, per_block)
        queries = qkv_s[q_at, :].astype(BF)
        keys = qkv_s[k_at, :].astype(BF)
        values = qkv_s[v_at, :].astype(BF)
        scores = tn(keys, queries) * scale + bias_ref[first_head + head]
        here = pl.ds(pl.multiple_of(head * HEAD_DIM, 8), HEAD_DIM)

        def attend(scores):
            top = jnp.max(scores, axis=0, keepdims=True)
            weights = jnp.exp2(scores - top)
            total = jnp.sum(weights, axis=0, keepdims=True)
            probs = (weights * (1.0 / total)).astype(BF)
            return nn(values, probs), top + jnp.log2(total)

        att_s[here, :], lse_s[pl.ds(head, 1), :] = attend(scores)
        attk_s[here, :], lse_s[pl.ds(heads + head, 1), :] = attend(scores + mask)
        return carry

    lax.fori_loop(0, heads, one_head, 0, unroll=4 if heads % 4 == 0 else 2)


def own_heads_kernel(
    per_block, tok_ref, mod_ref, pick_ref, bias_ref, weight_ref,
    first_ref, qkv_ref, att_ref, lse_ref, qkv_s, att_s, attk_s, lse_s,
):
    shift_one, scale_one = mod_ref[0, 0:1], mod_ref[0, 1:2]
    normed, _ = normalize(tok_ref[...].astype(F32))
    first = (normed * (1.0 + scale_one) + shift_one).astype(BF)
    first_ref[...] = first
    project(weight_ref, first, qkv_s, qkv_ref, 0)
    mask = key_mask(pick_ref[0])
    attend_heads(per_block, 0, qkv_s, bias_ref, mask, att_s, attk_s, lse_s)
    att_ref[:, :PATCHES] = att_s[...].astype(BF)
    att_ref[:, PATCHES:] = attk_s[...].astype(BF)
    lse_ref[0] = lse_s[...]


def own_heads(tokens, mod, pick, bias, weight, per_block):
    images, padded = pick.shape[0], pick.shape[1]
    width = tokens.shape[1]
    proj = weight.shape[0]
    heads = proj // (3 * HEAD_DIM)
    inner = heads * HEAD_DIM
    return pl.pallas_call(
        functools.partial(own_heads_kernel, per_block),
        grid=(images,),
        in_specs=[
            pl.BlockSpec((PATCHES, width), lambda i: (i, 0)),
            pl.BlockSpec((1, 8, width), lambda i: (i, 0, 0)),
            pl.BlockSpec((1, padded, PATCHES), lambda i: (i, 0, 0)),
            const_spec(bias.shape),
            const_spec(weight.shape),
        ],
        out_specs=[
            pl.BlockSpec((PATCHES, width), lambda i: (i, 0)),
            pl.BlockSpec((proj, PATCHES), lambda i: (0, i)),
            pl.BlockSpec((inner, 2 * PATCHES), lambda i: (0, i)),
            pl.BlockSpec((1, 2 * heads, PATCHES), lambda i: (i, 0, 0)),
        ],
        out_shape=[
            jax.ShapeDtypeStruct((images * PATCHES, width), BF),
            jax.ShapeDtypeStruct((proj, images * PATCHES), BF),
            jax.ShapeDtypeStruct((inner, images * 2 * PATCHES), BF),
            jax.ShapeDtypeStruct((images, 2 * heads, PATCHES), F32),
        ],
        scratch_shapes=[
            pltpu.VMEM((proj, PATCHES), F32),
            pltpu.VMEM((inner, PATCHES), F32),
            pltpu.VMEM((inner, PATCHES), F32),
            pltpu.VMEM((2 * heads, PATCHES), F32),
        ],
        compiler_params=params(),
        cost_estimate=cost(1e7, 1e5),
    )(tokens, mod, pick, bias, weight)


def forward_kernel(per_block, weight_layout, out_layout, fetch, *refs):
    first_ref, own_qkv, own_att, own_lse, tok_ref, mod_ref, pick_ref, bias_ref = refs[:8]
    refs = refs[8:]
    weight_parts, refs = refs[: len(weight_layout)], refs[len(weight_layout) :]
    out_parts, refs = refs[: len(out_layout)], refs[len(out_layout) :]
    if fetch:
        send_ref, refs = refs[0], refs[1:]
    qkv_ref, att_ref, lse_ref, middle_ref, second_ref, branch_ref = refs[:6]
    refs = refs[6:]
    if fetch:
        got_ref, refs = refs[0], refs[1:]
    qkv_s, att_s, attk_s, lse_s, weight_ref, out_w_ref, part_sems, fetch_sems = refs

    def fetching():
        half = send_ref.shape[0] // 2
        return fetch_copy(send_ref, core_rows(half, 0, got_ref.shape[0]), got_ref, fetch_sems, 0)

    @pl.when(pl.program_id(0) == 0)
    def _():
        copies = part_copies(weight_layout, weight_parts, weight_ref, part_sems.at[0])
        copies += part_copies(out_layout, out_parts, out_w_ref, part_sems.at[1])
        if fetch:
            greet_peers(())
            fetching().start()
        run_copies(copies)

    own = own_qkv.shape[0]
    own_inner = own // 3
    own_count = own_inner // HEAD_DIM
    heads = bias_ref.shape[0]
    others = heads - own_count
    pick = pick_ref[0]
    qkv_ref[:own, :] = own_qkv[...]
    project(weight_ref, first_ref[...], qkv_s, qkv_ref, own)
    mask = key_mask(pick)
    attend_heads(per_block, own_count, qkv_s, bias_ref, mask, att_s, attk_s, lse_s)
    att_ref[:own_inner, :] = own_att[...]
    att_ref[own_inner:, :PATCHES] = att_s[...].astype(BF)
    att_ref[own_inner:, PATCHES:] = attk_s[...].astype(BF)
    lse_ref[0, :own_count, :] = own_lse[0, :own_count]
    lse_ref[0, own_count:heads, :] = lse_s[:others]
    lse_ref[0, heads : heads + own_count, :] = own_lse[0, own_count:]
    lse_ref[0, heads + own_count :, :] = lse_s[others:]
    gate_one = mod_ref[0, 2:3]
    shift_two, scale_two = mod_ref[0, 3:4], mod_ref[0, 4:5]
    out_w = out_w_ref[...]
    kept_att = nt(pick, att_ref[:, PATCHES:]).astype(BF)
    for rows, source, residual in (
        (slice(0, PATCHES), att_ref[:, :PATCHES].T, tok_ref[...].astype(F32)),
        (slice(PATCHES, PATCHES + pick.shape[0]), kept_att, nn(pick, tok_ref[...])),
    ):
        branch = nn(source, out_w)
        branch_ref[rows, :] = branch.astype(BF)
        middle = residual + gate_one * branch
        middle_ref[rows, :] = middle
        second_ref[rows, :] = (normalize(middle)[0] * (1.0 + scale_two) + shift_two).astype(BF)
    if fetch:

        @pl.when(pl.program_id(0) == pl.num_programs(0) - 1)
        def _():
            fetching().wait()


def whole_rows(layout, parts):
    return sum(part.shape[0] for part in parts)


ANYWHERE = pl.BlockSpec(memory_space=pl.ANY)


def forward(own, tokens, mod, pick, bias, weight, out_weight, per_block, send=None, count=0):
    images, padded = pick.shape[0], pick.shape[1]
    width = tokens.shape[1]
    rows = PATCHES + padded
    heads = bias.shape[0]
    (weight_layout, weight_parts), (out_layout, out_parts) = weight, out_weight
    proj_others = whole_rows(*weight)
    proj = own[1].shape[0] + proj_others
    own_inner, own_heads_count = own[2].shape[0], own[3].shape[1] // 2
    others = heads - own_heads_count
    fetch = send is not None
    most = max(len(weight_parts), len(out_parts))
    extra_shapes, extra = [], []
    compiler_params = params()
    if fetch:
        extra_shapes = [jax.ShapeDtypeStruct((count, send.shape[1]), BF)]
        extra = [send]
        compiler_params = pltpu.CompilerParams(
            vmem_limit_bytes=VMEM_LIMIT, dimension_semantics=("arbitrary",),
            collective_id=2, has_side_effects=True,
        )
    by_row = pl.BlockSpec((rows, width), lambda i: (i, 0))
    return pl.pallas_call(
        functools.partial(forward_kernel, per_block, weight_layout, out_layout, fetch),
        grid=(images,),
        in_specs=[
            pl.BlockSpec((PATCHES, width), lambda i: (i, 0)),
            pl.BlockSpec((own[1].shape[0], PATCHES), lambda i: (0, i)),
            pl.BlockSpec((own_inner, 2 * PATCHES), lambda i: (0, i)),
            pl.BlockSpec((1, 2 * own_heads_count, PATCHES), lambda i: (i, 0, 0)),
            pl.BlockSpec((PATCHES, width), lambda i: (i, 0)),
            pl.BlockSpec((1, 8, width), lambda i: (i, 0, 0)),
            pl.BlockSpec((1, padded, PATCHES), lambda i: (i, 0, 0)),
            const_spec(bias.shape),
        ]
        + [ANYWHERE] * (len(weight_parts) + len(out_parts) + len(extra)),
        out_specs=[
            pl.BlockSpec((proj, PATCHES), lambda i: (0, i)),
            pl.BlockSpec((width, 2 * PATCHES), lambda i: (0, i)),
            pl.BlockSpec((1, 2 * heads, PATCHES), lambda i: (i, 0, 0)),
            by_row,
            by_row,
            by_row,
        ]
        + [ANYWHERE] * len(extra),
        out_shape=[
            jax.ShapeDtypeStruct((proj, images * PATCHES), BF),
            jax.ShapeDtypeStruct((width, images * 2 * PATCHES), BF),
            jax.ShapeDtypeStruct((images, 2 * heads, PATCHES), F32),
            jax.ShapeDtypeStruct((images * rows, width), F32),
            jax.ShapeDtypeStruct((images * rows, width), BF),
            jax.ShapeDtypeStruct((images * rows, width), BF),
        ]
        + extra_shapes,
        scratch_shapes=[
            pltpu.VMEM((proj_others, PATCHES), F32),
            pltpu.VMEM((others * HEAD_DIM, PATCHES), F32),
            pltpu.VMEM((others * HEAD_DIM, PATCHES), F32),
            pltpu.VMEM((2 * others, PATCHES), F32),
            pltpu.VMEM((proj_others, width), BF),
            pltpu.VMEM((width, width), BF),
            pltpu.SemaphoreType.DMA((2, most)),
            pltpu.SemaphoreType.DMA((2,)),
        ],
        compiler_params=compiler_params,
        cost_estimate=cost(images * 2e9, images * 8e6),
    )(*own, tokens, mod, pick, bias, *weight_parts, *out_parts, *extra)


def gelu_pair(pre):
    root = math.sqrt(2.0 / math.pi)
    square = pre * pre
    bend = jnp.tanh(pre * (root + (root * 0.044715) * square))
    half = 0.5 + 0.5 * bend
    slope = half + (0.5 * pre) * (1.0 - bend * bend) * (root + (3.0 * root * 0.044715) * square)
    return pre * half, slope


def mlp_kernel(
    chunk, fresh, fetch, second_ref, dmlp_ref, up_ref, down_ref, *refs
):
    if fetch:
        near_ref, send_up, send_down = refs[:3]
        *refs, moves, fetch_sems = refs[3:]
        up_all, down_all = refs[3:5]
        refs = refs[:3] + refs[5:]
    if fresh:
        branch_ref, dsecond_ref, grads_ref, second_t, dmlp_t, hidden_s, dpre_s, sem = refs
    else:
        branch_in, dsecond_in, branch_ref, dsecond_ref, grads_ref = refs[:5]
        second_t, dmlp_t, hidden_s, dpre_s, sem = refs[5:]
    rows = second_ref.shape[0]
    tile = up_ref.shape[1]
    width = second_ref.shape[1]

    if fetch:
        up_half, down_half = up_all.shape[0] // 2, down_all.shape[0] // 2
        cut, quarter = near_ref.shape[0], down_half // 2
        place = lax.axis_index("dp")
        side = place_bit(place, 2)
        up_a = up_all.at[core_rows(up_half, 0, cut), :]
        up_b = up_all.at[core_rows(up_half, cut, up_half - cut), :]
        down_a = down_all.at[core_rows(down_half, 0, down_half), :]
        down_q_rows = core_rows(down_half, side * quarter, quarter)
        down_q = down_all.at[down_q_rows, :]
        lay_a = pltpu.make_async_copy(near_ref, up_a, moves.at[0])
        pass_a = core_copy(near_ref, up_a, moves, 1)
        pass_b = core_copy(up_b, up_b, moves, 3)
        pass_down = core_copy(down_a, down_a, moves, 5)
        pass_y = pltpu.make_async_remote_copy(
            src_ref=down_q,
            dst_ref=down_q,
            send_sem=moves.at[7],
            recv_sem=moves.at[8],
            device_id={"dp": place + 2 - 4 * side},
            device_id_type=pl.DeviceIdType.MESH,
        )
        fetch_b = fetch_copy(
            send_up, core_rows(up_half, cut, up_half - cut), up_b, fetch_sems, 0
        )
        fetch_down = fetch_copy(send_down, down_q_rows, down_q, fetch_sems, 2)
    step, last = pl.program_id(0), pl.num_programs(0) - 1

    @pl.when(step == 0)
    def _():
        if fetch:
            greet_peers((1, 2))
            fetch_down.start()
            lay_a.start()
            pass_a.start()
        if fresh:
            branch_ref[...] = jnp.zeros_like(branch_ref)
            dsecond_ref[...] = jnp.zeros_like(dsecond_ref)
        else:
            one = pltpu.make_async_copy(branch_in, branch_ref, sem.at[0])
            two = pltpu.make_async_copy(dsecond_in, dsecond_ref, sem.at[1])
            one.start()
            two.start()
        for at in range(0, rows, chunk):
            second_t[:, at : at + chunk] = second_ref[at : at + chunk, :].T
            dmlp_t[:, at : at + chunk] = dmlp_ref[at : at + chunk, :].T
        if not fresh:
            one.wait()
            two.wait()

    def one_chunk(index, carry):
        at = pl.ds(pl.multiple_of(index * chunk, chunk), chunk)
        pre = nn(second_ref[at, :], up_ref[...])
        dhidden = nt(dmlp_ref[at, :], down_ref[...])
        value, slope = gelu_pair(pre)
        hidden = value.astype(BF)
        dpre = (dhidden * slope).astype(BF)
        hidden_s[at, :] = hidden
        dpre_s[at, :] = dpre
        branch_ref[at, :] += nn(hidden, down_ref[...])
        dsecond_ref[at, :] += nt(dpre, up_ref[...])
        if fetch:

            @pl.when(jnp.logical_and(step == jnp.minimum(1, last), index == 0))
            def _():
                fetch_down.wait_recv()
                pass_y.start()
                fetch_b.start()

        return carry

    lax.fori_loop(0, rows // chunk, one_chunk, 0)
    if fetch:

        @pl.when(step == last)
        def _():
            fetch_b.wait_recv()
            pass_b.start()
            pass_y.wait_recv()
            pass_down.start()

    part = width // 3
    for c in range(3):
        at = slice(c * part, (c + 1) * part)
        grads_ref[at, :tile] = nn(second_t[at, :], dpre_s[...]).astype(BF)
        grads_ref[at, tile:] = nn(dmlp_t[at, :], hidden_s[...]).astype(BF)

    if fetch:

        @pl.when(step == last)
        def _():
            for copy in (lay_a, pass_a, pass_b, pass_down):
                copy.wait()
            pass_y.wait_send()
            fetch_b.wait_send()
            fetch_down.wait_send()


def mlp_chunk(rows):
    for chunk in (896, 448, 64):
        if rows % chunk == 0:
            return chunk
    return rows


def mlp(second, dmlp, up, down, sums=None, fetch=None):
    rows, width = second.shape
    hidden = up.shape[1]
    tile = 768 if hidden % 768 == 0 else hidden
    fresh = sums is None
    chunk = mlp_chunk(rows)
    in_specs = [
        const_spec(second.shape),
        const_spec(second.shape),
        pl.BlockSpec((width, tile), lambda f: (0, f)),
        pl.BlockSpec((tile, width), lambda f: (f, 0)),
    ]
    operands = [second, dmlp, up, down]
    out_specs = [
        const_spec(second.shape),
        const_spec(second.shape),
        pl.BlockSpec((width, 2 * tile), lambda f: (0, f)),
    ]
    out_shape = [
        jax.ShapeDtypeStruct(second.shape, F32),
        jax.ShapeDtypeStruct(second.shape, F32),
        jax.ShapeDtypeStruct((width, 2 * hidden), BF),
    ]
    scratch = [
        pltpu.VMEM((width, rows), BF),
        pltpu.VMEM((width, rows), BF),
        pltpu.VMEM((rows, tile), BF),
        pltpu.VMEM((rows, tile), BF),
        pltpu.SemaphoreType.DMA((2,)),
    ]
    compiler_params = params()
    if not fresh:
        in_specs += [ANYWHERE] * 2
        operands += list(sums)
    if fetch is not None:
        in_specs += [ANYWHERE] * 3
        operands += list(fetch)
        out_specs += [ANYWHERE] * 2
        out_shape += [jax.ShapeDtypeStruct(up.shape, BF), jax.ShapeDtypeStruct(down.shape, BF)]
        scratch += [pltpu.SemaphoreType.DMA((9,)), pltpu.SemaphoreType.DMA((4,))]
        compiler_params = pltpu.CompilerParams(
            vmem_limit_bytes=VMEM_LIMIT, dimension_semantics=("arbitrary",),
            collective_id=3, has_side_effects=True,
        )
    return pl.pallas_call(
        functools.partial(mlp_kernel, chunk, fresh, fetch is not None),
        grid=(hidden // tile,),
        in_specs=in_specs,
        out_specs=out_specs,
        out_shape=out_shape,
        scratch_shapes=scratch,
        compiler_params=compiler_params,
        cost_estimate=cost(6e10, 6e7) if fresh else cost(1e7, 1e5),
    )(*operands), tile


def split_mlp_grads(grads, tile):
    parts = grads.reshape(grads.shape[0], -1, 2, tile)
    return (
        parts[:, :, 0].reshape(grads.shape[0], -1),
        parts[:, :, 1].reshape(grads.shape[0], -1),
    )


def backward_kernel(per_block, keep, weight_layout, out_layout, *refs):
    count = len(weight_layout) + len(out_layout)
    weight_parts = refs[: len(weight_layout)]
    out_parts = refs[len(weight_layout) : count]
    weight_ref, out_w_ref, sems = refs[-3:]

    @pl.when(pl.program_id(0) == 0)
    def _():
        run_copies(
            part_copies(weight_layout, weight_parts, weight_ref, sems.at[0])
            + part_copies(out_layout, out_parts, out_w_ref, sems.at[1])
        )

    backward_body(per_block, keep, weight_ref, out_w_ref, *refs[count:-3])


def backward_body(
    per_block, keep, weight_ref, out_w_ref, tok_ref, mod_ref, pick_ref, bias_ref,
    qkv_ref, lse_ref, middle_ref, branch_ref, mlp_ref, dsecond_ref, grad_ref,
    out_full_ref, out_kept_ref, dtok_ref, dmod_ref, dattn_ref, dqkv_ref, strips_ref,
    qkv_s, datt_s, dattk_s, dscores_s,
):
    heads = bias_ref.shape[0]
    step = pl.program_id(0)
    shift_one, scale_one, gate_one = mod_ref[0, 0:1], mod_ref[0, 1:2], mod_ref[0, 2:3]
    scale_two, gate_two = mod_ref[0, 4:5], mod_ref[0, 5:6]
    pick = pick_ref[0]
    dmiddles = []
    sums = [0.0, 0.0, 0.0, 0.0]
    for rows in (slice(0, PATCHES), slice(PATCHES, PATCHES + pick.shape[0])):
        middle = middle_ref[rows, :]
        branch_mlp = mlp_ref[rows, :]
        dsecond = dsecond_ref[rows, :]
        grad = grad_ref[rows, :].astype(F32)
        out = (middle + gate_two * branch_mlp).astype(BF)
        if rows.start == 0:
            out_full_ref[...] = out
        else:
            for image in range(out_kept_ref.shape[0] // keep):

                @pl.when(step == image)
                def _():
                    out_kept_ref[image * keep : (image + 1) * keep, :] = out[:keep]

        normed, inverse = normalize(middle)
        dmiddle = grad + norm_back(normed, inverse, dsecond * (1.0 + scale_two))
        branch = branch_ref[rows, :].astype(F32)
        for c, term in enumerate(
            (dmiddle * branch, dsecond, dsecond * normed, grad * branch_mlp)
        ):
            sums[c] = sums[c] + jnp.sum(term, axis=0, keepdims=True)
        dmiddles.append(dmiddle)
    for c in range(4):
        dmod_ref[0, 2 + c : 3 + c, :] = sums[c]
    dattn = (gate_one * dmiddles[0]).astype(BF)
    dattn_kept = tn(pick, (gate_one * dmiddles[1]).astype(BF)).astype(BF)
    dattn_ref[:PATCHES, :] = dattn
    dattn_ref[PATCHES:, :] = dattn_kept
    high = dmiddles[1].astype(BF)
    low = (dmiddles[1] - high.astype(F32)).astype(BF)
    dresid = dmiddles[0] + tn(pick, high) + tn(pick, low)
    datt_s[...] = nt(out_w_ref[...], dattn)
    dattk_s[...] = nt(out_w_ref[...], dattn_kept)
    qkv_s[...] = qkv_ref[...].astype(F32)
    mask = key_mask(pick)
    scale = HEAD_DIM ** (-0.5)

    @pl.when(step == 0)
    def _():
        dscores_s[...] = jnp.zeros_like(dscores_s)

    def one_head(head, carry):
        q_at, k_at, v_at = head_rows(head, per_block)
        queries = qkv_s[q_at, :].astype(BF)
        keys = qkv_s[k_at, :].astype(BF)
        values = qkv_s[v_at, :].astype(BF)
        here = pl.ds(pl.multiple_of(head * HEAD_DIM, 8), HEAD_DIM)
        scores = tn(keys, queries) * (scale * LOG2E) + bias_ref[head]

        def pull(scores, top, upstream):
            probs = jnp.exp2(scores - top)
            dprobs = tn(values, upstream)
            dvalues = nt(upstream, probs.astype(BF))
            weighted = jnp.sum(probs * dprobs, axis=0, keepdims=True)
            return probs * (dprobs - weighted), dvalues

        dscores, dvalues = pull(
            scores, lse_ref[0, pl.ds(head, 1), :], datt_s[here, :].astype(BF)
        )
        dscores_kept, dvalues_kept = pull(
            scores + mask, lse_ref[0, pl.ds(heads + head, 1), :], dattk_s[here, :].astype(BF)
        )
        dscores = dscores + dscores_kept
        dscores_s[head] += dscores
        rounded = dscores.astype(BF)
        qkv_s[q_at, :] = nn(keys, rounded) * scale
        qkv_s[k_at, :] = nt(queries, rounded) * scale
        qkv_s[v_at, :] = dvalues + dvalues_kept
        return carry

    lax.fori_loop(0, heads, one_head, 0, unroll=4)
    dqkv = qkv_s[...].astype(BF)
    dqkv_ref[...] = dqkv
    dfirst = tn(dqkv, weight_ref[...])
    normed, inverse = normalize(tok_ref[...].astype(F32))
    dmod_ref[0, 0:1, :] = jnp.sum(dfirst, axis=0, keepdims=True)
    dmod_ref[0, 1:2, :] = jnp.sum(dfirst * normed, axis=0, keepdims=True)
    dmod_ref[0, 6:8, :] = jnp.zeros((2, dfirst.shape[1]), F32)
    dtok_ref[...] = (dresid + norm_back(normed, inverse, dfirst * (1.0 + scale_one))).astype(BF)

    @pl.when(step == pl.num_programs(0) - 1)
    def _():
        def fold(head, carry):
            strip = jnp.zeros((GRID, 512), F32)
            for key_row in range(GRID):
                start = (GRID - 1 - key_row) * GRID
                block = dscores_s[head, key_row * GRID : (key_row + 1) * GRID, :]
                block = jnp.concatenate([block, jnp.zeros((GRID, 512 - PATCHES), F32)], axis=1)
                strip = strip + pltpu.roll(block, start, 1)
            strips_ref[head] = strip
            return carry

        lax.fori_loop(0, heads, fold, 0)


def backward(
    tokens, mod, pick, bias, qkv, lse, middle, branch, branch_mlp, dsecond, grads,
    weight, out_weight, per_block, keep,
):
    (weight_layout, weight_parts), (out_layout, out_parts) = weight, out_weight
    most = max(len(weight_parts), len(out_parts))
    proj = whole_rows(*weight)
    images, padded = pick.shape[0], pick.shape[1]
    width = tokens.shape[1]
    rows = PATCHES + padded
    heads = bias.shape[0]
    by_row = pl.BlockSpec((rows, width), lambda i: (i, 0))
    one_row = pl.BlockSpec((rows, width), lambda i: (i, 0), pipeline_mode=pl.Buffered(1))
    return pl.pallas_call(
        functools.partial(backward_kernel, per_block, keep, weight_layout, out_layout),
        grid=(images,),
        in_specs=[ANYWHERE] * (len(weight_parts) + len(out_parts))
        + [
            pl.BlockSpec((PATCHES, width), lambda i: (i, 0), pipeline_mode=pl.Buffered(1)),
            pl.BlockSpec((1, 8, width), lambda i: (i, 0, 0)),
            pl.BlockSpec((1, padded, PATCHES), lambda i: (i, 0, 0)),
            const_spec(bias.shape),
            pl.BlockSpec((proj, PATCHES), lambda i: (0, i)),
            pl.BlockSpec((1, 2 * heads, PATCHES), lambda i: (i, 0, 0)),
            by_row,
            one_row,
            by_row,
            by_row,
            one_row,
        ],
        out_specs=[
            pl.BlockSpec((PATCHES, width), lambda i: (i, 0)),
            const_spec((images * keep, width)),
            pl.BlockSpec((PATCHES, width), lambda i: (i, 0)),
            pl.BlockSpec((1, 8, width), lambda i: (i, 0, 0)),
            pl.BlockSpec((2 * PATCHES, width), lambda i: (i, 0)),
            pl.BlockSpec((proj, PATCHES), lambda i: (0, i)),
            const_spec((heads, GRID, 512)),
        ],
        out_shape=[
            jax.ShapeDtypeStruct((images * PATCHES, width), BF),
            jax.ShapeDtypeStruct((images * keep, width), BF),
            jax.ShapeDtypeStruct((images * PATCHES, width), BF),
            jax.ShapeDtypeStruct((images, 8, width), F32),
            jax.ShapeDtypeStruct((images * 2 * PATCHES, width), BF),
            jax.ShapeDtypeStruct((proj, images * PATCHES), BF),
            jax.ShapeDtypeStruct((heads, GRID, 512), F32),
        ],
        scratch_shapes=[
            pltpu.VMEM((proj, PATCHES), F32),
            pltpu.VMEM((width, PATCHES), F32),
            pltpu.VMEM((width, PATCHES), F32),
            pltpu.VMEM((heads, PATCHES, PATCHES), F32),
            pltpu.VMEM((proj, width), BF),
            pltpu.VMEM((width, width), BF),
            pltpu.SemaphoreType.DMA((2, most)),
        ],
        compiler_params=params(),
        cost_estimate=cost(1e7, 1e5),
    )(
        *weight_parts, *out_parts, tokens, mod, pick, bias, qkv, lse, middle, branch, branch_mlp,
        dsecond, grads,
    )


SUM_PLACES = 16
HALVING = (1, 2, 8)
FINAL = 4


def place_bit(place, bit):
    return (place // bit) % 2


def unit_start(owner, share):
    index = 0
    for bit in HALVING + (FINAL,):
        index = index * 2 + place_bit(owner, bit)
    return index * share


def store_by_owner(buffer, tile, at, block, share):
    first_owner = at // share
    owners = block.shape[0] // share
    for k in range(owners):
        owner = first_owner + k
        if place_bit(owner, FINAL):
            continue
        pair = k + FINAL
        both = jnp.concatenate(
            [block[k * share : (k + 1) * share], block[pair * share : (pair + 1) * share]], axis=0
        )
        start = unit_start(owner, share)
        buffer[tile, start : start + 2 * share, :] = both.astype(BF)


class GroupSum:
    def __init__(self, own, other, lands, land_other, land_cross, sends, recvs):
        self.own, self.other, self.lands = own, other, lands
        self.land_other, self.land_cross = land_other, land_cross
        self.sends, self.recvs = sends, recvs
        self.place = lax.axis_index("dp")
        self.rows = own.shape[1]

    def partner(self, bit):
        return {"dp": self.place + bit - 2 * bit * place_bit(self.place, bit)}

    def greet(self, barrier):
        for bit in HALVING + (FINAL,):
            pl.semaphore_signal(
                barrier, inc=1, device_id=self.partner(bit), device_id_type=pl.DeviceIdType.MESH
            )

    def spans(self, stage):
        start, size = 0, self.rows
        for k, bit in enumerate(HALVING):
            size = size // 2
            mine = place_bit(self.place, bit)
            if k == stage:
                return start + mine * size, start + (1 - mine) * size, size
            start = start + mine * size
        return start, start, size

    def remote(self, source, target, index, tile, peer):
        return pltpu.make_async_remote_copy(
            src_ref=source,
            dst_ref=target,
            send_sem=self.sends.at[index, tile],
            recv_sem=self.recvs.at[index, tile],
            device_id=peer,
            device_id_type=pl.DeviceIdType.MESH,
        )

    def copy(self, stage, tile):
        bit = (HALVING + (FINAL, HALVING[0]))[stage]
        buffer, land = (self.other, self.land_other) if stage == 4 else (self.own, self.lands[stage])
        _, away, size = self.spans(0 if stage == 4 else stage)
        rows = buffer.at[tile, pl.ds(pl.multiple_of(away, 16), size), :]
        return self.remote(rows, land.at[tile], stage, tile, self.partner(bit))

    def cross_rows(self, part):
        keep, away, size = self.spans(1)
        return (keep if part else away), size

    def cross(self, part, tile):
        start, size = self.cross_rows(part)
        base = self.spans(0)[0]
        return self.remote(
            self.other.at[tile, pl.ds(pl.multiple_of(start, 16), size), :],
            self.land_cross.at[tile, pl.ds(pl.multiple_of(start - base, 16), size), :],
            5 + part,
            tile,
            {"mp": 1 - lax.axis_index("mp")},
        )

    def total(self, stage, tile):
        self.copy(stage, tile).wait_recv()
        keep, _, size = self.spans(0 if stage == 4 else stage)
        at = pl.ds(pl.multiple_of(keep, 16), size)
        buffer, land = (self.other, self.land_other) if stage == 4 else (self.own, self.lands[stage])
        return buffer, at, buffer[tile, at, :].astype(F32) + land[tile].astype(F32)

    def add(self, stage, tile):
        buffer, at, total = self.total(stage, tile)
        buffer[tile, at, :] = total.astype(BF)

    def add_cross(self, part, tile):
        self.cross(part, tile).wait_recv()
        start, size = self.cross_rows(part)
        base = self.spans(0)[0]
        at = pl.ds(pl.multiple_of(start, 16), size)
        landed = pl.ds(pl.multiple_of(start - base, 16), size)
        total = self.own[tile, at, :].astype(F32) + self.land_cross[tile, landed, :].astype(F32)
        self.own[tile, at, :] = total.astype(BF)

    def wait_sends(self, tile):
        for stage in range(5):
            self.copy(stage, tile).wait_send()
        for part in range(2):
            self.cross(part, tile).wait_send()


def pack_slot(place):
    return sum(
        place_bit(place, SUM_PLACES >> (k + 1)) << k for k in range(SUM_PLACES.bit_length() - 1)
    )


class PackGather:
    def __init__(self, own, other, packs, sends, recvs):
        self.own, self.other, self.packs, self.sends, self.recvs = own, other, packs, sends, recvs
        self.place, self.side = lax.axis_index("dp"), lax.axis_index("mp")
        self.stages = SUM_PLACES.bit_length() - 1
        self.slot = pack_slot(self.place)

    def greet(self, barrier):
        pl.semaphore_signal(
            barrier, inc=1, device_id={"mp": 1 - self.side}, device_id_type=pl.DeviceIdType.MESH
        )

    def cross(self):
        return pltpu.make_async_remote_copy(
            src_ref=self.other,
            dst_ref=self.packs.at[self.slot, self.side],
            send_sem=self.sends.at[self.stages],
            recv_sem=self.recvs.at[self.stages],
            device_id={"mp": 1 - self.side},
            device_id_type=pl.DeviceIdType.MESH,
        )

    def copy(self, stage):
        size = 1 << stage
        bit = SUM_PLACES >> (stage + 1)
        rows = self.packs.at[pl.ds((self.slot // size) * size, size)]
        return pltpu.make_async_remote_copy(
            src_ref=rows,
            dst_ref=rows,
            send_sem=self.sends.at[stage],
            recv_sem=self.recvs.at[stage],
            device_id={"dp": self.place + bit - 2 * bit * place_bit(self.place, bit)},
            device_id_type=pl.DeviceIdType.MESH,
        )

    def start(self):
        self.packs[self.slot, self.side] = self.own[...]
        self.cross().start()

    def advance(self, stage):
        (self.cross() if stage == 0 else self.copy(stage - 1)).wait_recv()
        self.copy(stage).start()

    def finish(self):
        self.copy(self.stages - 1).wait_recv()
        self.cross().wait_send()
        for stage in range(self.stages):
            self.copy(stage).wait_send()


class SmallGrads:
    def __init__(
        self, images, pieces, table_rows, ring, ada, ada_s, part_s, silu_own, silu_got, sems
    ):
        self.images, self.pieces, self.table_rows = images, pieces, table_rows
        self.ring, self.ada, self.ada_s, self.part_s = ring, ada, ada_s, part_s
        self.silu_own, self.silu_got, self.sems = silu_own, silu_got, sems
        self.rows = ring.packs.shape[2]
        self.first_cond = images * pieces

    def row_of(self, shape, axis):
        return lax.broadcasted_iota(jnp.int32, shape, axis) & (self.rows - 1)

    def any_image(self, test):
        found = test(0)
        for image in range(1, self.images):
            found = jnp.logical_or(found, test(image))
        return found

    def of_piece(self, row, piece):
        return self.any_image(lambda image: row == image * self.pieces + piece)

    def piece(self, index):
        width = self.ada_s.shape[1]
        return pltpu.make_async_copy(
            self.ada.at[:, index * width : (index + 1) * width], self.ada_s, self.sems.at[0]
        )

    def exchange(self):
        return pltpu.make_async_remote_copy(
            src_ref=self.silu_own.at[1],
            dst_ref=self.silu_got,
            send_sem=self.sems.at[1],
            recv_sem=self.sems.at[2],
            device_id={"mp": 1 - self.ring.side},
            device_id_type=pl.DeviceIdType.MESH,
        )

    def add_piece(self, index):
        mine = self.ring.packs[self.ring.slot]
        mine = mine.reshape(2 * self.rows, mine.shape[-1]).astype(F32)
        masked = jnp.where(self.of_piece(self.row_of(mine.shape, 0), index), mine, 0.0)
        self.piece(index).wait()
        product = nt(masked.astype(BF), self.ada_s[...])
        if index:
            self.part_s[...] += product
        else:
            self.part_s[...] = product
        if index + 1 < self.pieces:
            self.piece(index + 1).start()
            return
        for k, side in enumerate((self.ring.side, 1 - self.ring.side)):
            block = self.part_s[pl.ds(pl.multiple_of(side * self.rows, 8), self.rows), :]
            found = [
                jnp.sum(block[n * self.pieces : (n + 1) * self.pieces], axis=0, keepdims=True)
                for n in range(self.images)
            ]
            found.append(jnp.zeros((self.silu_got.shape[0] - self.images, block.shape[1]), F32))
            self.silu_own[k] = jnp.concatenate(found, axis=0).astype(BF)
        self.exchange().start()

    def reduce(self, ada_grad_ref, small_ref):
        group = 128 // (2 * self.rows)
        width, share = self.ada_s.shape[1], ada_grad_ref.shape[1]
        left, right = self.row_of((128, 128), 0), self.row_of((128, 128), 1)
        left_all = lax.broadcasted_iota(jnp.int32, (128, 128), 0)
        right_all = lax.broadcasted_iota(jnp.int32, (128, 128), 1)
        same = (left_all - left) == (right_all - right)
        spread = jnp.logical_and(
            same,
            self.any_image(
                lambda n: jnp.logical_and(
                    jnp.logical_and(left >= n * self.pieces, left < (n + 1) * self.pieces),
                    right == self.first_cond + n,
                )
            ),
        )
        spread = jnp.where(spread, 1.0, 0.0).astype(BF)
        line = lax.broadcasted_iota(jnp.int32, (16, 128), 0)
        at = self.row_of((16, 128), 1)
        chosen = jnp.logical_and(
            jnp.logical_and(line >= self.pieces, line < self.pieces + self.table_rows),
            at == line - self.pieces + self.first_cond + self.images,
        )
        for p in range(self.pieces):
            chosen = jnp.logical_or(chosen, jnp.logical_and(line == p, self.of_piece(at, p)))
        chosen = jnp.where(chosen, 1.0, 0.0).astype(BF)
        wanted = lax.broadcasted_iota(jnp.int32, (width, 128), 0) - self.ring.place * share
        lane = lax.broadcasted_iota(jnp.int32, (width, 128), 1)
        wanted = jnp.where(wanted == lane, 1.0, 0.0).astype(BF)
        ada_grad_ref[...] = jnp.zeros_like(ada_grad_ref)
        small_ref[...] = jnp.zeros_like(small_ref)

        def one(k, carry):
            block = self.ring.packs[pl.ds(k * group, group)].reshape(128, width)
            cond = nn(spread, nn(block, wanted).astype(BF))
            for p in range(self.pieces):
                mine = jnp.where(self.of_piece(left, p), cond, 0.0).astype(BF)
                ada_grad_ref[p] += tn(mine, block)[:share]
            small_ref[...] += nn(chosen, block)
            return carry

        lax.fori_loop(0, SUM_PLACES // group, one, 0)

    def finish(self, silu_ref):
        self.exchange().wait()
        silu_ref[...] = self.silu_own[0].astype(F32) + self.silu_got[...].astype(F32)


def attn_grads_kernel(
    images, pieces, table_rows, first_ref, dattn_hbm, dqkv_ref, att_hbm, pack_own_ref,
    pack_other_ref, ada_ref, sums_ref, ada_grad_ref, small_ref, silu_ref, first_t,
    dattn_t, own, other, land0, land1, land2, land3, land_other, land_cross,
    sends, recvs, packs, pack_sends, pack_recvs, ada_s, part_s, silu_own, silu_got, small_sems,
    dattn_ref, att_ref, load_sems,
):
    width = first_t.shape[0]
    tiles, _, columns = own.shape
    share = width // SUM_PLACES
    group = GroupSum(own, other, (land0, land1, land2, land3), land_other, land_cross, sends, recvs)
    ring = PackGather(pack_own_ref, pack_other_ref, packs, pack_sends, pack_recvs)
    load_dattn = pltpu.make_async_copy(dattn_hbm, dattn_ref, load_sems.at[0])
    load_att = pltpu.make_async_copy(att_hbm, att_ref, load_sems.at[1])
    load_dattn.start()
    load_att.start()
    barrier = pltpu.get_barrier_semaphore()
    small = SmallGrads(
        images, pieces, table_rows, ring, ada_ref, ada_s, part_s, silu_own, silu_got, small_sems
    )
    group.greet(barrier)
    ring.greet(barrier)
    pl.semaphore_wait(barrier, len(HALVING) + 2)
    ring.start()

    def turn(source, target):
        for at in range(0, source.shape[0], 512):
            target[:, at : at + 512] = source[at : at + 512, :].T

    turn(first_ref, first_t)
    half = width // 2

    def produce(s, left, right_ref, row):
        for buffer, offset, stage in ((other, right_ref.shape[0] // 2, 4), (own, 0, 0)):
            right = right_ref[pl.ds(pl.multiple_of(row + offset, 16), columns), :]
            for at in (0, half):
                store_by_owner(buffer, s, at, nt(left[at : at + half, :], right), share)
            group.copy(stage, s).start()

    def step(s, carry):
        @pl.when(s < tiles - 1)
        def _():
            produce(s, first_t, dqkv_ref, s * columns)

        @pl.when(s == tiles - 1)
        def _():
            produce(s, dattn_t, att_ref, 0)

        @pl.when(s < tiles)
        def _():
            group.add(4, s)
            group.cross(0, s).start()
            group.cross(1, s).start()

        @pl.when(s == 0)
        def _():
            small.piece(0).start()
            load_dattn.wait()
            turn(dattn_ref, dattn_t)
            load_att.wait()

        for stage in range(ring.stages):

            @pl.when(s == stage)
            def _():
                ring.advance(stage)

        for piece in range(pieces):

            @pl.when(s == 1 + piece)
            def _():
                small.add_piece(piece)

        @pl.when(s == ring.stages)
        def _():
            ring.finish()
            small.reduce(ada_grad_ref, small_ref)

        @pl.when(jnp.logical_and(s >= 1, s - 1 < tiles))
        def _():
            group.add(0, s - 1)
            group.add_cross(0, s - 1)
            group.copy(1, s - 1).start()
            group.add_cross(1, s - 1)

        for stage in (1, 2):
            tile = s - 1 - stage

            @pl.when(jnp.logical_and(tile >= 0, tile < tiles))
            def _():
                group.add(stage, tile)
                group.copy(stage + 1, tile).start()

        tile = s - 4

        @pl.when(tile >= 0)
        def _():
            sums_ref[tile] = group.total(3, tile)[2].astype(BF)

        return carry

    lax.fori_loop(0, tiles + 4, step, 0)
    small.finish(silu_ref)

    def finish(tile, carry):
        group.wait_sends(tile)
        return carry

    lax.fori_loop(0, tiles, finish, 0)


def can_sum_here(width, proj, inner):
    places = lax.axis_size("dp")
    return (
        places == SUM_PLACES
        and lax.axis_size("mp") == 2
        and width % (8 * places) == 0
        and proj == 3 * inner
        and inner % 32 == 0
    )


def attn_grads(first, dattn, dqkv, att, pack_own, pack_other, ada_weight, images, table_rows):
    width = first.shape[1]
    tiles, tile = 4, att.shape[0] // 2
    share = width // SUM_PLACES
    pieces = ada_weight.shape[1] // width
    vmem = pl.BlockSpec(memory_space=pltpu.VMEM)
    sums, ada_grad, small, silu = pl.pallas_call(
        functools.partial(attn_grads_kernel, images, pieces, table_rows),
        in_specs=[vmem, ANYWHERE, vmem, ANYWHERE, vmem, vmem, ANYWHERE],
        out_specs=[vmem] * 4,
        out_shape=[
            jax.ShapeDtypeStruct((tiles, 2 * share, tile), BF),
            jax.ShapeDtypeStruct((pieces, share, width), F32),
            jax.ShapeDtypeStruct((16, width), F32),
            jax.ShapeDtypeStruct((16, width), F32),
        ],
        scratch_shapes=[
            pltpu.VMEM((width, first.shape[0]), BF),
            pltpu.VMEM((width, dattn.shape[0]), BF),
            pltpu.VMEM((tiles, width, tile), BF),
            pltpu.VMEM((tiles, width, tile), BF),
            pltpu.VMEM((tiles, width // 2, tile), BF),
            pltpu.VMEM((tiles, width // 4, tile), BF),
            pltpu.VMEM((tiles, width // 8, tile), BF),
            pltpu.VMEM((tiles, width // 8, tile), BF),
            pltpu.VMEM((tiles, width // 2, tile), BF),
            pltpu.VMEM((tiles, width // 2, tile), BF),
            pltpu.SemaphoreType.DMA((7, tiles)),
            pltpu.SemaphoreType.DMA((7, tiles)),
            pltpu.VMEM((SUM_PLACES, 2) + pack_own.shape, BF),
            pltpu.SemaphoreType.DMA((SUM_PLACES.bit_length(),)),
            pltpu.SemaphoreType.DMA((SUM_PLACES.bit_length(),)),
            pltpu.VMEM((width, width), BF),
            pltpu.VMEM((2 * pack_own.shape[0], width), F32),
            pltpu.VMEM((2, 16, width), BF),
            pltpu.VMEM((16, width), BF),
            pltpu.SemaphoreType.DMA((3,)),
            pltpu.VMEM(dattn.shape, BF),
            pltpu.VMEM(att.shape, BF),
            pltpu.SemaphoreType.DMA((2,)),
        ],
        compiler_params=pltpu.CompilerParams(
            vmem_limit_bytes=VMEM_LIMIT, collective_id=1, has_side_effects=True
        ),
        cost_estimate=cost(1e7, 1e5),
    )(first, dattn, dqkv, att, pack_own, pack_other, ada_weight)
    here = place_bit(lax.axis_index("dp"), FINAL) * share
    mine = lax.dynamic_slice_in_dim(sums, here, share, 1)
    return (
        jnp.transpose(mine, (1, 0, 2)).reshape(share, -1),
        jnp.transpose(ada_grad, (1, 0, 2)).reshape(share, -1),
        small[:pieces].reshape(-1),
        small[pieces : pieces + table_rows, :BUCKETS],
        silu[:images],
    )


def shift_mp(value, steps):
    ways = lax.axis_size("mp")
    return lax.ppermute(value, "mp", [(i, (i - steps) % ways) for i in range(ways)])


def near_halves(block):
    half = block.shape[0] // 2
    core = lax.axis_index("dp") % 2
    mine = lax.dynamic_slice_in_dim(block, core * half, half, 0)
    return [shift_mp(mine, steps) for steps in range(1, lax.axis_size("mp"))]


def with_far_halves(nears):
    places = lax.axis_size("dp")
    core = lax.axis_index("dp") % 2
    got = []
    for near in nears:
        half = near.shape[0]
        far = lax.ppermute(near, "dp", [(i, i ^ 1) for i in range(places)])
        whole = jnp.zeros((2 * half,) + near.shape[1:], near.dtype)
        whole = lax.dynamic_update_slice_in_dim(whole, near, core * half, 0)
        got.append(lax.dynamic_update_slice_in_dim(whole, far, (1 - core) * half, 0))
    return got


def gathered_parts(nears, own=None):
    half = nears[0].shape[0]
    layout, parts, base = [], [], 0
    if own is not None:
        layout, parts, base = [(0, 0, True)], [own], own.shape[0]
    if half % 16:
        return [(0, 0, True)], [jnp.concatenate(parts + with_far_halves(nears), axis=0)]
    places = lax.axis_size("dp")
    for near in nears:
        far = lax.ppermute(near, "dp", [(i, i ^ 1) for i in range(places)])
        layout += [(base, half, True), (base, half, False)]
        parts += [near, far]
        base += 2 * half
    return layout, parts


def after_own(gathered, own):
    layout, parts = gathered
    return [(0, 0, True)] + [(base + own.shape[0], half, near) for base, half, near in layout], [
        own
    ] + parts


def home(parts):
    total = parts[0].astype(F32)
    for steps in range(1, len(parts)):
        total = total + shift_mp(parts[steps], -steps).astype(F32)
    return total


def scatter_dp(part):
    return lax.psum_scatter(part, "dp", scatter_dimension=0, tiled=True)


def local(
    tokens, conditioning, kept_ids, ada_weight, ada_bias, attn_qkv, attn_out, mlp_up, mlp_down,
    rel_table, grad_out_kept, grad_out_full,
):
    ways = lax.axis_size("mp")
    place = lax.axis_index("mp")
    images_group = conditioning.shape[0]
    images = images_group // ways
    width = tokens.shape[1]
    keep = kept_ids.shape[1]
    padded = -(-keep // 64) * 64
    per_block = rel_table.shape[0]
    cols = ada_bias.shape[0]

    silu_cond = jax.nn.silu(conditioning.astype(F32)).astype(BF)
    columns = (jnp.dot(silu_cond, ada_weight, preferred_element_type=F32) + ada_bias).astype(BF)
    near_o = near_halves(attn_out)
    mod = lax.all_to_all(columns, "mp", split_axis=0, concat_axis=1, tiled=True)
    mod = jnp.pad(mod.astype(F32).reshape(images, 6, width), ((0, 0), (0, 2), (0, 0)))

    weight_own = jnp.transpose(attn_qkv.reshape(width, -1))
    tables = [rel_table] + [shift_mp(rel_table, s) for s in range(1, ways)]
    mod, tables, near_o, weight_sent = lax.optimization_barrier(
        (mod, tables, near_o, weight_own)
    )
    near_w = near_halves(weight_sent)
    fetch = ways == 2 and lax.axis_size("dp") % 4 == 0 and mlp_up.shape[0] % 32 == 0
    fetch = fetch and mlp_down.shape[0] % 64 == 0
    bias = bias_whole(jnp.concatenate(tables, axis=0))

    own_kept = lax.dynamic_slice_in_dim(kept_ids, place * images, images, 0)
    own_kept = jnp.pad(own_kept, ((0, 0), (0, padded - keep)), constant_values=-1)
    pick = (own_kept[:, :, None] == jnp.arange(PATCHES, dtype=jnp.int32)).astype(BF)
    grads = jnp.concatenate(
        [
            grad_out_full.reshape(images, PATCHES, width),
            jnp.pad(
                grad_out_kept.reshape(images, keep, width), ((0, 0), (0, padded - keep), (0, 0))
            ),
        ],
        axis=1,
    )
    dmlp = (mod[:, 5:6] * grads.astype(F32)).astype(BF).reshape(-1, width)
    grads = grads.reshape(-1, width)

    own = own_heads(tokens, mod, pick, bias, weight_own, per_block)
    near_w, near_o, own = lax.optimization_barrier((near_w, near_o, own))
    first = own[0]
    weight_others = gathered_parts(near_w)
    weight = after_own(weight_others, weight_own)
    out_weight = gathered_parts(near_o, attn_out)
    cut = (mlp_up.shape[0] * 6 // 18) // 16 * 16
    qkv, att, lse, middle, second, branch, *near_up = forward(
        own, tokens, mod, pick, bias, weight_others, out_weight, per_block,
        mlp_up if fetch else None, cut,
    )
    (branch_mlp, dsecond, grads_own, *whole), tile_own = mlp(
        second, dmlp, mlp_up, mlp_down, None, (near_up[0], mlp_up, mlp_down) if fetch else None
    )
    if fetch:
        up_others, down_others = [whole[0]], [whole[1]]
    else:
        up_others = with_far_halves(near_halves(mlp_up))
        down_others = with_far_halves(near_halves(mlp_down))
    reduced = [scatter_dp(grads_own)]
    for up, down in zip(up_others, down_others):
        (branch_mlp, dsecond, grads_next), _ = mlp(
            second, dmlp, up, down, (branch_mlp, dsecond)
        )
        reduced.append(scatter_dp(grads_next))
    out_full, out_kept, dtok, dmod, dattn, dqkv, strips = backward(
        tokens, mod, pick, bias, qkv, lse, middle, branch, branch_mlp, dsecond, grads,
        weight, out_weight, per_block, keep,
    )
    proj_block, out_block = weight_own.shape[0], attn_out.shape[0]
    dqkv, reduced[0] = lax.optimization_barrier((dqkv, reduced[0]))
    dtables = table_of_strips(strips)
    pieces = cols // width
    used = images * (pieces + 1) + per_block
    here = can_sum_here(width, dqkv.shape[0], att.shape[0]) and cols % width == 0
    here = here and used <= 32 and pieces + per_block <= 16 and pieces <= 3
    if here:
        own_cond_rows = lax.dynamic_slice_in_dim(silu_cond, place * images, images, 0)
        packs = []
        for steps in range(ways):
            at = (place + steps) % ways
            table = dtables[steps * per_block : (steps + 1) * per_block]
            pack = jnp.concatenate(
                [
                    lax.dynamic_slice_in_dim(dmod, at * pieces, pieces, 1)
                    .astype(BF)
                    .reshape(-1, width),
                    own_cond_rows,
                    jnp.pad(table, ((0, 0), (0, width - BUCKETS))).astype(BF),
                ],
                axis=0,
            )
            packs.append(jnp.pad(pack, ((0, 32 - used), (0, 0))))
        attn_total, grad_ada_weight, grad_ada_bias, dtable, grad_silu = attn_grads(
            first, dattn, dqkv, att, *packs, ada_weight, images, per_block
        )
    else:
        dweight = dot(first, dqkv, (0, 1)).astype(BF)
        dout_t = dot(dattn, att, (0, 1)).astype(BF)
        attn_sums = scatter_dp(jnp.concatenate([dweight, dout_t], axis=1))
        dmod_rows = dmod[:, :6].reshape(images, 6 * width)
        dcolumns = lax.all_to_all(dmod_rows, "mp", split_axis=1, concat_axis=0, tiled=True)
        dtable = home(list(jnp.split(dtables, ways, axis=0)))
        all_columns = lax.all_gather(dcolumns, "dp", axis=0, tiled=True)
        dtable = lax.psum(dtable, "dp")
        all_cond = lax.all_gather(silu_cond, "dp", axis=0, tiled=True).astype(F32)
        slice_width = width // lax.axis_size("dp")
        cond_slice = lax.dynamic_slice_in_dim(
            all_cond, lax.axis_index("dp") * slice_width, slice_width, 1
        )
        grad_ada_weight = lax.dot_general(
            cond_slice, all_columns, (((0,), (0,)), ((), ())), precision=PRECISE
        )
        grad_ada_bias = jnp.sum(all_columns, axis=0)
        dcolumns_high = dcolumns.astype(BF)
        dcolumns_low = (dcolumns - dcolumns_high.astype(F32)).astype(BF)
        silu_part = nt(jnp.concatenate([dcolumns_high, dcolumns_low], axis=0), ada_weight)
        silu_part = silu_part[:images_group] + silu_part[images_group:]
        shares = lax.all_to_all(
            silu_part.astype(BF).reshape(ways, images, width), "mp", split_axis=0, concat_axis=0,
            tiled=True,
        )
        grad_silu = jnp.sum(shares.astype(F32), axis=0)
        split = ways * proj_block
        attn_total = home(
            [
                jnp.concatenate(
                    [
                        attn_sums[:, j * proj_block : (j + 1) * proj_block],
                        attn_sums[:, split + j * out_block : split + (j + 1) * out_block],
                    ],
                    axis=1,
                )
                for j in range(ways)
            ]
        )
    mlp_grads = home(reduced)
    attn_total = attn_total.astype(F32)
    grad_up, grad_down_t = split_mlp_grads(mlp_grads, tile_own)
    grad_qkv = attn_total[:, :proj_block].reshape(-1, 3, proj_block // 3)
    grad_out = jnp.transpose(attn_total[:, proj_block:])

    own_cond = lax.dynamic_slice_in_dim(conditioning, place * images, images, 0).astype(F32)
    grad_cond = jax.vjp(jax.nn.silu, own_cond)[1](grad_silu)[0].astype(BF)

    return (
        out_kept, out_full, dtok, grad_cond, grad_ada_weight, grad_ada_bias, grad_qkv, grad_out,
        grad_up, jnp.transpose(grad_down_t), dtable,
    )


def solution(mesh):
    both = P(("dp", "mp"), None)
    return jax.shard_map(
        local,
        mesh=mesh,
        in_specs=(
            both, P("dp", None), P("dp", None), P(None, "mp"), P("mp"), P(None, None, "mp"),
            P("mp", None), P(None, "mp"), P("mp", None), P("mp", None), both, both,
        ),
        out_specs=(
            both, both, both, both, P("dp", "mp"), P("mp"), P("dp", None, "mp"), P("mp", "dp"),
            P("dp", "mp"), P("mp", "dp"), P("mp", None),
        ),
        check_vma=False,
    )
```

```python
import functools
import math

import jax
import jax.numpy as jnp
import numpy as np
from jax import lax
from jax.experimental import pallas as pl
from jax.experimental.pallas import tpu as pltpu
from jax.sharding import PartitionSpec as P

HEAD_DIM = 72
GRID = 16
PATCHES = 256
BUCKETS = 961
SPAN = 2 * GRID - 1
EPSILON = 1e-06
PRECISE = lax.Precision.HIGHEST
BF = jnp.bfloat16
F32 = jnp.float32
LOG2E = math.log2(math.e)
VMEM_LIMIT = 60 * 1024 * 1024


def dot(a, b, dims):
    return lax.dot_general(a, b, ((dims[0:1], dims[1:2]), ((), ())), preferred_element_type=F32)


def nn(a, b):
    return dot(a, b, (1, 0))


def nt(a, b):
    return dot(a, b, (1, 1))


def tn(a, b):
    return dot(a, b, (0, 0))


def normalize(rows):
    centered = rows - jnp.mean(rows, axis=-1, keepdims=True)
    inverse = lax.rsqrt(jnp.mean(centered * centered, axis=-1, keepdims=True) + EPSILON)
    return centered * inverse, inverse


def norm_back(normed, inverse, upstream):
    return inverse * (
        upstream
        - jnp.mean(upstream, axis=-1, keepdims=True)
        - normed * jnp.mean(upstream * normed, axis=-1, keepdims=True)
    )


def params(n_grid=1):
    return pltpu.CompilerParams(
        vmem_limit_bytes=VMEM_LIMIT, dimension_semantics=("arbitrary",) * n_grid
    )


def cost(flops, bytes_accessed, transcendentals=0):
    return pl.CostEstimate(
        flops=int(flops), bytes_accessed=int(bytes_accessed), transcendentals=int(transcendentals)
    )


def const_spec(shape):
    return pl.BlockSpec(shape, lambda *_: (0,) * len(shape), pipeline_mode=pl.Buffered(1))


def bias_kernel(strip_ref, bias_ref):
    strip = strip_ref[0]
    for key_row in range(GRID):
        start = (GRID - 1 - key_row) * GRID
        bias_ref[0, key_row * GRID : (key_row + 1) * GRID, :] = strip[:, start : start + PATCHES]


def bias_whole(table):
    heads = table.shape[0]
    grid_table = table.reshape(heads * SPAN, SPAN) * LOG2E
    place = np.arange(GRID)
    gap = place[None, :] - place[:, None] + GRID - 1
    chooser = (np.arange(SPAN)[:, None, None] == gap[None]).astype(np.float32)
    strip = jnp.dot(grid_table, chooser.reshape(SPAN, GRID * GRID), precision=PRECISE)
    strip = strip.reshape(heads, SPAN, GRID, GRID).transpose(0, 2, 1, 3)
    strip = strip.reshape(heads, GRID, SPAN * GRID)
    strip = jnp.pad(strip, ((0, 0), (0, 0), (0, 512 - SPAN * GRID)))
    return pl.pallas_call(
        bias_kernel,
        grid=(heads,),
        in_specs=[pl.BlockSpec((1, GRID, 512), lambda h: (h, 0, 0))],
        out_specs=pl.BlockSpec((1, PATCHES, PATCHES), lambda h: (h, 0, 0)),
        out_shape=jax.ShapeDtypeStruct((heads, PATCHES, PATCHES), F32),
        compiler_params=params(),
        cost_estimate=cost(1e6, 1e5),
    )(strip)


def table_of_strips(strips):
    heads = strips.shape[0]
    parts = strips[:, :, : SPAN * GRID].reshape(heads, GRID, SPAN, GRID)
    total = jnp.zeros((heads, SPAN, SPAN), F32)
    for c in range(GRID):
        total = total + jnp.pad(parts[:, c], ((0, 0), (0, 0), (GRID - 1 - c, c)))
    return total.reshape(heads, BUCKETS)


def head_rows(head, per_block):
    base = (head // per_block) * (3 * per_block * HEAD_DIM) + (head % per_block) * HEAD_DIM
    step = per_block * HEAD_DIM
    return [pl.ds(pl.multiple_of(base + c * step, 8), HEAD_DIM) for c in range(3)]


def key_mask(pick):
    ones = jnp.ones((pick.shape[0], PATCHES), BF)
    return (tn(pick, ones) - 1.0) * 1e30


def part_copies(layout, parts, whole, sems):
    core = lax.axis_index("dp") % 2
    copies = []
    for index, ((base, half, near), part) in enumerate(zip(layout, parts)):
        start = base + (core if near else 1 - core) * half
        rows = pl.ds(pl.multiple_of(start, 16), part.shape[0])
        copies.append(pltpu.make_async_copy(part, whole.at[rows, :], sems.at[index]))
    return copies


def run_copies(copies):
    for copy in copies:
        copy.start()
    for copy in copies:
        copy.wait()


def core_rows(half, skip, count):
    start = (lax.axis_index("dp") % 2) * half + skip
    return pl.ds(pl.multiple_of(start, 16), count)


def fetch_copy(own, rows, target, sems, at):
    return pltpu.make_async_remote_copy(
        src_ref=own.at[rows, :],
        dst_ref=target,
        send_sem=sems.at[at],
        recv_sem=sems.at[at + 1],
        device_id={"mp": 1 - lax.axis_index("mp")},
        device_id_type=pl.DeviceIdType.MESH,
    )


def core_copy(source, target, sems, at):
    place = lax.axis_index("dp")
    return pltpu.make_async_remote_copy(
        src_ref=source,
        dst_ref=target,
        send_sem=sems.at[at],
        recv_sem=sems.at[at + 1],
        device_id={"dp": place + 1 - 2 * (place % 2)},
        device_id_type=pl.DeviceIdType.MESH,
    )


def greet_peers(bits):
    barrier = pltpu.get_barrier_semaphore()
    peers = [{"mp": 1 - lax.axis_index("mp")}]
    place = lax.axis_index("dp")
    for bit in bits:
        peers.append({"dp": place + bit - 2 * bit * place_bit(place, bit)})
    for peer in peers:
        pl.semaphore_signal(
            barrier, inc=1, device_id=peer, device_id_type=pl.DeviceIdType.MESH
        )
    pl.semaphore_wait(barrier, len(peers))


def project(weight_ref, first, qkv_s, qkv_ref, base):
    step = weight_ref.shape[0] // 3
    for c in range(3):
        part = nt(weight_ref[c * step : (c + 1) * step, :], first)
        qkv_s[c * step : (c + 1) * step, :] = part
        qkv_ref[base + c * step : base + (c + 1) * step, :] = part.astype(BF)


def attend_heads(per_block, first_head, qkv_s, bias_ref, mask, att_s, attk_s, lse_s):
    scale = HEAD_DIM ** (-0.5) * LOG2E
    heads = qkv_s.shape[0] // (3 * HEAD_DIM)

    def one_head(head, carry):
        q_at, k_at, v_at = head_rows(head, per_block)
        queries = qkv_s[q_at, :].astype(BF)
        keys = qkv_s[k_at, :].astype(BF)
        values = qkv_s[v_at, :].astype(BF)
        scores = tn(keys, queries) * scale + bias_ref[first_head + head]
        here = pl.ds(pl.multiple_of(head * HEAD_DIM, 8), HEAD_DIM)

        def attend(scores):
            top = jnp.max(scores, axis=0, keepdims=True)
            weights = jnp.exp2(scores - top)
            total = jnp.sum(weights, axis=0, keepdims=True)
            probs = (weights * (1.0 / total)).astype(BF)
            return nn(values, probs), top + jnp.log2(total)

        att_s[here, :], lse_s[pl.ds(head, 1), :] = attend(scores)
        attk_s[here, :], lse_s[pl.ds(heads + head, 1), :] = attend(scores + mask)
        return carry

    lax.fori_loop(0, heads, one_head, 0, unroll=4 if heads % 4 == 0 else 2)


def own_heads_kernel(
    per_block, tok_ref, mod_ref, pick_ref, bias_ref, weight_ref,
    first_ref, qkv_ref, att_ref, lse_ref, qkv_s, att_s, attk_s, lse_s,
):
    shift_one, scale_one = mod_ref[0, 0:1], mod_ref[0, 1:2]
    normed, _ = normalize(tok_ref[...].astype(F32))
    first = (normed * (1.0 + scale_one) + shift_one).astype(BF)
    first_ref[...] = first
    project(weight_ref, first, qkv_s, qkv_ref, 0)
    mask = key_mask(pick_ref[0])
    attend_heads(per_block, 0, qkv_s, bias_ref, mask, att_s, attk_s, lse_s)
    att_ref[:, :PATCHES] = att_s[...].astype(BF)
    att_ref[:, PATCHES:] = attk_s[...].astype(BF)
    lse_ref[0] = lse_s[...]


def own_heads(tokens, mod, pick, bias, weight, per_block):
    images, padded = pick.shape[0], pick.shape[1]
    width = tokens.shape[1]
    proj = weight.shape[0]
    heads = proj // (3 * HEAD_DIM)
    inner = heads * HEAD_DIM
    return pl.pallas_call(
        functools.partial(own_heads_kernel, per_block),
        grid=(images,),
        in_specs=[
            pl.BlockSpec((PATCHES, width), lambda i: (i, 0)),
            pl.BlockSpec((1, 8, width), lambda i: (i, 0, 0)),
            pl.BlockSpec((1, padded, PATCHES), lambda i: (i, 0, 0)),
            const_spec(bias.shape),
            const_spec(weight.shape),
        ],
        out_specs=[
            pl.BlockSpec((PATCHES, width), lambda i: (i, 0)),
            pl.BlockSpec((proj, PATCHES), lambda i: (0, i)),
            pl.BlockSpec((inner, 2 * PATCHES), lambda i: (0, i)),
            pl.BlockSpec((1, 2 * heads, PATCHES), lambda i: (i, 0, 0)),
        ],
        out_shape=[
            jax.ShapeDtypeStruct((images * PATCHES, width), BF),
            jax.ShapeDtypeStruct((proj, images * PATCHES), BF),
            jax.ShapeDtypeStruct((inner, images * 2 * PATCHES), BF),
            jax.ShapeDtypeStruct((images, 2 * heads, PATCHES), F32),
        ],
        scratch_shapes=[
            pltpu.VMEM((proj, PATCHES), F32),
            pltpu.VMEM((inner, PATCHES), F32),
            pltpu.VMEM((inner, PATCHES), F32),
            pltpu.VMEM((2 * heads, PATCHES), F32),
        ],
        compiler_params=params(),
        cost_estimate=cost(1e7, 1e5),
    )(tokens, mod, pick, bias, weight)


def forward_kernel(per_block, weight_layout, out_layout, fetch, *refs):
    first_ref, own_qkv, own_att, own_lse, tok_ref, mod_ref, pick_ref, bias_ref = refs[:8]
    refs = refs[8:]
    weight_parts, refs = refs[: len(weight_layout)], refs[len(weight_layout) :]
    out_parts, refs = refs[: len(out_layout)], refs[len(out_layout) :]
    if fetch:
        send_ref, refs = refs[0], refs[1:]
    qkv_ref, att_ref, lse_ref, middle_ref, second_ref, branch_ref = refs[:6]
    refs = refs[6:]
    if fetch:
        got_ref, refs = refs[0], refs[1:]
    qkv_s, att_s, attk_s, lse_s, weight_ref, out_w_ref, part_sems, fetch_sems = refs

    def fetching():
        half = send_ref.shape[0] // 2
        return fetch_copy(send_ref, core_rows(half, 0, got_ref.shape[0]), got_ref, fetch_sems, 0)

    @pl.when(pl.program_id(0) == 0)
    def _():
        copies = part_copies(weight_layout, weight_parts, weight_ref, part_sems.at[0])
        copies += part_copies(out_layout, out_parts, out_w_ref, part_sems.at[1])
        if fetch:
            greet_peers(())
            fetching().start()
        run_copies(copies)

    own = own_qkv.shape[0]
    own_inner = own // 3
    own_count = own_inner // HEAD_DIM
    heads = bias_ref.shape[0]
    others = heads - own_count
    pick = pick_ref[0]
    qkv_ref[:own, :] = own_qkv[...]
    project(weight_ref, first_ref[...], qkv_s, qkv_ref, own)
    mask = key_mask(pick)
    attend_heads(per_block, own_count, qkv_s, bias_ref, mask, att_s, attk_s, lse_s)
    att_ref[:own_inner, :] = own_att[...]
    att_ref[own_inner:, :PATCHES] = att_s[...].astype(BF)
    att_ref[own_inner:, PATCHES:] = attk_s[...].astype(BF)
    lse_ref[0, :own_count, :] = own_lse[0, :own_count]
    lse_ref[0, own_count:heads, :] = lse_s[:others]
    lse_ref[0, heads : heads + own_count, :] = own_lse[0, own_count:]
    lse_ref[0, heads + own_count :, :] = lse_s[others:]
    gate_one = mod_ref[0, 2:3]
    shift_two, scale_two = mod_ref[0, 3:4], mod_ref[0, 4:5]
    out_w = out_w_ref[...]
    kept_att = nt(pick, att_ref[:, PATCHES:]).astype(BF)
    for rows, source, residual in (
        (slice(0, PATCHES), att_ref[:, :PATCHES].T, tok_ref[...].astype(F32)),
        (slice(PATCHES, PATCHES + pick.shape[0]), kept_att, nn(pick, tok_ref[...])),
    ):
        branch = nn(source, out_w)
        branch_ref[rows, :] = branch.astype(BF)
        middle = residual + gate_one * branch
        middle_ref[rows, :] = middle
        second_ref[rows, :] = (normalize(middle)[0] * (1.0 + scale_two) + shift_two).astype(BF)
    if fetch:

        @pl.when(pl.program_id(0) == pl.num_programs(0) - 1)
        def _():
            fetching().wait()


def whole_rows(layout, parts):
    return sum(part.shape[0] for part in parts)


ANYWHERE = pl.BlockSpec(memory_space=pl.ANY)


def forward(own, tokens, mod, pick, bias, weight, out_weight, per_block, send=None, count=0):
    images, padded = pick.shape[0], pick.shape[1]
    width = tokens.shape[1]
    rows = PATCHES + padded
    heads = bias.shape[0]
    (weight_layout, weight_parts), (out_layout, out_parts) = weight, out_weight
    proj_others = whole_rows(*weight)
    proj = own[1].shape[0] + proj_others
    own_inner, own_heads_count = own[2].shape[0], own[3].shape[1] // 2
    others = heads - own_heads_count
    fetch = send is not None
    most = max(len(weight_parts), len(out_parts))
    extra_shapes, extra = [], []
    compiler_params = params()
    if fetch:
        extra_shapes = [jax.ShapeDtypeStruct((count, send.shape[1]), BF)]
        extra = [send]
        compiler_params = pltpu.CompilerParams(
            vmem_limit_bytes=VMEM_LIMIT, dimension_semantics=("arbitrary",),
            collective_id=2, has_side_effects=True,
        )
    by_row = pl.BlockSpec((rows, width), lambda i: (i, 0))
    return pl.pallas_call(
        functools.partial(forward_kernel, per_block, weight_layout, out_layout, fetch),
        grid=(images,),
        in_specs=[
            pl.BlockSpec((PATCHES, width), lambda i: (i, 0)),
            pl.BlockSpec((own[1].shape[0], PATCHES), lambda i: (0, i)),
            pl.BlockSpec((own_inner, 2 * PATCHES), lambda i: (0, i)),
            pl.BlockSpec((1, 2 * own_heads_count, PATCHES), lambda i: (i, 0, 0)),
            pl.BlockSpec((PATCHES, width), lambda i: (i, 0)),
            pl.BlockSpec((1, 8, width), lambda i: (i, 0, 0)),
            pl.BlockSpec((1, padded, PATCHES), lambda i: (i, 0, 0)),
            const_spec(bias.shape),
        ]
        + [ANYWHERE] * (len(weight_parts) + len(out_parts) + len(extra)),
        out_specs=[
            pl.BlockSpec((proj, PATCHES), lambda i: (0, i)),
            pl.BlockSpec((width, 2 * PATCHES), lambda i: (0, i)),
            pl.BlockSpec((1, 2 * heads, PATCHES), lambda i: (i, 0, 0)),
            by_row,
            by_row,
            by_row,
        ]
        + [ANYWHERE] * len(extra),
        out_shape=[
            jax.ShapeDtypeStruct((proj, images * PATCHES), BF),
            jax.ShapeDtypeStruct((width, images * 2 * PATCHES), BF),
            jax.ShapeDtypeStruct((images, 2 * heads, PATCHES), F32),
            jax.ShapeDtypeStruct((images * rows, width), F32),
            jax.ShapeDtypeStruct((images * rows, width), BF),
            jax.ShapeDtypeStruct((images * rows, width), BF),
        ]
        + extra_shapes,
        scratch_shapes=[
            pltpu.VMEM((proj_others, PATCHES), F32),
            pltpu.VMEM((others * HEAD_DIM, PATCHES), F32),
            pltpu.VMEM((others * HEAD_DIM, PATCHES), F32),
            pltpu.VMEM((2 * others, PATCHES), F32),
            pltpu.VMEM((proj_others, width), BF),
            pltpu.VMEM((width, width), BF),
            pltpu.SemaphoreType.DMA((2, most)),
            pltpu.SemaphoreType.DMA((2,)),
        ],
        compiler_params=compiler_params,
        cost_estimate=cost(images * 2e9, images * 8e6),
    )(*own, tokens, mod, pick, bias, *weight_parts, *out_parts, *extra)


def gelu_pair(pre):
    root = math.sqrt(2.0 / math.pi)
    square = pre * pre
    bend = jnp.tanh(pre * (root + (root * 0.044715) * square))
    half = 0.5 + 0.5 * bend
    slope = half + (0.5 * pre) * (1.0 - bend * bend) * (root + (3.0 * root * 0.044715) * square)
    return pre * half, slope


def mlp_kernel(
    chunk, fresh, fetch, second_ref, dmlp_ref, up_ref, down_ref, *refs
):
    if fetch:
        near_ref, send_up, send_down = refs[:3]
        *refs, moves, fetch_sems = refs[3:]
        up_all, down_all = refs[3:5]
        refs = refs[:3] + refs[5:]
    if fresh:
        branch_ref, dsecond_ref, grads_ref, second_t, dmlp_t, hidden_s, dpre_s, sem = refs
    else:
        branch_in, dsecond_in, branch_ref, dsecond_ref, grads_ref = refs[:5]
        second_t, dmlp_t, hidden_s, dpre_s, sem = refs[5:]
    rows = second_ref.shape[0]
    tile = up_ref.shape[1]
    width = second_ref.shape[1]

    if fetch:
        up_half, down_half = up_all.shape[0] // 2, down_all.shape[0] // 2
        cut, quarter = near_ref.shape[0], down_half // 2
        place = lax.axis_index("dp")
        side = place_bit(place, 2)
        up_a = up_all.at[core_rows(up_half, 0, cut), :]
        up_b = up_all.at[core_rows(up_half, cut, up_half - cut), :]
        down_a = down_all.at[core_rows(down_half, 0, down_half), :]
        down_q_rows = core_rows(down_half, side * quarter, quarter)
        down_q = down_all.at[down_q_rows, :]
        lay_a = pltpu.make_async_copy(near_ref, up_a, moves.at[0])
        pass_a = core_copy(near_ref, up_a, moves, 1)
        pass_b = core_copy(up_b, up_b, moves, 3)
        pass_down = core_copy(down_a, down_a, moves, 5)
        pass_y = pltpu.make_async_remote_copy(
            src_ref=down_q,
            dst_ref=down_q,
            send_sem=moves.at[7],
            recv_sem=moves.at[8],
            device_id={"dp": place + 2 - 4 * side},
            device_id_type=pl.DeviceIdType.MESH,
        )
        fetch_b = fetch_copy(
            send_up, core_rows(up_half, cut, up_half - cut), up_b, fetch_sems, 0
        )
        fetch_down = fetch_copy(send_down, down_q_rows, down_q, fetch_sems, 2)
    step, last = pl.program_id(0), pl.num_programs(0) - 1

    @pl.when(step == 0)
    def _():
        if fetch:
            greet_peers((1, 2))
            fetch_down.start()
            lay_a.start()
            pass_a.start()
        if fresh:
            branch_ref[...] = jnp.zeros_like(branch_ref)
            dsecond_ref[...] = jnp.zeros_like(dsecond_ref)
        else:
            one = pltpu.make_async_copy(branch_in, branch_ref, sem.at[0])
            two = pltpu.make_async_copy(dsecond_in, dsecond_ref, sem.at[1])
            one.start()
            two.start()
        for at in range(0, rows, chunk):
            second_t[:, at : at + chunk] = second_ref[at : at + chunk, :].T
            dmlp_t[:, at : at + chunk] = dmlp_ref[at : at + chunk, :].T
        if not fresh:
            one.wait()
            two.wait()

    def one_chunk(index, carry):
        at = pl.ds(pl.multiple_of(index * chunk, chunk), chunk)
        pre = nn(second_ref[at, :], up_ref[...])
        dhidden = nt(dmlp_ref[at, :], down_ref[...])
        value, slope = gelu_pair(pre)
        hidden = value.astype(BF)
        dpre = (dhidden * slope).astype(BF)
        hidden_s[at, :] = hidden
        dpre_s[at, :] = dpre
        branch_ref[at, :] += nn(hidden, down_ref[...])
        dsecond_ref[at, :] += nt(dpre, up_ref[...])
        if fetch:

            @pl.when(jnp.logical_and(step == jnp.minimum(1, last), index == 0))
            def _():
                fetch_down.wait_recv()
                pass_y.start()
                fetch_b.start()

        return carry

    lax.fori_loop(0, rows // chunk, one_chunk, 0)
    if fetch:

        @pl.when(step == last)
        def _():
            fetch_b.wait_recv()
            pass_b.start()
            pass_y.wait_recv()
            pass_down.start()

    part = width // 3
    for c in range(3):
        at = slice(c * part, (c + 1) * part)
        grads_ref[at, :tile] = nn(second_t[at, :], dpre_s[...]).astype(BF)
        grads_ref[at, tile:] = nn(dmlp_t[at, :], hidden_s[...]).astype(BF)

    if fetch:

        @pl.when(step == last)
        def _():
            for copy in (lay_a, pass_a, pass_b, pass_down):
                copy.wait()
            pass_y.wait_send()
            fetch_b.wait_send()
            fetch_down.wait_send()


def mlp_chunk(rows):
    for chunk in (896, 448, 64):
        if rows % chunk == 0:
            return chunk
    return rows


def mlp(second, dmlp, up, down, sums=None, fetch=None):
    rows, width = second.shape
    hidden = up.shape[1]
    tile = 768 if hidden % 768 == 0 else hidden
    fresh = sums is None
    chunk = mlp_chunk(rows)
    in_specs = [
        const_spec(second.shape),
        const_spec(second.shape),
        pl.BlockSpec((width, tile), lambda f: (0, f)),
        pl.BlockSpec((tile, width), lambda f: (f, 0)),
    ]
    operands = [second, dmlp, up, down]
    out_specs = [
        const_spec(second.shape),
        const_spec(second.shape),
        pl.BlockSpec((width, 2 * tile), lambda f: (0, f)),
    ]
    out_shape = [
        jax.ShapeDtypeStruct(second.shape, F32),
        jax.ShapeDtypeStruct(second.shape, F32),
        jax.ShapeDtypeStruct((width, 2 * hidden), BF),
    ]
    scratch = [
        pltpu.VMEM((width, rows), BF),
        pltpu.VMEM((width, rows), BF),
        pltpu.VMEM((rows, tile), BF),
        pltpu.VMEM((rows, tile), BF),
        pltpu.SemaphoreType.DMA((2,)),
    ]
    compiler_params = params()
    if not fresh:
        in_specs += [ANYWHERE] * 2
        operands += list(sums)
    if fetch is not None:
        in_specs += [ANYWHERE] * 3
        operands += list(fetch)
        out_specs += [ANYWHERE] * 2
        out_shape += [jax.ShapeDtypeStruct(up.shape, BF), jax.ShapeDtypeStruct(down.shape, BF)]
        scratch += [pltpu.SemaphoreType.DMA((9,)), pltpu.SemaphoreType.DMA((4,))]
        compiler_params = pltpu.CompilerParams(
            vmem_limit_bytes=VMEM_LIMIT, dimension_semantics=("arbitrary",),
            collective_id=3, has_side_effects=True,
        )
    return pl.pallas_call(
        functools.partial(mlp_kernel, chunk, fresh, fetch is not None),
        grid=(hidden // tile,),
        in_specs=in_specs,
        out_specs=out_specs,
        out_shape=out_shape,
        scratch_shapes=scratch,
        compiler_params=compiler_params,
        cost_estimate=cost(6e10, 6e7) if fresh else cost(1e7, 1e5),
    )(*operands), tile


def split_mlp_grads(grads, tile):
    parts = grads.reshape(grads.shape[0], -1, 2, tile)
    return (
        parts[:, :, 0].reshape(grads.shape[0], -1),
        parts[:, :, 1].reshape(grads.shape[0], -1),
    )


def backward_kernel(per_block, weight_layout, out_layout, *refs):
    count = len(weight_layout) + len(out_layout)
    weight_parts = refs[: len(weight_layout)]
    out_parts = refs[len(weight_layout) : count]
    weight_ref, out_w_ref, sems = refs[-3:]

    weight_copies = part_copies(weight_layout, weight_parts, weight_ref, sems.at[0])

    @pl.when(pl.program_id(0) == 0)
    def _():
        out_copies = part_copies(out_layout, out_parts, out_w_ref, sems.at[1])
        for copy in out_copies + weight_copies:
            copy.start()
        for copy in out_copies:
            copy.wait()

    def wait_weight():
        @pl.when(pl.program_id(0) == 0)
        def _():
            for copy in weight_copies:
                copy.wait()

    backward_body(per_block, wait_weight, weight_ref, out_w_ref, *refs[count:-3])


def backward_body(
    per_block, wait_weight, weight_ref, out_w_ref, tok_ref, mod_ref, pick_ref, bias_ref,
    qkv_ref, lse_ref, middle_ref, branch_ref, mlp_ref, dsecond_ref, grad_ref,
    out_full_ref, out_kept_ref, dtok_ref, dmod_ref, dattn_ref, dqkv_ref, strips_ref,
    qkv_s, datt_s, dattk_s, dscores_s,
):
    heads = bias_ref.shape[0]
    step = pl.program_id(0)
    shift_one, scale_one, gate_one = mod_ref[0, 0:1], mod_ref[0, 1:2], mod_ref[0, 2:3]
    scale_two, gate_two = mod_ref[0, 4:5], mod_ref[0, 5:6]
    pick = pick_ref[0]
    dmiddles = []
    sums = [0.0, 0.0, 0.0, 0.0]
    for rows, out_ref in (
        (slice(0, PATCHES), out_full_ref),
        (slice(PATCHES, PATCHES + pick.shape[0]), out_kept_ref),
    ):
        middle = middle_ref[rows, :]
        branch_mlp = mlp_ref[rows, :]
        dsecond = dsecond_ref[rows, :]
        grad = grad_ref[rows, :].astype(F32)
        out_ref[...] = (middle + gate_two * branch_mlp).astype(BF)
        normed, inverse = normalize(middle)
        dmiddle = grad + norm_back(normed, inverse, dsecond * (1.0 + scale_two))
        branch = branch_ref[rows, :].astype(F32)
        for c, term in enumerate(
            (dmiddle * branch, dsecond, dsecond * normed, grad * branch_mlp)
        ):
            sums[c] = sums[c] + jnp.sum(term, axis=0, keepdims=True)
        dmiddles.append(dmiddle)
    for c in range(4):
        dmod_ref[0, 2 + c : 3 + c, :] = sums[c]
    dattn = (gate_one * dmiddles[0]).astype(BF)
    dattn_kept = tn(pick, (gate_one * dmiddles[1]).astype(BF)).astype(BF)
    dattn_ref[:PATCHES, :] = dattn
    dattn_ref[PATCHES:, :] = dattn_kept
    high = dmiddles[1].astype(BF)
    low = (dmiddles[1] - high.astype(F32)).astype(BF)
    dresid = dmiddles[0] + tn(pick, high) + tn(pick, low)
    datt_s[...] = nt(out_w_ref[...], dattn)
    dattk_s[...] = nt(out_w_ref[...], dattn_kept)
    qkv_s[...] = qkv_ref[...].astype(F32)
    mask = key_mask(pick)
    scale = HEAD_DIM ** (-0.5)

    @pl.when(step == 0)
    def _():
        dscores_s[...] = jnp.zeros_like(dscores_s)

    def one_head(head, carry):
        q_at, k_at, v_at = head_rows(head, per_block)
        queries = qkv_s[q_at, :].astype(BF)
        keys = qkv_s[k_at, :].astype(BF)
        values = qkv_s[v_at, :].astype(BF)
        here = pl.ds(pl.multiple_of(head * HEAD_DIM, 8), HEAD_DIM)
        scores = tn(keys, queries) * (scale * LOG2E) + bias_ref[head]

        def pull(scores, top, upstream):
            probs = jnp.exp2(scores - top)
            dprobs = tn(values, upstream)
            dvalues = nt(upstream, probs.astype(BF))
            weighted = jnp.sum(probs * dprobs, axis=0, keepdims=True)
            return probs * (dprobs - weighted), dvalues

        dscores, dvalues = pull(
            scores, lse_ref[0, pl.ds(head, 1), :], datt_s[here, :].astype(BF)
        )
        dscores_kept, dvalues_kept = pull(
            scores + mask, lse_ref[0, pl.ds(heads + head, 1), :], dattk_s[here, :].astype(BF)
        )
        dscores = dscores + dscores_kept
        dscores_s[head] += dscores
        rounded = dscores.astype(BF)
        qkv_s[q_at, :] = nn(keys, rounded) * scale
        qkv_s[k_at, :] = nt(queries, rounded) * scale
        qkv_s[v_at, :] = dvalues + dvalues_kept
        return carry

    lax.fori_loop(0, heads, one_head, 0, unroll=4)
    dqkv = qkv_s[...].astype(BF)
    dqkv_ref[...] = dqkv
    wait_weight()
    dfirst = tn(dqkv, weight_ref[...])
    normed, inverse = normalize(tok_ref[...].astype(F32))
    dmod_ref[0, 0:1, :] = jnp.sum(dfirst, axis=0, keepdims=True)
    dmod_ref[0, 1:2, :] = jnp.sum(dfirst * normed, axis=0, keepdims=True)
    dmod_ref[0, 6:8, :] = jnp.zeros((2, dfirst.shape[1]), F32)
    dtok_ref[...] = (dresid + norm_back(normed, inverse, dfirst * (1.0 + scale_one))).astype(BF)

    @pl.when(step == pl.num_programs(0) - 1)
    def _():
        def fold(head, carry):
            strip = jnp.zeros((GRID, 512), F32)
            for key_row in range(GRID):
                start = (GRID - 1 - key_row) * GRID
                block = dscores_s[head, key_row * GRID : (key_row + 1) * GRID, :]
                block = jnp.concatenate([block, jnp.zeros((GRID, 512 - PATCHES), F32)], axis=1)
                strip = strip + pltpu.roll(block, start, 1)
            strips_ref[head] = strip
            return carry

        lax.fori_loop(0, heads, fold, 0)


def backward(
    tokens, mod, pick, bias, qkv, lse, middle, branch, branch_mlp, dsecond, grads,
    weight, out_weight, per_block,
):
    (weight_layout, weight_parts), (out_layout, out_parts) = weight, out_weight
    most = max(len(weight_parts), len(out_parts))
    proj = whole_rows(*weight)
    images, padded = pick.shape[0], pick.shape[1]
    width = tokens.shape[1]
    rows = PATCHES + padded
    heads = bias.shape[0]
    by_row = pl.BlockSpec((rows, width), lambda i: (i, 0))
    return pl.pallas_call(
        functools.partial(backward_kernel, per_block, weight_layout, out_layout),
        grid=(images,),
        in_specs=[ANYWHERE] * (len(weight_parts) + len(out_parts))
        + [
            pl.BlockSpec((PATCHES, width), lambda i: (i, 0)),
            pl.BlockSpec((1, 8, width), lambda i: (i, 0, 0)),
            pl.BlockSpec((1, padded, PATCHES), lambda i: (i, 0, 0)),
            const_spec(bias.shape),
            pl.BlockSpec((proj, PATCHES), lambda i: (0, i)),
            pl.BlockSpec((1, 2 * heads, PATCHES), lambda i: (i, 0, 0)),
            by_row,
            by_row,
            by_row,
            by_row,
            by_row,
        ],
        out_specs=[
            pl.BlockSpec((PATCHES, width), lambda i: (i, 0)),
            pl.BlockSpec((padded, width), lambda i: (i, 0)),
            pl.BlockSpec((PATCHES, width), lambda i: (i, 0)),
            pl.BlockSpec((1, 8, width), lambda i: (i, 0, 0)),
            pl.BlockSpec((2 * PATCHES, width), lambda i: (i, 0)),
            pl.BlockSpec((proj, PATCHES), lambda i: (0, i)),
            const_spec((heads, GRID, 512)),
        ],
        out_shape=[
            jax.ShapeDtypeStruct((images * PATCHES, width), BF),
            jax.ShapeDtypeStruct((images * padded, width), BF),
            jax.ShapeDtypeStruct((images * PATCHES, width), BF),
            jax.ShapeDtypeStruct((images, 8, width), F32),
            jax.ShapeDtypeStruct((images * 2 * PATCHES, width), BF),
            jax.ShapeDtypeStruct((proj, images * PATCHES), BF),
            jax.ShapeDtypeStruct((heads, GRID, 512), F32),
        ],
        scratch_shapes=[
            pltpu.VMEM((proj, PATCHES), F32),
            pltpu.VMEM((width, PATCHES), F32),
            pltpu.VMEM((width, PATCHES), F32),
            pltpu.VMEM((heads, PATCHES, PATCHES), F32),
            pltpu.VMEM((proj, width), BF),
            pltpu.VMEM((width, width), BF),
            pltpu.SemaphoreType.DMA((2, most)),
        ],
        compiler_params=params(),
        cost_estimate=cost(1e7, 1e5),
    )(
        *weight_parts, *out_parts, tokens, mod, pick, bias, qkv, lse, middle, branch, branch_mlp,
        dsecond, grads,
    )


SUM_PLACES = 16
HALVING = (1, 2, 8)
FINAL = 4


def place_bit(place, bit):
    return (place // bit) % 2


def unit_start(owner, share):
    index = 0
    for bit in HALVING + (FINAL,):
        index = index * 2 + place_bit(owner, bit)
    return index * share


def store_by_owner(buffer, tile, at, block, share):
    first_owner = at // share
    owners = block.shape[0] // share
    for k in range(owners):
        owner = first_owner + k
        if place_bit(owner, FINAL):
            continue
        pair = k + FINAL
        both = jnp.concatenate(
            [block[k * share : (k + 1) * share], block[pair * share : (pair + 1) * share]], axis=0
        )
        start = unit_start(owner, share)
        buffer[tile, start : start + 2 * share, :] = both.astype(BF)


class GroupSum:
    def __init__(self, own, other, lands, land_other, land_cross, sends, recvs):
        self.own, self.other, self.lands = own, other, lands
        self.land_other, self.land_cross = land_other, land_cross
        self.sends, self.recvs = sends, recvs
        self.place = lax.axis_index("dp")
        self.rows = own.shape[1]

    def partner(self, bit):
        return {"dp": self.place + bit - 2 * bit * place_bit(self.place, bit)}

    def greet(self, barrier):
        for bit in HALVING + (FINAL,):
            pl.semaphore_signal(
                barrier, inc=1, device_id=self.partner(bit), device_id_type=pl.DeviceIdType.MESH
            )

    def spans(self, stage):
        start, size = 0, self.rows
        for k, bit in enumerate(HALVING):
            size = size // 2
            mine = place_bit(self.place, bit)
            if k == stage:
                return start + mine * size, start + (1 - mine) * size, size
            start = start + mine * size
        return start, start, size

    def remote(self, source, target, index, tile, peer):
        return pltpu.make_async_remote_copy(
            src_ref=source,
            dst_ref=target,
            send_sem=self.sends.at[index, tile],
            recv_sem=self.recvs.at[index, tile],
            device_id=peer,
            device_id_type=pl.DeviceIdType.MESH,
        )

    def copy(self, stage, tile):
        bit = (HALVING + (FINAL, HALVING[0]))[stage]
        buffer, land = (self.other, self.land_other) if stage == 4 else (self.own, self.lands[stage])
        _, away, size = self.spans(0 if stage == 4 else stage)
        rows = buffer.at[tile, pl.ds(pl.multiple_of(away, 16), size), :]
        return self.remote(rows, land.at[tile], stage, tile, self.partner(bit))

    def cross_rows(self, part):
        keep, away, size = self.spans(1)
        return (keep if part else away), size

    def cross(self, part, tile):
        start, size = self.cross_rows(part)
        base = self.spans(0)[0]
        return self.remote(
            self.other.at[tile, pl.ds(pl.multiple_of(start, 16), size), :],
            self.land_cross.at[tile, pl.ds(pl.multiple_of(start - base, 16), size), :],
            5 + part,
            tile,
            {"mp": 1 - lax.axis_index("mp")},
        )

    def total(self, stage, tile):
        self.copy(stage, tile).wait_recv()
        keep, _, size = self.spans(0 if stage == 4 else stage)
        at = pl.ds(pl.multiple_of(keep, 16), size)
        buffer, land = (self.other, self.land_other) if stage == 4 else (self.own, self.lands[stage])
        return buffer, at, buffer[tile, at, :].astype(F32) + land[tile].astype(F32)

    def add(self, stage, tile):
        buffer, at, total = self.total(stage, tile)
        buffer[tile, at, :] = total.astype(BF)

    def add_cross(self, part, tile):
        self.cross(part, tile).wait_recv()
        start, size = self.cross_rows(part)
        base = self.spans(0)[0]
        at = pl.ds(pl.multiple_of(start, 16), size)
        landed = pl.ds(pl.multiple_of(start - base, 16), size)
        total = self.own[tile, at, :].astype(F32) + self.land_cross[tile, landed, :].astype(F32)
        self.own[tile, at, :] = total.astype(BF)

    def wait_sends(self, tile):
        for stage in range(5):
            self.copy(stage, tile).wait_send()
        for part in range(2):
            self.cross(part, tile).wait_send()


def pack_slot(place):
    return sum(
        place_bit(place, SUM_PLACES >> (k + 1)) << k for k in range(SUM_PLACES.bit_length() - 1)
    )


class PackGather:
    def __init__(self, own, other, packs, sends, recvs):
        self.own, self.other, self.packs, self.sends, self.recvs = own, other, packs, sends, recvs
        self.place, self.side = lax.axis_index("dp"), lax.axis_index("mp")
        self.stages = SUM_PLACES.bit_length() - 1
        self.slot = pack_slot(self.place)

    def greet(self, barrier):
        pl.semaphore_signal(
            barrier, inc=1, device_id={"mp": 1 - self.side}, device_id_type=pl.DeviceIdType.MESH
        )

    def cross(self):
        return pltpu.make_async_remote_copy(
            src_ref=self.other,
            dst_ref=self.packs.at[self.slot, self.side],
            send_sem=self.sends.at[self.stages],
            recv_sem=self.recvs.at[self.stages],
            device_id={"mp": 1 - self.side},
            device_id_type=pl.DeviceIdType.MESH,
        )

    def copy(self, stage):
        size = 1 << stage
        bit = SUM_PLACES >> (stage + 1)
        rows = self.packs.at[pl.ds((self.slot // size) * size, size)]
        return pltpu.make_async_remote_copy(
            src_ref=rows,
            dst_ref=rows,
            send_sem=self.sends.at[stage],
            recv_sem=self.recvs.at[stage],
            device_id={"dp": self.place + bit - 2 * bit * place_bit(self.place, bit)},
            device_id_type=pl.DeviceIdType.MESH,
        )

    def start(self):
        self.packs[self.slot, self.side] = self.own[...]
        self.cross().start()

    def advance(self, stage):
        (self.cross() if stage == 0 else self.copy(stage - 1)).wait_recv()
        self.copy(stage).start()

    def finish(self):
        self.copy(self.stages - 1).wait_recv()
        self.cross().wait_send()
        for stage in range(self.stages):
            self.copy(stage).wait_send()


class SmallGrads:
    def __init__(
        self, images, pieces, table_rows, ring, ada, ada_s, part_s, silu_own, silu_got, sems
    ):
        self.images, self.pieces, self.table_rows = images, pieces, table_rows
        self.ring, self.ada, self.ada_s, self.part_s = ring, ada, ada_s, part_s
        self.silu_own, self.silu_got, self.sems = silu_own, silu_got, sems
        self.rows = ring.packs.shape[2]
        self.first_cond = images * pieces

    def row_of(self, shape, axis):
        return lax.broadcasted_iota(jnp.int32, shape, axis) & (self.rows - 1)

    def any_image(self, test):
        found = test(0)
        for image in range(1, self.images):
            found = jnp.logical_or(found, test(image))
        return found

    def of_piece(self, row, piece):
        return self.any_image(lambda image: row == image * self.pieces + piece)

    def piece(self, index):
        width = self.ada_s.shape[1]
        return pltpu.make_async_copy(
            self.ada.at[:, index * width : (index + 1) * width], self.ada_s, self.sems.at[0]
        )

    def exchange(self):
        return pltpu.make_async_remote_copy(
            src_ref=self.silu_own.at[1],
            dst_ref=self.silu_got,
            send_sem=self.sems.at[1],
            recv_sem=self.sems.at[2],
            device_id={"mp": 1 - self.ring.side},
            device_id_type=pl.DeviceIdType.MESH,
        )

    def add_piece(self, index):
        mine = self.ring.packs[self.ring.slot]
        mine = mine.reshape(2 * self.rows, mine.shape[-1]).astype(F32)
        masked = jnp.where(self.of_piece(self.row_of(mine.shape, 0), index), mine, 0.0)
        self.piece(index).wait()
        product = nt(masked.astype(BF), self.ada_s[...])
        if index:
            self.part_s[...] += product
        else:
            self.part_s[...] = product
        if index + 1 < self.pieces:
            self.piece(index + 1).start()
            return
        for k, side in enumerate((self.ring.side, 1 - self.ring.side)):
            block = self.part_s[pl.ds(pl.multiple_of(side * self.rows, 8), self.rows), :]
            found = [
                jnp.sum(block[n * self.pieces : (n + 1) * self.pieces], axis=0, keepdims=True)
                for n in range(self.images)
            ]
            found.append(jnp.zeros((self.silu_got.shape[0] - self.images, block.shape[1]), F32))
            self.silu_own[k] = jnp.concatenate(found, axis=0).astype(BF)
        self.exchange().start()

    def reduce(self, ada_grad_ref, small_ref):
        group = 128 // (2 * self.rows)
        width, share = self.ada_s.shape[1], ada_grad_ref.shape[1]
        left, right = self.row_of((128, 128), 0), self.row_of((128, 128), 1)
        left_all = lax.broadcasted_iota(jnp.int32, (128, 128), 0)
        right_all = lax.broadcasted_iota(jnp.int32, (128, 128), 1)
        same = (left_all - left) == (right_all - right)
        spread = jnp.logical_and(
            same,
            self.any_image(
                lambda n: jnp.logical_and(
                    jnp.logical_and(left >= n * self.pieces, left < (n + 1) * self.pieces),
                    right == self.first_cond + n,
                )
            ),
        )
        spread = jnp.where(spread, 1.0, 0.0).astype(BF)
        line = lax.broadcasted_iota(jnp.int32, (16, 128), 0)
        at = self.row_of((16, 128), 1)
        chosen = jnp.logical_and(
            jnp.logical_and(line >= self.pieces, line < self.pieces + self.table_rows),
            at == line - self.pieces + self.first_cond + self.images,
        )
        for p in range(self.pieces):
            chosen = jnp.logical_or(chosen, jnp.logical_and(line == p, self.of_piece(at, p)))
        chosen = jnp.where(chosen, 1.0, 0.0).astype(BF)
        wanted = lax.broadcasted_iota(jnp.int32, (width, 128), 0) - self.ring.place * share
        lane = lax.broadcasted_iota(jnp.int32, (width, 128), 1)
        wanted = jnp.where(wanted == lane, 1.0, 0.0).astype(BF)
        ada_grad_ref[...] = jnp.zeros_like(ada_grad_ref)
        small_ref[...] = jnp.zeros_like(small_ref)

        def one(k, carry):
            block = self.ring.packs[pl.ds(k * group, group)].reshape(128, width)
            cond = nn(spread, nn(block, wanted).astype(BF))
            for p in range(self.pieces):
                mine = jnp.where(self.of_piece(left, p), cond, 0.0).astype(BF)
                ada_grad_ref[p] += tn(mine, block)[:share]
            small_ref[...] += nn(chosen, block)
            return carry

        lax.fori_loop(0, SUM_PLACES // group, one, 0)

    def finish(self, silu_ref):
        self.exchange().wait()
        silu_ref[...] = self.silu_own[0].astype(F32) + self.silu_got[...].astype(F32)


def attn_grads_kernel(
    images, pieces, table_rows, first_ref, dattn_hbm, dqkv_ref, att_hbm, pack_own_ref,
    pack_other_ref, ada_ref, sums_ref, ada_grad_ref, small_ref, silu_ref, first_t,
    dattn_t, own, other, land0, land1, land2, land3, land_other, land_cross,
    sends, recvs, packs, pack_sends, pack_recvs, ada_s, part_s, silu_own, silu_got, small_sems,
    dattn_ref, att_ref, load_sems,
):
    width = first_t.shape[0]
    tiles, _, columns = own.shape
    share = width // SUM_PLACES
    group = GroupSum(own, other, (land0, land1, land2, land3), land_other, land_cross, sends, recvs)
    ring = PackGather(pack_own_ref, pack_other_ref, packs, pack_sends, pack_recvs)
    load_dattn = pltpu.make_async_copy(dattn_hbm, dattn_ref, load_sems.at[0])
    load_att = pltpu.make_async_copy(att_hbm, att_ref, load_sems.at[1])
    load_dattn.start()
    load_att.start()
    barrier = pltpu.get_barrier_semaphore()
    small = SmallGrads(
        images, pieces, table_rows, ring, ada_ref, ada_s, part_s, silu_own, silu_got, small_sems
    )
    group.greet(barrier)
    ring.greet(barrier)
    pl.semaphore_wait(barrier, len(HALVING) + 2)
    ring.start()

    def turn(source, target):
        for at in range(0, source.shape[0], 512):
            target[:, at : at + 512] = source[at : at + 512, :].T

    turn(first_ref, first_t)
    half = width // 2

    def produce(s, left, right_ref, row):
        for buffer, offset, stage in ((other, right_ref.shape[0] // 2, 4), (own, 0, 0)):
            right = right_ref[pl.ds(pl.multiple_of(row + offset, 16), columns), :]
            for at in (0, half):
                store_by_owner(buffer, s, at, nt(left[at : at + half, :], right), share)
            group.copy(stage, s).start()

    def step(s, carry):
        @pl.when(s < tiles - 1)
        def _():
            produce(s, first_t, dqkv_ref, s * columns)

        @pl.when(s == tiles - 1)
        def _():
            produce(s, dattn_t, att_ref, 0)

        @pl.when(s < tiles)
        def _():
            group.add(4, s)
            group.cross(0, s).start()
            group.cross(1, s).start()

        @pl.when(s == 0)
        def _():
            small.piece(0).start()
            load_dattn.wait()
            turn(dattn_ref, dattn_t)
            load_att.wait()

        for stage in range(ring.stages):

            @pl.when(s == stage)
            def _():
                ring.advance(stage)

        for piece in range(pieces):

            @pl.when(s == 1 + piece)
            def _():
                small.add_piece(piece)

        @pl.when(s == ring.stages)
        def _():
            ring.finish()
            small.reduce(ada_grad_ref, small_ref)

        @pl.when(jnp.logical_and(s >= 1, s - 1 < tiles))
        def _():
            group.add(0, s - 1)
            group.add_cross(0, s - 1)
            group.copy(1, s - 1).start()
            group.add_cross(1, s - 1)

        for stage in (1, 2):
            tile = s - 1 - stage

            @pl.when(jnp.logical_and(tile >= 0, tile < tiles))
            def _():
                group.add(stage, tile)
                group.copy(stage + 1, tile).start()

        tile = s - 4

        @pl.when(tile >= 0)
        def _():
            sums_ref[tile] = group.total(3, tile)[2].astype(BF)

        return carry

    lax.fori_loop(0, tiles + 4, step, 0)
    small.finish(silu_ref)

    def finish(tile, carry):
        group.wait_sends(tile)
        return carry

    lax.fori_loop(0, tiles, finish, 0)


def can_sum_here(width, proj, inner):
    places = lax.axis_size("dp")
    return (
        places == SUM_PLACES
        and lax.axis_size("mp") == 2
        and width % (8 * places) == 0
        and proj == 3 * inner
        and inner % 32 == 0
    )


def attn_grads(first, dattn, dqkv, att, pack_own, pack_other, ada_weight, images, table_rows):
    width = first.shape[1]
    tiles, tile = 4, att.shape[0] // 2
    share = width // SUM_PLACES
    pieces = ada_weight.shape[1] // width
    vmem = pl.BlockSpec(memory_space=pltpu.VMEM)
    sums, ada_grad, small, silu = pl.pallas_call(
        functools.partial(attn_grads_kernel, images, pieces, table_rows),
        in_specs=[vmem, ANYWHERE, vmem, ANYWHERE, vmem, vmem, ANYWHERE],
        out_specs=[vmem] * 4,
        out_shape=[
            jax.ShapeDtypeStruct((tiles, 2 * share, tile), BF),
            jax.ShapeDtypeStruct((pieces, share, width), F32),
            jax.ShapeDtypeStruct((16, width), F32),
            jax.ShapeDtypeStruct((16, width), F32),
        ],
        scratch_shapes=[
            pltpu.VMEM((width, first.shape[0]), BF),
            pltpu.VMEM((width, dattn.shape[0]), BF),
            pltpu.VMEM((tiles, width, tile), BF),
            pltpu.VMEM((tiles, width, tile), BF),
            pltpu.VMEM((tiles, width // 2, tile), BF),
            pltpu.VMEM((tiles, width // 4, tile), BF),
            pltpu.VMEM((tiles, width // 8, tile), BF),
            pltpu.VMEM((tiles, width // 8, tile), BF),
            pltpu.VMEM((tiles, width // 2, tile), BF),
            pltpu.VMEM((tiles, width // 2, tile), BF),
            pltpu.SemaphoreType.DMA((7, tiles)),
            pltpu.SemaphoreType.DMA((7, tiles)),
            pltpu.VMEM((SUM_PLACES, 2) + pack_own.shape, BF),
            pltpu.SemaphoreType.DMA((SUM_PLACES.bit_length(),)),
            pltpu.SemaphoreType.DMA((SUM_PLACES.bit_length(),)),
            pltpu.VMEM((width, width), BF),
            pltpu.VMEM((2 * pack_own.shape[0], width), F32),
            pltpu.VMEM((2, 16, width), BF),
            pltpu.VMEM((16, width), BF),
            pltpu.SemaphoreType.DMA((3,)),
            pltpu.VMEM(dattn.shape, BF),
            pltpu.VMEM(att.shape, BF),
            pltpu.SemaphoreType.DMA((2,)),
        ],
        compiler_params=pltpu.CompilerParams(
            vmem_limit_bytes=VMEM_LIMIT, collective_id=1, has_side_effects=True
        ),
        cost_estimate=cost(1e7, 1e5),
    )(first, dattn, dqkv, att, pack_own, pack_other, ada_weight)
    here = place_bit(lax.axis_index("dp"), FINAL) * share
    mine = lax.dynamic_slice_in_dim(sums, here, share, 1)
    return (
        jnp.transpose(mine, (1, 0, 2)).reshape(share, -1),
        jnp.transpose(ada_grad, (1, 0, 2)).reshape(share, -1),
        small[:pieces].reshape(-1),
        small[pieces : pieces + table_rows, :BUCKETS],
        silu[:images],
    )


def shift_mp(value, steps):
    ways = lax.axis_size("mp")
    return lax.ppermute(value, "mp", [(i, (i - steps) % ways) for i in range(ways)])


def near_halves(block):
    half = block.shape[0] // 2
    core = lax.axis_index("dp") % 2
    mine = lax.dynamic_slice_in_dim(block, core * half, half, 0)
    return [shift_mp(mine, steps) for steps in range(1, lax.axis_size("mp"))]


def with_far_halves(nears):
    places = lax.axis_size("dp")
    core = lax.axis_index("dp") % 2
    got = []
    for near in nears:
        half = near.shape[0]
        far = lax.ppermute(near, "dp", [(i, i ^ 1) for i in range(places)])
        whole = jnp.zeros((2 * half,) + near.shape[1:], near.dtype)
        whole = lax.dynamic_update_slice_in_dim(whole, near, core * half, 0)
        got.append(lax.dynamic_update_slice_in_dim(whole, far, (1 - core) * half, 0))
    return got


def gathered_parts(nears, own=None):
    half = nears[0].shape[0]
    layout, parts, base = [], [], 0
    if own is not None:
        layout, parts, base = [(0, 0, True)], [own], own.shape[0]
    if half % 16:
        return [(0, 0, True)], [jnp.concatenate(parts + with_far_halves(nears), axis=0)]
    places = lax.axis_size("dp")
    for near in nears:
        far = lax.ppermute(near, "dp", [(i, i ^ 1) for i in range(places)])
        layout += [(base, half, True), (base, half, False)]
        parts += [near, far]
        base += 2 * half
    return layout, parts


def after_own(gathered, own):
    layout, parts = gathered
    return [(0, 0, True)] + [(base + own.shape[0], half, near) for base, half, near in layout], [
        own
    ] + parts


def home(parts):
    total = parts[0].astype(F32)
    for steps in range(1, len(parts)):
        total = total + shift_mp(parts[steps], -steps).astype(F32)
    return total


def scatter_dp(part):
    return lax.psum_scatter(part, "dp", scatter_dimension=0, tiled=True)


def local(
    tokens, conditioning, kept_ids, ada_weight, ada_bias, attn_qkv, attn_out, mlp_up, mlp_down,
    rel_table, grad_out_kept, grad_out_full,
):
    ways = lax.axis_size("mp")
    place = lax.axis_index("mp")
    images_group = conditioning.shape[0]
    images = images_group // ways
    width = tokens.shape[1]
    keep = kept_ids.shape[1]
    padded = -(-keep // 64) * 64
    per_block = rel_table.shape[0]
    cols = ada_bias.shape[0]

    silu_cond = jax.nn.silu(conditioning.astype(F32)).astype(BF)
    columns = (jnp.dot(silu_cond, ada_weight, preferred_element_type=F32) + ada_bias).astype(BF)
    near_o = near_halves(attn_out)
    mod = lax.all_to_all(columns, "mp", split_axis=0, concat_axis=1, tiled=True)
    mod = jnp.pad(mod.astype(F32).reshape(images, 6, width), ((0, 0), (0, 2), (0, 0)))

    weight_own = jnp.transpose(attn_qkv.reshape(width, -1))
    tables = [rel_table] + [shift_mp(rel_table, s) for s in range(1, ways)]
    mod, tables, near_o, weight_sent = lax.optimization_barrier(
        (mod, tables, near_o, weight_own)
    )
    near_w = near_halves(weight_sent)
    fetch = ways == 2 and lax.axis_size("dp") % 4 == 0 and mlp_up.shape[0] % 32 == 0
    fetch = fetch and mlp_down.shape[0] % 64 == 0
    bias = bias_whole(jnp.concatenate(tables, axis=0))

    own_kept = lax.dynamic_slice_in_dim(kept_ids, place * images, images, 0)
    own_kept = jnp.pad(own_kept, ((0, 0), (0, padded - keep)), constant_values=-1)
    pick = (own_kept[:, :, None] == jnp.arange(PATCHES, dtype=jnp.int32)).astype(BF)
    grads = jnp.concatenate(
        [
            grad_out_full.reshape(images, PATCHES, width),
            jnp.pad(
                grad_out_kept.reshape(images, keep, width), ((0, 0), (0, padded - keep), (0, 0))
            ),
        ],
        axis=1,
    )
    dmlp = (mod[:, 5:6] * grads.astype(F32)).astype(BF).reshape(-1, width)
    grads = grads.reshape(-1, width)

    own = own_heads(tokens, mod, pick, bias, weight_own, per_block)
    near_w, near_o, own = lax.optimization_barrier((near_w, near_o, own))
    first = own[0]
    weight_others = gathered_parts(near_w)
    weight = after_own(weight_others, weight_own)
    out_weight = gathered_parts(near_o, attn_out)
    cut = (mlp_up.shape[0] * 5 // 18) // 16 * 16
    qkv, att, lse, middle, second, branch, *near_up = forward(
        own, tokens, mod, pick, bias, weight_others, out_weight, per_block,
        mlp_up if fetch else None, cut,
    )
    (branch_mlp, dsecond, grads_own, *whole), tile_own = mlp(
        second, dmlp, mlp_up, mlp_down, None, (near_up[0], mlp_up, mlp_down) if fetch else None
    )
    if fetch:
        up_others, down_others = [whole[0]], [whole[1]]
    else:
        up_others = with_far_halves(near_halves(mlp_up))
        down_others = with_far_halves(near_halves(mlp_down))
    reduced = [scatter_dp(grads_own)]
    for up, down in zip(up_others, down_others):
        (branch_mlp, dsecond, grads_next), _ = mlp(
            second, dmlp, up, down, (branch_mlp, dsecond)
        )
        reduced.append(scatter_dp(grads_next))
    out_full, out_kept, dtok, dmod, dattn, dqkv, strips = backward(
        tokens, mod, pick, bias, qkv, lse, middle, branch, branch_mlp, dsecond, grads,
        weight, out_weight, per_block,
    )
    proj_block, out_block = weight_own.shape[0], attn_out.shape[0]
    dqkv, reduced[0] = lax.optimization_barrier((dqkv, reduced[0]))
    dtables = table_of_strips(strips)
    pieces = cols // width
    used = images * (pieces + 1) + per_block
    here = can_sum_here(width, dqkv.shape[0], att.shape[0]) and cols % width == 0
    here = here and used <= 32 and pieces + per_block <= 16 and pieces <= 3
    if here:
        own_cond_rows = lax.dynamic_slice_in_dim(silu_cond, place * images, images, 0)
        packs = []
        for steps in range(ways):
            at = (place + steps) % ways
            table = dtables[steps * per_block : (steps + 1) * per_block]
            pack = jnp.concatenate(
                [
                    lax.dynamic_slice_in_dim(dmod, at * pieces, pieces, 1)
                    .astype(BF)
                    .reshape(-1, width),
                    own_cond_rows,
                    jnp.pad(table, ((0, 0), (0, width - BUCKETS))).astype(BF),
                ],
                axis=0,
            )
            packs.append(jnp.pad(pack, ((0, 32 - used), (0, 0))))
        attn_total, grad_ada_weight, grad_ada_bias, dtable, grad_silu = attn_grads(
            first, dattn, dqkv, att, *packs, ada_weight, images, per_block
        )
    else:
        dweight = dot(first, dqkv, (0, 1)).astype(BF)
        dout_t = dot(dattn, att, (0, 1)).astype(BF)
        attn_sums = scatter_dp(jnp.concatenate([dweight, dout_t], axis=1))
        dmod_rows = dmod[:, :6].reshape(images, 6 * width)
        dcolumns = lax.all_to_all(dmod_rows, "mp", split_axis=1, concat_axis=0, tiled=True)
        dtable = home(list(jnp.split(dtables, ways, axis=0)))
        all_columns = lax.all_gather(dcolumns, "dp", axis=0, tiled=True)
        dtable = lax.psum(dtable, "dp")
        all_cond = lax.all_gather(silu_cond, "dp", axis=0, tiled=True).astype(F32)
        slice_width = width // lax.axis_size("dp")
        cond_slice = lax.dynamic_slice_in_dim(
            all_cond, lax.axis_index("dp") * slice_width, slice_width, 1
        )
        grad_ada_weight = lax.dot_general(
            cond_slice, all_columns, (((0,), (0,)), ((), ())), precision=PRECISE
        )
        grad_ada_bias = jnp.sum(all_columns, axis=0)
        dcolumns_high = dcolumns.astype(BF)
        dcolumns_low = (dcolumns - dcolumns_high.astype(F32)).astype(BF)
        silu_part = nt(jnp.concatenate([dcolumns_high, dcolumns_low], axis=0), ada_weight)
        silu_part = silu_part[:images_group] + silu_part[images_group:]
        shares = lax.all_to_all(
            silu_part.astype(BF).reshape(ways, images, width), "mp", split_axis=0, concat_axis=0,
            tiled=True,
        )
        grad_silu = jnp.sum(shares.astype(F32), axis=0)
        split = ways * proj_block
        attn_total = home(
            [
                jnp.concatenate(
                    [
                        attn_sums[:, j * proj_block : (j + 1) * proj_block],
                        attn_sums[:, split + j * out_block : split + (j + 1) * out_block],
                    ],
                    axis=1,
                )
                for j in range(ways)
            ]
        )
    mlp_grads = home(reduced)
    attn_total = attn_total.astype(F32)
    grad_up, grad_down_t = split_mlp_grads(mlp_grads, tile_own)
    grad_qkv = attn_total[:, :proj_block].reshape(-1, 3, proj_block // 3)
    grad_out = jnp.transpose(attn_total[:, proj_block:])

    own_cond = lax.dynamic_slice_in_dim(conditioning, place * images, images, 0).astype(F32)
    grad_cond = jax.vjp(jax.nn.silu, own_cond)[1](grad_silu)[0].astype(BF)

    out_kept = out_kept.reshape(images, padded, width)[:, :keep].reshape(-1, width)
    return (
        out_kept, out_full, dtok, grad_cond, grad_ada_weight, grad_ada_bias, grad_qkv, grad_out,
        grad_up, jnp.transpose(grad_down_t), dtable,
    )


def solution(mesh):
    both = P(("dp", "mp"), None)
    return jax.shard_map(
        local,
        mesh=mesh,
        in_specs=(
            both, P("dp", None), P("dp", None), P(None, "mp"), P("mp"), P(None, None, "mp"),
            P("mp", None), P(None, "mp"), P("mp", None), P("mp", None), both, both,
        ),
        out_specs=(
            both, both, both, both, P("dp", "mp"), P("mp"), P("dp", None, "mp"), P("mp", "dp"),
            P("dp", "mp"), P("mp", "dp"), P("mp", None),
        ),
        check_vma=False,
    )
```

```python
import functools
import math

import jax
import jax.numpy as jnp
import numpy as np
from jax import lax
from jax.experimental import pallas as pl
from jax.experimental.pallas import tpu as pltpu
from jax.sharding import PartitionSpec as P

HEAD_DIM = 72
GRID = 16
PATCHES = 256
BUCKETS = 961
SPAN = 2 * GRID - 1
EPSILON = 1e-06
PRECISE = lax.Precision.HIGHEST
BF = jnp.bfloat16
F32 = jnp.float32
LOG2E = math.log2(math.e)
VMEM_LIMIT = 60 * 1024 * 1024


def dot(a, b, dims):
    return lax.dot_general(a, b, ((dims[0:1], dims[1:2]), ((), ())), preferred_element_type=F32)


def nn(a, b):
    return dot(a, b, (1, 0))


def nt(a, b):
    return dot(a, b, (1, 1))


def tn(a, b):
    return dot(a, b, (0, 0))


def normalize(rows):
    centered = rows - jnp.mean(rows, axis=-1, keepdims=True)
    inverse = lax.rsqrt(jnp.mean(centered * centered, axis=-1, keepdims=True) + EPSILON)
    return centered * inverse, inverse


def norm_back(normed, inverse, upstream):
    return inverse * (
        upstream
        - jnp.mean(upstream, axis=-1, keepdims=True)
        - normed * jnp.mean(upstream * normed, axis=-1, keepdims=True)
    )


def params(n_grid=1):
    return pltpu.CompilerParams(
        vmem_limit_bytes=VMEM_LIMIT, dimension_semantics=("arbitrary",) * n_grid
    )


def cost(flops, bytes_accessed, transcendentals=0):
    return pl.CostEstimate(
        flops=int(flops), bytes_accessed=int(bytes_accessed), transcendentals=int(transcendentals)
    )


def const_spec(shape):
    return pl.BlockSpec(shape, lambda *_: (0,) * len(shape), pipeline_mode=pl.Buffered(1))


def bias_kernel(strip_ref, bias_ref):
    strip = strip_ref[0]
    for key_row in range(GRID):
        start = (GRID - 1 - key_row) * GRID
        bias_ref[0, key_row * GRID : (key_row + 1) * GRID, :] = strip[:, start : start + PATCHES]


def bias_whole(table):
    heads = table.shape[0]
    grid_table = table.reshape(heads * SPAN, SPAN) * LOG2E
    place = np.arange(GRID)
    gap = place[None, :] - place[:, None] + GRID - 1
    chooser = (np.arange(SPAN)[:, None, None] == gap[None]).astype(np.float32)
    strip = jnp.dot(grid_table, chooser.reshape(SPAN, GRID * GRID), precision=PRECISE)
    strip = strip.reshape(heads, SPAN, GRID, GRID).transpose(0, 2, 1, 3)
    strip = strip.reshape(heads, GRID, SPAN * GRID)
    strip = jnp.pad(strip, ((0, 0), (0, 0), (0, 512 - SPAN * GRID)))
    return pl.pallas_call(
        bias_kernel,
        grid=(heads,),
        in_specs=[pl.BlockSpec((1, GRID, 512), lambda h: (h, 0, 0))],
        out_specs=pl.BlockSpec((1, PATCHES, PATCHES), lambda h: (h, 0, 0)),
        out_shape=jax.ShapeDtypeStruct((heads, PATCHES, PATCHES), F32),
        compiler_params=params(),
        cost_estimate=cost(1e6, 1e5),
    )(strip)


def table_of_strips(strips):
    heads = strips.shape[0]
    parts = strips[:, :, : SPAN * GRID].reshape(heads, GRID, SPAN, GRID)
    total = jnp.zeros((heads, SPAN, SPAN), F32)
    for c in range(GRID):
        total = total + jnp.pad(parts[:, c], ((0, 0), (0, 0), (GRID - 1 - c, c)))
    return total.reshape(heads, BUCKETS)


def head_rows(head, per_block):
    base = (head // per_block) * (3 * per_block * HEAD_DIM) + (head % per_block) * HEAD_DIM
    step = per_block * HEAD_DIM
    return [pl.ds(pl.multiple_of(base + c * step, 8), HEAD_DIM) for c in range(3)]


def key_mask(pick):
    ones = jnp.ones((pick.shape[0], PATCHES), BF)
    return (tn(pick, ones) - 1.0) * 1e30


def part_copies(layout, parts, whole, sems):
    core = lax.axis_index("dp") % 2
    copies = []
    for index, ((base, half, near), part) in enumerate(zip(layout, parts)):
        start = base + (core if near else 1 - core) * half
        rows = pl.ds(pl.multiple_of(start, 16), part.shape[0])
        copies.append(pltpu.make_async_copy(part, whole.at[rows, :], sems.at[index]))
    return copies


def run_copies(copies):
    for copy in copies:
        copy.start()
    for copy in copies:
        copy.wait()


def core_rows(half, skip, count):
    start = (lax.axis_index("dp") % 2) * half + skip
    return pl.ds(pl.multiple_of(start, 16), count)


def fetch_copy(own, rows, target, sems, at):
    return pltpu.make_async_remote_copy(
        src_ref=own.at[rows, :],
        dst_ref=target,
        send_sem=sems.at[at],
        recv_sem=sems.at[at + 1],
        device_id={"mp": 1 - lax.axis_index("mp")},
        device_id_type=pl.DeviceIdType.MESH,
    )


def core_copy(source, target, sems, at):
    place = lax.axis_index("dp")
    return pltpu.make_async_remote_copy(
        src_ref=source,
        dst_ref=target,
        send_sem=sems.at[at],
        recv_sem=sems.at[at + 1],
        device_id={"dp": place + 1 - 2 * (place % 2)},
        device_id_type=pl.DeviceIdType.MESH,
    )


def greet_peers(bits):
    barrier = pltpu.get_barrier_semaphore()
    peers = [{"mp": 1 - lax.axis_index("mp")}]
    place = lax.axis_index("dp")
    for bit in bits:
        peers.append({"dp": place + bit - 2 * bit * place_bit(place, bit)})
    for peer in peers:
        pl.semaphore_signal(
            barrier, inc=1, device_id=peer, device_id_type=pl.DeviceIdType.MESH
        )
    pl.semaphore_wait(barrier, len(peers))


def project(weight_ref, first, qkv_s, qkv_ref, base):
    step = weight_ref.shape[0] // 3
    for c in range(3):
        part = nt(weight_ref[c * step : (c + 1) * step, :], first)
        qkv_s[c * step : (c + 1) * step, :] = part
        qkv_ref[base + c * step : base + (c + 1) * step, :] = part.astype(BF)


def attend_heads(per_block, first_head, qkv_s, bias_ref, mask, att_s, attk_s, lse_s):
    scale = HEAD_DIM ** (-0.5) * LOG2E
    heads = qkv_s.shape[0] // (3 * HEAD_DIM)

    def one_head(head, carry):
        q_at, k_at, v_at = head_rows(head, per_block)
        queries = qkv_s[q_at, :].astype(BF)
        keys = qkv_s[k_at, :].astype(BF)
        values = qkv_s[v_at, :].astype(BF)
        scores = tn(keys, queries) * scale + bias_ref[first_head + head]
        here = pl.ds(pl.multiple_of(head * HEAD_DIM, 8), HEAD_DIM)

        def attend(scores):
            top = jnp.max(scores, axis=0, keepdims=True)
            weights = jnp.exp2(scores - top)
            total = jnp.sum(weights, axis=0, keepdims=True)
            probs = (weights * (1.0 / total)).astype(BF)
            return nn(values, probs), top + jnp.log2(total)

        att_s[here, :], lse_s[pl.ds(head, 1), :] = attend(scores)
        attk_s[here, :], lse_s[pl.ds(heads + head, 1), :] = attend(scores + mask)
        return carry

    lax.fori_loop(0, heads, one_head, 0, unroll=4 if heads % 4 == 0 else 2)


def own_heads_kernel(
    per_block, tok_ref, mod_ref, pick_ref, bias_ref, weight_ref,
    first_ref, qkv_ref, att_ref, lse_ref, qkv_s, att_s, attk_s, lse_s,
):
    shift_one, scale_one = mod_ref[0, 0:1], mod_ref[0, 1:2]
    normed, _ = normalize(tok_ref[...].astype(F32))
    first = (normed * (1.0 + scale_one) + shift_one).astype(BF)
    first_ref[...] = first
    project(weight_ref, first, qkv_s, qkv_ref, 0)
    mask = key_mask(pick_ref[0])
    attend_heads(per_block, 0, qkv_s, bias_ref, mask, att_s, attk_s, lse_s)
    att_ref[:, :PATCHES] = att_s[...].astype(BF)
    att_ref[:, PATCHES:] = attk_s[...].astype(BF)
    lse_ref[0] = lse_s[...]


def own_heads(tokens, mod, pick, bias, weight, per_block):
    images, padded = pick.shape[0], pick.shape[1]
    width = tokens.shape[1]
    proj = weight.shape[0]
    heads = proj // (3 * HEAD_DIM)
    inner = heads * HEAD_DIM
    return pl.pallas_call(
        functools.partial(own_heads_kernel, per_block),
        grid=(images,),
        in_specs=[
            pl.BlockSpec((PATCHES, width), lambda i: (i, 0)),
            pl.BlockSpec((1, 8, width), lambda i: (i, 0, 0)),
            pl.BlockSpec((1, padded, PATCHES), lambda i: (i, 0, 0)),
            const_spec(bias.shape),
            const_spec(weight.shape),
        ],
        out_specs=[
            pl.BlockSpec((PATCHES, width), lambda i: (i, 0)),
            pl.BlockSpec((proj, PATCHES), lambda i: (0, i)),
            pl.BlockSpec((inner, 2 * PATCHES), lambda i: (0, i)),
            pl.BlockSpec((1, 2 * heads, PATCHES), lambda i: (i, 0, 0)),
        ],
        out_shape=[
            jax.ShapeDtypeStruct((images * PATCHES, width), BF),
            jax.ShapeDtypeStruct((proj, images * PATCHES), BF),
            jax.ShapeDtypeStruct((inner, images * 2 * PATCHES), BF),
            jax.ShapeDtypeStruct((images, 2 * heads, PATCHES), F32),
        ],
        scratch_shapes=[
            pltpu.VMEM((proj, PATCHES), F32),
            pltpu.VMEM((inner, PATCHES), F32),
            pltpu.VMEM((inner, PATCHES), F32),
            pltpu.VMEM((2 * heads, PATCHES), F32),
        ],
        compiler_params=params(),
        cost_estimate=cost(1e7, 1e5),
    )(tokens, mod, pick, bias, weight)


def forward_kernel(per_block, weight_layout, out_layout, fetch, *refs):
    first_ref, own_qkv, own_att, own_lse, tok_ref, mod_ref, pick_ref, bias_ref = refs[:8]
    refs = refs[8:]
    weight_parts, refs = refs[: len(weight_layout)], refs[len(weight_layout) :]
    out_parts, refs = refs[: len(out_layout)], refs[len(out_layout) :]
    if fetch:
        send_ref, refs = refs[0], refs[1:]
    qkv_ref, att_ref, lse_ref, middle_ref, second_ref, branch_ref = refs[:6]
    refs = refs[6:]
    if fetch:
        got_ref, refs = refs[0], refs[1:]
    qkv_s, att_s, attk_s, lse_s, weight_ref, out_w_ref, part_sems, fetch_sems = refs

    def fetching():
        half = send_ref.shape[0] // 2
        return fetch_copy(send_ref, core_rows(half, 0, got_ref.shape[0]), got_ref, fetch_sems, 0)

    @pl.when(pl.program_id(0) == 0)
    def _():
        copies = part_copies(weight_layout, weight_parts, weight_ref, part_sems.at[0])
        copies += part_copies(out_layout, out_parts, out_w_ref, part_sems.at[1])
        if fetch:
            greet_peers(())
            fetching().start()
        run_copies(copies)

    own = own_qkv.shape[0]
    own_inner = own // 3
    own_count = own_inner // HEAD_DIM
    heads = bias_ref.shape[0]
    others = heads - own_count
    pick = pick_ref[0]
    qkv_ref[:own, :] = own_qkv[...]
    project(weight_ref, first_ref[...], qkv_s, qkv_ref, own)
    mask = key_mask(pick)
    attend_heads(per_block, own_count, qkv_s, bias_ref, mask, att_s, attk_s, lse_s)
    att_ref[:own_inner, :] = own_att[...]
    att_ref[own_inner:, :PATCHES] = att_s[...].astype(BF)
    att_ref[own_inner:, PATCHES:] = attk_s[...].astype(BF)
    lse_ref[0, :own_count, :] = own_lse[0, :own_count]
    lse_ref[0, own_count:heads, :] = lse_s[:others]
    lse_ref[0, heads : heads + own_count, :] = own_lse[0, own_count:]
    lse_ref[0, heads + own_count :, :] = lse_s[others:]
    gate_one = mod_ref[0, 2:3]
    shift_two, scale_two = mod_ref[0, 3:4], mod_ref[0, 4:5]
    out_w = out_w_ref[...]
    kept_att = nt(pick, att_ref[:, PATCHES:]).astype(BF)
    for rows, source, residual in (
        (slice(0, PATCHES), att_ref[:, :PATCHES].T, tok_ref[...].astype(F32)),
        (slice(PATCHES, PATCHES + pick.shape[0]), kept_att, nn(pick, tok_ref[...])),
    ):
        branch = nn(source, out_w)
        branch_ref[rows, :] = branch.astype(BF)
        middle = residual + gate_one * branch
        middle_ref[rows, :] = middle
        second_ref[rows, :] = (normalize(middle)[0] * (1.0 + scale_two) + shift_two).astype(BF)
    if fetch:

        @pl.when(pl.program_id(0) == pl.num_programs(0) - 1)
        def _():
            fetching().wait()


def whole_rows(layout, parts):
    return sum(part.shape[0] for part in parts)


ANYWHERE = pl.BlockSpec(memory_space=pl.ANY)


def forward(own, tokens, mod, pick, bias, weight, out_weight, per_block, send=None, count=0):
    images, padded = pick.shape[0], pick.shape[1]
    width = tokens.shape[1]
    rows = PATCHES + padded
    heads = bias.shape[0]
    (weight_layout, weight_parts), (out_layout, out_parts) = weight, out_weight
    proj_others = whole_rows(*weight)
    proj = own[1].shape[0] + proj_others
    own_inner, own_heads_count = own[2].shape[0], own[3].shape[1] // 2
    others = heads - own_heads_count
    fetch = send is not None
    most = max(len(weight_parts), len(out_parts))
    extra_shapes, extra = [], []
    compiler_params = params()
    if fetch:
        extra_shapes = [jax.ShapeDtypeStruct((count, send.shape[1]), BF)]
        extra = [send]
        compiler_params = pltpu.CompilerParams(
            vmem_limit_bytes=VMEM_LIMIT, dimension_semantics=("arbitrary",),
            collective_id=2, has_side_effects=True,
        )
    by_row = pl.BlockSpec((rows, width), lambda i: (i, 0))
    return pl.pallas_call(
        functools.partial(forward_kernel, per_block, weight_layout, out_layout, fetch),
        grid=(images,),
        in_specs=[
            pl.BlockSpec((PATCHES, width), lambda i: (i, 0)),
            pl.BlockSpec((own[1].shape[0], PATCHES), lambda i: (0, i)),
            pl.BlockSpec((own_inner, 2 * PATCHES), lambda i: (0, i)),
            pl.BlockSpec((1, 2 * own_heads_count, PATCHES), lambda i: (i, 0, 0)),
            pl.BlockSpec((PATCHES, width), lambda i: (i, 0)),
            pl.BlockSpec((1, 8, width), lambda i: (i, 0, 0)),
            pl.BlockSpec((1, padded, PATCHES), lambda i: (i, 0, 0)),
            const_spec(bias.shape),
        ]
        + [ANYWHERE] * (len(weight_parts) + len(out_parts) + len(extra)),
        out_specs=[
            pl.BlockSpec((proj, PATCHES), lambda i: (0, i)),
            pl.BlockSpec((width, 2 * PATCHES), lambda i: (0, i)),
            pl.BlockSpec((1, 2 * heads, PATCHES), lambda i: (i, 0, 0)),
            by_row,
            by_row,
            by_row,
        ]
        + [ANYWHERE] * len(extra),
        out_shape=[
            jax.ShapeDtypeStruct((proj, images * PATCHES), BF),
            jax.ShapeDtypeStruct((width, images * 2 * PATCHES), BF),
            jax.ShapeDtypeStruct((images, 2 * heads, PATCHES), F32),
            jax.ShapeDtypeStruct((images * rows, width), F32),
            jax.ShapeDtypeStruct((images * rows, width), BF),
            jax.ShapeDtypeStruct((images * rows, width), BF),
        ]
        + extra_shapes,
        scratch_shapes=[
            pltpu.VMEM((proj_others, PATCHES), F32),
            pltpu.VMEM((others * HEAD_DIM, PATCHES), F32),
            pltpu.VMEM((others * HEAD_DIM, PATCHES), F32),
            pltpu.VMEM((2 * others, PATCHES), F32),
            pltpu.VMEM((proj_others, width), BF),
            pltpu.VMEM((width, width), BF),
            pltpu.SemaphoreType.DMA((2, most)),
            pltpu.SemaphoreType.DMA((2,)),
        ],
        compiler_params=compiler_params,
        cost_estimate=cost(images * 2e9, images * 8e6),
    )(*own, tokens, mod, pick, bias, *weight_parts, *out_parts, *extra)


def gelu_pair(pre):
    root = math.sqrt(2.0 / math.pi)
    square = pre * pre
    bend = jnp.tanh(pre * (root + (root * 0.044715) * square))
    half = 0.5 + 0.5 * bend
    slope = half + (0.5 * pre) * (1.0 - bend * bend) * (root + (3.0 * root * 0.044715) * square)
    return pre * half, slope


def mlp_kernel(
    chunk, fresh, fetch, second_ref, dmlp_ref, up_ref, down_ref, *refs
):
    if fetch:
        near_ref, send_up, send_down = refs[:3]
        *refs, moves, fetch_sems = refs[3:]
        up_all, down_all = refs[3:5]
        refs = refs[:3] + refs[5:]
    if fresh:
        branch_ref, dsecond_ref, grads_ref, second_t, dmlp_t, hidden_s, dpre_s, sem = refs
    else:
        branch_in, dsecond_in, branch_ref, dsecond_ref, grads_ref = refs[:5]
        second_t, dmlp_t, hidden_s, dpre_s, sem = refs[5:]
    rows = second_ref.shape[0]
    tile = up_ref.shape[1]
    width = second_ref.shape[1]

    if fetch:
        up_half, down_half = up_all.shape[0] // 2, down_all.shape[0] // 2
        cut, quarter = near_ref.shape[0], down_half // 2
        place = lax.axis_index("dp")
        side = place_bit(place, 2)
        up_a = up_all.at[core_rows(up_half, 0, cut), :]
        up_b = up_all.at[core_rows(up_half, cut, up_half - cut), :]
        down_a = down_all.at[core_rows(down_half, 0, down_half), :]
        down_q_rows = core_rows(down_half, side * quarter, quarter)
        down_q = down_all.at[down_q_rows, :]
        lay_a = pltpu.make_async_copy(near_ref, up_a, moves.at[0])
        pass_a = core_copy(near_ref, up_a, moves, 1)
        pass_b = core_copy(up_b, up_b, moves, 3)
        pass_down = core_copy(down_a, down_a, moves, 5)
        pass_y = pltpu.make_async_remote_copy(
            src_ref=down_q,
            dst_ref=down_q,
            send_sem=moves.at[7],
            recv_sem=moves.at[8],
            device_id={"dp": place + 2 - 4 * side},
            device_id_type=pl.DeviceIdType.MESH,
        )
        fetch_b = fetch_copy(
            send_up, core_rows(up_half, cut, up_half - cut), up_b, fetch_sems, 0
        )
        fetch_down = fetch_copy(send_down, down_q_rows, down_q, fetch_sems, 2)
    step, last = pl.program_id(0), pl.num_programs(0) - 1

    @pl.when(step == 0)
    def _():
        if fetch:
            greet_peers((1, 2))
            fetch_down.start()
            lay_a.start()
            pass_a.start()
        if fresh:
            branch_ref[...] = jnp.zeros_like(branch_ref)
            dsecond_ref[...] = jnp.zeros_like(dsecond_ref)
        else:
            one = pltpu.make_async_copy(branch_in, branch_ref, sem.at[0])
            two = pltpu.make_async_copy(dsecond_in, dsecond_ref, sem.at[1])
            one.start()
            two.start()
        for at in range(0, rows, chunk):
            second_t[:, at : at + chunk] = second_ref[at : at + chunk, :].T
            dmlp_t[:, at : at + chunk] = dmlp_ref[at : at + chunk, :].T
        if not fresh:
            one.wait()
            two.wait()

    def one_chunk(index, carry):
        at = pl.ds(pl.multiple_of(index * chunk, chunk), chunk)
        pre = nn(second_ref[at, :], up_ref[...])
        dhidden = nt(dmlp_ref[at, :], down_ref[...])
        value, slope = gelu_pair(pre)
        hidden = value.astype(BF)
        dpre = (dhidden * slope).astype(BF)
        hidden_s[at, :] = hidden
        dpre_s[at, :] = dpre
        branch_ref[at, :] += nn(hidden, down_ref[...])
        dsecond_ref[at, :] += nt(dpre, up_ref[...])
        if fetch:

            @pl.when(jnp.logical_and(step == jnp.minimum(1, last), index == 0))
            def _():
                fetch_down.wait_recv()
                pass_y.start()
                fetch_b.start()

        return carry

    lax.fori_loop(0, rows // chunk, one_chunk, 0)
    if fetch:

        @pl.when(step == last)
        def _():
            fetch_b.wait_recv()
            pass_b.start()
            pass_y.wait_recv()
            pass_down.start()

    part = width // 3
    for c in range(3):
        at = slice(c * part, (c + 1) * part)
        grads_ref[at, :tile] = nn(second_t[at, :], dpre_s[...]).astype(BF)
        grads_ref[at, tile:] = nn(dmlp_t[at, :], hidden_s[...]).astype(BF)

    if fetch:

        @pl.when(step == last)
        def _():
            for copy in (lay_a, pass_a, pass_b, pass_down):
                copy.wait()
            pass_y.wait_send()
            fetch_b.wait_send()
            fetch_down.wait_send()


def mlp_chunk(rows):
    for chunk in (896, 448, 64):
        if rows % chunk == 0:
            return chunk
    return rows


def mlp(second, dmlp, up, down, sums=None, fetch=None):
    rows, width = second.shape
    hidden = up.shape[1]
    tile = 768 if hidden % 768 == 0 else hidden
    fresh = sums is None
    chunk = mlp_chunk(rows)
    in_specs = [
        const_spec(second.shape),
        const_spec(second.shape),
        pl.BlockSpec((width, tile), lambda f: (0, f)),
        pl.BlockSpec((tile, width), lambda f: (f, 0)),
    ]
    operands = [second, dmlp, up, down]
    out_specs = [
        const_spec(second.shape),
        const_spec(second.shape),
        pl.BlockSpec((width, 2 * tile), lambda f: (0, f)),
    ]
    out_shape = [
        jax.ShapeDtypeStruct(second.shape, F32),
        jax.ShapeDtypeStruct(second.shape, F32),
        jax.ShapeDtypeStruct((width, 2 * hidden), BF),
    ]
    scratch = [
        pltpu.VMEM((width, rows), BF),
        pltpu.VMEM((width, rows), BF),
        pltpu.VMEM((rows, tile), BF),
        pltpu.VMEM((rows, tile), BF),
        pltpu.SemaphoreType.DMA((2,)),
    ]
    compiler_params = params()
    if not fresh:
        in_specs += [ANYWHERE] * 2
        operands += list(sums)
    if fetch is not None:
        in_specs += [ANYWHERE] * 3
        operands += list(fetch)
        out_specs += [ANYWHERE] * 2
        out_shape += [jax.ShapeDtypeStruct(up.shape, BF), jax.ShapeDtypeStruct(down.shape, BF)]
        scratch += [pltpu.SemaphoreType.DMA((9,)), pltpu.SemaphoreType.DMA((4,))]
        compiler_params = pltpu.CompilerParams(
            vmem_limit_bytes=VMEM_LIMIT, dimension_semantics=("arbitrary",),
            collective_id=3, has_side_effects=True,
        )
    return pl.pallas_call(
        functools.partial(mlp_kernel, chunk, fresh, fetch is not None),
        grid=(hidden // tile,),
        in_specs=in_specs,
        out_specs=out_specs,
        out_shape=out_shape,
        scratch_shapes=scratch,
        compiler_params=compiler_params,
        cost_estimate=cost(6e10, 6e7) if fresh else cost(1e7, 1e5),
    )(*operands), tile


def split_mlp_grads(grads, tile):
    parts = grads.reshape(grads.shape[0], -1, 2, tile)
    return (
        parts[:, :, 0].reshape(grads.shape[0], -1),
        parts[:, :, 1].reshape(grads.shape[0], -1),
    )


def backward_kernel(per_block, weight_layout, out_layout, *refs):
    count = len(weight_layout) + len(out_layout)
    weight_parts = refs[: len(weight_layout)]
    out_parts = refs[len(weight_layout) : count]
    weight_ref, out_w_ref, sems = refs[-3:]

    weight_copies = part_copies(weight_layout, weight_parts, weight_ref, sems.at[0])

    @pl.when(pl.program_id(0) == 0)
    def _():
        out_copies = part_copies(out_layout, out_parts, out_w_ref, sems.at[1])
        for copy in out_copies + weight_copies:
            copy.start()
        for copy in out_copies:
            copy.wait()

    def wait_weight():
        @pl.when(pl.program_id(0) == 0)
        def _():
            for copy in weight_copies:
                copy.wait()

    backward_body(per_block, wait_weight, weight_ref, out_w_ref, *refs[count:-3])


def backward_body(
    per_block, wait_weight, weight_ref, out_w_ref, tok_ref, mod_ref, pick_ref, bias_ref,
    qkv_ref, lse_ref, middle_ref, branch_ref, mlp_ref, dsecond_ref, grad_ref,
    out_full_ref, out_kept_ref, dtok_ref, dmod_ref, dattn_ref, dqkv_ref, strips_ref,
    qkv_s, datt_s, dattk_s, dscores_s,
):
    heads = bias_ref.shape[0]
    step = pl.program_id(0)
    shift_one, scale_one, gate_one = mod_ref[0, 0:1], mod_ref[0, 1:2], mod_ref[0, 2:3]
    scale_two, gate_two = mod_ref[0, 4:5], mod_ref[0, 5:6]
    pick = pick_ref[0]
    dmiddles = []
    sums = [0.0, 0.0, 0.0, 0.0]
    for rows, out_ref in (
        (slice(0, PATCHES), out_full_ref),
        (slice(PATCHES, PATCHES + pick.shape[0]), out_kept_ref),
    ):
        middle = middle_ref[rows, :]
        branch_mlp = mlp_ref[rows, :]
        dsecond = dsecond_ref[rows, :]
        grad = grad_ref[rows, :].astype(F32)
        out_ref[...] = (middle + gate_two * branch_mlp).astype(BF)
        normed, inverse = normalize(middle)
        dmiddle = grad + norm_back(normed, inverse, dsecond * (1.0 + scale_two))
        branch = branch_ref[rows, :].astype(F32)
        for c, term in enumerate(
            (dmiddle * branch, dsecond, dsecond * normed, grad * branch_mlp)
        ):
            sums[c] = sums[c] + jnp.sum(term, axis=0, keepdims=True)
        dmiddles.append(dmiddle)
    for c in range(4):
        dmod_ref[0, 2 + c : 3 + c, :] = sums[c]
    dattn = (gate_one * dmiddles[0]).astype(BF)
    dattn_kept = tn(pick, (gate_one * dmiddles[1]).astype(BF)).astype(BF)
    dattn_ref[:PATCHES, :] = dattn
    dattn_ref[PATCHES:, :] = dattn_kept
    high = dmiddles[1].astype(BF)
    low = (dmiddles[1] - high.astype(F32)).astype(BF)
    dresid = dmiddles[0] + tn(pick, high) + tn(pick, low)
    datt_s[...] = nt(out_w_ref[...], dattn)
    dattk_s[...] = nt(out_w_ref[...], dattn_kept)
    qkv_s[...] = qkv_ref[...].astype(F32)
    mask = key_mask(pick)
    scale = HEAD_DIM ** (-0.5)

    @pl.when(step == 0)
    def _():
        dscores_s[...] = jnp.zeros_like(dscores_s)

    def one_head(head, carry):
        q_at, k_at, v_at = head_rows(head, per_block)
        queries = qkv_s[q_at, :].astype(BF)
        keys = qkv_s[k_at, :].astype(BF)
        values = qkv_s[v_at, :].astype(BF)
        here = pl.ds(pl.multiple_of(head * HEAD_DIM, 8), HEAD_DIM)
        scores = tn(keys, queries) * (scale * LOG2E) + bias_ref[head]

        def pull(scores, top, upstream):
            probs = jnp.exp2(scores - top)
            dprobs = tn(values, upstream)
            dvalues = nt(upstream, probs.astype(BF))
            weighted = jnp.sum(probs * dprobs, axis=0, keepdims=True)
            return probs * (dprobs - weighted), dvalues

        dscores, dvalues = pull(
            scores, lse_ref[0, pl.ds(head, 1), :], datt_s[here, :].astype(BF)
        )
        dscores_kept, dvalues_kept = pull(
            scores + mask, lse_ref[0, pl.ds(heads + head, 1), :], dattk_s[here, :].astype(BF)
        )
        dscores = dscores + dscores_kept
        dscores_s[head] += dscores
        rounded = dscores.astype(BF)
        qkv_s[q_at, :] = nn(keys, rounded) * scale
        qkv_s[k_at, :] = nt(queries, rounded) * scale
        qkv_s[v_at, :] = dvalues + dvalues_kept
        return carry

    lax.fori_loop(0, heads, one_head, 0, unroll=4)
    dqkv = qkv_s[...].astype(BF)
    dqkv_ref[...] = dqkv
    wait_weight()
    dfirst = tn(dqkv, weight_ref[...])
    normed, inverse = normalize(tok_ref[...].astype(F32))
    dmod_ref[0, 0:1, :] = jnp.sum(dfirst, axis=0, keepdims=True)
    dmod_ref[0, 1:2, :] = jnp.sum(dfirst * normed, axis=0, keepdims=True)
    dmod_ref[0, 6:8, :] = jnp.zeros((2, dfirst.shape[1]), F32)
    dtok_ref[...] = (dresid + norm_back(normed, inverse, dfirst * (1.0 + scale_one))).astype(BF)

    @pl.when(step == pl.num_programs(0) - 1)
    def _():
        def fold(head, carry):
            strip = jnp.zeros((GRID, 512), F32)
            for key_row in range(GRID):
                start = (GRID - 1 - key_row) * GRID
                block = dscores_s[head, key_row * GRID : (key_row + 1) * GRID, :]
                block = jnp.concatenate([block, jnp.zeros((GRID, 512 - PATCHES), F32)], axis=1)
                strip = strip + pltpu.roll(block, start, 1)
            strips_ref[head] = strip
            return carry

        lax.fori_loop(0, heads, fold, 0)


def backward(
    tokens, mod, pick, bias, qkv, lse, middle, branch, branch_mlp, dsecond, grads,
    weight, out_weight, per_block,
):
    (weight_layout, weight_parts), (out_layout, out_parts) = weight, out_weight
    most = max(len(weight_parts), len(out_parts))
    proj = whole_rows(*weight)
    images, padded = pick.shape[0], pick.shape[1]
    width = tokens.shape[1]
    rows = PATCHES + padded
    heads = bias.shape[0]
    by_row = pl.BlockSpec((rows, width), lambda i: (i, 0))
    return pl.pallas_call(
        functools.partial(backward_kernel, per_block, weight_layout, out_layout),
        grid=(images,),
        in_specs=[ANYWHERE] * (len(weight_parts) + len(out_parts))
        + [
            pl.BlockSpec((PATCHES, width), lambda i: (i, 0)),
            pl.BlockSpec((1, 8, width), lambda i: (i, 0, 0)),
            pl.BlockSpec((1, padded, PATCHES), lambda i: (i, 0, 0)),
            const_spec(bias.shape),
            pl.BlockSpec((proj, PATCHES), lambda i: (0, i)),
            pl.BlockSpec((1, 2 * heads, PATCHES), lambda i: (i, 0, 0)),
            by_row,
            by_row,
            by_row,
            by_row,
            by_row,
        ],
        out_specs=[
            pl.BlockSpec((PATCHES, width), lambda i: (i, 0)),
            pl.BlockSpec((padded, width), lambda i: (i, 0)),
            pl.BlockSpec((PATCHES, width), lambda i: (i, 0)),
            pl.BlockSpec((1, 8, width), lambda i: (i, 0, 0)),
            pl.BlockSpec((2 * PATCHES, width), lambda i: (i, 0)),
            pl.BlockSpec((proj, PATCHES), lambda i: (0, i)),
            const_spec((heads, GRID, 512)),
        ],
        out_shape=[
            jax.ShapeDtypeStruct((images * PATCHES, width), BF),
            jax.ShapeDtypeStruct((images * padded, width), BF),
            jax.ShapeDtypeStruct((images * PATCHES, width), BF),
            jax.ShapeDtypeStruct((images, 8, width), F32),
            jax.ShapeDtypeStruct((images * 2 * PATCHES, width), BF),
            jax.ShapeDtypeStruct((proj, images * PATCHES), BF),
            jax.ShapeDtypeStruct((heads, GRID, 512), F32),
        ],
        scratch_shapes=[
            pltpu.VMEM((proj, PATCHES), F32),
            pltpu.VMEM((width, PATCHES), F32),
            pltpu.VMEM((width, PATCHES), F32),
            pltpu.VMEM((heads, PATCHES, PATCHES), F32),
            pltpu.VMEM((proj, width), BF),
            pltpu.VMEM((width, width), BF),
            pltpu.SemaphoreType.DMA((2, most)),
        ],
        compiler_params=params(),
        cost_estimate=cost(1e7, 1e5),
    )(
        *weight_parts, *out_parts, tokens, mod, pick, bias, qkv, lse, middle, branch, branch_mlp,
        dsecond, grads,
    )


SUM_PLACES = 16
HALVING = (1, 2, 8)
FINAL = 4


def place_bit(place, bit):
    return (place // bit) % 2


def unit_start(owner, share):
    index = 0
    for bit in HALVING + (FINAL,):
        index = index * 2 + place_bit(owner, bit)
    return index * share


def store_by_owner(buffer, tile, at, block, share):
    first_owner = at // share
    owners = block.shape[0] // share
    for k in range(owners):
        owner = first_owner + k
        if place_bit(owner, FINAL):
            continue
        pair = k + FINAL
        both = jnp.concatenate(
            [block[k * share : (k + 1) * share], block[pair * share : (pair + 1) * share]], axis=0
        )
        start = unit_start(owner, share)
        buffer[tile, start : start + 2 * share, :] = both.astype(BF)


class GroupSum:
    def __init__(self, own, other, lands, land_other, land_cross, sends, recvs):
        self.own, self.other, self.lands = own, other, lands
        self.land_other, self.land_cross = land_other, land_cross
        self.sends, self.recvs = sends, recvs
        self.place = lax.axis_index("dp")
        self.rows = own.shape[1]

    def partner(self, bit):
        return {"dp": self.place + bit - 2 * bit * place_bit(self.place, bit)}

    def greet(self, barrier):
        for bit in HALVING + (FINAL,):
            pl.semaphore_signal(
                barrier, inc=1, device_id=self.partner(bit), device_id_type=pl.DeviceIdType.MESH
            )

    def spans(self, stage):
        start, size = 0, self.rows
        for k, bit in enumerate(HALVING):
            size = size // 2
            mine = place_bit(self.place, bit)
            if k == stage:
                return start + mine * size, start + (1 - mine) * size, size
            start = start + mine * size
        return start, start, size

    def remote(self, source, target, index, tile, peer):
        return pltpu.make_async_remote_copy(
            src_ref=source,
            dst_ref=target,
            send_sem=self.sends.at[index, tile],
            recv_sem=self.recvs.at[index, tile],
            device_id=peer,
            device_id_type=pl.DeviceIdType.MESH,
        )

    def copy(self, stage, tile):
        bit = (HALVING + (FINAL, HALVING[0]))[stage]
        buffer, land = (self.other, self.land_other) if stage == 4 else (self.own, self.lands[stage])
        _, away, size = self.spans(0 if stage == 4 else stage)
        rows = buffer.at[tile, pl.ds(pl.multiple_of(away, 16), size), :]
        return self.remote(rows, land.at[tile], stage, tile, self.partner(bit))

    def cross_rows(self, part):
        keep, away, size = self.spans(1)
        return (keep if part else away), size

    def cross(self, part, tile):
        start, size = self.cross_rows(part)
        base = self.spans(0)[0]
        return self.remote(
            self.other.at[tile, pl.ds(pl.multiple_of(start, 16), size), :],
            self.land_cross.at[tile, pl.ds(pl.multiple_of(start - base, 16), size), :],
            5 + part,
            tile,
            {"mp": 1 - lax.axis_index("mp")},
        )

    def total(self, stage, tile):
        self.copy(stage, tile).wait_recv()
        keep, _, size = self.spans(0 if stage == 4 else stage)
        at = pl.ds(pl.multiple_of(keep, 16), size)
        buffer, land = (self.other, self.land_other) if stage == 4 else (self.own, self.lands[stage])
        return buffer, at, buffer[tile, at, :].astype(F32) + land[tile].astype(F32)

    def add(self, stage, tile):
        buffer, at, total = self.total(stage, tile)
        buffer[tile, at, :] = total.astype(BF)

    def add_cross(self, part, tile):
        self.cross(part, tile).wait_recv()
        start, size = self.cross_rows(part)
        base = self.spans(0)[0]
        at = pl.ds(pl.multiple_of(start, 16), size)
        landed = pl.ds(pl.multiple_of(start - base, 16), size)
        total = self.own[tile, at, :].astype(F32) + self.land_cross[tile, landed, :].astype(F32)
        self.own[tile, at, :] = total.astype(BF)

    def wait_sends(self, tile):
        for stage in range(5):
            self.copy(stage, tile).wait_send()
        for part in range(2):
            self.cross(part, tile).wait_send()


def pack_slot(place):
    return sum(
        place_bit(place, SUM_PLACES >> (k + 1)) << k for k in range(SUM_PLACES.bit_length() - 1)
    )


class PackGather:
    def __init__(self, own, other, packs, sends, recvs):
        self.own, self.other, self.packs, self.sends, self.recvs = own, other, packs, sends, recvs
        self.place, self.side = lax.axis_index("dp"), lax.axis_index("mp")
        self.stages = SUM_PLACES.bit_length() - 1
        self.slot = pack_slot(self.place)

    def greet(self, barrier):
        pl.semaphore_signal(
            barrier, inc=1, device_id={"mp": 1 - self.side}, device_id_type=pl.DeviceIdType.MESH
        )

    def cross(self):
        return pltpu.make_async_remote_copy(
            src_ref=self.other,
            dst_ref=self.packs.at[self.slot, self.side],
            send_sem=self.sends.at[self.stages],
            recv_sem=self.recvs.at[self.stages],
            device_id={"mp": 1 - self.side},
            device_id_type=pl.DeviceIdType.MESH,
        )

    def copy(self, stage):
        size = 1 << stage
        bit = SUM_PLACES >> (stage + 1)
        rows = self.packs.at[pl.ds((self.slot // size) * size, size)]
        return pltpu.make_async_remote_copy(
            src_ref=rows,
            dst_ref=rows,
            send_sem=self.sends.at[stage],
            recv_sem=self.recvs.at[stage],
            device_id={"dp": self.place + bit - 2 * bit * place_bit(self.place, bit)},
            device_id_type=pl.DeviceIdType.MESH,
        )

    def start(self):
        self.packs[self.slot, self.side] = self.own[...]
        self.cross().start()

    def advance(self, stage):
        (self.cross() if stage == 0 else self.copy(stage - 1)).wait_recv()
        self.copy(stage).start()

    def finish(self):
        self.copy(self.stages - 1).wait_recv()
        self.cross().wait_send()
        for stage in range(self.stages):
            self.copy(stage).wait_send()


class SmallGrads:
    def __init__(
        self, images, pieces, table_rows, ring, ada, ada_s, part_s, silu_own, silu_got, sems
    ):
        self.images, self.pieces, self.table_rows = images, pieces, table_rows
        self.ring, self.ada, self.ada_s, self.part_s = ring, ada, ada_s, part_s
        self.silu_own, self.silu_got, self.sems = silu_own, silu_got, sems
        self.rows = ring.packs.shape[2]
        self.first_cond = images * pieces

    def row_of(self, shape, axis):
        return lax.broadcasted_iota(jnp.int32, shape, axis) & (self.rows - 1)

    def any_image(self, test):
        found = test(0)
        for image in range(1, self.images):
            found = jnp.logical_or(found, test(image))
        return found

    def of_piece(self, row, piece):
        return self.any_image(lambda image: row == image * self.pieces + piece)

    def piece(self, index):
        width = self.ada_s.shape[1]
        return pltpu.make_async_copy(
            self.ada.at[:, index * width : (index + 1) * width], self.ada_s, self.sems.at[0]
        )

    def exchange(self):
        return pltpu.make_async_remote_copy(
            src_ref=self.silu_own.at[1],
            dst_ref=self.silu_got,
            send_sem=self.sems.at[1],
            recv_sem=self.sems.at[2],
            device_id={"mp": 1 - self.ring.side},
            device_id_type=pl.DeviceIdType.MESH,
        )

    def add_piece(self, index):
        mine = self.ring.packs[self.ring.slot]
        mine = mine.reshape(2 * self.rows, mine.shape[-1]).astype(F32)
        masked = jnp.where(self.of_piece(self.row_of(mine.shape, 0), index), mine, 0.0)
        self.piece(index).wait()
        product = nt(masked.astype(BF), self.ada_s[...])
        if index:
            self.part_s[...] += product
        else:
            self.part_s[...] = product
        if index + 1 < self.pieces:
            self.piece(index + 1).start()
            return
        for k, side in enumerate((self.ring.side, 1 - self.ring.side)):
            block = self.part_s[pl.ds(pl.multiple_of(side * self.rows, 8), self.rows), :]
            found = [
                jnp.sum(block[n * self.pieces : (n + 1) * self.pieces], axis=0, keepdims=True)
                for n in range(self.images)
            ]
            found.append(jnp.zeros((self.silu_got.shape[0] - self.images, block.shape[1]), F32))
            self.silu_own[k] = jnp.concatenate(found, axis=0).astype(BF)
        self.exchange().start()

    def reduce(self, ada_grad_ref, small_ref):
        group = 128 // (2 * self.rows)
        width, share = self.ada_s.shape[1], ada_grad_ref.shape[1]
        left, right = self.row_of((128, 128), 0), self.row_of((128, 128), 1)
        left_all = lax.broadcasted_iota(jnp.int32, (128, 128), 0)
        right_all = lax.broadcasted_iota(jnp.int32, (128, 128), 1)
        same = (left_all - left) == (right_all - right)
        spread = jnp.logical_and(
            same,
            self.any_image(
                lambda n: jnp.logical_and(
                    jnp.logical_and(left >= n * self.pieces, left < (n + 1) * self.pieces),
                    right == self.first_cond + n,
                )
            ),
        )
        spread = jnp.where(spread, 1.0, 0.0).astype(BF)
        line = lax.broadcasted_iota(jnp.int32, (16, 128), 0)
        at = self.row_of((16, 128), 1)
        chosen = jnp.logical_and(
            jnp.logical_and(line >= self.pieces, line < self.pieces + self.table_rows),
            at == line - self.pieces + self.first_cond + self.images,
        )
        for p in range(self.pieces):
            chosen = jnp.logical_or(chosen, jnp.logical_and(line == p, self.of_piece(at, p)))
        chosen = jnp.where(chosen, 1.0, 0.0).astype(BF)
        wanted = lax.broadcasted_iota(jnp.int32, (width, 128), 0) - self.ring.place * share
        lane = lax.broadcasted_iota(jnp.int32, (width, 128), 1)
        wanted = jnp.where(wanted == lane, 1.0, 0.0).astype(BF)
        ada_grad_ref[...] = jnp.zeros_like(ada_grad_ref)
        small_ref[...] = jnp.zeros_like(small_ref)

        def one(k, carry):
            block = self.ring.packs[pl.ds(k * group, group)].reshape(128, width)
            cond = nn(spread, nn(block, wanted).astype(BF))
            for p in range(self.pieces):
                mine = jnp.where(self.of_piece(left, p), cond, 0.0).astype(BF)
                ada_grad_ref[p] += tn(mine, block)[:share]
            small_ref[...] += nn(chosen, block)
            return carry

        lax.fori_loop(0, SUM_PLACES // group, one, 0)

    def finish(self, silu_ref):
        self.exchange().wait()
        silu_ref[...] = self.silu_own[0].astype(F32) + self.silu_got[...].astype(F32)


def attn_grads_kernel(
    images, pieces, table_rows, first_ref, dattn_hbm, dqkv_ref, att_hbm, pack_own_ref,
    pack_other_ref, ada_ref, sums_ref, ada_grad_ref, small_ref, silu_ref, first_t,
    dattn_t, own, other, land0, land1, land2, land3, land_other, land_cross,
    sends, recvs, packs, pack_sends, pack_recvs, ada_s, part_s, silu_own, silu_got, small_sems,
    dattn_ref, att_ref, load_sems,
):
    width = first_t.shape[0]
    tiles, _, columns = own.shape
    share = width // SUM_PLACES
    group = GroupSum(own, other, (land0, land1, land2, land3), land_other, land_cross, sends, recvs)
    ring = PackGather(pack_own_ref, pack_other_ref, packs, pack_sends, pack_recvs)
    load_dattn = pltpu.make_async_copy(dattn_hbm, dattn_ref, load_sems.at[0])
    load_att = pltpu.make_async_copy(att_hbm, att_ref, load_sems.at[1])
    load_dattn.start()
    load_att.start()
    barrier = pltpu.get_barrier_semaphore()
    small = SmallGrads(
        images, pieces, table_rows, ring, ada_ref, ada_s, part_s, silu_own, silu_got, small_sems
    )
    group.greet(barrier)
    ring.greet(barrier)
    pl.semaphore_wait(barrier, len(HALVING) + 2)
    ring.start()

    def turn(source, target):
        for at in range(0, source.shape[0], 512):
            target[:, at : at + 512] = source[at : at + 512, :].T

    turn(first_ref, first_t)
    half = width // 2

    def produce(s, left, right_ref, row):
        for buffer, offset, stage in ((other, right_ref.shape[0] // 2, 4), (own, 0, 0)):
            right = right_ref[pl.ds(pl.multiple_of(row + offset, 16), columns), :]
            for at in (0, half):
                store_by_owner(buffer, s, at, nt(left[at : at + half, :], right), share)
            group.copy(stage, s).start()

    def step(s, carry):
        @pl.when(s < tiles - 1)
        def _():
            produce(s, first_t, dqkv_ref, s * columns)

        @pl.when(s == tiles - 1)
        def _():
            produce(s, dattn_t, att_ref, 0)

        @pl.when(s < tiles)
        def _():
            group.add(4, s)
            group.cross(0, s).start()
            group.cross(1, s).start()

        @pl.when(s == 0)
        def _():
            small.piece(0).start()
            load_dattn.wait()
            turn(dattn_ref, dattn_t)
            load_att.wait()

        for stage in range(ring.stages):

            @pl.when(s == stage)
            def _():
                ring.advance(stage)

        for piece in range(pieces):

            @pl.when(s == 1 + piece)
            def _():
                small.add_piece(piece)

        @pl.when(s == ring.stages)
        def _():
            ring.finish()
            small.reduce(ada_grad_ref, small_ref)

        @pl.when(jnp.logical_and(s >= 1, s - 1 < tiles))
        def _():
            group.add(0, s - 1)
            group.add_cross(0, s - 1)
            group.copy(1, s - 1).start()
            group.add_cross(1, s - 1)

        for stage in (1, 2):
            tile = s - 1 - stage

            @pl.when(jnp.logical_and(tile >= 0, tile < tiles))
            def _():
                group.add(stage, tile)
                group.copy(stage + 1, tile).start()

        tile = s - 4

        @pl.when(tile >= 0)
        def _():
            sums_ref[tile] = group.total(3, tile)[2].astype(BF)

        return carry

    lax.fori_loop(0, tiles + 4, step, 0)
    small.finish(silu_ref)

    def finish(tile, carry):
        group.wait_sends(tile)
        return carry

    lax.fori_loop(0, tiles, finish, 0)


def can_sum_here(width, proj, inner):
    places = lax.axis_size("dp")
    return (
        places == SUM_PLACES
        and lax.axis_size("mp") == 2
        and width % (8 * places) == 0
        and proj == 3 * inner
        and inner % 32 == 0
    )


def attn_grads(first, dattn, dqkv, att, pack_own, pack_other, ada_weight, images, table_rows):
    width = first.shape[1]
    tiles, tile = 4, att.shape[0] // 2
    share = width // SUM_PLACES
    pieces = ada_weight.shape[1] // width
    vmem = pl.BlockSpec(memory_space=pltpu.VMEM)
    sums, ada_grad, small, silu = pl.pallas_call(
        functools.partial(attn_grads_kernel, images, pieces, table_rows),
        in_specs=[vmem, ANYWHERE, vmem, ANYWHERE, vmem, vmem, ANYWHERE],
        out_specs=[vmem] * 4,
        out_shape=[
            jax.ShapeDtypeStruct((tiles, 2 * share, tile), BF),
            jax.ShapeDtypeStruct((pieces, share, width), F32),
            jax.ShapeDtypeStruct((16, width), F32),
            jax.ShapeDtypeStruct((16, width), F32),
        ],
        scratch_shapes=[
            pltpu.VMEM((width, first.shape[0]), BF),
            pltpu.VMEM((width, dattn.shape[0]), BF),
            pltpu.VMEM((tiles, width, tile), BF),
            pltpu.VMEM((tiles, width, tile), BF),
            pltpu.VMEM((tiles, width // 2, tile), BF),
            pltpu.VMEM((tiles, width // 4, tile), BF),
            pltpu.VMEM((tiles, width // 8, tile), BF),
            pltpu.VMEM((tiles, width // 8, tile), BF),
            pltpu.VMEM((tiles, width // 2, tile), BF),
            pltpu.VMEM((tiles, width // 2, tile), BF),
            pltpu.SemaphoreType.DMA((7, tiles)),
            pltpu.SemaphoreType.DMA((7, tiles)),
            pltpu.VMEM((SUM_PLACES, 2) + pack_own.shape, BF),
            pltpu.SemaphoreType.DMA((SUM_PLACES.bit_length(),)),
            pltpu.SemaphoreType.DMA((SUM_PLACES.bit_length(),)),
            pltpu.VMEM((width, width), BF),
            pltpu.VMEM((2 * pack_own.shape[0], width), F32),
            pltpu.VMEM((2, 16, width), BF),
            pltpu.VMEM((16, width), BF),
            pltpu.SemaphoreType.DMA((3,)),
            pltpu.VMEM(dattn.shape, BF),
            pltpu.VMEM(att.shape, BF),
            pltpu.SemaphoreType.DMA((2,)),
        ],
        compiler_params=pltpu.CompilerParams(
            vmem_limit_bytes=VMEM_LIMIT, collective_id=1, has_side_effects=True
        ),
        cost_estimate=cost(1e7, 1e5),
    )(first, dattn, dqkv, att, pack_own, pack_other, ada_weight)
    here = place_bit(lax.axis_index("dp"), FINAL) * share
    mine = lax.dynamic_slice_in_dim(sums, here, share, 1).astype(F32)
    return (
        jnp.transpose(mine[:3], (1, 0, 2)),
        jnp.transpose(mine[3]),
        jnp.transpose(ada_grad, (1, 0, 2)).reshape(share, -1),
        small[:pieces].reshape(-1),
        small[pieces : pieces + table_rows, :BUCKETS],
        silu[:images],
    )


def home_kernel(tile, own_ref, send_ref, up_ref, down_ref, sent, land, sems):
    rows = own_ref.shape[0]
    sent[:rows, :] = send_ref[...]
    sent[rows:, :] = jnp.zeros((sent.shape[0] - rows, sent.shape[1]), BF)
    greet_peers(())
    copy = pltpu.make_async_remote_copy(
        src_ref=sent,
        dst_ref=land,
        send_sem=sems.at[0],
        recv_sem=sems.at[1],
        device_id={"mp": 1 - lax.axis_index("mp")},
        device_id_type=pl.DeviceIdType.MESH,
    )
    copy.start()
    copy.wait()
    for t in range(up_ref.shape[1] // tile):
        for k, out_ref in enumerate((up_ref, down_ref)):
            at = slice((2 * t + k) * tile, (2 * t + k + 1) * tile)
            total = own_ref[:, at].astype(F32) + land[:rows, at].astype(F32)
            out_ref[:, t * tile : (t + 1) * tile] = total


def mlp_home(own, send, tile):
    rows, columns = own.shape
    padded = -(-rows // 16) * 16
    vmem = pl.BlockSpec(memory_space=pltpu.VMEM)
    half = jax.ShapeDtypeStruct((rows, columns // 2), F32)
    return pl.pallas_call(
        functools.partial(home_kernel, tile),
        in_specs=[vmem] * 2,
        out_specs=[vmem] * 2,
        out_shape=[half, half],
        scratch_shapes=[
            pltpu.VMEM((padded, columns), BF),
            pltpu.VMEM((padded, columns), BF),
            pltpu.SemaphoreType.DMA((2,)),
        ],
        compiler_params=pltpu.CompilerParams(collective_id=4, has_side_effects=True),
        cost_estimate=cost(1e7, 1e5),
    )(own, send)


def shift_mp(value, steps):
    ways = lax.axis_size("mp")
    return lax.ppermute(value, "mp", [(i, (i - steps) % ways) for i in range(ways)])


def near_halves(block):
    half = block.shape[0] // 2
    core = lax.axis_index("dp") % 2
    mine = lax.dynamic_slice_in_dim(block, core * half, half, 0)
    return [shift_mp(mine, steps) for steps in range(1, lax.axis_size("mp"))]


def with_far_halves(nears):
    places = lax.axis_size("dp")
    core = lax.axis_index("dp") % 2
    got = []
    for near in nears:
        half = near.shape[0]
        far = lax.ppermute(near, "dp", [(i, i ^ 1) for i in range(places)])
        whole = jnp.zeros((2 * half,) + near.shape[1:], near.dtype)
        whole = lax.dynamic_update_slice_in_dim(whole, near, core * half, 0)
        got.append(lax.dynamic_update_slice_in_dim(whole, far, (1 - core) * half, 0))
    return got


def gathered_parts(nears, own=None):
    half = nears[0].shape[0]
    layout, parts, base = [], [], 0
    if own is not None:
        layout, parts, base = [(0, 0, True)], [own], own.shape[0]
    if half % 16:
        return [(0, 0, True)], [jnp.concatenate(parts + with_far_halves(nears), axis=0)]
    places = lax.axis_size("dp")
    for near in nears:
        far = lax.ppermute(near, "dp", [(i, i ^ 1) for i in range(places)])
        layout += [(base, half, True), (base, half, False)]
        parts += [near, far]
        base += 2 * half
    return layout, parts


def after_own(gathered, own):
    layout, parts = gathered
    return [(0, 0, True)] + [(base + own.shape[0], half, near) for base, half, near in layout], [
        own
    ] + parts


def home(parts):
    total = parts[0].astype(F32)
    for steps in range(1, len(parts)):
        total = total + shift_mp(parts[steps], -steps).astype(F32)
    return total


def scatter_dp(part):
    return lax.psum_scatter(part, "dp", scatter_dimension=0, tiled=True)


def local(
    tokens, conditioning, kept_ids, ada_weight, ada_bias, attn_qkv, attn_out, mlp_up, mlp_down,
    rel_table, grad_out_kept, grad_out_full,
):
    ways = lax.axis_size("mp")
    place = lax.axis_index("mp")
    images_group = conditioning.shape[0]
    images = images_group // ways
    width = tokens.shape[1]
    keep = kept_ids.shape[1]
    padded = -(-keep // 64) * 64
    per_block = rel_table.shape[0]
    cols = ada_bias.shape[0]

    silu_cond = jax.nn.silu(conditioning.astype(F32)).astype(BF)
    columns = (jnp.dot(silu_cond, ada_weight, preferred_element_type=F32) + ada_bias).astype(BF)
    near_o = near_halves(attn_out)
    mod = lax.all_to_all(columns, "mp", split_axis=0, concat_axis=1, tiled=True)
    mod = jnp.pad(mod.astype(F32).reshape(images, 6, width), ((0, 0), (0, 2), (0, 0)))

    weight_own = jnp.transpose(attn_qkv.reshape(width, -1))
    tables = [rel_table] + [shift_mp(rel_table, s) for s in range(1, ways)]
    mod, tables, near_o, weight_sent = lax.optimization_barrier(
        (mod, tables, near_o, weight_own)
    )
    near_w = near_halves(weight_sent)
    fetch = ways == 2 and lax.axis_size("dp") % 4 == 0 and mlp_up.shape[0] % 32 == 0
    fetch = fetch and mlp_down.shape[0] % 64 == 0
    bias = bias_whole(jnp.concatenate(tables, axis=0))

    own_kept = lax.dynamic_slice_in_dim(kept_ids, place * images, images, 0)
    own_kept = jnp.pad(own_kept, ((0, 0), (0, padded - keep)), constant_values=-1)
    pick = (own_kept[:, :, None] == jnp.arange(PATCHES, dtype=jnp.int32)).astype(BF)
    grads = jnp.concatenate(
        [
            grad_out_full.reshape(images, PATCHES, width),
            jnp.pad(
                grad_out_kept.reshape(images, keep, width), ((0, 0), (0, padded - keep), (0, 0))
            ),
        ],
        axis=1,
    )
    dmlp = (mod[:, 5:6] * grads.astype(F32)).astype(BF).reshape(-1, width)
    grads = grads.reshape(-1, width)

    own = own_heads(tokens, mod, pick, bias, weight_own, per_block)
    near_w, near_o, own = lax.optimization_barrier((near_w, near_o, own))
    first = own[0]
    weight_others = gathered_parts(near_w)
    weight = after_own(weight_others, weight_own)
    out_weight = gathered_parts(near_o, attn_out)
    cut = (mlp_up.shape[0] * 5 // 18) // 16 * 16
    qkv, att, lse, middle, second, branch, *near_up = forward(
        own, tokens, mod, pick, bias, weight_others, out_weight, per_block,
        mlp_up if fetch else None, cut,
    )
    (branch_mlp, dsecond, grads_own, *whole), tile_own = mlp(
        second, dmlp, mlp_up, mlp_down, None, (near_up[0], mlp_up, mlp_down) if fetch else None
    )
    if fetch:
        up_others, down_others = [whole[0]], [whole[1]]
    else:
        up_others = with_far_halves(near_halves(mlp_up))
        down_others = with_far_halves(near_halves(mlp_down))
    reduced = [scatter_dp(grads_own)]
    for up, down in zip(up_others, down_others):
        (branch_mlp, dsecond, grads_next), _ = mlp(
            second, dmlp, up, down, (branch_mlp, dsecond)
        )
        reduced.append(scatter_dp(grads_next))
    out_full, out_kept, dtok, dmod, dattn, dqkv, strips = backward(
        tokens, mod, pick, bias, qkv, lse, middle, branch, branch_mlp, dsecond, grads,
        weight, out_weight, per_block,
    )
    proj_block, out_block = weight_own.shape[0], attn_out.shape[0]
    dqkv, reduced[0] = lax.optimization_barrier((dqkv, reduced[0]))
    dtables = table_of_strips(strips)
    pieces = cols // width
    used = images * (pieces + 1) + per_block
    here = can_sum_here(width, dqkv.shape[0], att.shape[0]) and cols % width == 0
    here = here and used <= 32 and pieces + per_block <= 16 and pieces <= 3
    if here:
        own_cond_rows = lax.dynamic_slice_in_dim(silu_cond, place * images, images, 0)
        packs = []
        for steps in range(ways):
            at = (place + steps) % ways
            table = dtables[steps * per_block : (steps + 1) * per_block]
            pack = jnp.concatenate(
                [
                    lax.dynamic_slice_in_dim(dmod, at * pieces, pieces, 1)
                    .astype(BF)
                    .reshape(-1, width),
                    own_cond_rows,
                    jnp.pad(table, ((0, 0), (0, width - BUCKETS))).astype(BF),
                ],
                axis=0,
            )
            packs.append(jnp.pad(pack, ((0, 32 - used), (0, 0))))
        grad_qkv, grad_out, grad_ada_weight, grad_ada_bias, dtable, grad_silu = attn_grads(
            first, dattn, dqkv, att, *packs, ada_weight, images, per_block
        )
    else:
        dweight = dot(first, dqkv, (0, 1)).astype(BF)
        dout_t = dot(dattn, att, (0, 1)).astype(BF)
        attn_sums = scatter_dp(jnp.concatenate([dweight, dout_t], axis=1))
        dmod_rows = dmod[:, :6].reshape(images, 6 * width)
        dcolumns = lax.all_to_all(dmod_rows, "mp", split_axis=1, concat_axis=0, tiled=True)
        dtable = home(list(jnp.split(dtables, ways, axis=0)))
        all_columns = lax.all_gather(dcolumns, "dp", axis=0, tiled=True)
        dtable = lax.psum(dtable, "dp")
        all_cond = lax.all_gather(silu_cond, "dp", axis=0, tiled=True).astype(F32)
        slice_width = width // lax.axis_size("dp")
        cond_slice = lax.dynamic_slice_in_dim(
            all_cond, lax.axis_index("dp") * slice_width, slice_width, 1
        )
        grad_ada_weight = lax.dot_general(
            cond_slice, all_columns, (((0,), (0,)), ((), ())), precision=PRECISE
        )
        grad_ada_bias = jnp.sum(all_columns, axis=0)
        dcolumns_high = dcolumns.astype(BF)
        dcolumns_low = (dcolumns - dcolumns_high.astype(F32)).astype(BF)
        silu_part = nt(jnp.concatenate([dcolumns_high, dcolumns_low], axis=0), ada_weight)
        silu_part = silu_part[:images_group] + silu_part[images_group:]
        shares = lax.all_to_all(
            silu_part.astype(BF).reshape(ways, images, width), "mp", split_axis=0, concat_axis=0,
            tiled=True,
        )
        grad_silu = jnp.sum(shares.astype(F32), axis=0)
        split = ways * proj_block
        attn_total = home(
            [
                jnp.concatenate(
                    [
                        attn_sums[:, j * proj_block : (j + 1) * proj_block],
                        attn_sums[:, split + j * out_block : split + (j + 1) * out_block],
                    ],
                    axis=1,
                )
                for j in range(ways)
            ]
        )
        grad_qkv = attn_total[:, :proj_block].reshape(-1, 3, proj_block // 3)
        grad_out = jnp.transpose(attn_total[:, proj_block:])
    if here and tile_own % 128 == 0:
        grad_up, grad_down_t = mlp_home(*reduced, tile_own)
    else:
        grad_up, grad_down_t = split_mlp_grads(home(reduced), tile_own)

    own_cond = lax.dynamic_slice_in_dim(conditioning, place * images, images, 0).astype(F32)
    grad_cond = jax.vjp(jax.nn.silu, own_cond)[1](grad_silu)[0].astype(BF)

    out_kept = out_kept.reshape(images, padded, width)[:, :keep].reshape(-1, width)
    return (
        out_kept, out_full, dtok, grad_cond, grad_ada_weight, grad_ada_bias, grad_qkv, grad_out,
        grad_up, jnp.transpose(grad_down_t), dtable,
    )


def solution(mesh):
    both = P(("dp", "mp"), None)
    return jax.shard_map(
        local,
        mesh=mesh,
        in_specs=(
            both, P("dp", None), P("dp", None), P(None, "mp"), P("mp"), P(None, None, "mp"),
            P("mp", None), P(None, "mp"), P("mp", None), P("mp", None), both, both,
        ),
        out_specs=(
            both, both, both, both, P("dp", "mp"), P("mp"), P("dp", None, "mp"), P("mp", "dp"),
            P("dp", "mp"), P("mp", "dp"), P("mp", None),
        ),
        check_vma=False,
    )
```

```python
import functools
import math

import jax
import jax.numpy as jnp
import numpy as np
from jax import lax
from jax.experimental import pallas as pl
from jax.experimental.pallas import tpu as pltpu
from jax.sharding import PartitionSpec as P

HEAD_DIM = 72
GRID = 16
PATCHES = 256
BUCKETS = 961
SPAN = 2 * GRID - 1
EPSILON = 1e-06
PRECISE = lax.Precision.HIGHEST
BF = jnp.bfloat16
F32 = jnp.float32
LOG2E = math.log2(math.e)
VMEM_LIMIT = 60 * 1024 * 1024


def dot(a, b, dims):
    return lax.dot_general(a, b, ((dims[0:1], dims[1:2]), ((), ())), preferred_element_type=F32)


def nn(a, b):
    return dot(a, b, (1, 0))


def nt(a, b):
    return dot(a, b, (1, 1))


def tn(a, b):
    return dot(a, b, (0, 0))


def normalize(rows):
    centered = rows - jnp.mean(rows, axis=-1, keepdims=True)
    inverse = lax.rsqrt(jnp.mean(centered * centered, axis=-1, keepdims=True) + EPSILON)
    return centered * inverse, inverse


def norm_back(normed, inverse, upstream):
    return inverse * (
        upstream
        - jnp.mean(upstream, axis=-1, keepdims=True)
        - normed * jnp.mean(upstream * normed, axis=-1, keepdims=True)
    )


def params(n_grid=1):
    return pltpu.CompilerParams(
        vmem_limit_bytes=VMEM_LIMIT, dimension_semantics=("arbitrary",) * n_grid
    )


def cost(flops, bytes_accessed, transcendentals=0):
    return pl.CostEstimate(
        flops=int(flops), bytes_accessed=int(bytes_accessed), transcendentals=int(transcendentals)
    )


def const_spec(shape):
    return pl.BlockSpec(shape, lambda *_: (0,) * len(shape), pipeline_mode=pl.Buffered(1))


def bias_kernel(strip_ref, bias_ref):
    strip = strip_ref[0]
    for key_row in range(GRID):
        start = (GRID - 1 - key_row) * GRID
        bias_ref[0, key_row * GRID : (key_row + 1) * GRID, :] = strip[:, start : start + PATCHES]


def bias_whole(table):
    heads = table.shape[0]
    grid_table = table.reshape(heads * SPAN, SPAN) * LOG2E
    place = np.arange(GRID)
    gap = place[None, :] - place[:, None] + GRID - 1
    chooser = (np.arange(SPAN)[:, None, None] == gap[None]).astype(np.float32)
    strip = jnp.dot(grid_table, chooser.reshape(SPAN, GRID * GRID), precision=PRECISE)
    strip = strip.reshape(heads, SPAN, GRID, GRID).transpose(0, 2, 1, 3)
    strip = strip.reshape(heads, GRID, SPAN * GRID)
    strip = jnp.pad(strip, ((0, 0), (0, 0), (0, 512 - SPAN * GRID)))
    return pl.pallas_call(
        bias_kernel,
        grid=(heads,),
        in_specs=[pl.BlockSpec((1, GRID, 512), lambda h: (h, 0, 0))],
        out_specs=pl.BlockSpec((1, PATCHES, PATCHES), lambda h: (h, 0, 0)),
        out_shape=jax.ShapeDtypeStruct((heads, PATCHES, PATCHES), F32),
        compiler_params=params(),
        cost_estimate=cost(1e6, 1e5),
    )(strip)


def table_of_strips(strips):
    heads = strips.shape[0]
    parts = strips[:, :, : SPAN * GRID].reshape(heads, GRID, SPAN, GRID)
    total = jnp.zeros((heads, SPAN, SPAN), F32)
    for c in range(GRID):
        total = total + jnp.pad(parts[:, c], ((0, 0), (0, 0), (GRID - 1 - c, c)))
    return total.reshape(heads, BUCKETS)


def head_rows(head, per_block):
    base = (head // per_block) * (3 * per_block * HEAD_DIM) + (head % per_block) * HEAD_DIM
    step = per_block * HEAD_DIM
    return [pl.ds(pl.multiple_of(base + c * step, 8), HEAD_DIM) for c in range(3)]


def key_mask(pick):
    ones = jnp.ones((pick.shape[0], PATCHES), BF)
    return (tn(pick, ones) - 1.0) * 1e30


def part_copies(layout, parts, whole, sems):
    core = lax.axis_index("dp") % 2
    copies = []
    for index, ((base, half, near), part) in enumerate(zip(layout, parts)):
        start = base + (core if near else 1 - core) * half
        rows = pl.ds(pl.multiple_of(start, 16), part.shape[0])
        copies.append(pltpu.make_async_copy(part, whole.at[rows, :], sems.at[index]))
    return copies


def run_copies(copies):
    for copy in copies:
        copy.start()
    for copy in copies:
        copy.wait()


def core_rows(half, skip, count):
    start = (lax.axis_index("dp") % 2) * half + skip
    return pl.ds(pl.multiple_of(start, 16), count)


def fetch_copy(own, rows, target, sems, at):
    return pltpu.make_async_remote_copy(
        src_ref=own.at[rows, :],
        dst_ref=target,
        send_sem=sems.at[at],
        recv_sem=sems.at[at + 1],
        device_id={"mp": 1 - lax.axis_index("mp")},
        device_id_type=pl.DeviceIdType.MESH,
    )


def core_copy(source, target, sems, at):
    place = lax.axis_index("dp")
    return pltpu.make_async_remote_copy(
        src_ref=source,
        dst_ref=target,
        send_sem=sems.at[at],
        recv_sem=sems.at[at + 1],
        device_id={"dp": place + 1 - 2 * (place % 2)},
        device_id_type=pl.DeviceIdType.MESH,
    )


def greet_peers(bits):
    barrier = pltpu.get_barrier_semaphore()
    peers = [{"mp": 1 - lax.axis_index("mp")}]
    place = lax.axis_index("dp")
    for bit in bits:
        peers.append({"dp": place + bit - 2 * bit * place_bit(place, bit)})
    for peer in peers:
        pl.semaphore_signal(
            barrier, inc=1, device_id=peer, device_id_type=pl.DeviceIdType.MESH
        )
    pl.semaphore_wait(barrier, len(peers))


def project(weight_ref, first, qkv_s, qkv_ref, base):
    step = weight_ref.shape[0] // 3
    for c in range(3):
        part = nt(weight_ref[c * step : (c + 1) * step, :], first)
        qkv_s[c * step : (c + 1) * step, :] = part
        qkv_ref[base + c * step : base + (c + 1) * step, :] = part.astype(BF)


def attend_heads(per_block, first_head, qkv_s, bias_ref, mask, att_s, attk_s, lse_s):
    scale = HEAD_DIM ** (-0.5) * LOG2E
    heads = qkv_s.shape[0] // (3 * HEAD_DIM)

    def one_head(head, carry):
        q_at, k_at, v_at = head_rows(head, per_block)
        queries = qkv_s[q_at, :].astype(BF)
        keys = qkv_s[k_at, :].astype(BF)
        values = qkv_s[v_at, :].astype(BF)
        scores = tn(keys, queries) * scale + bias_ref[first_head + head]
        here = pl.ds(pl.multiple_of(head * HEAD_DIM, 8), HEAD_DIM)

        def attend(scores):
            top = jnp.max(scores, axis=0, keepdims=True)
            weights = jnp.exp2(scores - top)
            total = jnp.sum(weights, axis=0, keepdims=True)
            probs = (weights * (1.0 / total)).astype(BF)
            return nn(values, probs), top + jnp.log2(total)

        att_s[here, :], lse_s[pl.ds(head, 1), :] = attend(scores)
        attk_s[here, :], lse_s[pl.ds(heads + head, 1), :] = attend(scores + mask)
        return carry

    lax.fori_loop(0, heads, one_head, 0, unroll=4 if heads % 4 == 0 else 2)


def own_heads_kernel(
    per_block, tok_ref, mod_ref, pick_ref, bias_ref, weight_ref,
    first_ref, qkv_ref, att_ref, lse_ref, qkv_s, att_s, attk_s, lse_s,
):
    shift_one, scale_one = mod_ref[0, 0:1], mod_ref[0, 1:2]
    normed, _ = normalize(tok_ref[...].astype(F32))
    first = (normed * (1.0 + scale_one) + shift_one).astype(BF)
    first_ref[...] = first
    project(weight_ref, first, qkv_s, qkv_ref, 0)
    mask = key_mask(pick_ref[0])
    attend_heads(per_block, 0, qkv_s, bias_ref, mask, att_s, attk_s, lse_s)
    att_ref[:, :PATCHES] = att_s[...].astype(BF)
    att_ref[:, PATCHES:] = attk_s[...].astype(BF)
    lse_ref[0] = lse_s[...]


def own_heads(tokens, mod, pick, bias, weight, per_block):
    images, padded = pick.shape[0], pick.shape[1]
    width = tokens.shape[1]
    proj = weight.shape[0]
    heads = proj // (3 * HEAD_DIM)
    inner = heads * HEAD_DIM
    return pl.pallas_call(
        functools.partial(own_heads_kernel, per_block),
        grid=(images,),
        in_specs=[
            pl.BlockSpec((PATCHES, width), lambda i: (i, 0)),
            pl.BlockSpec((1, 8, width), lambda i: (i, 0, 0)),
            pl.BlockSpec((1, padded, PATCHES), lambda i: (i, 0, 0)),
            const_spec(bias.shape),
            const_spec(weight.shape),
        ],
        out_specs=[
            pl.BlockSpec((PATCHES, width), lambda i: (i, 0)),
            pl.BlockSpec((proj, PATCHES), lambda i: (0, i)),
            pl.BlockSpec((inner, 2 * PATCHES), lambda i: (0, i)),
            pl.BlockSpec((1, 2 * heads, PATCHES), lambda i: (i, 0, 0)),
        ],
        out_shape=[
            jax.ShapeDtypeStruct((images * PATCHES, width), BF),
            jax.ShapeDtypeStruct((proj, images * PATCHES), BF),
            jax.ShapeDtypeStruct((inner, images * 2 * PATCHES), BF),
            jax.ShapeDtypeStruct((images, 2 * heads, PATCHES), F32),
        ],
        scratch_shapes=[
            pltpu.VMEM((proj, PATCHES), F32),
            pltpu.VMEM((inner, PATCHES), F32),
            pltpu.VMEM((inner, PATCHES), F32),
            pltpu.VMEM((2 * heads, PATCHES), F32),
        ],
        compiler_params=params(),
        cost_estimate=cost(1e7, 1e5),
    )(tokens, mod, pick, bias, weight)


def forward_kernel(per_block, weight_layout, out_layout, fetch, *refs):
    first_ref, own_qkv, own_att, own_lse, tok_ref, mod_ref, pick_ref, bias_ref = refs[:8]
    refs = refs[8:]
    weight_parts, refs = refs[: len(weight_layout)], refs[len(weight_layout) :]
    out_parts, refs = refs[: len(out_layout)], refs[len(out_layout) :]
    if fetch:
        send_ref, refs = refs[0], refs[1:]
    qkv_ref, att_ref, lse_ref, middle_ref, second_ref, branch_ref = refs[:6]
    refs = refs[6:]
    if fetch:
        got_ref, refs = refs[0], refs[1:]
    qkv_s, att_s, attk_s, lse_s, weight_ref, out_w_ref, part_sems, fetch_sems = refs

    def fetching():
        half = send_ref.shape[0] // 2
        return fetch_copy(send_ref, core_rows(half, 0, got_ref.shape[0]), got_ref, fetch_sems, 0)

    @pl.when(pl.program_id(0) == 0)
    def _():
        copies = part_copies(weight_layout, weight_parts, weight_ref, part_sems.at[0])
        copies += part_copies(out_layout, out_parts, out_w_ref, part_sems.at[1])
        if fetch:
            greet_peers(())
            fetching().start()
        run_copies(copies)

    own = own_qkv.shape[0]
    own_inner = own // 3
    own_count = own_inner // HEAD_DIM
    heads = bias_ref.shape[0]
    others = heads - own_count
    pick = pick_ref[0]
    qkv_ref[:own, :] = own_qkv[...]
    project(weight_ref, first_ref[...], qkv_s, qkv_ref, own)
    mask = key_mask(pick)
    attend_heads(per_block, own_count, qkv_s, bias_ref, mask, att_s, attk_s, lse_s)
    att_ref[:own_inner, :] = own_att[...]
    att_ref[own_inner:, :PATCHES] = att_s[...].astype(BF)
    att_ref[own_inner:, PATCHES:] = attk_s[...].astype(BF)
    lse_ref[0, :own_count, :] = own_lse[0, :own_count]
    lse_ref[0, own_count:heads, :] = lse_s[:others]
    lse_ref[0, heads : heads + own_count, :] = own_lse[0, own_count:]
    lse_ref[0, heads + own_count :, :] = lse_s[others:]
    gate_one = mod_ref[0, 2:3]
    shift_two, scale_two = mod_ref[0, 3:4], mod_ref[0, 4:5]
    out_w = out_w_ref[...]
    kept_att = nt(pick, att_ref[:, PATCHES:]).astype(BF)
    for rows, source, residual in (
        (slice(0, PATCHES), att_ref[:, :PATCHES].T, tok_ref[...].astype(F32)),
        (slice(PATCHES, PATCHES + pick.shape[0]), kept_att, nn(pick, tok_ref[...])),
    ):
        branch = nn(source, out_w)
        branch_ref[rows, :] = branch.astype(BF)
        middle = residual + gate_one * branch
        middle_ref[rows, :] = middle
        second_ref[rows, :] = (normalize(middle)[0] * (1.0 + scale_two) + shift_two).astype(BF)
    if fetch:

        @pl.when(pl.program_id(0) == pl.num_programs(0) - 1)
        def _():
            fetching().wait()


def whole_rows(layout, parts):
    return sum(part.shape[0] for part in parts)


ANYWHERE = pl.BlockSpec(memory_space=pl.ANY)


def forward(own, tokens, mod, pick, bias, weight, out_weight, per_block, send=None, count=0):
    images, padded = pick.shape[0], pick.shape[1]
    width = tokens.shape[1]
    rows = PATCHES + padded
    heads = bias.shape[0]
    (weight_layout, weight_parts), (out_layout, out_parts) = weight, out_weight
    proj_others = whole_rows(*weight)
    proj = own[1].shape[0] + proj_others
    own_inner, own_heads_count = own[2].shape[0], own[3].shape[1] // 2
    others = heads - own_heads_count
    fetch = send is not None
    most = max(len(weight_parts), len(out_parts))
    extra_shapes, extra = [], []
    compiler_params = params()
    if fetch:
        extra_shapes = [jax.ShapeDtypeStruct((count, send.shape[1]), BF)]
        extra = [send]
        compiler_params = pltpu.CompilerParams(
            vmem_limit_bytes=VMEM_LIMIT, dimension_semantics=("arbitrary",),
            collective_id=2, has_side_effects=True,
        )
    by_row = pl.BlockSpec((rows, width), lambda i: (i, 0))
    return pl.pallas_call(
        functools.partial(forward_kernel, per_block, weight_layout, out_layout, fetch),
        grid=(images,),
        in_specs=[
            pl.BlockSpec((PATCHES, width), lambda i: (i, 0)),
            pl.BlockSpec((own[1].shape[0], PATCHES), lambda i: (0, i)),
            pl.BlockSpec((own_inner, 2 * PATCHES), lambda i: (0, i)),
            pl.BlockSpec((1, 2 * own_heads_count, PATCHES), lambda i: (i, 0, 0)),
            pl.BlockSpec((PATCHES, width), lambda i: (i, 0)),
            pl.BlockSpec((1, 8, width), lambda i: (i, 0, 0)),
            pl.BlockSpec((1, padded, PATCHES), lambda i: (i, 0, 0)),
            const_spec(bias.shape),
        ]
        + [ANYWHERE] * (len(weight_parts) + len(out_parts) + len(extra)),
        out_specs=[
            pl.BlockSpec((proj, PATCHES), lambda i: (0, i)),
            pl.BlockSpec((width, 2 * PATCHES), lambda i: (0, i)),
            pl.BlockSpec((1, 2 * heads, PATCHES), lambda i: (i, 0, 0)),
            by_row,
            by_row,
            by_row,
        ]
        + [ANYWHERE] * len(extra),
        out_shape=[
            jax.ShapeDtypeStruct((proj, images * PATCHES), BF),
            jax.ShapeDtypeStruct((width, images * 2 * PATCHES), BF),
            jax.ShapeDtypeStruct((images, 2 * heads, PATCHES), F32),
            jax.ShapeDtypeStruct((images * rows, width), F32),
            jax.ShapeDtypeStruct((images * rows, width), BF),
            jax.ShapeDtypeStruct((images * rows, width), BF),
        ]
        + extra_shapes,
        scratch_shapes=[
            pltpu.VMEM((proj_others, PATCHES), F32),
            pltpu.VMEM((others * HEAD_DIM, PATCHES), F32),
            pltpu.VMEM((others * HEAD_DIM, PATCHES), F32),
            pltpu.VMEM((2 * others, PATCHES), F32),
            pltpu.VMEM((proj_others, width), BF),
            pltpu.VMEM((width, width), BF),
            pltpu.SemaphoreType.DMA((2, most)),
            pltpu.SemaphoreType.DMA((2,)),
        ],
        compiler_params=compiler_params,
        cost_estimate=cost(images * 2e9, images * 8e6),
    )(*own, tokens, mod, pick, bias, *weight_parts, *out_parts, *extra)


def gelu_pair(pre):
    root = math.sqrt(2.0 / math.pi)
    square = pre * pre
    bend = jnp.tanh(pre * (root + (root * 0.044715) * square))
    half = 0.5 + 0.5 * bend
    slope = half + (0.5 * pre) * (1.0 - bend * bend) * (root + (3.0 * root * 0.044715) * square)
    return pre * half, slope


def mlp_kernel(
    chunk, fresh, fetch, second_ref, dmlp_ref, up_ref, down_ref, *refs
):
    if fetch:
        near_ref, send_up, send_down = refs[:3]
        *refs, moves, fetch_sems = refs[3:]
        up_all, down_all = refs[3:5]
        refs = refs[:3] + refs[5:]
    if fresh:
        branch_ref, dsecond_ref, grads_ref, second_t, dmlp_t, hidden_s, dpre_s, sem = refs
    else:
        branch_in, dsecond_in, branch_ref, dsecond_ref, grads_ref = refs[:5]
        second_t, dmlp_t, hidden_s, dpre_s, sem = refs[5:]
    rows = second_ref.shape[0]
    tile = up_ref.shape[1]
    width = second_ref.shape[1]

    if fetch:
        up_half, down_half = up_all.shape[0] // 2, down_all.shape[0] // 2
        cut, quarter = near_ref.shape[0], down_half // 2
        place = lax.axis_index("dp")
        side = place_bit(place, 2)
        up_a = up_all.at[core_rows(up_half, 0, cut), :]
        up_b = up_all.at[core_rows(up_half, cut, up_half - cut), :]
        down_a = down_all.at[core_rows(down_half, 0, down_half), :]
        down_q_rows = core_rows(down_half, side * quarter, quarter)
        down_q = down_all.at[down_q_rows, :]
        lay_a = pltpu.make_async_copy(near_ref, up_a, moves.at[0])
        pass_a = core_copy(near_ref, up_a, moves, 1)
        pass_b = core_copy(up_b, up_b, moves, 3)
        pass_down = core_copy(down_a, down_a, moves, 5)
        pass_y = pltpu.make_async_remote_copy(
            src_ref=down_q,
            dst_ref=down_q,
            send_sem=moves.at[7],
            recv_sem=moves.at[8],
            device_id={"dp": place + 2 - 4 * side},
            device_id_type=pl.DeviceIdType.MESH,
        )
        fetch_b = fetch_copy(
            send_up, core_rows(up_half, cut, up_half - cut), up_b, fetch_sems, 0
        )
        fetch_down = fetch_copy(send_down, down_q_rows, down_q, fetch_sems, 2)
    step, last = pl.program_id(0), pl.num_programs(0) - 1

    @pl.when(step == 0)
    def _():
        if fetch:
            greet_peers((1, 2))
            fetch_down.start()
            lay_a.start()
            pass_a.start()
        if fresh:
            branch_ref[...] = jnp.zeros_like(branch_ref)
            dsecond_ref[...] = jnp.zeros_like(dsecond_ref)
        else:
            one = pltpu.make_async_copy(branch_in, branch_ref, sem.at[0])
            two = pltpu.make_async_copy(dsecond_in, dsecond_ref, sem.at[1])
            one.start()
            two.start()
        for at in range(0, rows, chunk):
            second_t[:, at : at + chunk] = second_ref[at : at + chunk, :].T
            dmlp_t[:, at : at + chunk] = dmlp_ref[at : at + chunk, :].T
        if not fresh:
            one.wait()
            two.wait()

    def one_chunk(index, carry):
        at = pl.ds(pl.multiple_of(index * chunk, chunk), chunk)
        pre = nn(second_ref[at, :], up_ref[...])
        dhidden = nt(dmlp_ref[at, :], down_ref[...])
        value, slope = gelu_pair(pre)
        hidden = value.astype(BF)
        dpre = (dhidden * slope).astype(BF)
        hidden_s[at, :] = hidden
        dpre_s[at, :] = dpre
        branch_ref[at, :] += nn(hidden, down_ref[...])
        dsecond_ref[at, :] += nt(dpre, up_ref[...])
        if fetch:

            @pl.when(jnp.logical_and(step == jnp.minimum(1, last), index == 0))
            def _():
                fetch_down.wait_recv()
                pass_y.start()
                fetch_b.start()

        return carry

    lax.fori_loop(0, rows // chunk, one_chunk, 0)
    if fetch:

        @pl.when(step == last)
        def _():
            fetch_b.wait_recv()
            pass_b.start()
            pass_y.wait_recv()
            pass_down.start()

    part = width // 3
    for c in range(3):
        at = slice(c * part, (c + 1) * part)
        grads_ref[at, :tile] = nn(second_t[at, :], dpre_s[...]).astype(BF)
        grads_ref[at, tile:] = nn(dmlp_t[at, :], hidden_s[...]).astype(BF)

    if fetch:

        @pl.when(step == last)
        def _():
            for copy in (lay_a, pass_a, pass_b, pass_down):
                copy.wait()
            pass_y.wait_send()
            fetch_b.wait_send()
            fetch_down.wait_send()


def mlp_chunk(rows):
    for chunk in (896, 448, 64):
        if rows % chunk == 0:
            return chunk
    return rows


def mlp(second, dmlp, up, down, sums=None, fetch=None):
    rows, width = second.shape
    hidden = up.shape[1]
    tile = 768 if hidden % 768 == 0 else hidden
    fresh = sums is None
    chunk = mlp_chunk(rows)
    in_specs = [
        const_spec(second.shape),
        const_spec(second.shape),
        pl.BlockSpec((width, tile), lambda f: (0, f)),
        pl.BlockSpec((tile, width), lambda f: (f, 0)),
    ]
    operands = [second, dmlp, up, down]
    out_specs = [
        const_spec(second.shape),
        const_spec(second.shape),
        pl.BlockSpec((width, 2 * tile), lambda f: (0, f)),
    ]
    out_shape = [
        jax.ShapeDtypeStruct(second.shape, F32),
        jax.ShapeDtypeStruct(second.shape, F32),
        jax.ShapeDtypeStruct((width, 2 * hidden), BF),
    ]
    scratch = [
        pltpu.VMEM((width, rows), BF),
        pltpu.VMEM((width, rows), BF),
        pltpu.VMEM((rows, tile), BF),
        pltpu.VMEM((rows, tile), BF),
        pltpu.SemaphoreType.DMA((2,)),
    ]
    compiler_params = params()
    if not fresh:
        in_specs += [ANYWHERE] * 2
        operands += list(sums)
    if fetch is not None:
        in_specs += [ANYWHERE] * 3
        operands += list(fetch)
        out_specs += [ANYWHERE] * 2
        out_shape += [jax.ShapeDtypeStruct(up.shape, BF), jax.ShapeDtypeStruct(down.shape, BF)]
        scratch += [pltpu.SemaphoreType.DMA((9,)), pltpu.SemaphoreType.DMA((4,))]
        compiler_params = pltpu.CompilerParams(
            vmem_limit_bytes=VMEM_LIMIT, dimension_semantics=("arbitrary",),
            collective_id=3, has_side_effects=True,
        )
    return pl.pallas_call(
        functools.partial(mlp_kernel, chunk, fresh, fetch is not None),
        grid=(hidden // tile,),
        in_specs=in_specs,
        out_specs=out_specs,
        out_shape=out_shape,
        scratch_shapes=scratch,
        compiler_params=compiler_params,
        cost_estimate=cost(6e10, 6e7) if fresh else cost(1e7, 1e5),
    )(*operands), tile


def split_mlp_grads(grads, tile):
    parts = grads.reshape(grads.shape[0], -1, 2, tile)
    return (
        parts[:, :, 0].reshape(grads.shape[0], -1),
        parts[:, :, 1].reshape(grads.shape[0], -1),
    )


def backward_kernel(per_block, weight_layout, out_layout, *refs):
    count = len(weight_layout) + len(out_layout)
    weight_parts = refs[: len(weight_layout)]
    out_parts = refs[len(weight_layout) : count]
    weight_ref, out_w_ref, sems = refs[-3:]

    weight_copies = part_copies(weight_layout, weight_parts, weight_ref, sems.at[0])

    @pl.when(pl.program_id(0) == 0)
    def _():
        out_copies = part_copies(out_layout, out_parts, out_w_ref, sems.at[1])
        for copy in out_copies + weight_copies:
            copy.start()
        for copy in out_copies:
            copy.wait()

    def wait_weight():
        @pl.when(pl.program_id(0) == 0)
        def _():
            for copy in weight_copies:
                copy.wait()

    backward_body(per_block, wait_weight, weight_ref, out_w_ref, *refs[count:-3])


def backward_body(
    per_block, wait_weight, weight_ref, out_w_ref, tok_ref, mod_ref, pick_ref, bias_ref,
    qkv_ref, lse_ref, middle_ref, branch_ref, mlp_ref, dsecond_ref, grad_ref,
    out_full_ref, out_kept_ref, dtok_ref, dmod_ref, dattn_ref, dqkv_ref, strips_ref,
    qkv_s, datt_s, dattk_s, dscores_s,
):
    heads = bias_ref.shape[0]
    step = pl.program_id(0)
    shift_one, scale_one, gate_one = mod_ref[0, 0:1], mod_ref[0, 1:2], mod_ref[0, 2:3]
    scale_two, gate_two = mod_ref[0, 4:5], mod_ref[0, 5:6]
    pick = pick_ref[0]
    dmiddles = []
    sums = [0.0, 0.0, 0.0, 0.0]
    for rows, out_ref in (
        (slice(0, PATCHES), out_full_ref),
        (slice(PATCHES, PATCHES + pick.shape[0]), out_kept_ref),
    ):
        middle = middle_ref[rows, :]
        branch_mlp = mlp_ref[rows, :]
        dsecond = dsecond_ref[rows, :]
        grad = grad_ref[rows, :].astype(F32)
        out_ref[...] = (middle + gate_two * branch_mlp).astype(BF)
        normed, inverse = normalize(middle)
        dmiddle = grad + norm_back(normed, inverse, dsecond * (1.0 + scale_two))
        branch = branch_ref[rows, :].astype(F32)
        for c, term in enumerate(
            (dmiddle * branch, dsecond, dsecond * normed, grad * branch_mlp)
        ):
            sums[c] = sums[c] + jnp.sum(term, axis=0, keepdims=True)
        dmiddles.append(dmiddle)
    for c in range(4):
        dmod_ref[0, 2 + c : 3 + c, :] = sums[c]
    dattn = (gate_one * dmiddles[0]).astype(BF)
    dattn_kept = tn(pick, (gate_one * dmiddles[1]).astype(BF)).astype(BF)
    dattn_ref[:PATCHES, :] = dattn
    dattn_ref[PATCHES:, :] = dattn_kept
    high = dmiddles[1].astype(BF)
    low = (dmiddles[1] - high.astype(F32)).astype(BF)
    dresid = dmiddles[0] + tn(pick, high) + tn(pick, low)
    datt_s[...] = nt(out_w_ref[...], dattn)
    dattk_s[...] = nt(out_w_ref[...], dattn_kept)
    qkv_s[...] = qkv_ref[...].astype(F32)
    mask = key_mask(pick)
    scale = HEAD_DIM ** (-0.5)

    @pl.when(step == 0)
    def _():
        dscores_s[...] = jnp.zeros_like(dscores_s)

    def one_head(head, carry):
        q_at, k_at, v_at = head_rows(head, per_block)
        queries = qkv_s[q_at, :].astype(BF)
        keys = qkv_s[k_at, :].astype(BF)
        values = qkv_s[v_at, :].astype(BF)
        here = pl.ds(pl.multiple_of(head * HEAD_DIM, 8), HEAD_DIM)
        scores = tn(keys, queries) * (scale * LOG2E) + bias_ref[head]

        def pull(scores, top, upstream):
            probs = jnp.exp2(scores - top)
            dprobs = tn(values, upstream)
            dvalues = nt(upstream, probs.astype(BF))
            weighted = jnp.sum(probs * dprobs, axis=0, keepdims=True)
            return probs * (dprobs - weighted), dvalues

        dscores, dvalues = pull(
            scores, lse_ref[0, pl.ds(head, 1), :], datt_s[here, :].astype(BF)
        )
        dscores_kept, dvalues_kept = pull(
            scores + mask, lse_ref[0, pl.ds(heads + head, 1), :], dattk_s[here, :].astype(BF)
        )
        dscores = dscores + dscores_kept
        dscores_s[head] += dscores
        rounded = dscores.astype(BF)
        qkv_s[q_at, :] = nn(keys, rounded) * scale
        qkv_s[k_at, :] = nt(queries, rounded) * scale
        qkv_s[v_at, :] = dvalues + dvalues_kept
        return carry

    lax.fori_loop(0, heads, one_head, 0, unroll=4)
    dqkv = qkv_s[...].astype(BF)
    dqkv_ref[...] = dqkv
    wait_weight()
    dfirst = tn(dqkv, weight_ref[...])
    normed, inverse = normalize(tok_ref[...].astype(F32))
    dmod_ref[0, 0:1, :] = jnp.sum(dfirst, axis=0, keepdims=True)
    dmod_ref[0, 1:2, :] = jnp.sum(dfirst * normed, axis=0, keepdims=True)
    dmod_ref[0, 6:8, :] = jnp.zeros((2, dfirst.shape[1]), F32)
    dtok_ref[...] = (dresid + norm_back(normed, inverse, dfirst * (1.0 + scale_one))).astype(BF)

    @pl.when(step == pl.num_programs(0) - 1)
    def _():
        def fold(head, carry):
            strip = jnp.zeros((GRID, 512), F32)
            for key_row in range(GRID):
                start = (GRID - 1 - key_row) * GRID
                block = dscores_s[head, key_row * GRID : (key_row + 1) * GRID, :]
                block = jnp.concatenate([block, jnp.zeros((GRID, 512 - PATCHES), F32)], axis=1)
                strip = strip + pltpu.roll(block, start, 1)
            strips_ref[head] = strip
            return carry

        lax.fori_loop(0, heads, fold, 0)


def backward(
    tokens, mod, pick, bias, qkv, lse, middle, branch, branch_mlp, dsecond, grads,
    weight, out_weight, per_block,
):
    (weight_layout, weight_parts), (out_layout, out_parts) = weight, out_weight
    most = max(len(weight_parts), len(out_parts))
    proj = whole_rows(*weight)
    images, padded = pick.shape[0], pick.shape[1]
    width = tokens.shape[1]
    rows = PATCHES + padded
    heads = bias.shape[0]
    by_row = pl.BlockSpec((rows, width), lambda i: (i, 0))
    return pl.pallas_call(
        functools.partial(backward_kernel, per_block, weight_layout, out_layout),
        grid=(images,),
        in_specs=[ANYWHERE] * (len(weight_parts) + len(out_parts))
        + [
            pl.BlockSpec((PATCHES, width), lambda i: (i, 0)),
            pl.BlockSpec((1, 8, width), lambda i: (i, 0, 0)),
            pl.BlockSpec((1, padded, PATCHES), lambda i: (i, 0, 0)),
            const_spec(bias.shape),
            pl.BlockSpec((proj, PATCHES), lambda i: (0, i)),
            pl.BlockSpec((1, 2 * heads, PATCHES), lambda i: (i, 0, 0)),
            by_row,
            by_row,
            by_row,
            by_row,
            by_row,
        ],
        out_specs=[
            pl.BlockSpec((PATCHES, width), lambda i: (i, 0)),
            pl.BlockSpec((padded, width), lambda i: (i, 0)),
            pl.BlockSpec((PATCHES, width), lambda i: (i, 0)),
            pl.BlockSpec((1, 8, width), lambda i: (i, 0, 0)),
            pl.BlockSpec((2 * PATCHES, width), lambda i: (i, 0)),
            pl.BlockSpec((proj, PATCHES), lambda i: (0, i)),
            const_spec((heads, GRID, 512)),
        ],
        out_shape=[
            jax.ShapeDtypeStruct((images * PATCHES, width), BF),
            jax.ShapeDtypeStruct((images * padded, width), BF),
            jax.ShapeDtypeStruct((images * PATCHES, width), BF),
            jax.ShapeDtypeStruct((images, 8, width), F32),
            jax.ShapeDtypeStruct((images * 2 * PATCHES, width), BF),
            jax.ShapeDtypeStruct((proj, images * PATCHES), BF),
            jax.ShapeDtypeStruct((heads, GRID, 512), F32),
        ],
        scratch_shapes=[
            pltpu.VMEM((proj, PATCHES), F32),
            pltpu.VMEM((width, PATCHES), F32),
            pltpu.VMEM((width, PATCHES), F32),
            pltpu.VMEM((heads, PATCHES, PATCHES), F32),
            pltpu.VMEM((proj, width), BF),
            pltpu.VMEM((width, width), BF),
            pltpu.SemaphoreType.DMA((2, most)),
        ],
        compiler_params=params(),
        cost_estimate=cost(1e7, 1e5),
    )(
        *weight_parts, *out_parts, tokens, mod, pick, bias, qkv, lse, middle, branch, branch_mlp,
        dsecond, grads,
    )


SUM_PLACES = 16
HALVING = (1, 2, 8)
FINAL = 4


def place_bit(place, bit):
    return (place // bit) % 2


def unit_start(owner, share):
    index = 0
    for bit in HALVING + (FINAL,):
        index = index * 2 + place_bit(owner, bit)
    return index * share


def store_by_owner(buffer, tile, at, block, share):
    first_owner = at // share
    owners = block.shape[0] // share
    for k in range(owners):
        owner = first_owner + k
        if place_bit(owner, FINAL):
            continue
        pair = k + FINAL
        both = jnp.concatenate(
            [block[k * share : (k + 1) * share], block[pair * share : (pair + 1) * share]], axis=0
        )
        start = unit_start(owner, share)
        buffer[tile, start : start + 2 * share, :] = both.astype(BF)


class GroupSum:
    def __init__(self, own, other, lands, land_other, land_cross, sends, recvs):
        self.own, self.other, self.lands = own, other, lands
        self.land_other, self.land_cross = land_other, land_cross
        self.sends, self.recvs = sends, recvs
        self.place = lax.axis_index("dp")
        self.rows = own.shape[1]

    def partner(self, bit):
        return {"dp": self.place + bit - 2 * bit * place_bit(self.place, bit)}

    def greet(self, barrier):
        for bit in HALVING + (FINAL,):
            pl.semaphore_signal(
                barrier, inc=1, device_id=self.partner(bit), device_id_type=pl.DeviceIdType.MESH
            )

    def spans(self, stage):
        start, size = 0, self.rows
        for k, bit in enumerate(HALVING):
            size = size // 2
            mine = place_bit(self.place, bit)
            if k == stage:
                return start + mine * size, start + (1 - mine) * size, size
            start = start + mine * size
        return start, start, size

    def remote(self, source, target, index, tile, peer):
        return pltpu.make_async_remote_copy(
            src_ref=source,
            dst_ref=target,
            send_sem=self.sends.at[index, tile],
            recv_sem=self.recvs.at[index, tile],
            device_id=peer,
            device_id_type=pl.DeviceIdType.MESH,
        )

    def copy(self, stage, tile):
        bit = (HALVING + (FINAL, HALVING[0]))[stage]
        buffer, land = (self.other, self.land_other) if stage == 4 else (self.own, self.lands[stage])
        _, away, size = self.spans(0 if stage == 4 else stage)
        rows = buffer.at[tile, pl.ds(pl.multiple_of(away, 16), size), :]
        return self.remote(rows, land.at[tile], stage, tile, self.partner(bit))

    def cross_rows(self, part):
        keep, away, size = self.spans(1)
        return (keep if part else away), size

    def cross(self, part, tile):
        start, size = self.cross_rows(part)
        base = self.spans(0)[0]
        return self.remote(
            self.other.at[tile, pl.ds(pl.multiple_of(start, 16), size), :],
            self.land_cross.at[tile, pl.ds(pl.multiple_of(start - base, 16), size), :],
            5 + part,
            tile,
            {"mp": 1 - lax.axis_index("mp")},
        )

    def total(self, stage, tile):
        self.copy(stage, tile).wait_recv()
        keep, _, size = self.spans(0 if stage == 4 else stage)
        at = pl.ds(pl.multiple_of(keep, 16), size)
        buffer, land = (self.other, self.land_other) if stage == 4 else (self.own, self.lands[stage])
        return buffer, at, buffer[tile, at, :].astype(F32) + land[tile].astype(F32)

    def add(self, stage, tile):
        buffer, at, total = self.total(stage, tile)
        buffer[tile, at, :] = total.astype(BF)

    def add_cross(self, part, tile):
        self.cross(part, tile).wait_recv()
        start, size = self.cross_rows(part)
        base = self.spans(0)[0]
        at = pl.ds(pl.multiple_of(start, 16), size)
        landed = pl.ds(pl.multiple_of(start - base, 16), size)
        total = self.own[tile, at, :].astype(F32) + self.land_cross[tile, landed, :].astype(F32)
        self.own[tile, at, :] = total.astype(BF)

    def wait_sends(self, tile):
        for stage in range(5):
            self.copy(stage, tile).wait_send()
        for part in range(2):
            self.cross(part, tile).wait_send()


def pack_slot(place):
    return sum(
        place_bit(place, SUM_PLACES >> (k + 1)) << k for k in range(SUM_PLACES.bit_length() - 1)
    )


class PackGather:
    def __init__(self, own, other, packs, sends, recvs):
        self.own, self.other, self.packs, self.sends, self.recvs = own, other, packs, sends, recvs
        self.place, self.side = lax.axis_index("dp"), lax.axis_index("mp")
        self.stages = SUM_PLACES.bit_length() - 1
        self.slot = pack_slot(self.place)

    def greet(self, barrier):
        pl.semaphore_signal(
            barrier, inc=1, device_id={"mp": 1 - self.side}, device_id_type=pl.DeviceIdType.MESH
        )

    def cross(self):
        return pltpu.make_async_remote_copy(
            src_ref=self.other,
            dst_ref=self.packs.at[self.slot, self.side],
            send_sem=self.sends.at[self.stages],
            recv_sem=self.recvs.at[self.stages],
            device_id={"mp": 1 - self.side},
            device_id_type=pl.DeviceIdType.MESH,
        )

    def copy(self, stage):
        size = 1 << stage
        bit = SUM_PLACES >> (stage + 1)
        rows = self.packs.at[pl.ds((self.slot // size) * size, size)]
        return pltpu.make_async_remote_copy(
            src_ref=rows,
            dst_ref=rows,
            send_sem=self.sends.at[stage],
            recv_sem=self.recvs.at[stage],
            device_id={"dp": self.place + bit - 2 * bit * place_bit(self.place, bit)},
            device_id_type=pl.DeviceIdType.MESH,
        )

    def start(self):
        self.packs[self.slot, self.side] = self.own[...]
        self.cross().start()

    def advance(self, stage):
        (self.cross() if stage == 0 else self.copy(stage - 1)).wait_recv()
        self.copy(stage).start()

    def finish(self):
        self.copy(self.stages - 1).wait_recv()
        self.cross().wait_send()
        for stage in range(self.stages):
            self.copy(stage).wait_send()


class SmallGrads:
    def __init__(
        self, images, pieces, table_rows, ring, ada, ada_s, part_s, silu_own, silu_got, sems
    ):
        self.images, self.pieces, self.table_rows = images, pieces, table_rows
        self.ring, self.ada, self.ada_s, self.part_s = ring, ada, ada_s, part_s
        self.silu_own, self.silu_got, self.sems = silu_own, silu_got, sems
        self.rows = ring.packs.shape[2]
        self.first_cond = images * pieces

    def row_of(self, shape, axis):
        return lax.broadcasted_iota(jnp.int32, shape, axis) & (self.rows - 1)

    def any_image(self, test):
        found = test(0)
        for image in range(1, self.images):
            found = jnp.logical_or(found, test(image))
        return found

    def of_piece(self, row, piece):
        return self.any_image(lambda image: row == image * self.pieces + piece)

    def piece(self, index):
        width = self.ada_s.shape[1]
        return pltpu.make_async_copy(
            self.ada.at[:, index * width : (index + 1) * width], self.ada_s, self.sems.at[0]
        )

    def exchange(self):
        return pltpu.make_async_remote_copy(
            src_ref=self.silu_own.at[1],
            dst_ref=self.silu_got,
            send_sem=self.sems.at[1],
            recv_sem=self.sems.at[2],
            device_id={"mp": 1 - self.ring.side},
            device_id_type=pl.DeviceIdType.MESH,
        )

    def add_piece(self, index):
        mine = self.ring.packs[self.ring.slot]
        mine = mine.reshape(2 * self.rows, mine.shape[-1]).astype(F32)
        masked = jnp.where(self.of_piece(self.row_of(mine.shape, 0), index), mine, 0.0)
        self.piece(index).wait()
        product = nt(masked.astype(BF), self.ada_s[...])
        if index:
            self.part_s[...] += product
        else:
            self.part_s[...] = product
        if index + 1 < self.pieces:
            self.piece(index + 1).start()
            return
        for k, side in enumerate((self.ring.side, 1 - self.ring.side)):
            block = self.part_s[pl.ds(pl.multiple_of(side * self.rows, 8), self.rows), :]
            found = [
                jnp.sum(block[n * self.pieces : (n + 1) * self.pieces], axis=0, keepdims=True)
                for n in range(self.images)
            ]
            found.append(jnp.zeros((self.silu_got.shape[0] - self.images, block.shape[1]), F32))
            self.silu_own[k] = jnp.concatenate(found, axis=0).astype(BF)
        self.exchange().start()

    def reduce(self, ada_grad_ref, small_ref):
        group = 128 // (2 * self.rows)
        width, share = self.ada_s.shape[1], ada_grad_ref.shape[1]
        left, right = self.row_of((128, 128), 0), self.row_of((128, 128), 1)
        left_all = lax.broadcasted_iota(jnp.int32, (128, 128), 0)
        right_all = lax.broadcasted_iota(jnp.int32, (128, 128), 1)
        same = (left_all - left) == (right_all - right)
        spread = jnp.logical_and(
            same,
            self.any_image(
                lambda n: jnp.logical_and(
                    jnp.logical_and(left >= n * self.pieces, left < (n + 1) * self.pieces),
                    right == self.first_cond + n,
                )
            ),
        )
        spread = jnp.where(spread, 1.0, 0.0).astype(BF)
        line = lax.broadcasted_iota(jnp.int32, (16, 128), 0)
        at = self.row_of((16, 128), 1)
        chosen = jnp.logical_and(
            jnp.logical_and(line >= self.pieces, line < self.pieces + self.table_rows),
            at == line - self.pieces + self.first_cond + self.images,
        )
        for p in range(self.pieces):
            chosen = jnp.logical_or(chosen, jnp.logical_and(line == p, self.of_piece(at, p)))
        chosen = jnp.where(chosen, 1.0, 0.0).astype(BF)
        wanted = lax.broadcasted_iota(jnp.int32, (width, 128), 0) - self.ring.place * share
        lane = lax.broadcasted_iota(jnp.int32, (width, 128), 1)
        wanted = jnp.where(wanted == lane, 1.0, 0.0).astype(BF)
        ada_grad_ref[...] = jnp.zeros_like(ada_grad_ref)
        small_ref[...] = jnp.zeros_like(small_ref)

        def one(k, carry):
            block = self.ring.packs[pl.ds(k * group, group)].reshape(128, width)
            cond = nn(spread, nn(block, wanted).astype(BF))
            for p in range(self.pieces):
                mine = jnp.where(self.of_piece(left, p), cond, 0.0).astype(BF)
                ada_grad_ref[p] += tn(mine, block)[:share]
            small_ref[...] += nn(chosen, block)
            return carry

        lax.fori_loop(0, SUM_PLACES // group, one, 0)

    def finish(self, silu_ref):
        self.exchange().wait()
        silu_ref[...] = self.silu_own[0].astype(F32) + self.silu_got[...].astype(F32)


def attn_grads_kernel(
    images, pieces, table_rows, first_ref, dattn_hbm, dqkv_ref, att_hbm, pack_own_ref,
    pack_other_ref, ada_ref, sums_ref, ada_grad_ref, small_ref, silu_ref, first_t,
    dattn_t, own, other, land0, land1, land2, land3, land_other, land_cross,
    sends, recvs, packs, pack_sends, pack_recvs, ada_s, part_s, silu_own, silu_got, small_sems,
    dattn_ref, att_ref, load_sems,
):
    width = first_t.shape[0]
    tiles, _, columns = own.shape
    share = width // SUM_PLACES
    group = GroupSum(own, other, (land0, land1, land2, land3), land_other, land_cross, sends, recvs)
    ring = PackGather(pack_own_ref, pack_other_ref, packs, pack_sends, pack_recvs)
    load_dattn = pltpu.make_async_copy(dattn_hbm, dattn_ref, load_sems.at[0])
    load_att = pltpu.make_async_copy(att_hbm, att_ref, load_sems.at[1])
    load_dattn.start()
    load_att.start()
    barrier = pltpu.get_barrier_semaphore()
    small = SmallGrads(
        images, pieces, table_rows, ring, ada_ref, ada_s, part_s, silu_own, silu_got, small_sems
    )
    group.greet(barrier)
    ring.greet(barrier)
    pl.semaphore_wait(barrier, len(HALVING) + 2)
    ring.start()

    def turn(source, target):
        for at in range(0, source.shape[0], 512):
            target[:, at : at + 512] = source[at : at + 512, :].T

    turn(first_ref, first_t)
    half = width // 2

    def produce(s, left, right_ref, row):
        for buffer, offset, stage in ((other, right_ref.shape[0] // 2, 4), (own, 0, 0)):
            right = right_ref[pl.ds(pl.multiple_of(row + offset, 16), columns), :]
            for at in (0, half):
                store_by_owner(buffer, s, at, nt(left[at : at + half, :], right), share)
            group.copy(stage, s).start()

    def step(s, carry):
        @pl.when(s < tiles - 1)
        def _():
            produce(s, first_t, dqkv_ref, s * columns)

        @pl.when(s == tiles - 1)
        def _():
            produce(s, dattn_t, att_ref, 0)

        @pl.when(s < tiles)
        def _():
            group.add(4, s)
            group.cross(0, s).start()
            group.cross(1, s).start()

        @pl.when(s == 0)
        def _():
            small.piece(0).start()
            load_dattn.wait()
            turn(dattn_ref, dattn_t)
            load_att.wait()

        for stage in range(ring.stages):

            @pl.when(s == stage)
            def _():
                ring.advance(stage)

        for piece in range(pieces):

            @pl.when(s == 1 + piece)
            def _():
                small.add_piece(piece)

        @pl.when(s == ring.stages)
        def _():
            ring.finish()
            small.reduce(ada_grad_ref, small_ref)

        @pl.when(jnp.logical_and(s >= 1, s - 1 < tiles))
        def _():
            group.add(0, s - 1)
            group.add_cross(0, s - 1)
            group.copy(1, s - 1).start()
            group.add_cross(1, s - 1)

        for stage in (1, 2):
            tile = s - 1 - stage

            @pl.when(jnp.logical_and(tile >= 0, tile < tiles))
            def _():
                group.add(stage, tile)
                group.copy(stage + 1, tile).start()

        tile = s - 4

        @pl.when(tile >= 0)
        def _():
            sums_ref[tile] = group.total(3, tile)[2].astype(BF)

        return carry

    lax.fori_loop(0, tiles + 4, step, 0)
    small.finish(silu_ref)

    def finish(tile, carry):
        group.wait_sends(tile)
        return carry

    lax.fori_loop(0, tiles, finish, 0)


def can_sum_here(width, proj, inner):
    places = lax.axis_size("dp")
    return (
        places == SUM_PLACES
        and lax.axis_size("mp") == 2
        and width % (8 * places) == 0
        and proj == 3 * inner
        and inner % 32 == 0
    )


def attn_grads(first, dattn, dqkv, att, pack_own, pack_other, ada_weight, images, table_rows):
    width = first.shape[1]
    tiles, tile = 4, att.shape[0] // 2
    share = width // SUM_PLACES
    pieces = ada_weight.shape[1] // width
    vmem = pl.BlockSpec(memory_space=pltpu.VMEM)
    sums, ada_grad, small, silu = pl.pallas_call(
        functools.partial(attn_grads_kernel, images, pieces, table_rows),
        in_specs=[vmem, ANYWHERE, vmem, ANYWHERE, vmem, vmem, ANYWHERE],
        out_specs=[vmem] * 4,
        out_shape=[
            jax.ShapeDtypeStruct((tiles, 2 * share, tile), BF),
            jax.ShapeDtypeStruct((pieces, share, width), F32),
            jax.ShapeDtypeStruct((16, width), F32),
            jax.ShapeDtypeStruct((16, width), F32),
        ],
        scratch_shapes=[
            pltpu.VMEM((width, first.shape[0]), BF),
            pltpu.VMEM((width, dattn.shape[0]), BF),
            pltpu.VMEM((tiles, width, tile), BF),
            pltpu.VMEM((tiles, width, tile), BF),
            pltpu.VMEM((tiles, width // 2, tile), BF),
            pltpu.VMEM((tiles, width // 4, tile), BF),
            pltpu.VMEM((tiles, width // 8, tile), BF),
            pltpu.VMEM((tiles, width // 8, tile), BF),
            pltpu.VMEM((tiles, width // 2, tile), BF),
            pltpu.VMEM((tiles, width // 2, tile), BF),
            pltpu.SemaphoreType.DMA((7, tiles)),
            pltpu.SemaphoreType.DMA((7, tiles)),
            pltpu.VMEM((SUM_PLACES, 2) + pack_own.shape, BF),
            pltpu.SemaphoreType.DMA((SUM_PLACES.bit_length(),)),
            pltpu.SemaphoreType.DMA((SUM_PLACES.bit_length(),)),
            pltpu.VMEM((width, width), BF),
            pltpu.VMEM((2 * pack_own.shape[0], width), F32),
            pltpu.VMEM((2, 16, width), BF),
            pltpu.VMEM((16, width), BF),
            pltpu.SemaphoreType.DMA((3,)),
            pltpu.VMEM(dattn.shape, BF),
            pltpu.VMEM(att.shape, BF),
            pltpu.SemaphoreType.DMA((2,)),
        ],
        compiler_params=pltpu.CompilerParams(
            vmem_limit_bytes=VMEM_LIMIT, collective_id=1, has_side_effects=True
        ),
        cost_estimate=cost(1e7, 1e5),
    )(first, dattn, dqkv, att, pack_own, pack_other, ada_weight)
    here = place_bit(lax.axis_index("dp"), FINAL) * share
    mine = lax.dynamic_slice_in_dim(sums, here, share, 1)
    return (
        jnp.transpose(mine, (1, 0, 2)).reshape(share, -1),
        jnp.transpose(ada_grad, (1, 0, 2)).reshape(share, -1),
        small[:pieces].reshape(-1),
        small[pieces : pieces + table_rows, :BUCKETS],
        silu[:images],
    )


def shift_mp(value, steps):
    ways = lax.axis_size("mp")
    return lax.ppermute(value, "mp", [(i, (i - steps) % ways) for i in range(ways)])


def core_half(block):
    half = block.shape[0] // 2
    return lax.dynamic_slice_in_dim(block, (lax.axis_index("dp") % 2) * half, half, 0)


def near_halves(block, mine=None):
    mine = core_half(block) if mine is None else mine
    return [shift_mp(mine, steps) for steps in range(1, lax.axis_size("mp"))]


def with_far_halves(nears):
    places = lax.axis_size("dp")
    core = lax.axis_index("dp") % 2
    got = []
    for near in nears:
        half = near.shape[0]
        far = lax.ppermute(near, "dp", [(i, i ^ 1) for i in range(places)])
        whole = jnp.zeros((2 * half,) + near.shape[1:], near.dtype)
        whole = lax.dynamic_update_slice_in_dim(whole, near, core * half, 0)
        got.append(lax.dynamic_update_slice_in_dim(whole, far, (1 - core) * half, 0))
    return got


def gathered_parts(nears, own=None):
    half = nears[0].shape[0]
    layout, parts, base = [], [], 0
    if own is not None:
        layout, parts, base = [(0, 0, True)], [own], own.shape[0]
    if half % 16:
        return [(0, 0, True)], [jnp.concatenate(parts + with_far_halves(nears), axis=0)]
    places = lax.axis_size("dp")
    for near in nears:
        far = lax.ppermute(near, "dp", [(i, i ^ 1) for i in range(places)])
        layout += [(base, half, True), (base, half, False)]
        parts += [near, far]
        base += 2 * half
    return layout, parts


def after_own(gathered, own):
    layout, parts = gathered
    return [(0, 0, True)] + [(base + own.shape[0], half, near) for base, half, near in layout], [
        own
    ] + parts


def home(parts):
    total = parts[0].astype(F32)
    for steps in range(1, len(parts)):
        total = total + shift_mp(parts[steps], -steps).astype(F32)
    return total


def scatter_dp(part):
    return lax.psum_scatter(part, "dp", scatter_dimension=0, tiled=True)


def local(
    tokens, conditioning, kept_ids, ada_weight, ada_bias, attn_qkv, attn_out, mlp_up, mlp_down,
    rel_table, grad_out_kept, grad_out_full,
):
    ways = lax.axis_size("mp")
    place = lax.axis_index("mp")
    images_group = conditioning.shape[0]
    images = images_group // ways
    width = tokens.shape[1]
    keep = kept_ids.shape[1]
    padded = -(-keep // 64) * 64
    per_block = rel_table.shape[0]
    cols = ada_bias.shape[0]

    silu_cond = jax.nn.silu(conditioning.astype(F32)).astype(BF)
    columns = (jnp.dot(silu_cond, ada_weight, preferred_element_type=F32) + ada_bias).astype(BF)
    near_o = near_halves(attn_out)
    mod = lax.all_to_all(columns, "mp", split_axis=0, concat_axis=1, tiled=True)
    mod = jnp.pad(mod.astype(F32).reshape(images, 6, width), ((0, 0), (0, 2), (0, 0)))

    weight_own = jnp.transpose(attn_qkv.reshape(width, -1))
    tables = [rel_table] + [shift_mp(rel_table, s) for s in range(1, ways)]
    mod, tables, near_o, weight_sent = lax.optimization_barrier(
        (mod, tables, near_o, core_half(weight_own))
    )
    near_w = near_halves(weight_own, weight_sent)
    fetch = ways == 2 and lax.axis_size("dp") % 4 == 0 and mlp_up.shape[0] % 32 == 0
    fetch = fetch and mlp_down.shape[0] % 64 == 0
    bias = bias_whole(jnp.concatenate(tables, axis=0))

    own_kept = lax.dynamic_slice_in_dim(kept_ids, place * images, images, 0)
    own_kept = jnp.pad(own_kept, ((0, 0), (0, padded - keep)), constant_values=-1)
    pick = (own_kept[:, :, None] == jnp.arange(PATCHES, dtype=jnp.int32)).astype(BF)
    grads = jnp.concatenate(
        [
            grad_out_full.reshape(images, PATCHES, width),
            jnp.pad(
                grad_out_kept.reshape(images, keep, width), ((0, 0), (0, padded - keep), (0, 0))
            ),
        ],
        axis=1,
    )
    dmlp = (mod[:, 5:6] * grads.astype(F32)).astype(BF).reshape(-1, width)
    grads = grads.reshape(-1, width)

    own = own_heads(tokens, mod, pick, bias, weight_own, per_block)
    near_w, near_o, own = lax.optimization_barrier((near_w, near_o, own))
    first = own[0]
    weight_others = gathered_parts(near_w)
    weight = after_own(weight_others, weight_own)
    out_weight = gathered_parts(near_o, attn_out)
    cut = (mlp_up.shape[0] * 4 // 18) // 16 * 16
    qkv, att, lse, middle, second, branch, *near_up = forward(
        own, tokens, mod, pick, bias, weight_others, out_weight, per_block,
        mlp_up if fetch else None, cut,
    )
    (branch_mlp, dsecond, grads_own, *whole), tile_own = mlp(
        second, dmlp, mlp_up, mlp_down, None, (near_up[0], mlp_up, mlp_down) if fetch else None
    )
    if fetch:
        up_others, down_others = [whole[0]], [whole[1]]
    else:
        up_others = with_far_halves(near_halves(mlp_up))
        down_others = with_far_halves(near_halves(mlp_down))
    reduced = [scatter_dp(grads_own)]
    for up, down in zip(up_others, down_others):
        (branch_mlp, dsecond, grads_next), _ = mlp(
            second, dmlp, up, down, (branch_mlp, dsecond)
        )
        reduced.append(scatter_dp(grads_next))
    out_full, out_kept, dtok, dmod, dattn, dqkv, strips = backward(
        tokens, mod, pick, bias, qkv, lse, middle, branch, branch_mlp, dsecond, grads,
        weight, out_weight, per_block,
    )
    proj_block, out_block = weight_own.shape[0], attn_out.shape[0]
    dqkv, reduced[0] = lax.optimization_barrier((dqkv, reduced[0]))
    dtables = table_of_strips(strips)
    pieces = cols // width
    used = images * (pieces + 1) + per_block
    here = can_sum_here(width, dqkv.shape[0], att.shape[0]) and cols % width == 0
    here = here and used <= 32 and pieces + per_block <= 16 and pieces <= 3
    if here:
        own_cond_rows = lax.dynamic_slice_in_dim(silu_cond, place * images, images, 0)
        packs = []
        for steps in range(ways):
            at = (place + steps) % ways
            table = dtables[steps * per_block : (steps + 1) * per_block]
            pack = jnp.concatenate(
                [
                    lax.dynamic_slice_in_dim(dmod, at * pieces, pieces, 1)
                    .astype(BF)
                    .reshape(-1, width),
                    own_cond_rows,
                    jnp.pad(table, ((0, 0), (0, width - BUCKETS))).astype(BF),
                ],
                axis=0,
            )
            packs.append(jnp.pad(pack, ((0, 32 - used), (0, 0))))
        attn_total, grad_ada_weight, grad_ada_bias, dtable, grad_silu = attn_grads(
            first, dattn, dqkv, att, *packs, ada_weight, images, per_block
        )
    else:
        dweight = dot(first, dqkv, (0, 1)).astype(BF)
        dout_t = dot(dattn, att, (0, 1)).astype(BF)
        attn_sums = scatter_dp(jnp.concatenate([dweight, dout_t], axis=1))
        dmod_rows = dmod[:, :6].reshape(images, 6 * width)
        dcolumns = lax.all_to_all(dmod_rows, "mp", split_axis=1, concat_axis=0, tiled=True)
        dtable = home(list(jnp.split(dtables, ways, axis=0)))
        all_columns = lax.all_gather(dcolumns, "dp", axis=0, tiled=True)
        dtable = lax.psum(dtable, "dp")
        all_cond = lax.all_gather(silu_cond, "dp", axis=0, tiled=True).astype(F32)
        slice_width = width // lax.axis_size("dp")
        cond_slice = lax.dynamic_slice_in_dim(
            all_cond, lax.axis_index("dp") * slice_width, slice_width, 1
        )
        grad_ada_weight = lax.dot_general(
            cond_slice, all_columns, (((0,), (0,)), ((), ())), precision=PRECISE
        )
        grad_ada_bias = jnp.sum(all_columns, axis=0)
        dcolumns_high = dcolumns.astype(BF)
        dcolumns_low = (dcolumns - dcolumns_high.astype(F32)).astype(BF)
        silu_part = nt(jnp.concatenate([dcolumns_high, dcolumns_low], axis=0), ada_weight)
        silu_part = silu_part[:images_group] + silu_part[images_group:]
        shares = lax.all_to_all(
            silu_part.astype(BF).reshape(ways, images, width), "mp", split_axis=0, concat_axis=0,
            tiled=True,
        )
        grad_silu = jnp.sum(shares.astype(F32), axis=0)
        split = ways * proj_block
        attn_total = home(
            [
                jnp.concatenate(
                    [
                        attn_sums[:, j * proj_block : (j + 1) * proj_block],
                        attn_sums[:, split + j * out_block : split + (j + 1) * out_block],
                    ],
                    axis=1,
                )
                for j in range(ways)
            ]
        )
    mlp_grads = home(reduced)
    attn_total = attn_total.astype(F32)
    grad_up, grad_down_t = split_mlp_grads(mlp_grads, tile_own)
    grad_qkv = attn_total[:, :proj_block].reshape(-1, 3, proj_block // 3)
    grad_out = jnp.transpose(attn_total[:, proj_block:])

    own_cond = lax.dynamic_slice_in_dim(conditioning, place * images, images, 0).astype(F32)
    grad_cond = jax.vjp(jax.nn.silu, own_cond)[1](grad_silu)[0].astype(BF)

    out_kept = out_kept.reshape(images, padded, width)[:, :keep].reshape(-1, width)
    return (
        out_kept, out_full, dtok, grad_cond, grad_ada_weight, grad_ada_bias, grad_qkv, grad_out,
        grad_up, jnp.transpose(grad_down_t), dtable,
    )


def solution(mesh):
    both = P(("dp", "mp"), None)
    return jax.shard_map(
        local,
        mesh=mesh,
        in_specs=(
            both, P("dp", None), P("dp", None), P(None, "mp"), P("mp"), P(None, None, "mp"),
            P("mp", None), P(None, "mp"), P("mp", None), P("mp", None), both, both,
        ),
        out_specs=(
            both, both, both, both, P("dp", "mp"), P("mp"), P("dp", None, "mp"), P("mp", "dp"),
            P("dp", "mp"), P("mp", "dp"), P("mp", None),
        ),
        check_vma=False,
    )
```
